32 devices in a mesh: py: 8 (over y, x, core), pz: 4 (over z).
Axes of the slice: x: 2, y: 2, z: 4, core: 2. Of those that a mesh axis runs over, the one named last changes fastest.
Arguments:
- solution: float32 [64, 64, 512], P('py', 'pz'), may hold values from -6 to 6
- right_side: float32 [64, 64, 512], P('py', 'pz'), may hold values from -6 to 6
- span_index: int32 [64, 64, 512], P('py', 'pz'), may hold values from 0 to 7
- coef_table: float32 [8], replicated, may hold values from 0.5 to 2
- xaxis_bands: float32 [2, 7, 512], replicated, may hold values from -0.5 to 0.5
- yaxis_bands: float32 [2, 7, 64], P(None, None, 'py'), may hold values from -0.5 to 0.5
- zaxis_bands: float32 [2, 7, 64], P(None, None, 'pz'), may hold values from -0.5 to 0.5
- xaxis_vectors: float32 [512, 512], replicated, may hold values from -0.25 to 0.25
- yaxis_vectors: float32 [64, 64], replicated, may hold values from -0.75 to 0.75
- zaxis_vectors: float32 [64, 64], replicated, may hold values from -0.75 to 0.75
- xaxis_values: float32 [512], replicated, may hold values from 0.25 to 2
- yaxis_values: float32 [64], replicated, may hold values from 0.25 to 2
- zaxis_values: float32 [64], replicated, may hold values from 0.25 to 2
Outputs:
- updated: float32 [64, 64, 512], P('py', 'pz')
- residual: float32 [64, 64, 512], P('py', 'pz')
The draws below stay inside these ranges and needn't reach their ends.
All inputs are finite; a program needn't handle non-finite values.
Results may differ from the reference program's by a relative error of at most 0.0001.
Values sent between devices are 32-bit elements; how exact they have to be, the bound alone decides.
No kernel may reach another device: no remote copies, remote signals or barrier semaphores. Data moves between devices by JAX's collectives and lax.ppermute only.
A program may use at most 64 MiB of HBM per device.

```python
import math
import jax
import jax.numpy as jnp
from jax import lax

NX = 512
TABLE = 8
ITERS = 2
NY = 64
NZ = 64


def set_ends(drawn, own_key, smallest, high):
    index_at = [jax.random.randint(jax.random.fold_in(own_key, axis), (), 0, length) for axis, length in enumerate(drawn.shape)]
    widest = drawn.shape.index(max(drawn.shape))
    neighbour = index_at[:widest] + [(index_at[widest] + 1) % drawn.shape[widest]] + index_at[widest + 1:]
    return drawn.at[tuple(index_at)].set(smallest).at[tuple(neighbour)].set(high)


def steps_of(stream_key, shape, cuts, least, largest):
    factor_of = 1.0
    for position, parts in cuts:
        draws = jax.random.uniform(jax.random.fold_in(jax.random.fold_in(stream_key, 6), position), (parts,), jnp.float32, least / len(cuts), largest / len(cuts))
        factor_of = factor_of * jnp.repeat(jnp.exp(draws), shape[position] // parts).reshape((-1,) + (1,) * (len(shape) - 1 - position))
    return factor_of


def centred(stream_key, dims, spread, limit, split=(), dtype=jnp.bfloat16):
    array = jax.random.normal(stream_key, dims, jnp.float32) * spread
    if len(split) > 0:
        array = steps_of(stream_key, dims, split, -0.22, 0.18) * array
    return jnp.clip(array, min=-limit, max=limit).astype(dtype)


def setup_inputs(seed: int = 0) -> dict:
    arg_keys = jax.random.split(jax.random.key(seed), 14)
    return {
        "solution": centred(arg_keys[0], (NY, NZ, NX), 1.0, 6.0, ((0, 8), (1, 4)), jnp.float32),
        "right_side": centred(arg_keys[1], (NY, NZ, NX), 1.0, 6.0, ((0, 8), (1, 4)), jnp.float32),
        "span_index": set_ends(jax.random.randint(arg_keys[2], (NY, NZ, NX), 0, TABLE), jax.random.fold_in(arg_keys[2], 1), 0, TABLE - 1).astype(jnp.int32),
        "coef_table": jnp.clip(jnp.exp(jax.random.uniform(arg_keys[3], (TABLE,), jnp.float32, math.log(0.5), math.log(2.0))), 0.5, 2.0),
        "xaxis_bands": jnp.clip(jax.random.uniform(arg_keys[4], (2, 7, NX), jnp.float32, -0.5, 0.5), -0.5, 0.5),
        "yaxis_bands": jnp.clip(jax.random.uniform(arg_keys[5], (2, 7, NY), jnp.float32, -0.5, 0.5) * steps_of(arg_keys[5], (2, 7, NY), ((2, 8),), -0.4, 0.0), -0.5, 0.5),
        "zaxis_bands": jnp.clip(jax.random.uniform(arg_keys[6], (2, 7, NZ), jnp.float32, -0.5, 0.5) * steps_of(arg_keys[6], (2, 7, NZ), ((2, 4),), -0.4, 0.0), -0.5, 0.5),
        "xaxis_vectors": centred(arg_keys[7], (NX, NX), NX ** -0.5, 0.25, (), jnp.float32),
        "yaxis_vectors": centred(arg_keys[8], (NY, NY), NY ** -0.5, 0.75, (), jnp.float32),
        "zaxis_vectors": centred(arg_keys[9], (NZ, NZ), NZ ** -0.5, 0.75, (), jnp.float32),
        "xaxis_values": jnp.clip(jnp.exp(jax.random.uniform(arg_keys[10], (NX,), jnp.float32, math.log(0.25), math.log(2.0))), 0.25, 2.0),
        "yaxis_values": jnp.clip(jnp.exp(jax.random.uniform(arg_keys[11], (NY,), jnp.float32, math.log(0.25), math.log(2.0))), 0.25, 2.0),
        "zaxis_values": jnp.clip(jnp.exp(jax.random.uniform(arg_keys[12], (NZ,), jnp.float32, math.log(0.25), math.log(2.0))), 0.25, 2.0),
    }


HIGH = lax.Precision.HIGHEST


def band_padded(padded, bands, axis):
    length = padded.shape[axis] - 6
    layout = [1, 1, 1]
    layout[axis] = length
    summed = None
    for offset in range(7):
        contrib = bands[offset].reshape(layout) * lax.slice_in_dim(padded, offset, offset + length, axis=axis)
        summed = contrib if summed is None else summed + contrib
    return summed


def band_apply(field, bands, axis):
    widths = [(0, 0), (0, 0), (0, 0)]
    widths[axis] = (3, 3)
    return band_padded(jnp.pad(field, widths), bands, axis)


def operate(field, coefficient, xaxis_bands, yaxis_bands, zaxis_bands):
    weighted = coefficient * field
    mass_part = band_apply(weighted, zaxis_bands[1], 1)
    stiff_part = band_apply(weighted, zaxis_bands[0], 1)
    mass_mass = band_apply(mass_part, yaxis_bands[1], 0)
    stiff_mass = band_apply(mass_part, yaxis_bands[0], 0)
    mass_stiff = band_apply(stiff_part, yaxis_bands[1], 0)
    return coefficient * (band_apply(mass_mass, xaxis_bands[0], 2) + band_apply(stiff_mass + mass_stiff, xaxis_bands[1], 2))


def reference(solution, right_side, span_index, coef_table, xaxis_bands, yaxis_bands, zaxis_bands, xaxis_vectors, yaxis_vectors, zaxis_vectors, xaxis_values, yaxis_values, zaxis_values):
    coefficient = coef_table[span_index]
    denominator = yaxis_values[:, None, None] + zaxis_values[None, :, None] + xaxis_values[None, None, :]
    updated = solution
    residual = right_side
    for iteration in range(ITERS):
        residual = right_side - operate(updated, coefficient, xaxis_bands, yaxis_bands, zaxis_bands)
        spectral = jnp.einsum('yzi,ij->yzj', residual, xaxis_vectors, precision=HIGH)
        spectral = jnp.einsum('izx,ij->jzx', spectral, yaxis_vectors, precision=HIGH)
        spectral = jnp.einsum('yix,ij->yjx', spectral, zaxis_vectors, precision=HIGH)
        spectral = spectral / denominator
        spectral = jnp.einsum('yjx,ij->yix', spectral, zaxis_vectors, precision=HIGH)
        spectral = jnp.einsum('jzx,ij->izx', spectral, yaxis_vectors, precision=HIGH)
        spectral = jnp.einsum('yzj,ij->yzi', spectral, xaxis_vectors, precision=HIGH)
        updated = updated + spectral
    return updated, residual
```

```python
import jax
import jax.numpy as jnp
import numpy as np
from jax import lax
from jax.experimental import pallas as pl
from jax.experimental.pallas import tpu as pltpu
from jax.sharding import PartitionSpec as P

ITERS = 2
REACH = 3
HIGH = lax.Precision.HIGHEST
BOTH = ("py", "pz")
F32 = jnp.float32
BF16 = jnp.bfloat16
VMEM = pl.BlockSpec(memory_space=pltpu.VMEM)
SMEM = pl.BlockSpec(memory_space=pltpu.SMEM)


def up8(count):
    return -(-count // 8) * 8


def split(value):
    high = value.astype(BF16)
    return high, (value - high.astype(F32)).astype(BF16)


def mul(left, right):
    return lax.dot_general(left, right, (((1,), (0,)), ((), ())), preferred_element_type=F32)


def mul_t(left, right):
    return lax.dot_general(left, right, (((1,), (1,)), ((), ())), preferred_element_type=F32)


def call(kernel, outs, specs, flops, cost_bytes, scratch=()):
    return pl.pallas_call(
        kernel,
        out_shape=[jax.ShapeDtypeStruct(shape, dtype) for shape, dtype in outs],
        in_specs=specs,
        out_specs=[VMEM] * len(outs),
        scratch_shapes=list(scratch),
        compiler_params=pltpu.CompilerParams(vmem_limit_bytes=32 * 1024 * 1024),
        cost_estimate=pl.CostEstimate(flops=flops, bytes_accessed=cost_bytes, transcendentals=0),
    )


def store_z_rims(ly, lz, weighted, low_ref, high_ref):
    for y in range(ly):
        low_ref[y * REACH : (y + 1) * REACH, :] = weighted[y * lz : y * lz + REACH, :]
        high_ref[y * REACH : (y + 1) * REACH, :] = weighted[(y + 1) * lz - REACH : (y + 1) * lz, :]


def coefficient_kernel(ly, lz, table_ref, span_ref, field_ref, coef_ref, weighted_ref, low_ref, high_ref):
    span = span_ref[...]
    coef = jnp.full(span.shape, table_ref[0], F32)
    for entry in range(1, table_ref.shape[0]):
        coef = jnp.where(span == entry, table_ref[entry], coef)
    coef_ref[...] = coef
    weighted = coef * field_ref[...]
    weighted_ref[...] = weighted
    store_z_rims(ly, lz, weighted, low_ref, high_ref)


def y_rims_kernel(ly, lz, weighted_ref, zlow_ref, zhigh_ref, low_ref, high_ref):
    own, side = REACH * lz, REACH * REACH
    for ref, start, zstart in ((low_ref, 0, 0), (high_ref, (ly - REACH) * lz, (ly - REACH) * REACH)):
        ref[own:, :] = jnp.zeros((ref.shape[0] - own, ref.shape[1]), F32)
        ref[0:own, :] = weighted_ref[start : start + own, :]
        ref[own : own + side, :] = zlow_ref[zstart : zstart + side, :]
        ref[own + side : own + 2 * side, :] = zhigh_ref[zstart : zstart + side, :]


def point_columns(ly, lz):
    own = [(y, z) for y in range(ly) for z in range(lz)]
    below, above = range(-REACH, 0), range(REACH)
    zlow = [(y, z) for y in range(ly) for z in below]
    zhigh = [(y, lz + z) for y in range(ly) for z in above]
    sides = []
    for ys in (below, [ly + y for y in above]):
        rim = [(y, z) for y in ys for z in range(lz)]
        rim += [(y, z) for y in ys for z in below]
        rim += [(y, lz + z) for y in ys for z in above]
        sides += rim + [(1 << 20, 1 << 20)] * (up8(len(rim)) - len(rim))
    points = own + zlow + zhigh + sides
    points += [(1 << 20, 1 << 20)] * (-len(points) % 128)
    return np.array(points, np.int32).T.copy()


def stencil_kernel(ly, lz, ny, nz, place_ref, points_ref, ybands_ref, zbands_ref, high_ref, low_ref):
    count = ly * lz
    rows = lax.broadcasted_iota(jnp.int32, (count, 1), 0)
    yrow, zrow = lax.div(rows, lz), lax.rem(rows, lz)
    factors = []
    for bands_ref, length, row, column, first, whole in (
        (ybands_ref, ly, yrow, points_ref[0:1, :], place_ref[0] * ly, ny),
        (zbands_ref, lz, zrow, points_ref[1:2, :], place_ref[1] * lz, nz),
    ):
        pick = (lax.broadcasted_iota(jnp.int32, (count, length), 1) == row).astype(F32)
        spot = column + first
        inside = (spot >= 0) & (spot < whole)
        distance = jnp.where(inside, column, 1 << 20) - row
        for matrix in range(2):
            taps = lax.dot_general(
                pick, bands_ref[matrix], (((1,), (1,)), ((), ())), precision=HIGH, preferred_element_type=F32
            )
            dense = jnp.zeros(distance.shape, F32)
            for offset in range(2 * REACH + 1):
                dense = jnp.where(distance == offset - REACH, taps[:, offset : offset + 1], dense)
            factors.append(dense)
    ystiff, ymass, zstiff, zmass = factors
    for part, value in enumerate((ymass * zmass, ystiff * zmass + ymass * zstiff)):
        high, low = split(value)
        high_ref[part * count : (part + 1) * count, :] = high
        low_ref[part * count : (part + 1) * count, :] = low


def xvectors_kernel(vectors_ref, high_ref, low_ref):
    high, low = split(vectors_ref[...].T)
    high_ref[...] = high
    low_ref[...] = low


def yz_vectors_kernel(
    npy, npz, ly, lz, yvec_ref, yvec_t_ref, zvec_ref, zhigh_ref, zlow_ref, ydown_ref, yup_ref
):
    ny, nz = npy * ly, npz * lz
    twice = (lax.broadcasted_iota(jnp.int32, (nz, 2 * nz), 0)
             == lax.rem(lax.broadcasted_iota(jnp.int32, (nz, 2 * nz), 1), nz)).astype(F32)
    pair = lax.dot_general(zvec_ref[...], twice, (((1,), (0,)), ((), ())), precision=HIGH, preferred_element_type=F32)
    half = lax.broadcasted_iota(jnp.int32, pair.shape, 1) >= nz
    zhigh_ref[...] = jnp.zeros(zhigh_ref.shape, BF16)
    zlow_ref[...] = jnp.zeros(zlow_ref.shape, BF16)
    for parity in range(2):
        high, low = split(jnp.where(half == (parity == 1), pair, 0.0))
        for yl in range(parity, ly, 2):
            for block in range(npz):
                to = (pl.ds((block * ly + yl) * lz, lz), pl.ds(yl // 2 * 2 * nz, 2 * nz))
                zhigh_ref[to] = high[block * lz : (block + 1) * lz, :]
                zlow_ref[to] = low[block * lz : (block + 1) * lz, :]
    def y_of(p):
        spot = lax.div(p, npy)
        return lax.rem(p, npy) * ly + 2 * lax.rem(spot, ly // 2) + lax.div(spot, ly // 2)

    def four(array):
        high, low = split(array)
        late = lax.broadcasted_iota(jnp.int32, array.shape, 1) >= 2 * ny
        return jnp.where(late, low.astype(F32), high.astype(F32)).astype(BF16)

    lane = lax.broadcasted_iota(jnp.int32, (ny, 4 * ny), 1)
    row = lax.broadcasted_iota(jnp.int32, (ny, 4 * ny), 0)
    moved = (row == y_of(lax.rem(lane, ny))).astype(F32)
    down = lax.dot_general(yvec_t_ref[...], moved, (((1,), (0,)), ((), ())), precision=HIGH, preferred_element_type=F32)
    ydown_ref[...] = four(down)
    order = (lax.broadcasted_iota(jnp.int32, (ny, ny), 1)
             == y_of(lax.broadcasted_iota(jnp.int32, (ny, ny), 0))).astype(F32)
    sorted_rows = lax.dot_general(order, yvec_ref[...], (((1,), (0,)), ((), ())), precision=HIGH, preferred_element_type=F32)
    copies = (row == lax.rem(lane, ny)).astype(F32)
    up = lax.dot_general(sorted_rows, copies, (((1,), (0,)), ((), ())), precision=HIGH, preferred_element_type=F32)
    yup_ref[...] = four(up)


def residual_kernel(
    weighted_ref, zlow_ref, zhigh_ref, ylow_ref, yhigh_ref, high_ref, low_ref, coef_ref, right_ref, xbands_ref,
    vhigh_ref, vlow_ref, residual_ref, spectral_ref,
):
    count, nx = weighted_ref.shape
    pieces = [ref[...] for ref in (weighted_ref, zlow_ref, zhigh_ref, ylow_ref, yhigh_ref)]
    missing = high_ref.shape[1] - sum(piece.shape[0] for piece in pieces)
    if missing:
        pieces.append(jnp.zeros((missing, nx), F32))
    point_high, point_low = split(jnp.concatenate(pieces, axis=0))
    stencil = high_ref[...]
    both = mul(stencil, point_high) + mul(stencil, point_low) + mul(low_ref[...], point_high)
    mass, stiff = both[:count], both[count:]
    spot = lax.broadcasted_iota(jnp.int32, (1, nx), 1)
    applied = None
    for offset in range(2 * REACH + 1):
        move = offset - REACH
        inside = (spot - move >= 0) & (spot - move < nx)
        taps = []
        for matrix in range(2):
            band = xbands_ref[matrix, offset : offset + 1, :]
            band = pltpu.roll(band, move % nx, 1) if move else band
            taps.append(jnp.where(inside, band, 0.0))
        term = taps[0] * mass + taps[1] * stiff
        term = pltpu.roll(term, -move % nx, 1) if move else term
        applied = term if applied is None else applied + term
    residual = right_ref[...] - coef_ref[...] * applied
    residual_ref[...] = residual
    high, low = split(residual)
    vhigh = vhigh_ref[...]
    spectral_ref[...] = mul_t(vhigh, high) + mul_t(vhigh, low) + mul_t(vlow_ref[...], high)


def modes_kernel(
    npy, npz, part_ref, xvalues_ref, yvalues_ref, zvalues_ref, zhigh_ref, zlow_ref, ydown_ref, yup_ref, in_ref, out_ref
):
    count = in_ref.shape[0] // (npy * npz)
    lanes = in_ref.shape[1]
    nz = zvalues_ref.shape[1] // 2
    ny = yvalues_ref.shape[1]
    chunks = zhigh_ref.shape[1] // (2 * nz)
    rows = [
        jnp.concatenate([in_ref[pl.ds(b * count + j, npy, stride=npz * count), :] for b in range(npz)], axis=1)
        for j in range(count)
    ]
    high, low = split(jnp.concatenate(rows, axis=0))
    zhigh, zlow = zhigh_ref[...], zlow_ref[...]
    part = mul(high, zhigh) + mul(low, zhigh) + mul(high, zlow)
    late = lax.broadcasted_iota(jnp.int32, (npy, 2 * nz), 1) >= nz

    def swap(value):
        return pltpu.roll(value, nz, 1)

    def tile(array, j, c):
        return array[j * npy : (j + 1) * npy, c * 2 * nz : (c + 1) * 2 * nz]

    pairs = []
    for j in range(0, count, 2):
        first = [tile(part, j, c) for c in range(chunks)]
        second = [tile(part, j + 1, c) for c in range(chunks)]
        even = [jnp.where(late, swap(second[c]), first[c]) for c in range(chunks)]
        odd = [jnp.where(late, second[c], swap(first[c])) for c in range(chunks)]
        pairs.append(jnp.concatenate(even + odd, axis=0))
    stacked = jnp.concatenate(pairs, axis=1)

    def four(value):
        high, low = split(value)
        return jnp.concatenate([high, low, high, low], axis=0)

    modes = mul(ydown_ref[...], four(stacked))
    diagonal = lax.broadcasted_iota(jnp.int32, (ny, ny), 0) == lax.broadcasted_iota(jnp.int32, (ny, ny), 1)
    ycolumn = jnp.sum(jnp.where(diagonal, yvalues_ref[...], 0.0), axis=1, keepdims=True)
    yz = ycolumn + zvalues_ref[...]
    lane = lax.broadcasted_iota(jnp.int32, (1, 2 * nz), 1)
    first_mode = part_ref[0] * count
    parts = []
    for pair in range(count // 2):
        x = jnp.where(lane >= nz, xvalues_ref[first_mode + 2 * pair + 1], xvalues_ref[first_mode + 2 * pair])
        parts.append(modes[:, pair * 2 * nz : (pair + 1) * 2 * nz] / (yz + x))
    restored = mul(yup_ref[...], four(jnp.concatenate(parts, axis=1)))
    half = npy * chunks
    rows = []
    for pair in range(count // 2):
        block = restored[:, pair * 2 * nz : (pair + 1) * 2 * nz]
        even = [block[c * npy : (c + 1) * npy] for c in range(chunks)]
        odd = [block[half + c * npy : half + (c + 1) * npy] for c in range(chunks)]
        rows.append(jnp.concatenate([jnp.where(late, swap(odd[c]), even[c]) for c in range(chunks)], axis=1))
        rows.append(jnp.concatenate([jnp.where(late, odd[c], swap(even[c])) for c in range(chunks)], axis=1))
    high, low = split(jnp.concatenate(rows, axis=0))
    back = mul_t(high, zhigh) + mul_t(low, zhigh) + mul_t(high, zlow)
    for j in range(count):
        for b in range(npz):
            out_ref[pl.ds(b * count + j, npy, stride=npz * count), :] = back[
                j * npy : (j + 1) * npy, b * lanes : (b + 1) * lanes
            ]


def from_modes(spectral_ref, vhigh_ref, vlow_ref):
    high, low = split(spectral_ref[...].T)
    vhigh = vhigh_ref[...]
    return mul(high, vhigh) + mul(low, vhigh) + mul(high, vlow_ref[...])


def update_kernel(
    ly, lz, spectral_ref, vhigh_ref, vlow_ref, field_ref, coef_ref, updated_ref, weighted_ref, low_ref, high_ref
):
    updated = field_ref[...] + from_modes(spectral_ref, vhigh_ref, vlow_ref)
    updated_ref[...] = updated
    weighted = coef_ref[...] * updated
    weighted_ref[...] = weighted
    store_z_rims(ly, lz, weighted, low_ref, high_ref)


def last_update_kernel(spectral_ref, vhigh_ref, vlow_ref, field_ref, updated_ref):
    updated_ref[...] = field_ref[...] + from_modes(spectral_ref, vhigh_ref, vlow_ref)


def around(value, axis, step):
    count = lax.axis_size(axis)
    return lax.ppermute(value, axis, [(i, (i + step) % count) for i in range(count)])


def plain_modes(received, npy, npz, ly, lz, xvalues, yvalues, zvalues, yvectors, zvectors):
    count = received.shape[0] // (npy * npz)
    field = received.reshape(npy, npz, count, ly, lz).transpose(2, 0, 3, 1, 4).reshape(count, npy * ly, npz * lz)
    field = jnp.einsum("xyz,yj->xjz", field, yvectors, precision=HIGH)
    field = jnp.einsum("xyz,zk->xyk", field, zvectors, precision=HIGH)
    field = field / (yvalues[None, :, None] + zvalues[None, None, :] + xvalues[:, None, None])
    field = jnp.einsum("xjz,yj->xyz", field, yvectors, precision=HIGH)
    field = jnp.einsum("xyk,zk->xyz", field, zvectors, precision=HIGH)
    field = field.reshape(count, npy, ly, npz, lz).transpose(1, 3, 0, 2, 4)
    return field.reshape(npy * npz * count, ly * lz)


def shards(
    solution,
    right_side,
    span_index,
    coef_table,
    xaxis_bands,
    yaxis_bands,
    zaxis_bands,
    xaxis_vectors,
    yaxis_vectors,
    zaxis_vectors,
    xaxis_values,
    yaxis_values,
    zaxis_values,
):
    npy, npz = lax.axis_size("py"), lax.axis_size("pz")
    ly, lz, nx = solution.shape
    ny, nz = npy * ly, npz * lz
    count, devices = ly * lz, npy * npz
    modes = nx // devices
    place = jnp.stack([lax.axis_index("py"), lax.axis_index("pz")])
    part = lax.axis_index(BOTH)
    field = solution.reshape(count, nx)
    right = right_side.reshape(count, nx)
    block, zrim, yrim = (count, nx), (ly * REACH, nx), (up8(REACH * lz + 2 * REACH * REACH), nx)
    cell = count * nx * 4

    coef, weighted, zlow, zhigh = call(
        lambda *refs: coefficient_kernel(ly, lz, *refs),
        [(block, F32), (block, F32), (zrim, F32), (zrim, F32)],
        [SMEM, VMEM, VMEM], count * nx * 16, 4 * cell,
    )(coef_table, span_index.reshape(count, nx), field)

    points = point_columns(ly, lz)
    width = points.shape[1]
    shigh, slow = call(
        lambda *refs: stencil_kernel(ly, lz, ny, nz, *refs),
        [((2 * count, width), BF16)] * 2,
        [SMEM, VMEM, VMEM, VMEM], count * width * 60, 8 * count * width,
    )(place, jnp.asarray(points), yaxis_bands, zaxis_bands)
    vhigh, vlow = call(
        xvectors_kernel, [((nx, nx), BF16)] * 2, [VMEM], nx * nx * 40, 8 * nx * nx
    )(xaxis_vectors)

    fast = modes % 2 == 0 and npy % 8 == 0 and lz % 16 == 0 and ly % 2 == 0 and nz == 64 and ny % 8 == 0 and 4 * ny <= 256 and count == 128
    if fast:
        zmat, ymat = (npz * count, ly * nz), (ny, 4 * ny)
        tables = call(
            lambda *refs: yz_vectors_kernel(npy, npz, ly, lz, *refs),
            [(zmat, BF16), (zmat, BF16), (ymat, BF16), (ymat, BF16)],
            [VMEM] * 3, npz * count * ly * nz * 8, npz * count * ly * nz * 4,
        )(yaxis_vectors, yaxis_vectors.T, zaxis_vectors)
        yrow = yaxis_values.reshape(1, ny)
        zrow = jnp.concatenate([zaxis_values, zaxis_values]).reshape(1, 2 * nz)

        def precondition(received):
            return call(
                lambda *refs: modes_kernel(npy, npz, *refs),
                [((nx, count), F32)],
                [SMEM, SMEM] + [VMEM] * 7, 6 * 2 * count * nx * ly * nz, 2 * cell,
            )(part.reshape(1), xaxis_values, yrow, zrow, *tables, received)[0]
    else:
        xpart = lax.dynamic_slice_in_dim(xaxis_values, part * modes, modes)

        def precondition(received):
            return plain_modes(
                received, npy, npz, ly, lz, xpart, yaxis_values, zaxis_values, yaxis_vectors, zaxis_vectors
            )

    for iteration in range(ITERS):
        from_low, from_high = around(zhigh, "pz", 1), around(zlow, "pz", -1)
        ylow, yhigh = call(
            lambda *refs: y_rims_kernel(ly, lz, *refs),
            [(yrim, F32)] * 2, [VMEM] * 3, nx, 4 * nx * 4 * yrim[0],
        )(weighted, from_low, from_high)
        below, above = around(yhigh, "py", 1), around(ylow, "py", -1)
        residual, spectral = call(
            residual_kernel,
            [(block, F32), ((nx, count), F32)],
            [VMEM] * 12, 6 * count * nx * (nx + 2 * width), 5 * cell + 4 * nx * nx,
        )(weighted, from_low, from_high, below, above, shigh, slow, coef, right, xaxis_bands, vhigh, vlow)
        spectral = lax.all_to_all(spectral, BOTH, split_axis=0, concat_axis=0, tiled=True)
        spectral = precondition(spectral)
        spectral = lax.all_to_all(spectral, BOTH, split_axis=0, concat_axis=0, tiled=True)
        cost = (6 * count * nx * nx, 4 * cell + 4 * nx * nx)
        if iteration + 1 < ITERS:
            field, weighted, zlow, zhigh = call(
                lambda *refs: update_kernel(ly, lz, *refs),
                [(block, F32), (block, F32), (zrim, F32), (zrim, F32)], [VMEM] * 5, *cost,
            )(spectral, vhigh, vlow, field, coef)
        else:
            field = call(last_update_kernel, [(block, F32)], [VMEM] * 4, *cost)(spectral, vhigh, vlow, field)[0]
    return (field.reshape(solution.shape), residual.reshape(solution.shape))


def solution(mesh):
    return jax.shard_map(
        shards,
        mesh=mesh,
        in_specs=(
            P("py", "pz", None),
            P("py", "pz", None),
            P("py", "pz", None),
            P(),
            P(),
            P(None, None, "py"),
            P(None, None, "pz"),
            P(),
            P(),
            P(),
            P(),
            P(),
            P(),
        ),
        out_specs=(P("py", "pz", None), P("py", "pz", None)),
        check_vma=False,
    )
```

```python
import jax
import jax.numpy as jnp
import numpy as np
from jax import lax
from jax.experimental import pallas as pl
from jax.experimental.pallas import tpu as pltpu
from jax.sharding import PartitionSpec as P

ITERS = 2
REACH = 3
LANES = 128
HIGH = lax.Precision.HIGHEST
BOTH = ("py", "pz")
F32 = jnp.float32
BF16 = jnp.bfloat16
VMEM = pl.BlockSpec(memory_space=pltpu.VMEM)
HBM = pl.BlockSpec(memory_space=pltpu.HBM)
ANY = pl.BlockSpec(memory_space=pl.ANY)


def up8(count):
    return -(-count // 8) * 8


def split(value):
    high = value.astype(BF16)
    return high, (value - high.astype(F32)).astype(BF16)


def exact(left, right, sides=(1, 0)):
    return lax.dot_general(
        left, right, (((sides[0],), (sides[1],)), ((), ())), precision=HIGH, preferred_element_type=F32
    )


def fetch(pairs, sem):
    copies = [pltpu.make_async_copy(source, target, sem.at[i]) for i, (source, target) in enumerate(pairs)]
    for copy in copies:
        copy.start()
    for copy in copies:
        copy.wait()


def mul(left, right):
    return lax.dot_general(left, right, (((1,), (0,)), ((), ())), preferred_element_type=F32)


def mul_t(left, right):
    return lax.dot_general(left, right, (((1,), (1,)), ((), ())), preferred_element_type=F32)


def call(kernel, outs, specs, flops, cost_bytes, scratch=(), out_specs=None):
    return pl.pallas_call(
        kernel,
        out_shape=[jax.ShapeDtypeStruct(shape, dtype) for shape, dtype in outs],
        in_specs=specs,
        out_specs=out_specs or [VMEM] * len(outs),
        scratch_shapes=list(scratch),
        compiler_params=pltpu.CompilerParams(vmem_limit_bytes=32 * 1024 * 1024),
        cost_estimate=pl.CostEstimate(flops=flops, bytes_accessed=cost_bytes, transcendentals=0),
    )


def store_z_rims(ly, lz, weighted, low_ref, high_ref):
    for y in range(ly):
        low_ref[y * REACH : (y + 1) * REACH, :] = weighted[y * lz : y * lz + REACH, :]
        high_ref[y * REACH : (y + 1) * REACH, :] = weighted[(y + 1) * lz - REACH : (y + 1) * lz, :]


def coefficient_kernel(
    ly, lz, table_ref, span_ref, field_ref, coef_ref, weighted_ref, low_ref, high_ref, table, span, field, sem
):
    fetch(((table_ref, table), (span_ref, span), (field_ref, field)), sem)
    entries = [table[entry] for entry in range(table_ref.shape[0])]
    for start in range(0, span.shape[0], lz):
        rows = pl.ds(start, lz)
        index = span[rows, :]
        coef = jnp.full(index.shape, entries[0], F32)
        for entry in range(1, len(entries)):
            coef = jnp.where(index == entry, entries[entry], coef)
        coef_ref[rows, :] = coef
        weighted = coef * field[rows, :]
        weighted_ref[rows, :] = weighted
        rim = pl.ds(start // lz * REACH, REACH)
        low_ref[rim, :] = weighted[:REACH]
        high_ref[rim, :] = weighted[lz - REACH :]


def y_rims_kernel(ly, lz, weighted_ref, zlow_ref, zhigh_ref, _, low_ref, high_ref):
    own, side = REACH * lz, REACH * REACH
    for ref, start, zstart in ((low_ref, 0, 0), (high_ref, (ly - REACH) * lz, (ly - REACH) * REACH)):
        ref[own:, :] = jnp.zeros((ref.shape[0] - own, ref.shape[1]), F32)
        ref[0:own, :] = weighted_ref[start : start + own, :]
        ref[own : own + side, :] = zlow_ref[zstart : zstart + side, :]
        ref[own + side : own + 2 * side, :] = zhigh_ref[zstart : zstart + side, :]


def point_columns(ly, lz):
    own = [(y, z) for y in range(ly) for z in range(lz)]
    below, above = range(-REACH, 0), range(REACH)
    zlow = [(y, z) for y in range(ly) for z in below]
    zhigh = [(y, lz + z) for y in range(ly) for z in above]
    sides = []
    for ys in (below, [ly + y for y in above]):
        rim = [(y, z) for y in ys for z in range(lz)]
        rim += [(y, z) for y in ys for z in below]
        rim += [(y, lz + z) for y in ys for z in above]
        sides += rim + [(1 << 20, 1 << 20)] * (up8(len(rim)) - len(rim))
    points = own + zlow + zhigh + sides
    points += [(1 << 20, 1 << 20)] * (-len(points) % 128)
    return np.array(points, np.int32).T.copy()


def stencil_kernel(
    ly, lz, ny, nz, points_hbm, ybands_hbm, zbands_hbm, xbands_hbm, _, out_ref, taps_ref,
    points_ref, ybands_ref, zbands_ref, xbands_ref, sem,
):
    fetch(
        (
            (points_hbm, points_ref), (ybands_hbm, ybands_ref), (zbands_hbm, zbands_ref), (xbands_hbm, xbands_ref),
        ),
        sem,
    )
    count = ly * lz
    rows = lax.broadcasted_iota(jnp.int32, (count, 1), 0)
    yrow, zrow = lax.div(rows, lz), lax.rem(rows, lz)
    factors = []
    for bands_ref, length, row, column, first, whole in (
        (ybands_ref, ly, yrow, points_ref[0:1, :], lax.axis_index("py") * ly, ny),
        (zbands_ref, lz, zrow, points_ref[1:2, :], lax.axis_index("pz") * lz, nz),
    ):
        pick = (lax.broadcasted_iota(jnp.int32, (count, length), 1) == row).astype(F32)
        spot = column + first
        inside = (spot >= 0) & (spot < whole)
        distance = jnp.where(inside, column, 1 << 20) - row
        here = [distance == offset - REACH for offset in range(2 * REACH + 1)]
        for matrix in range(2):
            taps = exact(pick, bands_ref[:, matrix, :], (1, 1))
            dense = jnp.zeros(distance.shape, F32)
            for offset in range(2 * REACH + 1):
                dense = jnp.where(here[offset], taps[:, offset : offset + 1], dense)
            factors.append(dense)
    ystiff, ymass, zstiff, zmass = factors
    for part, value in enumerate((ymass * zmass, ystiff * zmass + ymass * zstiff)):
        high, low = split(value)
        out_ref[part * count : (part + 1) * count, :] = high
        out_ref[(part + 2) * count : (part + 3) * count, :] = low
    nx = xbands_ref.shape[2]
    lane = lax.broadcasted_iota(jnp.int32, (1, nx), 1)
    for offset in range(2 * REACH + 1):
        move = offset - REACH
        inside = (lane - move >= 0) & (lane - move < nx)
        for matrix in range(2):
            band = xbands_ref[offset, matrix : matrix + 1, :]
            band = pltpu.roll(band, move % nx, 1) if move else band
            taps_ref[2 * offset + matrix] = jnp.broadcast_to(jnp.where(inside, band, 0.0), (8, nx))


def xvectors_kernel(source, out_ref, held, sem):
    fetch(((source, held),), sem)
    high, low = split(held[...].T)
    out_ref[: high.shape[0], :] = high
    out_ref[high.shape[0] :, :] = low


def tables_kernel(
    npy, npz, ly, lz, xvec_hbm, yvec_hbm, zvec_hbm, xval_hbm, yval_hbm, zval_hbm, _,
    xout_ref, zhigh_ref, zlow_ref, ydown_ref, yup_ref, sums_ref,
    xvec_ref, yvec_ref, zvec_ref, xval_ref, yval_ref, zval_ref, sem,
):
    fetch(
        (
            (xvec_hbm, xvec_ref), (yvec_hbm, yvec_ref), (zvec_hbm, zvec_ref),
            (xval_hbm, xval_ref), (yval_hbm, yval_ref), (zval_hbm, zval_ref),
        ),
        sem,
    )
    ny, nz = npy * ly, npz * lz
    nx = xvec_ref.shape[0]
    high, low = split(xvec_ref[...].T)
    xout_ref[:nx, :] = high
    xout_ref[nx:, :] = low
    twice = (
        lax.broadcasted_iota(jnp.int32, (nz, 2 * nz), 0)
        == lax.rem(lax.broadcasted_iota(jnp.int32, (nz, 2 * nz), 1), nz)
    ).astype(F32)
    pair = exact(zvec_ref[...], twice)
    half = lax.broadcasted_iota(jnp.int32, pair.shape, 1) >= nz
    zhigh_ref[...] = jnp.zeros(zhigh_ref.shape, BF16)
    zlow_ref[...] = jnp.zeros(zlow_ref.shape, BF16)
    for parity in range(2):
        high, low = split(jnp.where(half == (parity == 1), pair, 0.0))
        for yl in range(parity, ly, 2):
            for block in range(npz):
                to = (pl.ds((block * ly + yl) * lz, lz), pl.ds(yl // 2 * 2 * nz, 2 * nz))
                zhigh_ref[to] = high[block * lz : (block + 1) * lz, :]
                zlow_ref[to] = low[block * lz : (block + 1) * lz, :]

    def y_of(p):
        spot = lax.div(p, npy)
        return lax.rem(p, npy) * ly + 2 * lax.rem(spot, ly // 2) + lax.div(spot, ly // 2)

    def four(array):
        high, low = split(array)
        late = lax.broadcasted_iota(jnp.int32, array.shape, 1) >= 2 * ny
        return jnp.where(late, low.astype(F32), high.astype(F32)).astype(BF16)

    lane = lax.broadcasted_iota(jnp.int32, (ny, 4 * ny), 1)
    row = lax.broadcasted_iota(jnp.int32, (ny, 4 * ny), 0)
    moved = (row == y_of(lax.rem(lane, ny))).astype(F32)
    ydown_ref[...] = four(exact(yvec_ref[...].T, moved))
    order = (
        lax.broadcasted_iota(jnp.int32, (ny, ny), 1) == y_of(lax.broadcasted_iota(jnp.int32, (ny, ny), 0))
    ).astype(F32)
    copies = (row == lax.rem(lane, ny)).astype(F32)
    yup_ref[...] = four(exact(exact(order, yvec_ref[...]), copies))
    square = (ny, ny)
    diagonal = lax.broadcasted_iota(jnp.int32, square, 0) == lax.broadcasted_iota(jnp.int32, square, 1)
    ycolumn = jnp.sum(jnp.where(diagonal, yval_ref[...], 0.0), axis=1, keepdims=True)
    yz = ycolumn + exact(jnp.broadcast_to(zval_ref[...], (8, nz)), twice)[0:1]
    late = lax.broadcasted_iota(jnp.int32, (1, 2 * nz), 1) >= nz
    modes = nx // (npy * npz)
    first = (lax.axis_index("py") * npz + lax.axis_index("pz")) * modes
    for mode in range(0, modes, 2):
        x = jnp.where(late, xval_ref[first + mode + 1], xval_ref[first + mode])
        sums_ref[:, mode * nz : (mode + 2) * nz] = yz + x


def residual_kernel(
    weighted_ref, zlow_ref, zhigh_ref, ylow_ref, yhigh_ref, stencil_ref, taps_ref, coef_ref, right_ref, vectors_ref,
    _, residual_ref, spectral_ref,
):
    count, nx = weighted_ref.shape
    pieces = [ref[...] for ref in (weighted_ref, zlow_ref, zhigh_ref, ylow_ref, yhigh_ref)]
    missing = stencil_ref.shape[1] - sum(piece.shape[0] for piece in pieces)
    if missing:
        pieces.append(jnp.zeros((missing, nx), F32))
    high, low = split(jnp.concatenate(pieces, axis=0))
    both = mul(stencil_ref[...], high)
    both = both[: 2 * count] + both[2 * count :] + mul(stencil_ref[: 2 * count, :], low)
    for start in range(0, count, 8):
        mass = both[start : start + 8]
        stiff = both[count + start : count + start + 8]
        applied = None
        for offset in range(2 * REACH + 1):
            move = offset - REACH
            term = taps_ref[2 * offset] * mass + taps_ref[2 * offset + 1] * stiff
            term = pltpu.roll(term, -move % nx, 1) if move else term
            applied = term if applied is None else applied + term
        rows = pl.ds(start, 8)
        residual_ref[rows, :] = right_ref[rows, :] - coef_ref[rows, :] * applied
    high, low = split(residual_ref[...])
    product = mul_t(vectors_ref[...], jnp.concatenate([high, low], axis=0))
    spectral_ref[...] = (product[:nx, :count] + product[:nx, count:]) + (product[nx:, :count] + product[nx:, count:])


def modes_kernel(npy, npz, zhigh_ref, zlow_ref, ydown_ref, yup_ref, sums_ref, in_ref, out_ref):
    count = in_ref.shape[0] // (npy * npz)
    lanes = in_ref.shape[1]
    nz = sums_ref.shape[1] // count
    chunks = zhigh_ref.shape[1] // (2 * nz)
    rows = [
        jnp.concatenate([in_ref[pl.ds(b * count + j, npy, stride=npz * count), :] for b in range(npz)], axis=1)
        for j in range(count)
    ]
    zhigh, zlow = zhigh_ref[...], zlow_ref[...]

    def three(value, product):
        high, low = split(value)
        both = product(jnp.concatenate([high, low], axis=0), zhigh)
        return both[: count * npy] + both[count * npy :] + product(high, zlow)

    part = three(jnp.concatenate(rows, axis=0), mul)
    late = lax.broadcasted_iota(jnp.int32, (npy, 2 * nz), 1) >= nz

    def swap(value):
        return pltpu.roll(value, nz, 1)

    def tile(array, j, c):
        return array[j * npy : (j + 1) * npy, c * 2 * nz : (c + 1) * 2 * nz]

    pairs = []
    for j in range(0, count, 2):
        first = [tile(part, j, c) for c in range(chunks)]
        second = [tile(part, j + 1, c) for c in range(chunks)]
        even = [jnp.where(late, swap(second[c]), first[c]) for c in range(chunks)]
        odd = [jnp.where(late, second[c], swap(first[c])) for c in range(chunks)]
        pairs.append(jnp.concatenate(even + odd, axis=0))
    stacked = jnp.concatenate(pairs, axis=1)

    def four(value):
        high, low = split(value)
        return jnp.concatenate([high, low, high, low], axis=0)

    modes = mul(ydown_ref[...], four(stacked)) / sums_ref[...]
    restored = mul(yup_ref[...], four(modes))
    half = npy * chunks
    rows = []
    for pair in range(count // 2):
        block = restored[:, pair * 2 * nz : (pair + 1) * 2 * nz]
        even = [block[c * npy : (c + 1) * npy] for c in range(chunks)]
        odd = [block[half + c * npy : half + (c + 1) * npy] for c in range(chunks)]
        rows.append(jnp.concatenate([jnp.where(late, swap(odd[c]), even[c]) for c in range(chunks)], axis=1))
        rows.append(jnp.concatenate([jnp.where(late, odd[c], swap(even[c])) for c in range(chunks)], axis=1))
    back = three(jnp.concatenate(rows, axis=0), mul_t)
    for j in range(count):
        for b in range(npz):
            out_ref[pl.ds(b * count + j, npy, stride=npz * count), :] = back[
                j * npy : (j + 1) * npy, b * lanes : (b + 1) * lanes
            ]


def from_modes(spectral_ref, vectors_ref):
    nx, count = spectral_ref.shape
    high, low = split(spectral_ref[...].T)
    both = mul(jnp.concatenate([high, low], axis=0), vectors_ref[:nx, :])
    return both[:count] + both[count:] + mul(high, vectors_ref[nx:, :])


def update_kernel(ly, lz, spectral_ref, vectors_ref, field_ref, coef_ref, updated_ref, weighted_ref, low_ref, high_ref):
    updated = field_ref[...] + from_modes(spectral_ref, vectors_ref)
    updated_ref[...] = updated
    weighted = coef_ref[...] * updated
    weighted_ref[...] = weighted
    store_z_rims(ly, lz, weighted, low_ref, high_ref)


def last_update_kernel(spectral_ref, vectors_ref, field_ref, residual_ref, updated_hbm, residual_hbm, held, sem):
    leaving = pltpu.make_async_copy(residual_ref, residual_hbm, sem.at[0])
    leaving.start()
    held[...] = field_ref[...] + from_modes(spectral_ref, vectors_ref)
    fetch(((held, updated_hbm),), sem.at[pl.ds(1, 1)])
    leaving.wait()


def around(value, axis, step):
    count = lax.axis_size(axis)
    return lax.ppermute(value, axis, [(i, (i + step) % count) for i in range(count)])


def plain_modes(received, npy, npz, ly, lz, xvalues, yvalues, zvalues, yvectors, zvectors):
    count = received.shape[0] // (npy * npz)
    field = received.reshape(npy, npz, count, ly, lz).transpose(2, 0, 3, 1, 4).reshape(count, npy * ly, npz * lz)
    field = jnp.einsum("xyz,yj->xjz", field, yvectors, precision=HIGH)
    field = jnp.einsum("xyz,zk->xyk", field, zvectors, precision=HIGH)
    field = field / (yvalues[None, :, None] + zvalues[None, None, :] + xvalues[:, None, None])
    field = jnp.einsum("xjz,yj->xyz", field, yvectors, precision=HIGH)
    field = jnp.einsum("xyk,zk->xyz", field, zvectors, precision=HIGH)
    field = field.reshape(count, npy, ly, npz, lz).transpose(1, 3, 0, 2, 4)
    return field.reshape(npy * npz * count, ly * lz)


def shards(
    solution,
    right_side,
    span_index,
    coef_table,
    xaxis_bands,
    yaxis_bands,
    zaxis_bands,
    xaxis_vectors,
    yaxis_vectors,
    zaxis_vectors,
    xaxis_values,
    yaxis_values,
    zaxis_values,
):
    npy, npz = lax.axis_size("py"), lax.axis_size("pz")
    ly, lz, nx = solution.shape
    ny, nz = npy * ly, npz * lz
    count, devices = ly * lz, npy * npz
    modes = nx // devices
    field = solution.reshape(count, nx)
    right = right_side.reshape(count, nx)
    block, zrim, yrim = (count, nx), (ly * REACH, nx), (up8(REACH * lz + 2 * REACH * REACH), nx)
    cell = count * nx * 4
    dma = pltpu.SemaphoreType.DMA

    coef, weighted, zlow, zhigh = call(
        lambda *refs: coefficient_kernel(ly, lz, *refs),
        [(block, F32), (block, F32), (zrim, F32), (zrim, F32)],
        [HBM] * 3, count * nx * 16, 4 * cell,
        [pltpu.SMEM(coef_table.shape, F32), pltpu.VMEM(block, jnp.int32), pltpu.VMEM(block, F32), dma((3,))],
    )(coef_table, span_index.reshape(count, nx), field)

    points = point_columns(ly, lz)
    width = points.shape[1]
    bands = [array.transpose(1, 0, 2) for array in (yaxis_bands, zaxis_bands, xaxis_bands)]
    stencil, taps = call(
        lambda *refs: stencil_kernel(ly, lz, ny, nz, *refs),
        [((4 * count, width), BF16), ((2 * (2 * REACH + 1), 8, nx), F32)],
        [HBM] * 4 + [ANY], count * width * 60, 8 * count * width,
        [pltpu.VMEM(points.shape, jnp.int32)] + [pltpu.VMEM(array.shape, F32) for array in bands] + [dma((4,))],
    )(jnp.asarray(points), *bands, zlow)

    fast = (
        modes % 2 == 0 and npy % 8 == 0 and lz % 16 == 0 and ly % 2 == 0
        and 2 * nz == LANES and 2 * ny == LANES and count == LANES and nx % LANES == 0
    )
    if fast:
        zmat, ymat = (npz * count, ly * nz), (ny, 4 * ny)
        vectors, *tables = call(
            lambda *refs: tables_kernel(npy, npz, ly, lz, *refs),
            [((2 * nx, nx), BF16), (zmat, BF16), (zmat, BF16), (ymat, BF16), (ymat, BF16), ((ny, modes * nz), F32)],
            [HBM] * 6 + [ANY], npz * count * ly * nz * 8, npz * count * ly * nz * 4,
            [pltpu.VMEM(array.shape, F32) for array in (xaxis_vectors, yaxis_vectors, zaxis_vectors)]
            + [pltpu.SMEM((nx,), F32), pltpu.VMEM((1, ny), F32), pltpu.VMEM((1, nz), F32), dma((6,))],
        )(
            xaxis_vectors, yaxis_vectors, zaxis_vectors, xaxis_values,
            yaxis_values.reshape(1, ny), zaxis_values.reshape(1, nz), taps,
        )

        def precondition(received):
            return call(
                lambda *refs: modes_kernel(npy, npz, *refs),
                [((nx, count), F32)], [VMEM] * 6, 6 * 2 * count * nx * ly * nz, 2 * cell,
            )(*tables, received)[0]
    else:
        tables = [taps]
        vectors = call(
            xvectors_kernel, [((2 * nx, nx), BF16)], [HBM], nx * nx * 40, 8 * nx * nx,
            [pltpu.VMEM((nx, nx), F32), dma((1,))],
        )(xaxis_vectors)[0]
        part = lax.axis_index(BOTH)
        xpart = lax.dynamic_slice_in_dim(xaxis_values, part * modes, modes)

        def precondition(received):
            return plain_modes(
                received, npy, npz, ly, lz, xpart, yaxis_values, zaxis_values, yaxis_vectors, zaxis_vectors
            )

    for iteration in range(ITERS):
        last = iteration + 1 == ITERS
        from_low, from_high = around(zhigh, "pz", 1), around(zlow, "pz", -1)
        ylow, yhigh = call(
            lambda *refs: y_rims_kernel(ly, lz, *refs),
            [(yrim, F32)] * 2, [VMEM] * 3 + [ANY], nx, 4 * nx * 4 * yrim[0],
        )(weighted, from_low, from_high, taps)
        below, above = around(yhigh, "py", 1), around(ylow, "py", -1)
        residual, spectral = call(
            residual_kernel,
            [(block, F32), ((nx, count), F32)],
            [VMEM] * 10 + [ANY], 6 * count * nx * (nx + 2 * width), 5 * cell + 4 * nx * nx,
        )(weighted, from_low, from_high, below, above, stencil, taps, coef, right, vectors, tables[0])
        spectral = lax.all_to_all(spectral, BOTH, split_axis=0, concat_axis=0, tiled=True)
        spectral = precondition(spectral)
        spectral = lax.all_to_all(spectral, BOTH, split_axis=0, concat_axis=0, tiled=True)
        cost = (6 * count * nx * nx, 4 * cell + 4 * nx * nx)
        if not last:
            field, weighted, zlow, zhigh = call(
                lambda *refs: update_kernel(ly, lz, *refs),
                [(block, F32), (block, F32), (zrim, F32), (zrim, F32)], [VMEM] * 4, *cost,
            )(spectral, vectors, field, coef)
        else:
            field, residual = call(
                last_update_kernel, [(block, F32), (block, F32)], [VMEM] * 4, *cost,
                [pltpu.VMEM(block, F32), dma((2,))], [HBM] * 2,
            )(spectral, vectors, field, residual)
    return (field.reshape(solution.shape), residual.reshape(solution.shape))


def solution(mesh):
    return jax.shard_map(
        shards,
        mesh=mesh,
        in_specs=(
            P("py", "pz", None),
            P("py", "pz", None),
            P("py", "pz", None),
            P(),
            P(),
            P(None, None, "py"),
            P(None, None, "pz"),
            P(),
            P(),
            P(),
            P(),
            P(),
            P(),
        ),
        out_specs=(P("py", "pz", None), P("py", "pz", None)),
        check_vma=False,
    )
```

```python
import jax
import jax.numpy as jnp
import numpy as np
from jax import lax
from jax.experimental import pallas as pl
from jax.experimental.pallas import tpu as pltpu
from jax.sharding import PartitionSpec as P

ITERS = 2
REACH = 3
LANES = 128
HIGH = lax.Precision.HIGHEST
BOTH = ("py", "pz")
F32 = jnp.float32
BF16 = jnp.bfloat16
VMEM = pl.BlockSpec(memory_space=pltpu.VMEM)
HBM = pl.BlockSpec(memory_space=pltpu.HBM)
ANY = pl.BlockSpec(memory_space=pl.ANY)


def up8(count):
    return -(-count // 8) * 8


def split(value):
    high = value.astype(BF16)
    return high, (value - high.astype(F32)).astype(BF16)


def exact(left, right, sides=(1, 0)):
    return lax.dot_general(
        left, right, (((sides[0],), (sides[1],)), ((), ())), precision=HIGH, preferred_element_type=F32
    )


def fetch(pairs, sem):
    copies = [pltpu.make_async_copy(source, target, sem.at[i]) for i, (source, target) in enumerate(pairs)]
    for copy in copies:
        copy.start()
    for copy in copies:
        copy.wait()


def in_hbm(*arrays):
    return [pltpu.with_memory_space_constraint(array, pltpu.HBM) for array in arrays]


def mul(left, right):
    return lax.dot_general(left, right, (((1,), (0,)), ((), ())), preferred_element_type=F32)


def mul_t(left, right):
    return lax.dot_general(left, right, (((1,), (1,)), ((), ())), preferred_element_type=F32)


def call(kernel, outs, specs, flops, cost_bytes, scratch=(), out_specs=None):
    return pl.pallas_call(
        kernel,
        out_shape=[jax.ShapeDtypeStruct(shape, dtype) for shape, dtype in outs],
        in_specs=specs,
        out_specs=out_specs or [VMEM] * len(outs),
        scratch_shapes=list(scratch),
        compiler_params=pltpu.CompilerParams(vmem_limit_bytes=32 * 1024 * 1024),
        cost_estimate=pl.CostEstimate(flops=flops, bytes_accessed=cost_bytes, transcendentals=0),
    )


def store_z_rims(ly, lz, weighted, low_ref, high_ref):
    for y in range(ly):
        low_ref[y * REACH : (y + 1) * REACH, :] = weighted[y * lz : y * lz + REACH, :]
        high_ref[y * REACH : (y + 1) * REACH, :] = weighted[(y + 1) * lz - REACH : (y + 1) * lz, :]


def coefficient_kernel(
    ly, lz, table_ref, span_ref, field_ref, coef_ref, weighted_ref, low_ref, high_ref, table, span, field, sem
):
    fetch(((table_ref, table), (span_ref, span), (field_ref, field)), sem)
    entries = [table[entry] for entry in range(table_ref.shape[0])]
    for start in range(0, span.shape[0], lz):
        rows = pl.ds(start, lz)
        index = span[rows, :]
        coef = jnp.full(index.shape, entries[0], F32)
        for entry in range(1, len(entries)):
            coef = jnp.where(index == entry, entries[entry], coef)
        coef_ref[rows, :] = coef
        weighted = coef * field[rows, :]
        weighted_ref[rows, :] = weighted
        rim = pl.ds(start // lz * REACH, REACH)
        low_ref[rim, :] = weighted[:REACH]
        high_ref[rim, :] = weighted[lz - REACH :]


def y_rims_kernel(ly, lz, weighted_ref, zlow_ref, zhigh_ref, _, low_ref, high_ref):
    own, side = REACH * lz, REACH * REACH
    for ref, start, zstart in ((low_ref, 0, 0), (high_ref, (ly - REACH) * lz, (ly - REACH) * REACH)):
        ref[own:, :] = jnp.zeros((ref.shape[0] - own, ref.shape[1]), F32)
        ref[0:own, :] = weighted_ref[start : start + own, :]
        ref[own : own + side, :] = zlow_ref[zstart : zstart + side, :]
        ref[own + side : own + 2 * side, :] = zhigh_ref[zstart : zstart + side, :]


def point_columns(ly, lz):
    own = [(y, z) for y in range(ly) for z in range(lz)]
    below, above = range(-REACH, 0), range(REACH)
    zlow = [(y, z) for y in range(ly) for z in below]
    zhigh = [(y, lz + z) for y in range(ly) for z in above]
    sides = []
    for ys in (below, [ly + y for y in above]):
        rim = [(y, z) for y in ys for z in range(lz)]
        rim += [(y, z) for y in ys for z in below]
        rim += [(y, lz + z) for y in ys for z in above]
        sides += rim + [(1 << 20, 1 << 20)] * (up8(len(rim)) - len(rim))
    points = own + zlow + zhigh + sides
    points += [(1 << 20, 1 << 20)] * (-len(points) % 128)
    return np.array(points, np.int32).T.copy()


def stencil_kernel(
    ly, lz, ny, nz, points_hbm, ybands_hbm, zbands_hbm, xbands_hbm, _, out_ref, taps_ref,
    points_ref, ybands_ref, zbands_ref, xbands_ref, sem,
):
    fetch(
        (
            (points_hbm, points_ref), (ybands_hbm, ybands_ref), (zbands_hbm, zbands_ref), (xbands_hbm, xbands_ref),
        ),
        sem,
    )
    count = ly * lz
    rows = lax.broadcasted_iota(jnp.int32, (count, 1), 0)
    yrow, zrow = lax.div(rows, lz), lax.rem(rows, lz)
    factors = []
    for bands_ref, length, row, column, first, whole in (
        (ybands_ref, ly, yrow, points_ref[0:1, :], lax.axis_index("py") * ly, ny),
        (zbands_ref, lz, zrow, points_ref[1:2, :], lax.axis_index("pz") * lz, nz),
    ):
        pick = (lax.broadcasted_iota(jnp.int32, (count, length), 1) == row).astype(F32)
        spot = column + first
        inside = (spot >= 0) & (spot < whole)
        distance = jnp.where(inside, column, 1 << 20) - row
        here = [distance == offset - REACH for offset in range(2 * REACH + 1)]
        for matrix in range(2):
            taps = exact(pick, bands_ref[:, matrix, :], (1, 1))
            dense = jnp.zeros(distance.shape, F32)
            for offset in range(2 * REACH + 1):
                dense = jnp.where(here[offset], taps[:, offset : offset + 1], dense)
            factors.append(dense)
    ystiff, ymass, zstiff, zmass = factors
    for part, value in enumerate((ymass * zmass, ystiff * zmass + ymass * zstiff)):
        high, low = split(value)
        out_ref[part * count : (part + 1) * count, :] = high
        out_ref[(part + 2) * count : (part + 3) * count, :] = low
    nx = xbands_ref.shape[2]
    lane = lax.broadcasted_iota(jnp.int32, (1, nx), 1)
    for offset in range(2 * REACH + 1):
        move = offset - REACH
        inside = (lane - move >= 0) & (lane - move < nx)
        for matrix in range(2):
            band = xbands_ref[offset, matrix : matrix + 1, :]
            band = pltpu.roll(band, move % nx, 1) if move else band
            taps_ref[2 * offset + matrix] = jnp.broadcast_to(jnp.where(inside, band, 0.0), (8, nx))


def xvectors_kernel(source, out_ref, held, sem):
    fetch(((source, held),), sem)
    high, low = split(held[...].T)
    out_ref[: high.shape[0], :] = high
    out_ref[high.shape[0] :, :] = low


def tables_kernel(
    npy, npz, ly, lz, xvec_hbm, yvec_hbm, zvec_hbm, xval_hbm, yval_hbm, zval_hbm, _,
    xout_ref, zhigh_ref, zlow_ref, ydown_ref, yup_ref, sums_ref,
    xvec_ref, yvec_ref, zvec_ref, xval_ref, yval_ref, zval_ref, sem,
):
    fetch(
        (
            (xvec_hbm, xvec_ref), (yvec_hbm, yvec_ref), (zvec_hbm, zvec_ref),
            (xval_hbm, xval_ref), (yval_hbm, yval_ref), (zval_hbm, zval_ref),
        ),
        sem,
    )
    ny, nz = npy * ly, npz * lz
    nx = xvec_ref.shape[0]
    high, low = split(xvec_ref[...].T)
    xout_ref[:nx, :] = high
    xout_ref[nx:, :] = low
    twice = (
        lax.broadcasted_iota(jnp.int32, (nz, 2 * nz), 0)
        == lax.rem(lax.broadcasted_iota(jnp.int32, (nz, 2 * nz), 1), nz)
    ).astype(F32)
    pair = exact(zvec_ref[...], twice)
    half = lax.broadcasted_iota(jnp.int32, pair.shape, 1) >= nz
    zhigh_ref[...] = jnp.zeros(zhigh_ref.shape, BF16)
    zlow_ref[...] = jnp.zeros(zlow_ref.shape, BF16)
    for parity in range(2):
        high, low = split(jnp.where(half == (parity == 1), pair, 0.0))
        for yl in range(parity, ly, 2):
            for block in range(npz):
                to = (pl.ds((block * ly + yl) * lz, lz), pl.ds(yl // 2 * 2 * nz, 2 * nz))
                zhigh_ref[to] = high[block * lz : (block + 1) * lz, :]
                zlow_ref[to] = low[block * lz : (block + 1) * lz, :]

    def y_of(p):
        spot = lax.div(p, npy)
        return lax.rem(p, npy) * ly + 2 * lax.rem(spot, ly // 2) + lax.div(spot, ly // 2)

    def four(array):
        high, low = split(array)
        late = lax.broadcasted_iota(jnp.int32, array.shape, 1) >= 2 * ny
        return jnp.where(late, low.astype(F32), high.astype(F32)).astype(BF16)

    lane = lax.broadcasted_iota(jnp.int32, (ny, 4 * ny), 1)
    row = lax.broadcasted_iota(jnp.int32, (ny, 4 * ny), 0)
    moved = (row == y_of(lax.rem(lane, ny))).astype(F32)
    ydown_ref[...] = four(exact(yvec_ref[...].T, moved))
    order = (
        lax.broadcasted_iota(jnp.int32, (ny, ny), 1) == y_of(lax.broadcasted_iota(jnp.int32, (ny, ny), 0))
    ).astype(F32)
    copies = (row == lax.rem(lane, ny)).astype(F32)
    yup_ref[...] = four(exact(exact(order, yvec_ref[...]), copies))
    square = (ny, ny)
    diagonal = lax.broadcasted_iota(jnp.int32, square, 0) == lax.broadcasted_iota(jnp.int32, square, 1)
    ycolumn = jnp.sum(jnp.where(diagonal, yval_ref[...], 0.0), axis=1, keepdims=True)
    yz = ycolumn + exact(jnp.broadcast_to(zval_ref[...], (8, nz)), twice)[0:1]
    late = lax.broadcasted_iota(jnp.int32, (1, 2 * nz), 1) >= nz
    modes = nx // (npy * npz)
    first = (lax.axis_index("py") * npz + lax.axis_index("pz")) * modes
    for mode in range(0, modes, 2):
        x = jnp.where(late, xval_ref[first + mode + 1], xval_ref[first + mode])
        sums_ref[:, mode * nz : (mode + 2) * nz] = yz + x


def residual_kernel(
    weighted_ref, zlow_ref, zhigh_ref, ylow_ref, yhigh_ref, stencil_ref, taps_ref, coef_ref, right_ref, vectors_ref,
    _, *results,
):
    residual_ref, spectral_ref = results if results[0].shape == right_ref.shape else results[::-1]
    count, nx = weighted_ref.shape
    pieces = [ref[...] for ref in (weighted_ref, zlow_ref, zhigh_ref, ylow_ref, yhigh_ref)]
    missing = stencil_ref.shape[1] - sum(piece.shape[0] for piece in pieces)
    if missing:
        pieces.append(jnp.zeros((missing, nx), F32))
    high, low = split(jnp.concatenate(pieces, axis=0))
    both = mul(stencil_ref[...], high)
    both = both[: 2 * count] + both[2 * count :] + mul(stencil_ref[: 2 * count, :], low)
    for start in range(0, count, 8):
        mass = both[start : start + 8]
        stiff = both[count + start : count + start + 8]
        applied = None
        for offset in range(2 * REACH + 1):
            move = offset - REACH
            term = taps_ref[2 * offset] * mass + taps_ref[2 * offset + 1] * stiff
            term = pltpu.roll(term, -move % nx, 1) if move else term
            applied = term if applied is None else applied + term
        rows = pl.ds(start, 8)
        residual_ref[rows, :] = right_ref[rows, :] - coef_ref[rows, :] * applied
    high, low = split(residual_ref[...])
    product = mul_t(vectors_ref[...], jnp.concatenate([high, low], axis=0))
    spectral_ref[...] = (product[:nx, :count] + product[:nx, count:]) + (product[nx:, :count] + product[nx:, count:])


def modes_kernel(npy, npz, zhigh_ref, zlow_ref, ydown_ref, yup_ref, sums_ref, in_ref, out_ref):
    count = in_ref.shape[0] // (npy * npz)
    lanes = in_ref.shape[1]
    nz = sums_ref.shape[1] // count
    chunks = zhigh_ref.shape[1] // (2 * nz)
    rows = [
        jnp.concatenate([in_ref[pl.ds(b * count + j, npy, stride=npz * count), :] for b in range(npz)], axis=1)
        for j in range(count)
    ]
    zhigh, zlow = zhigh_ref[...], zlow_ref[...]

    def three(value, product):
        high, low = split(value)
        both = product(jnp.concatenate([high, low], axis=0), zhigh)
        return both[: count * npy] + both[count * npy :] + product(high, zlow)

    part = three(jnp.concatenate(rows, axis=0), mul)
    late = lax.broadcasted_iota(jnp.int32, (npy, 2 * nz), 1) >= nz

    def swap(value):
        return pltpu.roll(value, nz, 1)

    def tile(array, j, c):
        return array[j * npy : (j + 1) * npy, c * 2 * nz : (c + 1) * 2 * nz]

    pairs = []
    for j in range(0, count, 2):
        first = [tile(part, j, c) for c in range(chunks)]
        second = [tile(part, j + 1, c) for c in range(chunks)]
        even = [jnp.where(late, swap(second[c]), first[c]) for c in range(chunks)]
        odd = [jnp.where(late, second[c], swap(first[c])) for c in range(chunks)]
        pairs.append(jnp.concatenate(even + odd, axis=0))
    stacked = jnp.concatenate(pairs, axis=1)

    def four(value):
        high, low = split(value)
        return jnp.concatenate([high, low, high, low], axis=0)

    modes = mul(ydown_ref[...], four(stacked)) / sums_ref[...]
    restored = mul(yup_ref[...], four(modes))
    half = npy * chunks
    rows = []
    for pair in range(count // 2):
        block = restored[:, pair * 2 * nz : (pair + 1) * 2 * nz]
        even = [block[c * npy : (c + 1) * npy] for c in range(chunks)]
        odd = [block[half + c * npy : half + (c + 1) * npy] for c in range(chunks)]
        rows.append(jnp.concatenate([jnp.where(late, swap(odd[c]), even[c]) for c in range(chunks)], axis=1))
        rows.append(jnp.concatenate([jnp.where(late, odd[c], swap(even[c])) for c in range(chunks)], axis=1))
    back = three(jnp.concatenate(rows, axis=0), mul_t)
    for j in range(count):
        for b in range(npz):
            out_ref[pl.ds(b * count + j, npy, stride=npz * count), :] = back[
                j * npy : (j + 1) * npy, b * lanes : (b + 1) * lanes
            ]


def from_modes(spectral_ref, vectors_ref):
    nx, count = spectral_ref.shape
    high, low = split(spectral_ref[...].T)
    both = mul(jnp.concatenate([high, low], axis=0), vectors_ref[:nx, :])
    return both[:count] + both[count:] + mul(high, vectors_ref[nx:, :])


def update_kernel(ly, lz, spectral_ref, vectors_ref, field_ref, coef_ref, updated_ref, weighted_ref, low_ref, high_ref):
    updated = field_ref[...] + from_modes(spectral_ref, vectors_ref)
    updated_ref[...] = updated
    weighted = coef_ref[...] * updated
    weighted_ref[...] = weighted
    store_z_rims(ly, lz, weighted, low_ref, high_ref)


def last_update_kernel(spectral_ref, vectors_ref, field_ref, residual_ref, updated_hbm, residual_hbm, held, sem):
    leaving = pltpu.make_async_copy(residual_ref, residual_hbm, sem.at[0])
    leaving.start()
    held[...] = field_ref[...] + from_modes(spectral_ref, vectors_ref)
    fetch(((held, updated_hbm),), sem.at[pl.ds(1, 1)])
    leaving.wait()


def around(value, axis, step):
    count = lax.axis_size(axis)
    return lax.ppermute(value, axis, [(i, (i + step) % count) for i in range(count)])


def plain_modes(received, npy, npz, ly, lz, xvalues, yvalues, zvalues, yvectors, zvectors):
    count = received.shape[0] // (npy * npz)
    field = received.reshape(npy, npz, count, ly, lz).transpose(2, 0, 3, 1, 4).reshape(count, npy * ly, npz * lz)
    field = jnp.einsum("xyz,yj->xjz", field, yvectors, precision=HIGH)
    field = jnp.einsum("xyz,zk->xyk", field, zvectors, precision=HIGH)
    field = field / (yvalues[None, :, None] + zvalues[None, None, :] + xvalues[:, None, None])
    field = jnp.einsum("xjz,yj->xyz", field, yvectors, precision=HIGH)
    field = jnp.einsum("xyk,zk->xyz", field, zvectors, precision=HIGH)
    field = field.reshape(count, npy, ly, npz, lz).transpose(1, 3, 0, 2, 4)
    return field.reshape(npy * npz * count, ly * lz)


def shards(
    solution,
    right_side,
    span_index,
    coef_table,
    xaxis_bands,
    yaxis_bands,
    zaxis_bands,
    xaxis_vectors,
    yaxis_vectors,
    zaxis_vectors,
    xaxis_values,
    yaxis_values,
    zaxis_values,
):
    npy, npz = lax.axis_size("py"), lax.axis_size("pz")
    ly, lz, nx = solution.shape
    ny, nz = npy * ly, npz * lz
    count, devices = ly * lz, npy * npz
    modes = nx // devices
    field = solution.reshape(count, nx)
    right = right_side.reshape(count, nx)
    block, zrim, yrim = (count, nx), (ly * REACH, nx), (up8(REACH * lz + 2 * REACH * REACH), nx)
    cell = count * nx * 4
    dma = pltpu.SemaphoreType.DMA

    coef, weighted, zlow, zhigh = call(
        lambda *refs: coefficient_kernel(ly, lz, *refs),
        [(block, F32), (block, F32), (zrim, F32), (zrim, F32)],
        [HBM] * 3, count * nx * 16, 4 * cell,
        [pltpu.SMEM(coef_table.shape, F32), pltpu.VMEM(block, jnp.int32), pltpu.VMEM(block, F32), dma((3,))],
    )(*in_hbm(coef_table, span_index.reshape(count, nx), field))

    points = point_columns(ly, lz)
    width = points.shape[1]
    bands = [array.transpose(1, 0, 2) for array in (yaxis_bands, zaxis_bands, xaxis_bands)]
    stencil, taps = call(
        lambda *refs: stencil_kernel(ly, lz, ny, nz, *refs),
        [((4 * count, width), BF16), ((2 * (2 * REACH + 1), 8, nx), F32)],
        [HBM] * 4 + [ANY], count * width * 60, 8 * count * width,
        [pltpu.VMEM(points.shape, jnp.int32)] + [pltpu.VMEM(array.shape, F32) for array in bands] + [dma((4,))],
    )(*in_hbm(jnp.asarray(points), *bands), zlow)

    fast = (
        modes % 2 == 0 and npy % 8 == 0 and lz % 16 == 0 and ly % 2 == 0
        and 2 * nz == LANES and 2 * ny == LANES and count == LANES and nx % LANES == 0
    )
    if fast:
        zmat, ymat = (npz * count, ly * nz), (ny, 4 * ny)
        vectors, *tables = call(
            lambda *refs: tables_kernel(npy, npz, ly, lz, *refs),
            [((2 * nx, nx), BF16), (zmat, BF16), (zmat, BF16), (ymat, BF16), (ymat, BF16), ((ny, modes * nz), F32)],
            [HBM] * 6 + [ANY], npz * count * ly * nz * 8, npz * count * ly * nz * 4,
            [pltpu.VMEM(array.shape, F32) for array in (xaxis_vectors, yaxis_vectors, zaxis_vectors)]
            + [pltpu.SMEM((nx,), F32), pltpu.VMEM((1, ny), F32), pltpu.VMEM((1, nz), F32), dma((6,))],
        )(
            *in_hbm(
                xaxis_vectors, yaxis_vectors, zaxis_vectors, xaxis_values,
                yaxis_values.reshape(1, ny), zaxis_values.reshape(1, nz),
            ),
            taps,
        )

        def precondition(received):
            return call(
                lambda *refs: modes_kernel(npy, npz, *refs),
                [((nx, count), F32)], [VMEM] * 6, 6 * 2 * count * nx * ly * nz, 2 * cell,
            )(*tables, received)[0]
    else:
        tables = [taps]
        vectors = call(
            xvectors_kernel, [((2 * nx, nx), BF16)], [HBM], nx * nx * 40, 8 * nx * nx,
            [pltpu.VMEM((nx, nx), F32), dma((1,))],
        )(*in_hbm(xaxis_vectors))[0]
        part = lax.axis_index(BOTH)
        xpart = lax.dynamic_slice_in_dim(xaxis_values, part * modes, modes)

        def precondition(received):
            return plain_modes(
                received, npy, npz, ly, lz, xpart, yaxis_values, zaxis_values, yaxis_vectors, zaxis_vectors
            )

    for iteration in range(ITERS):
        last = iteration + 1 == ITERS
        from_low, from_high = around(zhigh, "pz", 1), around(zlow, "pz", -1)
        ylow, yhigh = call(
            lambda *refs: y_rims_kernel(ly, lz, *refs),
            [(yrim, F32)] * 2, [VMEM] * 3 + [ANY], nx, 4 * nx * 4 * yrim[0],
        )(weighted, from_low, from_high, taps)
        below, above = around(yhigh, "py", 1), around(ylow, "py", -1)
        *residual, spectral = call(
            residual_kernel,
            [(block, F32)] * last + [((nx, count), F32)],
            [VMEM] * 10 + [ANY], 6 * count * nx * (nx + 2 * width), 5 * cell + 4 * nx * nx,
            [pltpu.VMEM(block, F32)] * (not last),
        )(weighted, from_low, from_high, below, above, stencil, taps, coef, right, vectors, tables[0])
        spectral = lax.all_to_all(spectral, BOTH, split_axis=0, concat_axis=0, tiled=True)
        spectral = precondition(spectral)
        spectral = lax.all_to_all(spectral, BOTH, split_axis=0, concat_axis=0, tiled=True)
        cost = (6 * count * nx * nx, 4 * cell + 4 * nx * nx)
        if not last:
            field, weighted, zlow, zhigh = call(
                lambda *refs: update_kernel(ly, lz, *refs),
                [(block, F32), (block, F32), (zrim, F32), (zrim, F32)], [VMEM] * 4, *cost,
            )(spectral, vectors, field, coef)
        else:
            field, residual = call(
                last_update_kernel, [(block, F32), (block, F32)], [VMEM] * 4, *cost,
                [pltpu.VMEM(block, F32), dma((2,))], [HBM] * 2,
            )(spectral, vectors, field, *residual)
    return (field.reshape(solution.shape), residual.reshape(solution.shape))


def solution(mesh):
    return jax.shard_map(
        shards,
        mesh=mesh,
        in_specs=(
            P("py", "pz", None),
            P("py", "pz", None),
            P("py", "pz", None),
            P(),
            P(),
            P(None, None, "py"),
            P(None, None, "pz"),
            P(),
            P(),
            P(),
            P(),
            P(),
            P(),
        ),
        out_specs=(P("py", "pz", None), P("py", "pz", None)),
        check_vma=False,
    )
```

```python
import jax
import jax.numpy as jnp
import numpy as np
from jax import lax
from jax.experimental import pallas as pl
from jax.experimental.pallas import tpu as pltpu
from jax.sharding import PartitionSpec as P

ITERS = 2
REACH = 3
LANES = 128
HIGH = lax.Precision.HIGHEST
BOTH = ("py", "pz")
F32 = jnp.float32
BF16 = jnp.bfloat16
VMEM = pl.BlockSpec(memory_space=pltpu.VMEM)
HBM = pl.BlockSpec(memory_space=pltpu.HBM)
ANY = pl.BlockSpec(memory_space=pl.ANY)


def up8(count):
    return -(-count // 8) * 8


def split(value):
    high = value.astype(BF16)
    return high, (value - high.astype(F32)).astype(BF16)


def exact(left, right, sides=(1, 0)):
    return lax.dot_general(
        left, right, (((sides[0],), (sides[1],)), ((), ())), precision=HIGH, preferred_element_type=F32
    )


def fetch(pairs, sem):
    copies = [pltpu.make_async_copy(source, target, sem.at[i]) for i, (source, target) in enumerate(pairs)]
    for copy in copies:
        copy.start()
    for copy in copies:
        copy.wait()


def in_hbm(*arrays):
    return [pltpu.with_memory_space_constraint(array, pltpu.HBM) for array in arrays]


def mul(left, right):
    return lax.dot_general(left, right, (((1,), (0,)), ((), ())), preferred_element_type=F32)


def mul_t(left, right):
    return lax.dot_general(left, right, (((1,), (1,)), ((), ())), preferred_element_type=F32)


def call(kernel, outs, specs, flops, cost_bytes, scratch=(), out_specs=None):
    return pl.pallas_call(
        kernel,
        out_shape=[jax.ShapeDtypeStruct(shape, dtype) for shape, dtype in outs],
        in_specs=specs,
        out_specs=out_specs or [VMEM] * len(outs),
        scratch_shapes=list(scratch),
        compiler_params=pltpu.CompilerParams(vmem_limit_bytes=32 * 1024 * 1024),
        cost_estimate=pl.CostEstimate(flops=flops, bytes_accessed=cost_bytes, transcendentals=0),
    )


def store_z_rims(ly, lz, weighted, low_ref, high_ref):
    for y in range(ly):
        low_ref[y * REACH : (y + 1) * REACH, :] = weighted[y * lz : y * lz + REACH, :]
        high_ref[y * REACH : (y + 1) * REACH, :] = weighted[(y + 1) * lz - REACH : (y + 1) * lz, :]


def coefficient_kernel(
    ly, lz, table_ref, span_ref, field_ref, coef_ref, weighted_ref, even_ref, odd_ref, table, span, field, sem
):
    fetch(((table_ref, table), (span_ref, span), (field_ref, field)), sem)
    first = lax.rem(lax.axis_index("pz"), 2) == 0
    half = ly * REACH
    entries = [table[entry] for entry in range(table_ref.shape[0])]
    for start in range(0, span.shape[0], lz):
        rows = pl.ds(start, lz)
        index = span[rows, :]
        coef = jnp.full(index.shape, entries[0], F32)
        for entry in range(1, len(entries)):
            coef = jnp.where(index == entry, entries[entry], coef)
        coef_ref[rows, :] = coef
        weighted = coef * field[rows, :]
        weighted_ref[rows, :] = weighted
        for value, at in ((weighted, 0), (coef, half)):
            rim = pl.ds(at + start // lz * REACH, REACH)
            low, high = value[:REACH], value[lz - REACH :]
            even_ref[rim, :] = jnp.where(first, high, low)
            odd_ref[rim, :] = jnp.where(first, low, high)


def store_y_rims(ly, lz, weighted_ref, zlow, zhigh, low_ref, high_ref):
    own, side = REACH * lz, REACH * REACH
    for ref, start, zstart in ((low_ref, 0, 0), (high_ref, (ly - REACH) * lz, (ly - REACH) * REACH)):
        ref[own:, :] = jnp.zeros((ref.shape[0] - own, ref.shape[1]), F32)
        ref[0:own, :] = weighted_ref[start : start + own, :]
        ref[own : own + side, :] = zlow[zstart : zstart + side, :]
        ref[own + side : own + 2 * side, :] = zhigh[zstart : zstart + side, :]


def y_rims_kernel(ly, lz, weighted_ref, even_ref, odd_ref, _, zlow_ref, zhigh_ref, low_ref, high_ref):
    first = lax.rem(lax.axis_index("pz"), 2) == 0
    zlow_ref[...] = jnp.where(first, odd_ref[...], even_ref[...])
    zhigh_ref[...] = jnp.where(first, even_ref[...], odd_ref[...])
    store_y_rims(ly, lz, weighted_ref, zlow_ref, zhigh_ref, low_ref, high_ref)


def next_y_rims_kernel(ly, lz, weighted_ref, zlow_ref, zhigh_ref, low_ref, high_ref):
    store_y_rims(ly, lz, weighted_ref, zlow_ref, zhigh_ref, low_ref, high_ref)


def point_columns(ly, lz):
    own = [(y, z) for y in range(ly) for z in range(lz)]
    below, above = range(-REACH, 0), range(REACH)
    zlow = [(y, z) for y in range(ly) for z in below]
    zhigh = [(y, lz + z) for y in range(ly) for z in above]
    sides = []
    for ys in (below, [ly + y for y in above]):
        rim = [(y, z) for y in ys for z in range(lz)]
        rim += [(y, z) for y in ys for z in below]
        rim += [(y, lz + z) for y in ys for z in above]
        sides += rim + [(1 << 20, 1 << 20)] * (up8(len(rim)) - len(rim))
    points = own + zlow + zhigh + sides
    points += [(1 << 20, 1 << 20)] * (-len(points) % 128)
    return np.array(points, np.int32).T.copy()


def stencil_kernel(
    ly, lz, ny, nz, points_hbm, ybands_hbm, zbands_hbm, xbands_hbm, _, out_ref, taps_ref,
    points_ref, ybands_ref, zbands_ref, xbands_ref, sem,
):
    fetch(
        (
            (points_hbm, points_ref), (ybands_hbm, ybands_ref), (zbands_hbm, zbands_ref), (xbands_hbm, xbands_ref),
        ),
        sem,
    )
    count = ly * lz
    rows = lax.broadcasted_iota(jnp.int32, (count, 1), 0)
    yrow, zrow = lax.div(rows, lz), lax.rem(rows, lz)
    factors = []
    for bands_ref, length, row, column, first, whole in (
        (ybands_ref, ly, yrow, points_ref[0:1, :], lax.axis_index("py") * ly, ny),
        (zbands_ref, lz, zrow, points_ref[1:2, :], lax.axis_index("pz") * lz, nz),
    ):
        pick = (lax.broadcasted_iota(jnp.int32, (count, length), 1) == row).astype(F32)
        spot = column + first
        inside = (spot >= 0) & (spot < whole)
        distance = jnp.where(inside, column, 1 << 20) - row
        here = [distance == offset - REACH for offset in range(2 * REACH + 1)]
        for matrix in range(2):
            taps = exact(pick, bands_ref[:, matrix, :], (1, 1))
            dense = jnp.zeros(distance.shape, F32)
            for offset in range(2 * REACH + 1):
                dense = jnp.where(here[offset], taps[:, offset : offset + 1], dense)
            factors.append(dense)
    ystiff, ymass, zstiff, zmass = factors
    for part, value in enumerate((ymass * zmass, ystiff * zmass + ymass * zstiff)):
        high, low = split(value)
        out_ref[part * count : (part + 1) * count, :] = high
        out_ref[(part + 2) * count : (part + 3) * count, :] = low
    nx = xbands_ref.shape[2]
    lane = lax.broadcasted_iota(jnp.int32, (1, nx), 1)
    for offset in range(2 * REACH + 1):
        move = offset - REACH
        inside = (lane - move >= 0) & (lane - move < nx)
        for matrix in range(2):
            band = xbands_ref[offset, matrix : matrix + 1, :]
            band = pltpu.roll(band, move % nx, 1) if move else band
            taps_ref[2 * offset + matrix] = jnp.broadcast_to(jnp.where(inside, band, 0.0), (8, nx))


def xvectors_kernel(source, out_ref, held, sem):
    fetch(((source, held),), sem)
    high, low = split(held[...].T)
    out_ref[: high.shape[0], :] = high
    out_ref[high.shape[0] :, :] = low


def tables_kernel(
    npy, npz, ly, lz, xvec_hbm, yvec_hbm, zvec_hbm, xval_hbm, yval_hbm, zval_hbm, _,
    xout_ref, zhigh_ref, zlow_ref, ydown_ref, yup_ref, sums_ref, rimhigh_ref, rimlow_ref,
    xvec_ref, yvec_ref, zvec_ref, xval_ref, yval_ref, zval_ref, sem,
):
    fetch(
        (
            (xvec_hbm, xvec_ref), (yvec_hbm, yvec_ref), (zvec_hbm, zvec_ref),
            (xval_hbm, xval_ref), (yval_hbm, yval_ref), (zval_hbm, zval_ref),
        ),
        sem,
    )
    ny, nz = npy * ly, npz * lz
    nx = xvec_ref.shape[0]
    high, low = split(xvec_ref[...].T)
    xout_ref[:nx, :] = high
    xout_ref[nx:, :] = low
    twice = (
        lax.broadcasted_iota(jnp.int32, (nz, 2 * nz), 0)
        == lax.rem(lax.broadcasted_iota(jnp.int32, (nz, 2 * nz), 1), nz)
    ).astype(F32)
    pair = exact(zvec_ref[...], twice)
    half = lax.broadcasted_iota(jnp.int32, pair.shape, 1) >= nz
    zhigh_ref[...] = jnp.zeros(zhigh_ref.shape, BF16)
    zlow_ref[...] = jnp.zeros(zlow_ref.shape, BF16)
    for parity in range(2):
        high, low = split(jnp.where(half == (parity == 1), pair, 0.0))
        for yl in range(parity, ly, 2):
            for block in range(npz):
                to = (pl.ds((block * ly + yl) * lz, lz), pl.ds(yl // 2 * 2 * nz, 2 * nz))
                zhigh_ref[to] = high[block * lz : (block + 1) * lz, :]
                zlow_ref[to] = low[block * lz : (block + 1) * lz, :]

    shape = (rimhigh_ref.shape[0], 1)
    row = lax.broadcasted_iota(jnp.int32, shape, 0)
    block, spot = lax.div(row, LANES // 2), lax.rem(row, LANES // 2)
    above = spot >= ly * REACH
    spot = jnp.where(above, spot - ly * REACH, spot)
    yrow = jnp.where(spot < ly * REACH, lax.div(spot, REACH), 2 * ly)
    z = block * lz + lax.rem(spot, REACH) + jnp.where(above, lz, -REACH)
    rim = exact((lax.broadcasted_iota(jnp.int32, (shape[0], nz), 1) == z).astype(F32), pair)
    late = (lax.broadcasted_iota(jnp.int32, rim.shape, 1) >= nz).astype(jnp.int32)
    for chunk in range(ly // 2):
        columns = pl.ds(chunk * 2 * nz, 2 * nz)
        rimhigh_ref[:, columns], rimlow_ref[:, columns] = split(jnp.where(yrow - 2 * chunk == late, rim, 0.0))

    def y_of(p):
        spot = lax.div(p, npy)
        return lax.rem(p, npy) * ly + 2 * lax.rem(spot, ly // 2) + lax.div(spot, ly // 2)

    def four(array):
        high, low = split(array)
        late = lax.broadcasted_iota(jnp.int32, array.shape, 1) >= 2 * ny
        return jnp.where(late, low.astype(F32), high.astype(F32)).astype(BF16)

    lane = lax.broadcasted_iota(jnp.int32, (ny, 4 * ny), 1)
    row = lax.broadcasted_iota(jnp.int32, (ny, 4 * ny), 0)
    moved = (row == y_of(lax.rem(lane, ny))).astype(F32)
    ydown_ref[...] = four(exact(yvec_ref[...].T, moved))
    order = (
        lax.broadcasted_iota(jnp.int32, (ny, ny), 1) == y_of(lax.broadcasted_iota(jnp.int32, (ny, ny), 0))
    ).astype(F32)
    copies = (row == lax.rem(lane, ny)).astype(F32)
    yup_ref[...] = four(exact(exact(order, yvec_ref[...]), copies))
    square = (ny, ny)
    diagonal = lax.broadcasted_iota(jnp.int32, square, 0) == lax.broadcasted_iota(jnp.int32, square, 1)
    ycolumn = jnp.sum(jnp.where(diagonal, yval_ref[...], 0.0), axis=1, keepdims=True)
    yz = ycolumn + exact(jnp.broadcast_to(zval_ref[...], (8, nz)), twice)[0:1]
    late = lax.broadcasted_iota(jnp.int32, (1, 2 * nz), 1) >= nz
    modes = nx // (npy * npz)
    first = (lax.axis_index("py") * npz + lax.axis_index("pz")) * modes
    for mode in range(0, modes, 2):
        x = jnp.where(late, xval_ref[first + mode + 1], xval_ref[first + mode])
        sums_ref[:, mode * nz : (mode + 2) * nz] = yz + x


def residual_kernel(
    zrim, weighted_ref, zlow_ref, zhigh_ref, ylow_ref, yhigh_ref, stencil_ref, taps_ref, coef_ref, right_ref, vectors_ref,
    _, spectral_ref, residual_ref,
):
    count, nx = weighted_ref.shape
    pieces = [weighted_ref[...], zlow_ref[:zrim, :], zhigh_ref[:zrim, :], ylow_ref[...], yhigh_ref[...]]
    missing = stencil_ref.shape[1] - sum(piece.shape[0] for piece in pieces)
    if missing:
        pieces.append(jnp.zeros((missing, nx), F32))
    high, low = split(jnp.concatenate(pieces, axis=0))
    both = mul(stencil_ref[...], high)
    both = both[: 2 * count] + both[2 * count :] + mul(stencil_ref[: 2 * count, :], low)
    for start in range(0, count, 8):
        mass = both[start : start + 8]
        stiff = both[count + start : count + start + 8]
        applied = None
        for offset in range(2 * REACH + 1):
            move = offset - REACH
            term = taps_ref[2 * offset] * mass + taps_ref[2 * offset + 1] * stiff
            term = pltpu.roll(term, -move % nx, 1) if move else term
            applied = term if applied is None else applied + term
        rows = pl.ds(start, 8)
        residual_ref[rows, :] = right_ref[rows, :] - coef_ref[rows, :] * applied
    high, low = split(residual_ref[...])
    product = mul_t(vectors_ref[...], jnp.concatenate([high, low], axis=0))
    spectral_ref[...] = (product[:nx, :count] + product[:nx, count:]) + (product[nx:, :count] + product[nx:, count:])


def modes_kernel(npy, npz, rims, *refs):
    zhigh_ref, zlow_ref, ydown_ref, yup_ref, sums_ref, *rim_refs, in_ref, out_ref = refs
    count = in_ref.shape[0] // (npy * npz)
    lanes = in_ref.shape[1]
    nz = sums_ref.shape[1] // count
    chunks = zhigh_ref.shape[1] // (2 * nz)
    rows = [
        jnp.concatenate([in_ref[pl.ds(b * count + j, npy, stride=npz * count), :] for b in range(npz)], axis=1)
        for j in range(count)
    ]
    zhigh, zlow = zhigh_ref[...], zlow_ref[...]

    def three(value, product, whigh, wlow):
        high, low = split(value)
        both = product(jnp.concatenate([high, low], axis=0), whigh)
        return both[: count * npy] + both[count * npy :] + product(high, wlow)

    part = three(jnp.concatenate(rows, axis=0), mul, zhigh, zlow)
    late = lax.broadcasted_iota(jnp.int32, (npy, 2 * nz), 1) >= nz

    def swap(value):
        return pltpu.roll(value, nz, 1)

    def tile(array, j, c):
        return array[j * npy : (j + 1) * npy, c * 2 * nz : (c + 1) * 2 * nz]

    pairs = []
    for j in range(0, count, 2):
        first = [tile(part, j, c) for c in range(chunks)]
        second = [tile(part, j + 1, c) for c in range(chunks)]
        even = [jnp.where(late, swap(second[c]), first[c]) for c in range(chunks)]
        odd = [jnp.where(late, second[c], swap(first[c])) for c in range(chunks)]
        pairs.append(jnp.concatenate(even + odd, axis=0))
    stacked = jnp.concatenate(pairs, axis=1)

    def four(value):
        high, low = split(value)
        return jnp.concatenate([high, low, high, low], axis=0)

    modes = mul(ydown_ref[...], four(stacked)) / sums_ref[...]
    restored = mul(yup_ref[...], four(modes))
    half = npy * chunks
    rows = []
    for pair in range(count // 2):
        block = restored[:, pair * 2 * nz : (pair + 1) * 2 * nz]
        even = [block[c * npy : (c + 1) * npy] for c in range(chunks)]
        odd = [block[half + c * npy : half + (c + 1) * npy] for c in range(chunks)]
        rows.append(jnp.concatenate([jnp.where(late, swap(odd[c]), even[c]) for c in range(chunks)], axis=1))
        rows.append(jnp.concatenate([jnp.where(late, odd[c], swap(even[c])) for c in range(chunks)], axis=1))
    spectral = jnp.concatenate(rows, axis=0)
    back = three(spectral, mul_t, zhigh, zlow)
    size = out_ref.shape[0] // (npy * npz)
    for j in range(count):
        for b in range(npz):
            out_ref[pl.ds(b * size + j, npy, stride=npz * size), :] = back[
                j * npy : (j + 1) * npy, b * lanes : (b + 1) * lanes
            ]
    if rims:
        side = three(spectral, mul_t, rim_refs[0][...], rim_refs[1][...])
        for j in range(count // 2):
            for b in range(0, npz, 2):
                first, second = (
                    side[k * npy : (k + 1) * npy, b * lanes // 2 : b * lanes // 2 + lanes] for k in (j, j + count // 2)
                )
                at = b * size + count + j
                out_ref[pl.ds(at, npy, stride=npz * size), :] = jnp.where(late, swap(second), first)
                out_ref[pl.ds(at + size, npy, stride=npz * size), :] = jnp.where(late, second, swap(first))


def transformed(points, vectors_ref):
    rows, nx = points.shape
    high, low = split(points)
    both = mul(jnp.concatenate([high, low], axis=0), vectors_ref[:nx, :])
    return both[:rows] + both[rows:] + mul(high, vectors_ref[nx:, :])


def from_modes(spectral_ref, vectors_ref):
    return transformed(spectral_ref[...].T, vectors_ref)


def update_kernel(ly, lz, spectral_ref, vectors_ref, field_ref, coef_ref, updated_ref, weighted_ref, low_ref, high_ref):
    updated = field_ref[...] + from_modes(spectral_ref, vectors_ref)
    updated_ref[...] = updated
    weighted = coef_ref[...] * updated
    weighted_ref[...] = weighted
    store_z_rims(ly, lz, weighted, low_ref, high_ref)


def rim_update_kernel(
    ly, lz, devices, spectral_ref, vectors_ref, field_ref, coef_ref, before_low_ref, before_high_ref,
    updated_ref, weighted_ref, zlow_ref, zhigh_ref, low_ref, high_ref,
):
    nx = vectors_ref.shape[1]
    modes = nx // devices
    size = spectral_ref.shape[0] // devices
    own, rims = [], []
    for d in range(devices):
        own.append(spectral_ref[d * size : d * size + modes, :])
        rim = spectral_ref[d * size + modes : (d + 1) * size, :]
        rims += [rim, pltpu.roll(rim, LANES // 2, 1)]
    points = [jnp.concatenate(own, axis=0).T, jnp.concatenate(rims, axis=0).T[: LANES // 2]]
    update = transformed(jnp.concatenate(points, axis=0), vectors_ref)
    count, half = ly * lz, ly * REACH
    updated = field_ref[...] + update[:count]
    updated_ref[...] = updated
    weighted_ref[...] = coef_ref[...] * updated
    for side, (ref, before_ref) in enumerate(((zlow_ref, before_low_ref), (zhigh_ref, before_high_ref))):
        start = count + side * half
        ref[...] = before_ref[:half, :] + before_ref[half:, :] * update[start : start + half]
    store_y_rims(ly, lz, weighted_ref, zlow_ref, zhigh_ref, low_ref, high_ref)


def last_update_kernel(spectral_ref, vectors_ref, field_ref, residual_ref, updated_hbm, residual_hbm, held, sem):
    leaving = pltpu.make_async_copy(residual_ref, residual_hbm, sem.at[0])
    leaving.start()
    held[...] = field_ref[...] + from_modes(spectral_ref, vectors_ref)
    fetch(((held, updated_hbm),), sem.at[pl.ds(1, 1)])
    leaving.wait()


def pairwise(value, axis, odd):
    count = lax.axis_size(axis)
    other = [((i + odd) ^ 1) - odd for i in range(count)]
    return lax.ppermute(value, axis, [(i, j if 0 <= j < count else i) for i, j in enumerate(other)])


def around(value, axis, step):
    count = lax.axis_size(axis)
    return lax.ppermute(value, axis, [(i, (i + step) % count) for i in range(count)])


def plain_modes(received, npy, npz, ly, lz, xvalues, yvalues, zvalues, yvectors, zvectors):
    count = received.shape[0] // (npy * npz)
    field = received.reshape(npy, npz, count, ly, lz).transpose(2, 0, 3, 1, 4).reshape(count, npy * ly, npz * lz)
    field = jnp.einsum("xyz,yj->xjz", field, yvectors, precision=HIGH)
    field = jnp.einsum("xyz,zk->xyk", field, zvectors, precision=HIGH)
    field = field / (yvalues[None, :, None] + zvalues[None, None, :] + xvalues[:, None, None])
    field = jnp.einsum("xjz,yj->xyz", field, yvectors, precision=HIGH)
    field = jnp.einsum("xyk,zk->xyz", field, zvectors, precision=HIGH)
    field = field.reshape(count, npy, ly, npz, lz).transpose(1, 3, 0, 2, 4)
    return field.reshape(npy * npz * count, ly * lz)


def shards(
    solution,
    right_side,
    span_index,
    coef_table,
    xaxis_bands,
    yaxis_bands,
    zaxis_bands,
    xaxis_vectors,
    yaxis_vectors,
    zaxis_vectors,
    xaxis_values,
    yaxis_values,
    zaxis_values,
):
    npy, npz = lax.axis_size("py"), lax.axis_size("pz")
    ly, lz, nx = solution.shape
    ny, nz = npy * ly, npz * lz
    count, devices = ly * lz, npy * npz
    modes = nx // devices
    field = solution.reshape(count, nx)
    right = right_side.reshape(count, nx)
    block, zrim, yrim = (count, nx), (ly * REACH, nx), (up8(REACH * lz + 2 * REACH * REACH), nx)
    zrims = (2 * ly * REACH, nx)
    cell = count * nx * 4
    dma = pltpu.SemaphoreType.DMA

    coef, weighted, even, odd = call(
        lambda *refs: coefficient_kernel(ly, lz, *refs),
        [(block, F32), (block, F32), (zrims, F32), (zrims, F32)],
        [HBM] * 3, count * nx * 16, 4 * cell,
        [pltpu.SMEM(coef_table.shape, F32), pltpu.VMEM(block, jnp.int32), pltpu.VMEM(block, F32), dma((3,))],
    )(*in_hbm(coef_table, span_index.reshape(count, nx), field))

    points = point_columns(ly, lz)
    width = points.shape[1]
    bands = [array.transpose(1, 0, 2) for array in (yaxis_bands, zaxis_bands, xaxis_bands)]
    stencil, taps = call(
        lambda *refs: stencil_kernel(ly, lz, ny, nz, *refs),
        [((4 * count, width), BF16), ((2 * (2 * REACH + 1), 8, nx), F32)],
        [HBM] * 4 + [ANY], count * width * 60, 8 * count * width,
        [pltpu.VMEM(points.shape, jnp.int32)] + [pltpu.VMEM(array.shape, F32) for array in bands] + [dma((4,))],
    )(*in_hbm(jnp.asarray(points), *bands), even)

    fast = (
        modes % 16 == 0 and npz % 2 == 0 and 2 * ly * REACH <= LANES // 2 and npy % 8 == 0 and lz % 16 == 0 and ly % 2 == 0
        and 2 * nz == LANES and 2 * ny == LANES and count == LANES and nx % LANES == 0
    )
    if fast:
        zmat, ymat, rmat = (npz * count, ly * nz), (ny, 4 * ny), (npz * LANES // 2, ly * nz)
        vectors, *tables = call(
            lambda *refs: tables_kernel(npy, npz, ly, lz, *refs),
            [((2 * nx, nx), BF16), (zmat, BF16), (zmat, BF16), (ymat, BF16), (ymat, BF16), ((ny, modes * nz), F32)]
            + [(rmat, BF16)] * 2,
            [HBM] * 6 + [ANY], npz * count * ly * nz * 8, npz * count * ly * nz * 4,
            [pltpu.VMEM(array.shape, F32) for array in (xaxis_vectors, yaxis_vectors, zaxis_vectors)]
            + [pltpu.SMEM((nx,), F32), pltpu.VMEM((1, ny), F32), pltpu.VMEM((1, nz), F32), dma((6,))],
        )(
            *in_hbm(
                xaxis_vectors, yaxis_vectors, zaxis_vectors, xaxis_values,
                yaxis_values.reshape(1, ny), zaxis_values.reshape(1, nz),
            ),
            taps,
        )

        def precondition(received, rims):
            size = modes * 3 // 2 if rims else modes
            return call(
                lambda *refs: modes_kernel(npy, npz, rims, *refs),
                [((devices * size, count), F32)], [VMEM] * (8 if rims else 6), 6 * 2 * count * nx * ly * nz, 2 * cell,
            )(*(tables if rims else tables[:5]), received)[0]
    else:
        tables = [taps]
        vectors = call(
            xvectors_kernel, [((2 * nx, nx), BF16)], [HBM], nx * nx * 40, 8 * nx * nx,
            [pltpu.VMEM((nx, nx), F32), dma((1,))],
        )(*in_hbm(xaxis_vectors))[0]
        part = lax.axis_index(BOTH)
        xpart = lax.dynamic_slice_in_dim(xaxis_values, part * modes, modes)

        def precondition(received, rims):
            return plain_modes(
                received, npy, npz, ly, lz, xpart, yaxis_values, zaxis_values, yaxis_vectors, zaxis_vectors
            )

    even, odd = pairwise(even, "pz", 0), pairwise(odd, "pz", 1)
    zlow, zhigh, ylow, yhigh = call(
        lambda *refs: y_rims_kernel(ly, lz, *refs),
        [(zrims, F32)] * 2 + [(yrim, F32)] * 2, [VMEM] * 3 + [ANY], nx, 4 * nx * 4 * (yrim[0] + zrims[0]),
    )(weighted, even, odd, taps)
    for iteration in range(ITERS):
        last = iteration + 1 == ITERS
        below, above = around(yhigh, "py", 1), around(ylow, "py", -1)
        spectral, *residual = call(
            lambda *refs: residual_kernel(zrim[0], *refs),
            [((nx, count), F32)] + [(block, F32)] * last,
            [VMEM] * 10 + [ANY], 6 * count * nx * (nx + 2 * width), 5 * cell + 4 * nx * nx,
            [pltpu.VMEM(block, F32)] * (not last),
        )(weighted, zlow, zhigh, below, above, stencil, taps, coef, right, vectors, tables[0])
        spectral = lax.all_to_all(spectral, BOTH, split_axis=0, concat_axis=0, tiled=True)
        spectral = precondition(spectral, not last)
        spectral = lax.all_to_all(spectral, BOTH, split_axis=0, concat_axis=0, tiled=True)
        cost = (6 * count * nx * nx, 4 * cell + 4 * nx * nx)
        if last:
            field, residual = call(
                last_update_kernel, [(block, F32), (block, F32)], [VMEM] * 4, *cost,
                [pltpu.VMEM(block, F32), dma((2,))], [HBM] * 2,
            )(spectral, vectors, field, *residual)
        elif fast:
            field, weighted, zlow, zhigh, ylow, yhigh = call(
                lambda *refs: rim_update_kernel(ly, lz, devices, *refs),
                [(block, F32)] * 2 + [(zrim, F32)] * 2 + [(yrim, F32)] * 2, [VMEM] * 6, *cost,
            )(spectral, vectors, field, coef, zlow, zhigh)
        else:
            field, weighted, zlow, zhigh = call(
                lambda *refs: update_kernel(ly, lz, *refs), [(block, F32)] * 2 + [(zrim, F32)] * 2, [VMEM] * 4, *cost,
            )(spectral, vectors, field, coef)
            zlow, zhigh = around(zhigh, "pz", 1), around(zlow, "pz", -1)
            ylow, yhigh = call(
                lambda *refs: next_y_rims_kernel(ly, lz, *refs),
                [(yrim, F32)] * 2, [VMEM] * 3, nx, 4 * nx * 4 * yrim[0],
            )(weighted, zlow, zhigh)
    return (field.reshape(solution.shape), residual.reshape(solution.shape))


def solution(mesh):
    return jax.shard_map(
        shards,
        mesh=mesh,
        in_specs=(
            P("py", "pz", None),
            P("py", "pz", None),
            P("py", "pz", None),
            P(),
            P(),
            P(None, None, "py"),
            P(None, None, "pz"),
            P(),
            P(),
            P(),
            P(),
            P(),
            P(),
        ),
        out_specs=(P("py", "pz", None), P("py", "pz", None)),
        check_vma=False,
    )
```

```python
import jax
import jax.numpy as jnp
import numpy as np
from jax import lax
from jax.experimental import pallas as pl
from jax.experimental.pallas import tpu as pltpu
from jax.sharding import PartitionSpec as P

ITERS = 2
REACH = 3
LANES = 128
HIGH = lax.Precision.HIGHEST
BOTH = ("py", "pz")
F32 = jnp.float32
BF16 = jnp.bfloat16
VMEM = pl.BlockSpec(memory_space=pltpu.VMEM)
HBM = pl.BlockSpec(memory_space=pltpu.HBM)
ANY = pl.BlockSpec(memory_space=pl.ANY)


def up8(count):
    return -(-count // 8) * 8


def split(value):
    high = value.astype(BF16)
    return high, (value - high.astype(F32)).astype(BF16)


def exact(left, right, sides=(1, 0)):
    return lax.dot_general(
        left, right, (((sides[0],), (sides[1],)), ((), ())), precision=HIGH, preferred_element_type=F32
    )


def fetch(pairs, sem):
    copies = [pltpu.make_async_copy(source, target, sem.at[i]) for i, (source, target) in enumerate(pairs)]
    for copy in copies:
        copy.start()
    for copy in copies:
        copy.wait()


def in_hbm(*arrays):
    return [pltpu.with_memory_space_constraint(array, pltpu.HBM) for array in arrays]


def mul(left, right):
    return lax.dot_general(left, right, (((1,), (0,)), ((), ())), preferred_element_type=F32)


def mul_t(left, right):
    return lax.dot_general(left, right, (((1,), (1,)), ((), ())), preferred_element_type=F32)


def call(kernel, outs, specs, flops, cost_bytes, scratch=(), out_specs=None):
    return pl.pallas_call(
        kernel,
        out_shape=[jax.ShapeDtypeStruct(shape, dtype) for shape, dtype in outs],
        in_specs=specs,
        out_specs=out_specs or [VMEM] * len(outs),
        scratch_shapes=list(scratch),
        compiler_params=pltpu.CompilerParams(vmem_limit_bytes=32 * 1024 * 1024),
        cost_estimate=pl.CostEstimate(flops=flops, bytes_accessed=cost_bytes, transcendentals=0),
    )


def store_z_rims(ly, lz, weighted, low_ref, high_ref):
    for y in range(ly):
        low_ref[y * REACH : (y + 1) * REACH, :] = weighted[y * lz : y * lz + REACH, :]
        high_ref[y * REACH : (y + 1) * REACH, :] = weighted[(y + 1) * lz - REACH : (y + 1) * lz, :]


def coefficient_kernel(
    ly, lz, table_ref, span_ref, field_ref, coef_ref, weighted_ref, even_ref, odd_ref, table, span, field, sem
):
    fetch(((table_ref, table), (span_ref, span), (field_ref, field)), sem)
    first = lax.rem(lax.axis_index("pz"), 2) == 0
    half = ly * REACH
    entries = [table[entry] for entry in range(table_ref.shape[0])]
    for start in range(0, span.shape[0], lz):
        rows = pl.ds(start, lz)
        index = span[rows, :]
        coef = jnp.full(index.shape, entries[0], F32)
        for entry in range(1, len(entries)):
            coef = jnp.where(index == entry, entries[entry], coef)
        coef_ref[rows, :] = coef
        weighted = coef * field[rows, :]
        weighted_ref[rows, :] = weighted
        for value, at in ((weighted, 0), (coef, half)):
            rim = pl.ds(at + start // lz * REACH, REACH)
            low, high = value[:REACH], value[lz - REACH :]
            even_ref[rim, :] = jnp.where(first, high, low)
            odd_ref[rim, :] = jnp.where(first, low, high)


def store_y_rims(ly, lz, weighted_ref, zlow, zhigh, odd_ref, even_ref):
    first = lax.rem(lax.axis_index("py"), 2) == 0
    own, side = REACH * lz, REACH * REACH
    for at, count, ref, start, step in ((0, own, weighted_ref, ly - REACH, lz),) + tuple(
        (own + k * side, side, ref, ly - REACH, REACH) for k, ref in enumerate((zlow, zhigh))
    ):
        low, high = ref[:count, :], ref[start * step : start * step + count, :]
        even_ref[at : at + count, :] = jnp.where(first, high, low)
        odd_ref[at : at + count, :] = jnp.where(first, low, high)
    end = own + 2 * side
    for ref in (even_ref, odd_ref):
        ref[end:, :] = jnp.zeros((ref.shape[0] - end, ref.shape[1]), F32)


def y_rims_kernel(ly, lz, weighted_ref, odd_ref, even_ref, _, zlow_ref, zhigh_ref, yodd_ref, yeven_ref):
    first = lax.rem(lax.axis_index("pz"), 2) == 0
    zlow_ref[...] = jnp.where(first, odd_ref[...], even_ref[...])
    zhigh_ref[...] = jnp.where(first, even_ref[...], odd_ref[...])
    store_y_rims(ly, lz, weighted_ref, zlow_ref, zhigh_ref, yodd_ref, yeven_ref)


def next_y_rims_kernel(ly, lz, weighted_ref, zlow_ref, zhigh_ref, yodd_ref, yeven_ref):
    store_y_rims(ly, lz, weighted_ref, zlow_ref, zhigh_ref, yodd_ref, yeven_ref)


def point_columns(ly, lz):
    below, above = range(-REACH, 0), range(REACH)
    halves = []
    for half in range(2):
        first = 0 if half == 0 else ly // 2 - REACH
        points = [(first + y, z) for y in range(ly // 2 + REACH) for z in range(lz)]
        points += [(y, z) for y in range(ly) for z in below]
        points += [(y, lz + z) for y in range(ly) for z in above]
        ys = below if half == 0 else [ly + y for y in above]
        points += [(y, z) for y in ys for z in range(lz)]
        points += [(y, z) for y in ys for z in below]
        points += [(y, lz + z) for y in ys for z in above]
        halves += points + [(1 << 20, 1 << 20)] * (-len(points) % LANES)
    return np.array(halves, np.int32).T.copy()


def stencil_kernel(
    ly, lz, ny, nz, points_hbm, ybands_hbm, zbands_hbm, xbands_hbm, _, out_ref, taps_ref,
    points_ref, ybands_ref, zbands_ref, xbands_ref, sem,
):
    fetch(
        (
            (points_hbm, points_ref), (ybands_hbm, ybands_ref), (zbands_hbm, zbands_ref), (xbands_hbm, xbands_ref),
        ),
        sem,
    )
    count = ly * lz // 2
    width = out_ref.shape[1]
    for half in range(2):
        rows = lax.broadcasted_iota(jnp.int32, (count, 1), 0) + half * count
        columns = pl.ds(half * width, width)
        factors = []
        for bands_ref, length, row, column, first, whole in (
            (ybands_ref, ly, lax.div(rows, lz), points_ref[0:1, columns], lax.axis_index("py") * ly, ny),
            (zbands_ref, lz, lax.rem(rows, lz), points_ref[1:2, columns], lax.axis_index("pz") * lz, nz),
        ):
            pick = (lax.broadcasted_iota(jnp.int32, (count, length), 1) == row).astype(F32)
            spot = column + first
            inside = (spot >= 0) & (spot < whole)
            distance = jnp.where(inside, column, 1 << 20) - row
            here = [distance == offset - REACH for offset in range(2 * REACH + 1)]
            for matrix in range(2):
                taps = exact(pick, bands_ref[:, matrix, :], (1, 1))
                dense = jnp.zeros(distance.shape, F32)
                for offset in range(2 * REACH + 1):
                    dense = jnp.where(here[offset], taps[:, offset : offset + 1], dense)
                factors.append(dense)
        ystiff, ymass, zstiff, zmass = factors
        for part, value in enumerate((ymass * zmass, ystiff * zmass + ymass * zstiff)):
            at = (4 * half + part) * count
            out_ref[at : at + count, :], out_ref[at + 2 * count : at + 3 * count, :] = split(value)
    nx = xbands_ref.shape[2]
    lane = lax.broadcasted_iota(jnp.int32, (1, nx), 1)
    for offset in range(2 * REACH + 1):
        move = offset - REACH
        inside = (lane - move >= 0) & (lane - move < nx)
        for matrix in range(2):
            band = xbands_ref[offset, matrix : matrix + 1, :]
            band = pltpu.roll(band, move % nx, 1) if move else band
            taps_ref[2 * offset + matrix] = jnp.broadcast_to(jnp.where(inside, band, 0.0), (8, nx))


def xvectors_kernel(source, out_ref, held, sem):
    fetch(((source, held),), sem)
    high, low = split(held[...].T)
    out_ref[: high.shape[0], :] = high
    out_ref[high.shape[0] :, :] = low


def tables_kernel(
    npy, npz, ly, lz, xvec_hbm, yvec_hbm, zvec_hbm, xval_hbm, yval_hbm, zval_hbm, _,
    xout_ref, zhigh_ref, zlow_ref, ydown_ref, yup_ref, sums_ref, rimhigh_ref, rimlow_ref,
    xvec_ref, yvec_ref, zvec_ref, xval_ref, yval_ref, zval_ref, sem,
):
    fetch(
        (
            (xvec_hbm, xvec_ref), (yvec_hbm, yvec_ref), (zvec_hbm, zvec_ref),
            (xval_hbm, xval_ref), (yval_hbm, yval_ref), (zval_hbm, zval_ref),
        ),
        sem,
    )
    ny, nz = npy * ly, npz * lz
    nx = xvec_ref.shape[0]
    high, low = split(xvec_ref[...].T)
    xout_ref[:nx, :] = high
    xout_ref[nx:, :] = low
    twice = (
        lax.broadcasted_iota(jnp.int32, (nz, 2 * nz), 0)
        == lax.rem(lax.broadcasted_iota(jnp.int32, (nz, 2 * nz), 1), nz)
    ).astype(F32)
    pair = exact(zvec_ref[...], twice)
    half = lax.broadcasted_iota(jnp.int32, pair.shape, 1) >= nz
    zhigh_ref[...] = jnp.zeros(zhigh_ref.shape, BF16)
    zlow_ref[...] = jnp.zeros(zlow_ref.shape, BF16)
    for parity in range(2):
        high, low = split(jnp.where(half == (parity == 1), pair, 0.0))
        for yl in range(parity, ly, 2):
            for block in range(npz):
                to = (pl.ds((block * ly + yl) * lz, lz), pl.ds(yl // 2 * 2 * nz, 2 * nz))
                zhigh_ref[to] = high[block * lz : (block + 1) * lz, :]
                zlow_ref[to] = low[block * lz : (block + 1) * lz, :]

    shape = (rimhigh_ref.shape[0], 1)
    row = lax.broadcasted_iota(jnp.int32, shape, 0)
    block, spot = lax.div(row, LANES // 2), lax.rem(row, LANES // 2)
    above = spot >= ly * REACH
    spot = jnp.where(above, spot - ly * REACH, spot)
    yrow = jnp.where(spot < ly * REACH, lax.div(spot, REACH), 2 * ly)
    z = block * lz + lax.rem(spot, REACH) + jnp.where(above, lz, -REACH)
    rim = exact((lax.broadcasted_iota(jnp.int32, (shape[0], nz), 1) == z).astype(F32), pair)
    late = (lax.broadcasted_iota(jnp.int32, rim.shape, 1) >= nz).astype(jnp.int32)
    for chunk in range(ly // 2):
        columns = pl.ds(chunk * 2 * nz, 2 * nz)
        rimhigh_ref[:, columns], rimlow_ref[:, columns] = split(jnp.where(yrow - 2 * chunk == late, rim, 0.0))

    def y_of(p):
        spot = lax.div(p, npy)
        return lax.rem(p, npy) * ly + 2 * lax.rem(spot, ly // 2) + lax.div(spot, ly // 2)

    def four(array):
        high, low = split(array)
        late = lax.broadcasted_iota(jnp.int32, array.shape, 1) >= 2 * ny
        return jnp.where(late, low.astype(F32), high.astype(F32)).astype(BF16)

    lane = lax.broadcasted_iota(jnp.int32, (ny, 4 * ny), 1)
    row = lax.broadcasted_iota(jnp.int32, (ny, 4 * ny), 0)
    moved = (row == y_of(lax.rem(lane, ny))).astype(F32)
    ydown_ref[...] = four(exact(yvec_ref[...].T, moved))
    order = (
        lax.broadcasted_iota(jnp.int32, (ny, ny), 1) == y_of(lax.broadcasted_iota(jnp.int32, (ny, ny), 0))
    ).astype(F32)
    copies = (row == lax.rem(lane, ny)).astype(F32)
    yup_ref[...] = four(exact(exact(order, yvec_ref[...]), copies))
    square = (ny, ny)
    diagonal = lax.broadcasted_iota(jnp.int32, square, 0) == lax.broadcasted_iota(jnp.int32, square, 1)
    ycolumn = jnp.sum(jnp.where(diagonal, yval_ref[...], 0.0), axis=1, keepdims=True)
    yz = ycolumn + exact(jnp.broadcast_to(zval_ref[...], (8, nz)), twice)[0:1]
    late = lax.broadcasted_iota(jnp.int32, (1, 2 * nz), 1) >= nz
    modes = nx // (npy * npz)
    first = (lax.axis_index("py") * npz + lax.axis_index("pz")) * modes
    for mode in range(0, modes, 2):
        x = jnp.where(late, xval_ref[first + mode + 1], xval_ref[first + mode])
        sums_ref[:, mode * nz : (mode + 2) * nz] = yz + x


def residual_kernel(
    lz, zrim, weighted_ref, zlow_ref, zhigh_ref, yodd_ref, yeven_ref, stencil_ref, taps_ref, coef_ref, right_ref, vectors_ref,
    _, spectral_ref, residual_ref,
):
    count, nx = weighted_ref.shape
    part, need = count // 2, weighted_ref.shape[0] // 2 + REACH * lz
    own = split(weighted_ref[...])
    zrims = split(jnp.concatenate([zlow_ref[:zrim, :], zhigh_ref[:zrim, :]], axis=0))
    fields = []
    even = lax.rem(lax.axis_index("py"), 2) == 0
    below, above = jnp.where(even, yodd_ref[...], yeven_ref[...]), jnp.where(even, yeven_ref[...], yodd_ref[...])
    for half, rim in enumerate((below, above)):
        missing = stencil_ref.shape[1] - need - 2 * zrim - rim.shape[0]
        yrim = split(jnp.concatenate([rim, jnp.zeros((missing, nx), F32)], axis=0) if missing else rim)
        first = half * (count - need)
        high, low = (
            jnp.concatenate([own[k][first : first + need], zrims[k], yrim[k]], axis=0) for k in range(2)
        )
        stencil = stencil_ref[4 * half * part : 4 * (half + 1) * part, :]
        both = mul(stencil, high)
        both = both[: 2 * part] + both[2 * part :] + mul(stencil[: 2 * part], low)
        fields.append((both[:part], both[part:]))
    for start in range(0, count, 8):
        mass, stiff = (field[start % part : start % part + 8] for field in fields[start // part])
        applied = None
        for offset in range(2 * REACH + 1):
            move = offset - REACH
            term = taps_ref[2 * offset] * mass + taps_ref[2 * offset + 1] * stiff
            term = pltpu.roll(term, -move % nx, 1) if move else term
            applied = term if applied is None else applied + term
        rows = pl.ds(start, 8)
        residual_ref[rows, :] = right_ref[rows, :] - coef_ref[rows, :] * applied
    high, low = split(residual_ref[...])
    product = mul_t(jnp.concatenate([high, low], axis=0), vectors_ref[:nx, :])
    product = product[:count] + product[count:] + mul_t(high, vectors_ref[nx:, :])
    spectral_ref[...] = product.T


def modes_kernel(npy, npz, rims, *refs):
    zhigh_ref, zlow_ref, ydown_ref, yup_ref, sums_ref, *rim_refs, in_ref, out_ref = refs
    count = in_ref.shape[0] // (npy * npz)
    lanes = in_ref.shape[1]
    nz = sums_ref.shape[1] // count
    chunks = zhigh_ref.shape[1] // (2 * nz)
    rows = [
        jnp.concatenate([in_ref[pl.ds(b * count + j, npy, stride=npz * count), :] for b in range(npz)], axis=1)
        for j in range(count)
    ]
    zhigh, zlow = zhigh_ref[...], zlow_ref[...]

    def three(value, product, whigh, wlow):
        high, low = split(value)
        both = product(jnp.concatenate([high, low], axis=0), whigh)
        return both[: count * npy] + both[count * npy :] + product(high, wlow)

    part = three(jnp.concatenate(rows, axis=0), mul, zhigh, zlow)
    late = lax.broadcasted_iota(jnp.int32, (npy, 2 * nz), 1) >= nz

    def swap(value):
        return pltpu.roll(value, nz, 1)

    def tile(array, j, c):
        return array[j * npy : (j + 1) * npy, c * 2 * nz : (c + 1) * 2 * nz]

    pairs = []
    for j in range(0, count, 2):
        first = [tile(part, j, c) for c in range(chunks)]
        second = [tile(part, j + 1, c) for c in range(chunks)]
        even = [jnp.where(late, swap(second[c]), first[c]) for c in range(chunks)]
        odd = [jnp.where(late, second[c], swap(first[c])) for c in range(chunks)]
        pairs.append(jnp.concatenate(even + odd, axis=0))
    stacked = jnp.concatenate(pairs, axis=1)

    def four(value):
        high, low = split(value)
        return jnp.concatenate([high, low, high, low], axis=0)

    modes = mul(ydown_ref[...], four(stacked)) / sums_ref[...]
    restored = mul(yup_ref[...], four(modes))
    half = npy * chunks
    rows = []
    for pair in range(count // 2):
        block = restored[:, pair * 2 * nz : (pair + 1) * 2 * nz]
        even = [block[c * npy : (c + 1) * npy] for c in range(chunks)]
        odd = [block[half + c * npy : half + (c + 1) * npy] for c in range(chunks)]
        rows.append(jnp.concatenate([jnp.where(late, swap(odd[c]), even[c]) for c in range(chunks)], axis=1))
        rows.append(jnp.concatenate([jnp.where(late, odd[c], swap(even[c])) for c in range(chunks)], axis=1))
    spectral = jnp.concatenate(rows, axis=0)
    back = three(spectral, mul_t, zhigh, zlow)
    size = out_ref.shape[0] // (npy * npz)
    for j in range(count):
        for b in range(npz):
            out_ref[pl.ds(b * size + j, npy, stride=npz * size), :] = back[
                j * npy : (j + 1) * npy, b * lanes : (b + 1) * lanes
            ]
    if rims:
        side = three(spectral, mul_t, rim_refs[0][...], rim_refs[1][...])
        for j in range(count // 2):
            for b in range(0, npz, 2):
                first, second = (
                    side[k * npy : (k + 1) * npy, b * lanes // 2 : b * lanes // 2 + lanes] for k in (j, j + count // 2)
                )
                at = b * size + count + j
                out_ref[pl.ds(at, npy, stride=npz * size), :] = jnp.where(late, swap(second), first)
                out_ref[pl.ds(at + size, npy, stride=npz * size), :] = jnp.where(late, second, swap(first))


def transformed(points, vectors_ref):
    rows, nx = points.shape
    high, low = split(points)
    both = mul(jnp.concatenate([high, low], axis=0), vectors_ref[:nx, :])
    return both[:rows] + both[rows:] + mul(high, vectors_ref[nx:, :])


def from_modes(spectral_ref, vectors_ref):
    return transformed(spectral_ref[...].T, vectors_ref)


def update_kernel(ly, lz, spectral_ref, vectors_ref, field_ref, coef_ref, updated_ref, weighted_ref, low_ref, high_ref):
    updated = field_ref[...] + from_modes(spectral_ref, vectors_ref)
    updated_ref[...] = updated
    weighted = coef_ref[...] * updated
    weighted_ref[...] = weighted
    store_z_rims(ly, lz, weighted, low_ref, high_ref)


def rim_update_kernel(
    ly, lz, devices, spectral_ref, vectors_ref, field_ref, coef_ref, before_low_ref, before_high_ref,
    updated_ref, weighted_ref, zlow_ref, zhigh_ref, yodd_ref, yeven_ref,
):
    nx = vectors_ref.shape[1]
    modes = nx // devices
    size = spectral_ref.shape[0] // devices
    own, rims = [], []
    for d in range(devices):
        own.append(spectral_ref[d * size : d * size + modes, :])
        rim = spectral_ref[d * size + modes : (d + 1) * size, :]
        rims += [rim, pltpu.roll(rim, LANES // 2, 1)]
    points = [jnp.concatenate(own, axis=0).T, jnp.concatenate(rims, axis=0).T[: LANES // 2]]
    update = transformed(jnp.concatenate(points, axis=0), vectors_ref)
    count, half = ly * lz, ly * REACH
    updated = field_ref[...] + update[:count]
    updated_ref[...] = updated
    weighted_ref[...] = coef_ref[...] * updated
    for side, (ref, before_ref) in enumerate(((zlow_ref, before_low_ref), (zhigh_ref, before_high_ref))):
        start = count + side * half
        ref[...] = before_ref[:half, :] + before_ref[half:, :] * update[start : start + half]
    store_y_rims(ly, lz, weighted_ref, zlow_ref, zhigh_ref, yodd_ref, yeven_ref)


def last_update_kernel(spectral_ref, vectors_ref, field_ref, residual_ref, updated_hbm, residual_hbm, held, sem):
    leaving = pltpu.make_async_copy(residual_ref, residual_hbm, sem.at[0])
    leaving.start()
    held[...] = field_ref[...] + from_modes(spectral_ref, vectors_ref)
    fetch(((held, updated_hbm),), sem.at[pl.ds(1, 1)])
    leaving.wait()


def pairwise(value, axis, odd):
    count = lax.axis_size(axis)
    other = [((i + odd) ^ 1) - odd for i in range(count)]
    return lax.ppermute(value, axis, [(i, j if 0 <= j < count else i) for i, j in enumerate(other)])


def paired(value, axis):
    count = lax.axis_size(axis)
    return lax.ppermute(value, axis, [(i, (i + 1 if i % 2 else i - 1) % count) for i in range(count)])


def around(value, axis, step):
    count = lax.axis_size(axis)
    return lax.ppermute(value, axis, [(i, (i + step) % count) for i in range(count)])


def plain_modes(received, npy, npz, ly, lz, xvalues, yvalues, zvalues, yvectors, zvectors):
    count = received.shape[0] // (npy * npz)
    field = received.reshape(npy, npz, count, ly, lz).transpose(2, 0, 3, 1, 4).reshape(count, npy * ly, npz * lz)
    field = jnp.einsum("xyz,yj->xjz", field, yvectors, precision=HIGH)
    field = jnp.einsum("xyz,zk->xyk", field, zvectors, precision=HIGH)
    field = field / (yvalues[None, :, None] + zvalues[None, None, :] + xvalues[:, None, None])
    field = jnp.einsum("xjz,yj->xyz", field, yvectors, precision=HIGH)
    field = jnp.einsum("xyk,zk->xyz", field, zvectors, precision=HIGH)
    field = field.reshape(count, npy, ly, npz, lz).transpose(1, 3, 0, 2, 4)
    return field.reshape(npy * npz * count, ly * lz)


def shards(
    solution,
    right_side,
    span_index,
    coef_table,
    xaxis_bands,
    yaxis_bands,
    zaxis_bands,
    xaxis_vectors,
    yaxis_vectors,
    zaxis_vectors,
    xaxis_values,
    yaxis_values,
    zaxis_values,
):
    npy, npz = lax.axis_size("py"), lax.axis_size("pz")
    ly, lz, nx = solution.shape
    ny, nz = npy * ly, npz * lz
    count, devices = ly * lz, npy * npz
    modes = nx // devices
    field = solution.reshape(count, nx)
    right = right_side.reshape(count, nx)
    block, zrim, yrim = (count, nx), (ly * REACH, nx), (up8(REACH * lz + 2 * REACH * REACH), nx)
    zrims = (2 * ly * REACH, nx)
    cell = count * nx * 4
    dma = pltpu.SemaphoreType.DMA

    coef, weighted, even, odd = call(
        lambda *refs: coefficient_kernel(ly, lz, *refs),
        [(block, F32), (block, F32), (zrims, F32), (zrims, F32)],
        [HBM] * 3, count * nx * 16, 4 * cell,
        [pltpu.SMEM(coef_table.shape, F32), pltpu.VMEM(block, jnp.int32), pltpu.VMEM(block, F32), dma((3,))],
    )(*in_hbm(coef_table, span_index.reshape(count, nx), field))

    points = point_columns(ly, lz)
    width = points.shape[1] // 2
    bands = [array.transpose(1, 0, 2) for array in (yaxis_bands, zaxis_bands, xaxis_bands)]
    stencil, taps = call(
        lambda *refs: stencil_kernel(ly, lz, ny, nz, *refs),
        [((4 * count, width), BF16), ((2 * (2 * REACH + 1), 8, nx), F32)],
        [HBM] * 4 + [ANY], count * width * 60, 8 * count * width,
        [pltpu.VMEM(points.shape, jnp.int32)] + [pltpu.VMEM(array.shape, F32) for array in bands] + [dma((4,))],
    )(*in_hbm(jnp.asarray(points), *bands), even)

    fast = (
        modes % 16 == 0 and npz % 2 == 0 and 2 * ly * REACH <= LANES // 2 and npy % 8 == 0 and lz % 16 == 0 and ly % 2 == 0
        and 2 * nz == LANES and 2 * ny == LANES and count == LANES and nx % LANES == 0
    )
    if fast:
        zmat, ymat, rmat = (npz * count, ly * nz), (ny, 4 * ny), (npz * LANES // 2, ly * nz)
        vectors, *tables = call(
            lambda *refs: tables_kernel(npy, npz, ly, lz, *refs),
            [((2 * nx, nx), BF16), (zmat, BF16), (zmat, BF16), (ymat, BF16), (ymat, BF16), ((ny, modes * nz), F32)]
            + [(rmat, BF16)] * 2,
            [HBM] * 6 + [ANY], npz * count * ly * nz * 8, npz * count * ly * nz * 4,
            [pltpu.VMEM(array.shape, F32) for array in (xaxis_vectors, yaxis_vectors, zaxis_vectors)]
            + [pltpu.SMEM((nx,), F32), pltpu.VMEM((1, ny), F32), pltpu.VMEM((1, nz), F32), dma((6,))],
        )(
            *in_hbm(
                xaxis_vectors, yaxis_vectors, zaxis_vectors, xaxis_values,
                yaxis_values.reshape(1, ny), zaxis_values.reshape(1, nz),
            ),
            taps,
        )

        def precondition(received, rims):
            size = modes * 3 // 2 if rims else modes
            return call(
                lambda *refs: modes_kernel(npy, npz, rims, *refs),
                [((devices * size, count), F32)], [VMEM] * (8 if rims else 6), 6 * 2 * count * nx * ly * nz, 2 * cell,
            )(*(tables if rims else tables[:5]), received)[0]
    else:
        tables = [taps]
        vectors = call(
            xvectors_kernel, [((2 * nx, nx), BF16)], [HBM], nx * nx * 40, 8 * nx * nx,
            [pltpu.VMEM((nx, nx), F32), dma((1,))],
        )(*in_hbm(xaxis_vectors))[0]
        part = lax.axis_index(BOTH)
        xpart = lax.dynamic_slice_in_dim(xaxis_values, part * modes, modes)

        def precondition(received, rims):
            return plain_modes(
                received, npy, npz, ly, lz, xpart, yaxis_values, zaxis_values, yaxis_vectors, zaxis_vectors
            )

    even, odd = pairwise(even, "pz", 0), pairwise(odd, "pz", 1)
    zlow, zhigh, yodd, yeven = call(
        lambda *refs: y_rims_kernel(ly, lz, *refs),
        [(zrims, F32)] * 2 + [(yrim, F32)] * 2, [VMEM] * 3 + [ANY], nx, 4 * nx * 4 * (yrim[0] + zrims[0]),
    )(weighted, odd, even, taps)
    for iteration in range(ITERS):
        last = iteration + 1 == ITERS
        yodd, yeven = paired(yodd, "py"), pairwise(yeven, "py", 0)
        spectral, *residual = call(
            lambda *refs: residual_kernel(lz, zrim[0], *refs),
            [((nx, count), F32)] + [(block, F32)] * last,
            [VMEM] * 10 + [ANY], 6 * count * nx * (nx + 2 * width), 5 * cell + 4 * nx * nx,
            [pltpu.VMEM(block, F32)] * (not last),
        )(weighted, zlow, zhigh, yodd, yeven, stencil, taps, coef, right, vectors, tables[0])
        spectral = lax.all_to_all(spectral, BOTH, split_axis=0, concat_axis=0, tiled=True)
        spectral = precondition(spectral, not last)
        spectral = lax.all_to_all(spectral, BOTH, split_axis=0, concat_axis=0, tiled=True)
        cost = (6 * count * nx * nx, 4 * cell + 4 * nx * nx)
        if last:
            field, residual = call(
                last_update_kernel, [(block, F32), (block, F32)], [VMEM] * 4, *cost,
                [pltpu.VMEM(block, F32), dma((2,))], [HBM] * 2,
            )(spectral, vectors, field, *residual)
        elif fast:
            field, weighted, zlow, zhigh, yodd, yeven = call(
                lambda *refs: rim_update_kernel(ly, lz, devices, *refs),
                [(block, F32)] * 2 + [(zrim, F32)] * 2 + [(yrim, F32)] * 2, [VMEM] * 6, *cost,
            )(spectral, vectors, field, coef, zlow, zhigh)
        else:
            field, weighted, zlow, zhigh = call(
                lambda *refs: update_kernel(ly, lz, *refs), [(block, F32)] * 2 + [(zrim, F32)] * 2, [VMEM] * 4, *cost,
            )(spectral, vectors, field, coef)
            zlow, zhigh = around(zhigh, "pz", 1), around(zlow, "pz", -1)
            yodd, yeven = call(
                lambda *refs: next_y_rims_kernel(ly, lz, *refs),
                [(yrim, F32)] * 2, [VMEM] * 3, nx, 4 * nx * 4 * yrim[0],
            )(weighted, zlow, zhigh)
    return (field.reshape(solution.shape), residual.reshape(solution.shape))


def solution(mesh):
    return jax.shard_map(
        shards,
        mesh=mesh,
        in_specs=(
            P("py", "pz", None),
            P("py", "pz", None),
            P("py", "pz", None),
            P(),
            P(),
            P(None, None, "py"),
            P(None, None, "pz"),
            P(),
            P(),
            P(),
            P(),
            P(),
            P(),
        ),
        out_specs=(P("py", "pz", None), P("py", "pz", None)),
        check_vma=False,
    )
```

```python
import jax
import jax.numpy as jnp
import numpy as np
from jax import lax
from jax.experimental import pallas as pl
from jax.experimental.pallas import tpu as pltpu
from jax.sharding import PartitionSpec as P

ITERS = 2
REACH = 3
LANES = 128
HIGH = lax.Precision.HIGHEST
BOTH = ("py", "pz")
F32 = jnp.float32
BF16 = jnp.bfloat16
VMEM = pl.BlockSpec(memory_space=pltpu.VMEM)
HBM = pl.BlockSpec(memory_space=pltpu.HBM)
ANY = pl.BlockSpec(memory_space=pl.ANY)


def up8(count):
    return -(-count // 8) * 8


def split(value):
    high = value.astype(BF16)
    return high, (value - high.astype(F32)).astype(BF16)


def exact(left, right, sides=(1, 0)):
    return lax.dot_general(
        left, right, (((sides[0],), (sides[1],)), ((), ())), precision=HIGH, preferred_element_type=F32
    )


def fetch(pairs, sem):
    copies = [pltpu.make_async_copy(source, target, sem.at[i]) for i, (source, target) in enumerate(pairs)]
    for copy in copies:
        copy.start()
    for copy in copies:
        copy.wait()


def in_hbm(*arrays):
    return [pltpu.with_memory_space_constraint(array, pltpu.HBM) for array in arrays]


def mul(left, right):
    return lax.dot_general(left, right, (((1,), (0,)), ((), ())), preferred_element_type=F32)


def mul_t(left, right):
    return lax.dot_general(left, right, (((1,), (1,)), ((), ())), preferred_element_type=F32)


def call(kernel, outs, specs, flops, cost_bytes, scratch=(), out_specs=None):
    return pl.pallas_call(
        kernel,
        out_shape=[jax.ShapeDtypeStruct(shape, dtype) for shape, dtype in outs],
        in_specs=specs,
        out_specs=out_specs or [VMEM] * len(outs),
        scratch_shapes=list(scratch),
        compiler_params=pltpu.CompilerParams(vmem_limit_bytes=32 * 1024 * 1024),
        cost_estimate=pl.CostEstimate(flops=flops, bytes_accessed=cost_bytes, transcendentals=0),
    )


def store_z_rims(ly, lz, weighted, low_ref, high_ref):
    for y in range(ly):
        low_ref[y * REACH : (y + 1) * REACH, :] = weighted[y * lz : y * lz + REACH, :]
        high_ref[y * REACH : (y + 1) * REACH, :] = weighted[(y + 1) * lz - REACH : (y + 1) * lz, :]


def coefficient_kernel(
    ly, lz, table_ref, span_ref, field_ref, coef_ref, weighted_ref, even_ref, odd_ref, table, span, field, sem
):
    fetch(((table_ref, table), (span_ref, span), (field_ref, field)), sem)
    first = lax.rem(lax.axis_index("pz"), 2) == 0
    half = ly * REACH
    entries = [table[entry] for entry in range(table_ref.shape[0])]
    for start in range(0, span.shape[0], lz):
        rows = pl.ds(start, lz)
        index = span[rows, :]
        coef = jnp.full(index.shape, entries[0], F32)
        for entry in range(1, len(entries)):
            coef = jnp.where(index == entry, entries[entry], coef)
        coef_ref[rows, :] = coef
        weighted = coef * field[rows, :]
        weighted_ref[rows, :] = weighted
        for value, at in ((weighted, 0), (coef, half)):
            rim = pl.ds(at + start // lz * REACH, REACH)
            low, high = value[:REACH], value[lz - REACH :]
            even_ref[rim, :] = jnp.where(first, high, low)
            odd_ref[rim, :] = jnp.where(first, low, high)


def store_y_rims(ly, lz, weighted_ref, zlow, zhigh, odd_ref, even_ref):
    first = lax.rem(lax.axis_index("py"), 2) == 0
    own, side = REACH * lz, REACH * REACH
    for at, count, ref, start, step in ((0, own, weighted_ref, ly - REACH, lz),) + tuple(
        (own + k * side, side, ref, ly - REACH, REACH) for k, ref in enumerate((zlow, zhigh))
    ):
        low, high = ref[:count, :], ref[start * step : start * step + count, :]
        even_ref[at : at + count, :] = jnp.where(first, high, low)
        odd_ref[at : at + count, :] = jnp.where(first, low, high)
    end = own + 2 * side
    for ref in (even_ref, odd_ref):
        ref[end:, :] = jnp.zeros((ref.shape[0] - end, ref.shape[1]), F32)


def y_rims_kernel(ly, lz, weighted_ref, odd_ref, even_ref, _, zlow_ref, zhigh_ref, yodd_ref, yeven_ref):
    first = lax.rem(lax.axis_index("pz"), 2) == 0
    zlow_ref[...] = jnp.where(first, odd_ref[...], even_ref[...])
    zhigh_ref[...] = jnp.where(first, even_ref[...], odd_ref[...])
    store_y_rims(ly, lz, weighted_ref, zlow_ref, zhigh_ref, yodd_ref, yeven_ref)


def next_y_rims_kernel(ly, lz, weighted_ref, zlow_ref, zhigh_ref, yodd_ref, yeven_ref):
    store_y_rims(ly, lz, weighted_ref, zlow_ref, zhigh_ref, yodd_ref, yeven_ref)


def point_columns(ly, lz):
    below, above = range(-REACH, 0), range(REACH)
    halves = []
    for half in range(2):
        first = 0 if half == 0 else ly // 2 - REACH
        points = [(first + y, z) for y in range(ly // 2 + REACH) for z in range(lz)]
        points += [(y, z) for y in range(ly) for z in below]
        points += [(y, lz + z) for y in range(ly) for z in above]
        ys = below if half == 0 else [ly + y for y in above]
        points += [(y, z) for y in ys for z in range(lz)]
        points += [(y, z) for y in ys for z in below]
        points += [(y, lz + z) for y in ys for z in above]
        halves += points + [(1 << 20, 1 << 20)] * (-len(points) % LANES)
    return np.array(halves, np.int32).T.copy()


def stencil_kernel(
    ly, lz, ny, nz, points_hbm, ybands_hbm, zbands_hbm, xbands_hbm, _, out_ref, taps_ref,
    points_ref, ybands_ref, zbands_ref, xbands_ref, sem,
):
    fetch(
        (
            (points_hbm, points_ref), (ybands_hbm, ybands_ref), (zbands_hbm, zbands_ref), (xbands_hbm, xbands_ref),
        ),
        sem,
    )
    count = ly * lz // 2
    width = out_ref.shape[1]
    for half in range(2):
        rows = lax.broadcasted_iota(jnp.int32, (count, 1), 0) + half * count
        columns = pl.ds(half * width, width)
        factors = []
        for bands_ref, length, row, column, first, whole in (
            (ybands_ref, ly, lax.div(rows, lz), points_ref[0:1, columns], lax.axis_index("py") * ly, ny),
            (zbands_ref, lz, lax.rem(rows, lz), points_ref[1:2, columns], lax.axis_index("pz") * lz, nz),
        ):
            pick = (lax.broadcasted_iota(jnp.int32, (count, length), 1) == row).astype(F32)
            spot = column + first
            inside = (spot >= 0) & (spot < whole)
            distance = jnp.where(inside, column, 1 << 20) - row
            here = [distance == offset - REACH for offset in range(2 * REACH + 1)]
            for matrix in range(2):
                taps = exact(pick, bands_ref[:, matrix, :], (1, 1))
                dense = jnp.zeros(distance.shape, F32)
                for offset in range(2 * REACH + 1):
                    dense = jnp.where(here[offset], taps[:, offset : offset + 1], dense)
                factors.append(dense)
        ystiff, ymass, zstiff, zmass = factors
        for part, value in enumerate((ymass * zmass, ystiff * zmass + ymass * zstiff)):
            at = (4 * half + part) * count
            out_ref[at : at + count, :], out_ref[at + 2 * count : at + 3 * count, :] = split(value)
    nx = xbands_ref.shape[2]
    lane = lax.broadcasted_iota(jnp.int32, (1, nx), 1)
    for offset in range(2 * REACH + 1):
        move = offset - REACH
        inside = (lane - move >= 0) & (lane - move < nx)
        for matrix in range(2):
            band = xbands_ref[offset, matrix : matrix + 1, :]
            band = pltpu.roll(band, move % nx, 1) if move else band
            taps_ref[2 * offset + matrix] = jnp.broadcast_to(jnp.where(inside, band, 0.0), (8, nx))


def xvectors_kernel(source, out_ref, held, sem):
    fetch(((source, held),), sem)
    high, low = split(held[...].T)
    out_ref[: high.shape[0], :] = high
    out_ref[high.shape[0] :, :] = low


def tables_kernel(
    npy, npz, ly, lz, xvec_hbm, yvec_hbm, zvec_hbm, xval_hbm, yval_hbm, zval_hbm, _,
    xout_ref, zhigh_ref, zlow_ref, ydown_ref, yup_ref, sums_ref, rimhigh_ref, rimlow_ref,
    xvec_ref, yvec_ref, zvec_ref, xval_ref, yval_ref, zval_ref, sem,
):
    fetch(
        (
            (xvec_hbm, xvec_ref), (yvec_hbm, yvec_ref), (zvec_hbm, zvec_ref),
            (xval_hbm, xval_ref), (yval_hbm, yval_ref), (zval_hbm, zval_ref),
        ),
        sem,
    )
    ny, nz = npy * ly, npz * lz
    nx = xvec_ref.shape[0]
    high, low = split(xvec_ref[...].T)
    xout_ref[:nx, :] = high
    xout_ref[nx:, :] = low
    twice = (
        lax.broadcasted_iota(jnp.int32, (nz, 2 * nz), 0)
        == lax.rem(lax.broadcasted_iota(jnp.int32, (nz, 2 * nz), 1), nz)
    ).astype(F32)
    pair = exact(zvec_ref[...], twice)
    half = lax.broadcasted_iota(jnp.int32, pair.shape, 1) >= nz
    zhigh_ref[...] = jnp.zeros(zhigh_ref.shape, BF16)
    zlow_ref[...] = jnp.zeros(zlow_ref.shape, BF16)
    for parity in range(2):
        high, low = split(jnp.where(half == (parity == 1), pair, 0.0))
        for yl in range(parity, ly // 2, 2):
            for block in range(npz):
                to = (pl.ds((block * ly // 2 + yl) * lz, lz), pl.ds(yl // 2 * 2 * nz, 2 * nz))
                zhigh_ref[to] = high[block * lz : (block + 1) * lz, :]
                zlow_ref[to] = low[block * lz : (block + 1) * lz, :]
    shape = (rimhigh_ref.shape[0], 1)
    row = lax.broadcasted_iota(jnp.int32, shape, 0)
    block, spot = lax.div(row, LANES // 2), lax.rem(row, LANES // 2)
    above = spot >= ly * REACH
    spot = jnp.where(above, spot - ly * REACH, spot)
    yrow = jnp.where(spot < ly * REACH, lax.div(spot, REACH), 2 * ly)
    z = block * lz + lax.rem(spot, REACH) + jnp.where(above, lz, -REACH)
    rim = exact((lax.broadcasted_iota(jnp.int32, (shape[0], nz), 1) == z).astype(F32), pair)
    late = (lax.broadcasted_iota(jnp.int32, rim.shape, 1) >= nz).astype(jnp.int32)
    for chunk in range(ly // 2):
        columns = pl.ds(chunk * 2 * nz, 2 * nz)
        rimhigh_ref[:, columns], rimlow_ref[:, columns] = split(jnp.where(yrow - 2 * chunk == late, rim, 0.0))

    def y_of(p):
        spot = lax.div(p, npy)
        return lax.rem(p, npy) * ly + 2 * lax.rem(spot, ly // 2) + lax.div(spot, ly // 2)

    def four(array):
        high, low = split(array)
        late = lax.broadcasted_iota(jnp.int32, array.shape, 1) >= 2 * ny
        return jnp.where(late, low.astype(F32), high.astype(F32)).astype(BF16)

    lane = lax.broadcasted_iota(jnp.int32, (ny, 4 * ny), 1)
    row = lax.broadcasted_iota(jnp.int32, (ny, 4 * ny), 0)
    moved = (row == y_of(lax.rem(lane, ny))).astype(F32)
    ydown_ref[...] = four(exact(yvec_ref[...].T, moved))
    order = (
        lax.broadcasted_iota(jnp.int32, (ny, ny), 1) == y_of(lax.broadcasted_iota(jnp.int32, (ny, ny), 0))
    ).astype(F32)
    copies = (row == lax.rem(lane, ny)).astype(F32)
    yup_ref[...] = four(exact(exact(order, yvec_ref[...]), copies))
    square = (ny, ny)
    diagonal = lax.broadcasted_iota(jnp.int32, square, 0) == lax.broadcasted_iota(jnp.int32, square, 1)
    ycolumn = jnp.sum(jnp.where(diagonal, yval_ref[...], 0.0), axis=1, keepdims=True)
    yz = ycolumn + exact(jnp.broadcast_to(zval_ref[...], (8, nz)), twice)[0:1]
    late = lax.broadcasted_iota(jnp.int32, (1, 2 * nz), 1) >= nz
    modes = nx // (npy * npz)
    first = (lax.axis_index("py") * npz + lax.axis_index("pz")) * modes
    for mode in range(0, modes, 2):
        x = jnp.where(late, xval_ref[first + mode + 1], xval_ref[first + mode])
        sums_ref[:, mode * nz : (mode + 2) * nz] = yz + x


def residual_kernel(
    lz, zrim, weighted_ref, zlow_ref, zhigh_ref, yodd_ref, yeven_ref, stencil_ref, taps_ref, coef_ref, right_ref, vectors_ref,
    _, spectral_ref, residual_ref,
):
    count, nx = weighted_ref.shape
    part, need = count // 2, weighted_ref.shape[0] // 2 + REACH * lz
    own = split(weighted_ref[...])
    zrims = split(jnp.concatenate([zlow_ref[:zrim, :], zhigh_ref[:zrim, :]], axis=0))
    fields = []
    even = lax.rem(lax.axis_index("py"), 2) == 0
    below, above = jnp.where(even, yodd_ref[...], yeven_ref[...]), jnp.where(even, yeven_ref[...], yodd_ref[...])
    for half, rim in enumerate((below, above)):
        missing = stencil_ref.shape[1] - need - 2 * zrim - rim.shape[0]
        yrim = split(jnp.concatenate([rim, jnp.zeros((missing, nx), F32)], axis=0) if missing else rim)
        first = half * (count - need)
        high, low = (
            jnp.concatenate([own[k][first : first + need], zrims[k], yrim[k]], axis=0) for k in range(2)
        )
        stencil = stencil_ref[4 * half * part : 4 * (half + 1) * part, :]
        both = mul(stencil, high)
        both = both[: 2 * part] + both[2 * part :] + mul(stencil[: 2 * part], low)
        fields.append((both[:part], both[part:]))
    for start in range(0, count, 8):
        mass, stiff = (field[start % part : start % part + 8] for field in fields[start // part])
        applied = None
        for offset in range(2 * REACH + 1):
            move = offset - REACH
            term = taps_ref[2 * offset] * mass + taps_ref[2 * offset + 1] * stiff
            term = pltpu.roll(term, -move % nx, 1) if move else term
            applied = term if applied is None else applied + term
        rows = pl.ds(start, 8)
        residual_ref[rows, :] = right_ref[rows, :] - coef_ref[rows, :] * applied
    high, low = split(residual_ref[...])
    product = mul_t(jnp.concatenate([high, low], axis=0), vectors_ref[:nx, :])
    product = product[:count] + product[count:] + mul_t(high, vectors_ref[nx:, :])
    spectral_ref[...] = product.T


def modes_kernel(npy, npz, rims, *refs):
    zhigh_ref, zlow_ref, ydown_ref, yup_ref, sums_ref, *rim_refs, in_ref, out_ref, turn_ref = refs
    count = in_ref.shape[0] // (npy * npz)
    size = out_ref.shape[0] // (npy * npz)
    nz = sums_ref.shape[1] // count
    width = zhigh_ref.shape[1]
    chunks = 2 * width // LANES
    step = turn_ref.shape[0] // (npy * chunks)
    zhigh, zlow = zhigh_ref[...], zlow_ref[...]

    def three(value, product, whigh, wlow):
        rows = value.shape[0]
        high, low = split(value)
        both = product(jnp.concatenate([high, low], axis=0), whigh)
        return both[:rows] + both[rows:] + product(high, wlow)

    def early(first, second):
        late = lax.broadcasted_iota(jnp.int32, first.shape, 1) >= LANES // 2
        return jnp.where(late, pltpu.roll(second, LANES // 2, 1), first)

    def later(first, second):
        late = lax.broadcasted_iota(jnp.int32, first.shape, 1) >= LANES // 2
        return jnp.where(late, second, pltpu.roll(first, LANES // 2, 1))

    def by_mode(mode, chunk):
        return pl.ds(chunk * npy * step + mode, npy, stride=step)

    def by_device(device, chunk):
        return pl.ds((chunk * npy + device) * step, count)

    halves = [[], []]
    for p in range(npy):
        blocks = [in_ref[(p * npz + b) * count : (p * npz + b + 1) * count, :] for b in range(npz)]
        for half, joined in zip(halves, (early, later)):
            half.append(jnp.concatenate([joined(blocks[b], blocks[b + 1]) for b in range(0, npz, 2)], axis=1))
    part = three(jnp.concatenate(halves[0] + halves[1], axis=0), mul, zhigh, zlow)
    for chunk in range(chunks):
        half, lane = divmod(chunk * LANES, width)
        for p in range(npy):
            row = (half * npy + p) * count
            turn_ref[by_device(p, chunk), :] = part[row : row + count, lane : lane + LANES]
    pairs = []
    for mode in range(0, count, 2):
        tiles = [(turn_ref[by_mode(mode, c), :], turn_ref[by_mode(mode + 1, c), :]) for c in range(chunks)]
        pairs.append(jnp.concatenate([early(*tile) for tile in tiles] + [later(*tile) for tile in tiles], axis=0))
    stacked = jnp.concatenate(pairs, axis=1)

    def four(value):
        high, low = split(value)
        return jnp.concatenate([high, low, high, low], axis=0)

    modes = mul(ydown_ref[...], four(stacked)) / sums_ref[...]
    restored = mul(yup_ref[...], four(modes))
    for mode in range(0, count, 2):
        block = restored[:, mode * nz : (mode + 2) * nz]
        for c in range(chunks):
            even = block[c * npy : (c + 1) * npy]
            odd = block[(chunks + c) * npy : (chunks + c + 1) * npy]
            turn_ref[by_mode(mode, c), :] = early(even, odd)
            turn_ref[by_mode(mode + 1, c), :] = later(even, odd)
    rows = [
        jnp.concatenate(
            [turn_ref[by_device(p, half * chunks // 2 + c), :] for c in range(chunks // 2)], axis=1
        )
        for half in range(2)
        for p in range(npy)
    ]
    spectral = jnp.concatenate(rows, axis=0)
    back = three(spectral, mul_t, zhigh, zlow)
    total = npy * count
    if rims:
        side = [
            three(spectral[half * total : (half + 1) * total], mul_t, *(ref[:, pl.ds(half * width, width)] for ref in rim_refs))
            for half in range(2)
        ]
        side = side[0] + side[1]
    for p in range(npy):
        for b in range(0, npz, 2):
            first, second = (
                back[k * total + p * count : k * total + (p + 1) * count, b * LANES // 2 : b * LANES // 2 + LANES]
                for k in range(2)
            )
            at = (p * npz + b) * size
            out_ref[at : at + count, :] = early(first, second)
            out_ref[at + size : at + size + count, :] = later(first, second)
            if rims:
                row, middle = p * count, p * count + count // 2
                first = side[row:middle, b * LANES // 2 : b * LANES // 2 + LANES]
                second = side[middle : row + count, b * LANES // 2 : b * LANES // 2 + LANES]
                out_ref[at + count : at + size, :] = early(first, second)
                out_ref[at + size + count : at + 2 * size, :] = later(first, second)


def transformed(points, vectors_ref):
    rows, nx = points.shape
    high, low = split(points)
    both = mul(jnp.concatenate([high, low], axis=0), vectors_ref[:nx, :])
    return both[:rows] + both[rows:] + mul(high, vectors_ref[nx:, :])


def from_modes(spectral_ref, vectors_ref):
    return transformed(spectral_ref[...].T, vectors_ref)


def update_kernel(ly, lz, spectral_ref, vectors_ref, field_ref, coef_ref, updated_ref, weighted_ref, low_ref, high_ref):
    updated = field_ref[...] + from_modes(spectral_ref, vectors_ref)
    updated_ref[...] = updated
    weighted = coef_ref[...] * updated
    weighted_ref[...] = weighted
    store_z_rims(ly, lz, weighted, low_ref, high_ref)


def rim_update_kernel(
    ly, lz, devices, spectral_ref, vectors_ref, field_ref, coef_ref, before_low_ref, before_high_ref,
    updated_ref, weighted_ref, zlow_ref, zhigh_ref, yodd_ref, yeven_ref,
):
    nx = vectors_ref.shape[1]
    modes = nx // devices
    size = spectral_ref.shape[0] // devices
    own, rims = [], []
    for d in range(devices):
        own.append(spectral_ref[d * size : d * size + modes, :])
        rim = spectral_ref[d * size + modes : (d + 1) * size, :]
        rims += [rim, pltpu.roll(rim, LANES // 2, 1)]
    points = [jnp.concatenate(own, axis=0).T, jnp.concatenate(rims, axis=0).T[: LANES // 2]]
    update = transformed(jnp.concatenate(points, axis=0), vectors_ref)
    count, half = ly * lz, ly * REACH
    updated = field_ref[...] + update[:count]
    updated_ref[...] = updated
    weighted_ref[...] = coef_ref[...] * updated
    for side, (ref, before_ref) in enumerate(((zlow_ref, before_low_ref), (zhigh_ref, before_high_ref))):
        start = count + side * half
        ref[...] = before_ref[:half, :] + before_ref[half:, :] * update[start : start + half]
    store_y_rims(ly, lz, weighted_ref, zlow_ref, zhigh_ref, yodd_ref, yeven_ref)


def last_update_kernel(spectral_ref, vectors_ref, field_ref, residual_ref, updated_hbm, residual_hbm, held, sem):
    leaving = pltpu.make_async_copy(residual_ref, residual_hbm, sem.at[0])
    leaving.start()
    held[...] = field_ref[...] + from_modes(spectral_ref, vectors_ref)
    fetch(((held, updated_hbm),), sem.at[pl.ds(1, 1)])
    leaving.wait()


def pairwise(value, axis, odd):
    count = lax.axis_size(axis)
    other = [((i + odd) ^ 1) - odd for i in range(count)]
    return lax.ppermute(value, axis, [(i, j if 0 <= j < count else i) for i, j in enumerate(other)])


def paired(value, axis):
    count = lax.axis_size(axis)
    return lax.ppermute(value, axis, [(i, (i + 1 if i % 2 else i - 1) % count) for i in range(count)])


def odd_pairs(value, axis, other):
    count, across = lax.axis_size(axis), lax.axis_size(other)
    first = BOTH.index(axis) == 0

    def spot(i, k):
        return i * across + k if first else k * count + i

    pairs = []
    for i in range(count):
        for k in range(across):
            j = i + 1 if i % 2 else i - 1
            pairs.append((spot(i, k), spot(j, k) if 0 <= j < count else spot(i, k ^ 1)))
    return lax.ppermute(value, BOTH, pairs)


def around(value, axis, step):
    count = lax.axis_size(axis)
    return lax.ppermute(value, axis, [(i, (i + step) % count) for i in range(count)])


def plain_modes(received, npy, npz, ly, lz, xvalues, yvalues, zvalues, yvectors, zvectors):
    count = received.shape[0] // (npy * npz)
    field = received.reshape(npy, npz, count, ly, lz).transpose(2, 0, 3, 1, 4).reshape(count, npy * ly, npz * lz)
    field = jnp.einsum("xyz,yj->xjz", field, yvectors, precision=HIGH)
    field = jnp.einsum("xyz,zk->xyk", field, zvectors, precision=HIGH)
    field = field / (yvalues[None, :, None] + zvalues[None, None, :] + xvalues[:, None, None])
    field = jnp.einsum("xjz,yj->xyz", field, yvectors, precision=HIGH)
    field = jnp.einsum("xyk,zk->xyz", field, zvectors, precision=HIGH)
    field = field.reshape(count, npy, ly, npz, lz).transpose(1, 3, 0, 2, 4)
    return field.reshape(npy * npz * count, ly * lz)


def shards(
    solution,
    right_side,
    span_index,
    coef_table,
    xaxis_bands,
    yaxis_bands,
    zaxis_bands,
    xaxis_vectors,
    yaxis_vectors,
    zaxis_vectors,
    xaxis_values,
    yaxis_values,
    zaxis_values,
):
    npy, npz = lax.axis_size("py"), lax.axis_size("pz")
    ly, lz, nx = solution.shape
    ny, nz = npy * ly, npz * lz
    count, devices = ly * lz, npy * npz
    modes = nx // devices
    field = solution.reshape(count, nx)
    right = right_side.reshape(count, nx)
    block, zrim, yrim = (count, nx), (ly * REACH, nx), (up8(REACH * lz + 2 * REACH * REACH), nx)
    zrims = (2 * ly * REACH, nx)
    cell = count * nx * 4
    dma = pltpu.SemaphoreType.DMA

    coef, weighted, even, odd = call(
        lambda *refs: coefficient_kernel(ly, lz, *refs),
        [(block, F32), (block, F32), (zrims, F32), (zrims, F32)],
        [HBM] * 3, count * nx * 16, 4 * cell,
        [pltpu.SMEM(coef_table.shape, F32), pltpu.VMEM(block, jnp.int32), pltpu.VMEM(block, F32), dma((3,))],
    )(*in_hbm(coef_table, span_index.reshape(count, nx), field))

    points = point_columns(ly, lz)
    width = points.shape[1] // 2
    bands = [array.transpose(1, 0, 2) for array in (yaxis_bands, zaxis_bands, xaxis_bands)]
    stencil, taps = call(
        lambda *refs: stencil_kernel(ly, lz, ny, nz, *refs),
        [((4 * count, width), BF16), ((2 * (2 * REACH + 1), 8, nx), F32)],
        [HBM] * 4 + [ANY], count * width * 60, 8 * count * width,
        [pltpu.VMEM(points.shape, jnp.int32)] + [pltpu.VMEM(array.shape, F32) for array in bands] + [dma((4,))],
    )(*in_hbm(jnp.asarray(points), *bands), even)

    fast = (
        modes % 16 == 0 and npz % 2 == 0 and 2 * ly * REACH <= LANES // 2 and npy % 8 == 0 and lz % 16 == 0 and ly % 4 == 0
        and 2 * nz == LANES and 2 * ny == LANES and count == LANES and nx % LANES == 0
    )
    if fast:
        zmat, ymat, rmat = (npz * count // 2, ly * nz // 2), (ny, 4 * ny), (npz * LANES // 2, ly * nz)
        vectors, *tables = call(
            lambda *refs: tables_kernel(npy, npz, ly, lz, *refs),
            [((2 * nx, nx), BF16), (zmat, BF16), (zmat, BF16), (ymat, BF16), (ymat, BF16), ((ny, modes * nz), F32)]
            + [(rmat, BF16)] * 2,
            [HBM] * 6 + [ANY], npz * count * ly * nz * 8, npz * count * ly * nz * 4,
            [pltpu.VMEM(array.shape, F32) for array in (xaxis_vectors, yaxis_vectors, zaxis_vectors)]
            + [pltpu.SMEM((nx,), F32), pltpu.VMEM((1, ny), F32), pltpu.VMEM((1, nz), F32), dma((6,))],
        )(
            *in_hbm(
                xaxis_vectors, yaxis_vectors, zaxis_vectors, xaxis_values,
                yaxis_values.reshape(1, ny), zaxis_values.reshape(1, nz),
            ),
            taps,
        )

        def precondition(received, rims):
            size = modes * 3 // 2 if rims else modes
            return call(
                lambda *refs: modes_kernel(npy, npz, rims, *refs),
                [((devices * size, count), F32)], [VMEM] * (8 if rims else 6), 6 * 2 * count * nx * ly * nz, 2 * cell,
                [pltpu.VMEM((ly * nz // LANES * npy * (modes + 8), LANES), F32)],
            )(*(tables if rims else tables[:5]), received)[0]
    else:
        tables = [taps]
        vectors = call(
            xvectors_kernel, [((2 * nx, nx), BF16)], [HBM], nx * nx * 40, 8 * nx * nx,
            [pltpu.VMEM((nx, nx), F32), dma((1,))],
        )(*in_hbm(xaxis_vectors))[0]
        part = lax.axis_index(BOTH)
        xpart = lax.dynamic_slice_in_dim(xaxis_values, part * modes, modes)

        def precondition(received, rims):
            return plain_modes(
                received, npy, npz, ly, lz, xpart, yaxis_values, zaxis_values, yaxis_vectors, zaxis_vectors
            )

    even, odd = pairwise(even, "pz", 0), odd_pairs(odd, "pz", "py")
    zlow, zhigh, yodd, yeven = call(
        lambda *refs: y_rims_kernel(ly, lz, *refs),
        [(zrims, F32)] * 2 + [(yrim, F32)] * 2, [VMEM] * 3 + [ANY], nx, 4 * nx * 4 * (yrim[0] + zrims[0]),
    )(weighted, odd, even, taps)
    for iteration in range(ITERS):
        last = iteration + 1 == ITERS
        yodd, yeven = paired(yodd, "py"), pairwise(yeven, "py", 0)
        spectral, *residual = call(
            lambda *refs: residual_kernel(lz, zrim[0], *refs),
            [((nx, count), F32)] + [(block, F32)] * last,
            [VMEM] * 10 + [ANY], 6 * count * nx * (nx + 2 * width), 5 * cell + 4 * nx * nx,
            [pltpu.VMEM(block, F32)] * (not last),
        )(weighted, zlow, zhigh, yodd, yeven, stencil, taps, coef, right, vectors, tables[0])
        spectral = lax.all_to_all(spectral, BOTH, split_axis=0, concat_axis=0, tiled=True)
        spectral = precondition(spectral, not last)
        spectral = lax.all_to_all(spectral, BOTH, split_axis=0, concat_axis=0, tiled=True)
        cost = (6 * count * nx * nx, 4 * cell + 4 * nx * nx)
        if last:
            field, residual = call(
                last_update_kernel, [(block, F32), (block, F32)], [VMEM] * 4, *cost,
                [pltpu.VMEM(block, F32), dma((2,))], [HBM] * 2,
            )(spectral, vectors, field, *residual)
        elif fast:
            field, weighted, zlow, zhigh, yodd, yeven = call(
                lambda *refs: rim_update_kernel(ly, lz, devices, *refs),
                [(block, F32)] * 2 + [(zrim, F32)] * 2 + [(yrim, F32)] * 2, [VMEM] * 6, *cost,
            )(spectral, vectors, field, coef, zlow, zhigh)
        else:
            field, weighted, zlow, zhigh = call(
                lambda *refs: update_kernel(ly, lz, *refs), [(block, F32)] * 2 + [(zrim, F32)] * 2, [VMEM] * 4, *cost,
            )(spectral, vectors, field, coef)
            zlow, zhigh = around(zhigh, "pz", 1), around(zlow, "pz", -1)
            yodd, yeven = call(
                lambda *refs: next_y_rims_kernel(ly, lz, *refs),
                [(yrim, F32)] * 2, [VMEM] * 3, nx, 4 * nx * 4 * yrim[0],
            )(weighted, zlow, zhigh)
    return (field.reshape(solution.shape), residual.reshape(solution.shape))


def solution(mesh):
    return jax.shard_map(
        shards,
        mesh=mesh,
        in_specs=(
            P("py", "pz", None),
            P("py", "pz", None),
            P("py", "pz", None),
            P(),
            P(),
            P(None, None, "py"),
            P(None, None, "pz"),
            P(),
            P(),
            P(),
            P(),
            P(),
            P(),
        ),
        out_specs=(P("py", "pz", None), P("py", "pz", None)),
        check_vma=False,
    )
```

```python
import jax
import jax.numpy as jnp
import numpy as np
from jax import lax
from jax.experimental import pallas as pl
from jax.experimental.pallas import tpu as pltpu
from jax.sharding import PartitionSpec as P

ITERS = 2
REACH = 3
LANES = 128
HIGH = lax.Precision.HIGHEST
BOTH = ("py", "pz")
F32 = jnp.float32
BF16 = jnp.bfloat16
VMEM = pl.BlockSpec(memory_space=pltpu.VMEM)
HBM = pl.BlockSpec(memory_space=pltpu.HBM)
ANY = pl.BlockSpec(memory_space=pl.ANY)


def up8(count):
    return -(-count // 8) * 8


def split(value):
    high = value.astype(BF16)
    return high, (value - high.astype(F32)).astype(BF16)


def exact(left, right, sides=(1, 0)):
    return lax.dot_general(
        left, right, (((sides[0],), (sides[1],)), ((), ())), precision=HIGH, preferred_element_type=F32
    )


def fetch(pairs, sem):
    copies = [pltpu.make_async_copy(source, target, sem.at[i]) for i, (source, target) in enumerate(pairs)]
    for copy in copies:
        copy.start()
    for copy in copies:
        copy.wait()


def in_hbm(*arrays):
    return [pltpu.with_memory_space_constraint(array, pltpu.HBM) for array in arrays]


def mul(left, right):
    return lax.dot_general(left, right, (((1,), (0,)), ((), ())), preferred_element_type=F32)


def mul_t(left, right):
    return lax.dot_general(left, right, (((1,), (1,)), ((), ())), preferred_element_type=F32)


def call(kernel, outs, specs, flops, cost_bytes, scratch=(), out_specs=None):
    return pl.pallas_call(
        kernel,
        out_shape=[jax.ShapeDtypeStruct(shape, dtype) for shape, dtype in outs],
        in_specs=specs,
        out_specs=out_specs or [VMEM] * len(outs),
        scratch_shapes=list(scratch),
        compiler_params=pltpu.CompilerParams(vmem_limit_bytes=32 * 1024 * 1024),
        cost_estimate=pl.CostEstimate(flops=flops, bytes_accessed=cost_bytes, transcendentals=0),
    )


def store_z_rims(ly, lz, weighted, low_ref, high_ref):
    for y in range(ly):
        low_ref[y * REACH : (y + 1) * REACH, :] = weighted[y * lz : y * lz + REACH, :]
        high_ref[y * REACH : (y + 1) * REACH, :] = weighted[(y + 1) * lz - REACH : (y + 1) * lz, :]


def coefficient_kernel(
    ly, lz, table_ref, span_ref, field_ref, coef_ref, weighted_ref, even_ref, odd_ref, yodd_ref, yeven_ref,
    table, span, field, sem,
):
    fetch(((table_ref, table), (span_ref, span), (field_ref, field)), sem)
    first = lax.rem(lax.axis_index("py") + lax.axis_index("pz"), 2) == 1
    half = ly * REACH
    entries = [table[entry] for entry in range(table_ref.shape[0])]
    for start in range(0, span.shape[0], lz):
        rows = pl.ds(start, lz)
        index = span[rows, :]
        coef = jnp.full(index.shape, entries[0], F32)
        for entry in range(1, len(entries)):
            coef = jnp.where(index == entry, entries[entry], coef)
        coef_ref[rows, :] = coef
        weighted = coef * field[rows, :]
        weighted_ref[rows, :] = weighted
        for value, at in ((weighted, 0), (coef, half)):
            rim = pl.ds(at + start // lz * REACH, REACH)
            low, high = value[:REACH], value[lz - REACH :]
            even_ref[rim, :] = jnp.where(first, high, low)
            odd_ref[rim, :] = jnp.where(first, low, high)
    store_y_rims(own_rim(ly, lz, weighted_ref), yodd_ref, yeven_ref)


def store_y_rims(pieces, odd_ref, even_ref):
    first = lax.rem(lax.axis_index("py"), 2) == 0
    at = 0
    for value, count, rows in pieces:
        low, high = value[:count, :], value[rows - count : rows, :]
        even_ref[at : at + count, :] = jnp.where(first, high, low)
        odd_ref[at : at + count, :] = jnp.where(first, low, high)
        at += count
    if at < even_ref.shape[0]:
        for ref in (even_ref, odd_ref):
            ref[at:, :] = jnp.zeros((ref.shape[0] - at, ref.shape[1]), F32)


def own_rim(ly, lz, weighted):
    return [(weighted, REACH * lz, ly * lz)]


def corners(ly, zlow, zhigh):
    return [(value, REACH * REACH, ly * REACH) for value in (zlow, zhigh)]


def y_rims_kernel(ly, odd_ref, even_ref, _, zlow_ref, zhigh_ref, yodd_ref, yeven_ref):
    first = lax.rem(lax.axis_index("py") + lax.axis_index("pz"), 2) == 1
    zlow_ref[...] = jnp.where(first, odd_ref[...], even_ref[...])
    zhigh_ref[...] = jnp.where(first, even_ref[...], odd_ref[...])
    store_y_rims(corners(ly, zlow_ref, zhigh_ref), yodd_ref, yeven_ref)


def next_y_rims_kernel(ly, lz, weighted_ref, zlow_ref, zhigh_ref, yodd_ref, yeven_ref):
    store_y_rims(own_rim(ly, lz, weighted_ref) + corners(ly, zlow_ref, zhigh_ref), yodd_ref, yeven_ref)


def point_columns(ly, lz):
    below, above = range(-REACH, 0), range(REACH)
    halves = []
    for half in range(2):
        first = 0 if half == 0 else ly // 2 - REACH
        points = [(first + y, z) for y in range(ly // 2 + REACH) for z in range(lz)]
        points += [(y, z) for y in range(ly) for z in below]
        points += [(y, lz + z) for y in range(ly) for z in above]
        ys = below if half == 0 else [ly + y for y in above]
        points += [(y, z) for y in ys for z in range(lz)]
        points += [(y, z) for y in ys for z in below]
        points += [(y, lz + z) for y in ys for z in above]
        halves += points + [(1 << 20, 1 << 20)] * (-len(points) % LANES)
    return np.array(halves, np.int32).T.copy()


def stencil_kernel(
    ly, lz, ny, nz, points_hbm, ybands_hbm, zbands_hbm, xbands_hbm, _, out_ref, taps_ref,
    points_ref, ybands_ref, zbands_ref, xbands_ref, sem,
):
    fetch(
        (
            (points_hbm, points_ref), (ybands_hbm, ybands_ref), (zbands_hbm, zbands_ref), (xbands_hbm, xbands_ref),
        ),
        sem,
    )
    count = ly * lz // 2
    width = out_ref.shape[1]
    for half in range(2):
        rows = lax.broadcasted_iota(jnp.int32, (count, 1), 0) + half * count
        columns = pl.ds(half * width, width)
        factors = []
        for bands_ref, length, row, column, first, whole in (
            (ybands_ref, ly, lax.div(rows, lz), points_ref[0:1, columns], lax.axis_index("py") * ly, ny),
            (zbands_ref, lz, lax.rem(rows, lz), points_ref[1:2, columns], lax.axis_index("pz") * lz, nz),
        ):
            pick = (lax.broadcasted_iota(jnp.int32, (count, length), 1) == row).astype(F32)
            spot = column + first
            inside = (spot >= 0) & (spot < whole)
            distance = jnp.where(inside, column, 1 << 20) - row
            here = [distance == offset - REACH for offset in range(2 * REACH + 1)]
            for matrix in range(2):
                taps = exact(pick, bands_ref[:, matrix, :], (1, 1))
                dense = jnp.zeros(distance.shape, F32)
                for offset in range(2 * REACH + 1):
                    dense = jnp.where(here[offset], taps[:, offset : offset + 1], dense)
                factors.append(dense)
        ystiff, ymass, zstiff, zmass = factors
        for part, value in enumerate((ymass * zmass, ystiff * zmass + ymass * zstiff)):
            at = (4 * half + part) * count
            out_ref[at : at + count, :], out_ref[at + 2 * count : at + 3 * count, :] = split(value)
    nx = xbands_ref.shape[2]
    lane = lax.broadcasted_iota(jnp.int32, (1, nx), 1)
    for offset in range(2 * REACH + 1):
        move = offset - REACH
        inside = (lane - move >= 0) & (lane - move < nx)
        for matrix in range(2):
            band = xbands_ref[offset, matrix : matrix + 1, :]
            band = pltpu.roll(band, move % nx, 1) if move else band
            taps_ref[2 * offset + matrix] = jnp.broadcast_to(jnp.where(inside, band, 0.0), (8, nx))


def xvectors_kernel(source, out_ref, held, sem):
    fetch(((source, held),), sem)
    high, low = split(held[...].T)
    out_ref[: high.shape[0], :] = high
    out_ref[high.shape[0] :, :] = low


def tables_kernel(
    npy, npz, ly, lz, xvec_hbm, yvec_hbm, zvec_hbm, xval_hbm, yval_hbm, zval_hbm, _,
    xout_ref, zhigh_ref, zlow_ref, ydown_ref, yup_ref, sums_ref, rimhigh_ref, rimlow_ref,
    xvec_ref, yvec_ref, zvec_ref, xval_ref, yval_ref, zval_ref, sem,
):
    fetch(
        (
            (xvec_hbm, xvec_ref), (yvec_hbm, yvec_ref), (zvec_hbm, zvec_ref),
            (xval_hbm, xval_ref), (yval_hbm, yval_ref), (zval_hbm, zval_ref),
        ),
        sem,
    )
    ny, nz = npy * ly, npz * lz
    nx = xvec_ref.shape[0]
    high, low = split(xvec_ref[...].T)
    xout_ref[:nx, :] = high
    xout_ref[nx:, :] = low
    twice = (
        lax.broadcasted_iota(jnp.int32, (nz, 2 * nz), 0)
        == lax.rem(lax.broadcasted_iota(jnp.int32, (nz, 2 * nz), 1), nz)
    ).astype(F32)
    pair = exact(zvec_ref[...], twice)
    half = lax.broadcasted_iota(jnp.int32, pair.shape, 1) >= nz
    zhigh_ref[...] = jnp.zeros(zhigh_ref.shape, BF16)
    zlow_ref[...] = jnp.zeros(zlow_ref.shape, BF16)
    for parity in range(2):
        high, low = split(jnp.where(half == (parity == 1), pair, 0.0))
        for yl in range(parity, ly // 2, 2):
            for block in range(npz):
                to = (pl.ds((block * ly // 2 + yl) * lz, lz), pl.ds(yl // 2 * 2 * nz, 2 * nz))
                zhigh_ref[to] = high[block * lz : (block + 1) * lz, :]
                zlow_ref[to] = low[block * lz : (block + 1) * lz, :]
    shape = (rimhigh_ref.shape[0], 1)
    row = lax.broadcasted_iota(jnp.int32, shape, 0)
    block, spot = lax.div(row, LANES // 2), lax.rem(row, LANES // 2)
    above = spot >= ly * REACH
    spot = jnp.where(above, spot - ly * REACH, spot)
    yrow = jnp.where(spot < ly * REACH, lax.div(spot, REACH), 2 * ly)
    z = block * lz + lax.rem(spot, REACH) + jnp.where(above, lz, -REACH)
    rim = exact((lax.broadcasted_iota(jnp.int32, (shape[0], nz), 1) == z).astype(F32), pair)
    late = (lax.broadcasted_iota(jnp.int32, rim.shape, 1) >= nz).astype(jnp.int32)
    for chunk in range(ly // 2):
        columns = pl.ds(chunk * 2 * nz, 2 * nz)
        rimhigh_ref[:, columns], rimlow_ref[:, columns] = split(jnp.where(yrow - 2 * chunk == late, rim, 0.0))

    def y_of(p):
        spot = lax.div(p, npy)
        return lax.rem(p, npy) * ly + 2 * lax.rem(spot, ly // 2) + lax.div(spot, ly // 2)

    def four(array):
        high, low = split(array)
        late = lax.broadcasted_iota(jnp.int32, array.shape, 1) >= 2 * ny
        return jnp.where(late, low.astype(F32), high.astype(F32)).astype(BF16)

    lane = lax.broadcasted_iota(jnp.int32, (ny, 4 * ny), 1)
    row = lax.broadcasted_iota(jnp.int32, (ny, 4 * ny), 0)
    moved = (row == y_of(lax.rem(lane, ny))).astype(F32)
    ydown_ref[...] = four(exact(yvec_ref[...].T, moved))
    order = (
        lax.broadcasted_iota(jnp.int32, (ny, ny), 1) == y_of(lax.broadcasted_iota(jnp.int32, (ny, ny), 0))
    ).astype(F32)
    copies = (row == lax.rem(lane, ny)).astype(F32)
    yup_ref[...] = four(exact(exact(order, yvec_ref[...]), copies))
    square = (ny, ny)
    diagonal = lax.broadcasted_iota(jnp.int32, square, 0) == lax.broadcasted_iota(jnp.int32, square, 1)
    ycolumn = jnp.sum(jnp.where(diagonal, yval_ref[...], 0.0), axis=1, keepdims=True)
    yz = ycolumn + exact(jnp.broadcast_to(zval_ref[...], (8, nz)), twice)[0:1]
    late = lax.broadcasted_iota(jnp.int32, (1, 2 * nz), 1) >= nz
    modes = nx // (npy * npz)
    first = (lax.axis_index("py") * npz + lax.axis_index("pz")) * modes
    for mode in range(0, modes, 2):
        x = jnp.where(late, xval_ref[first + mode + 1], xval_ref[first + mode])
        sums_ref[:, mode * nz : (mode + 2) * nz] = yz + x


def residual_kernel(lz, zrim, parts, *refs):
    weighted_ref, zlow_ref, zhigh_ref, *refs = refs
    yodd_refs, yeven_refs, refs = refs[:parts], refs[parts : 2 * parts], refs[2 * parts :]
    stencil_ref, taps_ref, coef_ref, right_ref, vectors_ref, _, spectral_ref, residual_ref = refs
    count, nx = weighted_ref.shape
    part, need = count // 2, weighted_ref.shape[0] // 2 + REACH * lz
    own = split(weighted_ref[...])
    zrims = split(jnp.concatenate([zlow_ref[:zrim, :], zhigh_ref[:zrim, :]], axis=0))
    fields = []
    even = lax.rem(lax.axis_index("py"), 2) == 0
    yodd, yeven = (jnp.concatenate([ref[...] for ref in refs], axis=0) for refs in (yodd_refs, yeven_refs))
    below, above = jnp.where(even, yodd, yeven), jnp.where(even, yeven, yodd)
    for half, rim in enumerate((below, above)):
        missing = stencil_ref.shape[1] - need - 2 * zrim - rim.shape[0]
        yrim = split(jnp.concatenate([rim, jnp.zeros((missing, nx), F32)], axis=0) if missing else rim)
        first = half * (count - need)
        high, low = (
            jnp.concatenate([own[k][first : first + need], zrims[k], yrim[k]], axis=0) for k in range(2)
        )
        stencil = stencil_ref[4 * half * part : 4 * (half + 1) * part, :]
        both = mul(stencil, high)
        both = both[: 2 * part] + both[2 * part :] + mul(stencil[: 2 * part], low)
        fields.append((both[:part], both[part:]))
    for start in range(0, count, 8):
        mass, stiff = (field[start % part : start % part + 8] for field in fields[start // part])
        applied = None
        for offset in range(2 * REACH + 1):
            move = offset - REACH
            term = taps_ref[2 * offset] * mass + taps_ref[2 * offset + 1] * stiff
            term = pltpu.roll(term, -move % nx, 1) if move else term
            applied = term if applied is None else applied + term
        rows = pl.ds(start, 8)
        residual_ref[rows, :] = right_ref[rows, :] - coef_ref[rows, :] * applied
    high, low = split(residual_ref[...])
    product = mul_t(jnp.concatenate([high, low], axis=0), vectors_ref[:nx, :])
    product = product[:count] + product[count:] + mul_t(high, vectors_ref[nx:, :])
    spectral_ref[...] = product.T


def modes_kernel(npy, npz, rims, *refs):
    zhigh_ref, zlow_ref, ydown_ref, yup_ref, sums_ref, *rim_refs, in_ref, out_ref, turn_ref = refs
    count = in_ref.shape[0] // (npy * npz)
    size = out_ref.shape[0] // (npy * npz)
    nz = sums_ref.shape[1] // count
    width = zhigh_ref.shape[1]
    chunks = 2 * width // LANES
    step = turn_ref.shape[0] // (npy * chunks)
    zhigh, zlow = zhigh_ref[...], zlow_ref[...]

    def three(value, product, whigh, wlow):
        rows = value.shape[0]
        high, low = split(value)
        both = product(jnp.concatenate([high, low], axis=0), whigh)
        return both[:rows] + both[rows:] + product(high, wlow)

    def early(first, second):
        late = lax.broadcasted_iota(jnp.int32, first.shape, 1) >= LANES // 2
        return jnp.where(late, pltpu.roll(second, LANES // 2, 1), first)

    def later(first, second):
        late = lax.broadcasted_iota(jnp.int32, first.shape, 1) >= LANES // 2
        return jnp.where(late, second, pltpu.roll(first, LANES // 2, 1))

    def by_mode(mode, chunk):
        return pl.ds(chunk * npy * step + mode, npy, stride=step)

    def by_device(device, chunk):
        return pl.ds((chunk * npy + device) * step, count)

    halves = [[], []]
    for p in range(npy):
        blocks = [in_ref[(p * npz + b) * count : (p * npz + b + 1) * count, :] for b in range(npz)]
        for half, joined in zip(halves, (early, later)):
            half.append(jnp.concatenate([joined(blocks[b], blocks[b + 1]) for b in range(0, npz, 2)], axis=1))
    part = three(jnp.concatenate(halves[0] + halves[1], axis=0), mul, zhigh, zlow)
    for chunk in range(chunks):
        half, lane = divmod(chunk * LANES, width)
        for p in range(npy):
            row = (half * npy + p) * count
            turn_ref[by_device(p, chunk), :] = part[row : row + count, lane : lane + LANES]
    pairs = []
    for mode in range(0, count, 2):
        tiles = [(turn_ref[by_mode(mode, c), :], turn_ref[by_mode(mode + 1, c), :]) for c in range(chunks)]
        pairs.append(jnp.concatenate([early(*tile) for tile in tiles] + [later(*tile) for tile in tiles], axis=0))
    stacked = jnp.concatenate(pairs, axis=1)

    def four(value):
        high, low = split(value)
        return jnp.concatenate([high, low, high, low], axis=0)

    modes = mul(ydown_ref[...], four(stacked)) / sums_ref[...]
    restored = mul(yup_ref[...], four(modes))
    for mode in range(0, count, 2):
        block = restored[:, mode * nz : (mode + 2) * nz]
        for c in range(chunks):
            even = block[c * npy : (c + 1) * npy]
            odd = block[(chunks + c) * npy : (chunks + c + 1) * npy]
            turn_ref[by_mode(mode, c), :] = early(even, odd)
            turn_ref[by_mode(mode + 1, c), :] = later(even, odd)
    rows = [
        jnp.concatenate(
            [turn_ref[by_device(p, half * chunks // 2 + c), :] for c in range(chunks // 2)], axis=1
        )
        for half in range(2)
        for p in range(npy)
    ]
    spectral = jnp.concatenate(rows, axis=0)
    back = three(spectral, mul_t, zhigh, zlow)
    total = npy * count
    if rims:
        side = [
            three(spectral[half * total : (half + 1) * total], mul_t, *(ref[:, pl.ds(half * width, width)] for ref in rim_refs))
            for half in range(2)
        ]
        side = side[0] + side[1]
    for p in range(npy):
        for b in range(0, npz, 2):
            first, second = (
                back[k * total + p * count : k * total + (p + 1) * count, b * LANES // 2 : b * LANES // 2 + LANES]
                for k in range(2)
            )
            at = (p * npz + b) * size
            out_ref[at : at + count, :] = early(first, second)
            out_ref[at + size : at + size + count, :] = later(first, second)
            if rims:
                row, middle = p * count, p * count + count // 2
                first = side[row:middle, b * LANES // 2 : b * LANES // 2 + LANES]
                second = side[middle : row + count, b * LANES // 2 : b * LANES // 2 + LANES]
                out_ref[at + count : at + size, :] = early(first, second)
                out_ref[at + size + count : at + 2 * size, :] = later(first, second)


def transformed(points, vectors_ref):
    rows, nx = points.shape
    high, low = split(points)
    both = mul(jnp.concatenate([high, low], axis=0), vectors_ref[:nx, :])
    return both[:rows] + both[rows:] + mul(high, vectors_ref[nx:, :])


def from_modes(spectral_ref, vectors_ref):
    return transformed(spectral_ref[...].T, vectors_ref)


def update_kernel(ly, lz, spectral_ref, vectors_ref, field_ref, coef_ref, updated_ref, weighted_ref, low_ref, high_ref):
    updated = field_ref[...] + from_modes(spectral_ref, vectors_ref)
    updated_ref[...] = updated
    weighted = coef_ref[...] * updated
    weighted_ref[...] = weighted
    store_z_rims(ly, lz, weighted, low_ref, high_ref)


def rim_update_kernel(
    ly, lz, devices, spectral_ref, vectors_ref, field_ref, coef_ref, before_low_ref, before_high_ref,
    updated_ref, weighted_ref, zlow_ref, zhigh_ref, yodd_ref, yeven_ref,
):
    nx = vectors_ref.shape[1]
    modes = nx // devices
    size = spectral_ref.shape[0] // devices
    own, rims = [], []
    for d in range(devices):
        own.append(spectral_ref[d * size : d * size + modes, :])
        rim = spectral_ref[d * size + modes : (d + 1) * size, :]
        rims += [rim, pltpu.roll(rim, LANES // 2, 1)]
    points = [jnp.concatenate(own, axis=0).T, jnp.concatenate(rims, axis=0).T[: LANES // 2]]
    update = transformed(jnp.concatenate(points, axis=0), vectors_ref)
    count, half = ly * lz, ly * REACH
    updated = field_ref[...] + update[:count]
    updated_ref[...] = updated
    weighted_ref[...] = coef_ref[...] * updated
    for side, (ref, before_ref) in enumerate(((zlow_ref, before_low_ref), (zhigh_ref, before_high_ref))):
        start = count + side * half
        ref[...] = before_ref[:half, :] + before_ref[half:, :] * update[start : start + half]
    store_y_rims(own_rim(ly, lz, weighted_ref) + corners(ly, zlow_ref, zhigh_ref), yodd_ref, yeven_ref)


def last_update_kernel(spectral_ref, vectors_ref, field_ref, residual_ref, updated_hbm, residual_hbm, held, sem):
    leaving = pltpu.make_async_copy(residual_ref, residual_hbm, sem.at[0])
    leaving.start()
    held[...] = field_ref[...] + from_modes(spectral_ref, vectors_ref)
    fetch(((held, updated_hbm),), sem.at[pl.ds(1, 1)])
    leaving.wait()


def pairwise(value, axis, odd):
    count = lax.axis_size(axis)
    other = [((i + odd) ^ 1) - odd for i in range(count)]
    return lax.ppermute(value, axis, [(i, j if 0 <= j < count else i) for i, j in enumerate(other)])


def paired(value, axis):
    count = lax.axis_size(axis)
    return lax.ppermute(value, axis, [(i, (i + 1 if i % 2 else i - 1) % count) for i in range(count)])


def odd_pairs(value, axis, other):
    count, across = lax.axis_size(axis), lax.axis_size(other)
    first = BOTH.index(axis) == 0

    def spot(i, k):
        return i * across + k if first else k * count + i

    pairs = []
    for i in range(count):
        for k in range(across):
            j = i + 1 if i % 2 else i - 1
            pairs.append((spot(i, k), spot(j, k) if 0 <= j < count else spot(i, k ^ 1)))
    return lax.ppermute(value, BOTH, pairs)


def staggered(value, parity):
    across, count = lax.axis_size("py"), lax.axis_size("pz")
    pairs = []
    for i in range(across):
        for k in range(count):
            j = k + 1 if (i + k) % 2 == parity else k - 1
            other = i ^ 2 if i ^ 2 < across else i
            pairs.append((i * count + k, i * count + j if 0 <= j < count else other * count + k))
    return lax.ppermute(value, BOTH, pairs)


def around(value, axis, step):
    count = lax.axis_size(axis)
    return lax.ppermute(value, axis, [(i, (i + step) % count) for i in range(count)])


def plain_modes(received, npy, npz, ly, lz, xvalues, yvalues, zvalues, yvectors, zvectors):
    count = received.shape[0] // (npy * npz)
    field = received.reshape(npy, npz, count, ly, lz).transpose(2, 0, 3, 1, 4).reshape(count, npy * ly, npz * lz)
    field = jnp.einsum("xyz,yj->xjz", field, yvectors, precision=HIGH)
    field = jnp.einsum("xyz,zk->xyk", field, zvectors, precision=HIGH)
    field = field / (yvalues[None, :, None] + zvalues[None, None, :] + xvalues[:, None, None])
    field = jnp.einsum("xjz,yj->xyz", field, yvectors, precision=HIGH)
    field = jnp.einsum("xyk,zk->xyz", field, zvectors, precision=HIGH)
    field = field.reshape(count, npy, ly, npz, lz).transpose(1, 3, 0, 2, 4)
    return field.reshape(npy * npz * count, ly * lz)


def shards(
    solution,
    right_side,
    span_index,
    coef_table,
    xaxis_bands,
    yaxis_bands,
    zaxis_bands,
    xaxis_vectors,
    yaxis_vectors,
    zaxis_vectors,
    xaxis_values,
    yaxis_values,
    zaxis_values,
):
    npy, npz = lax.axis_size("py"), lax.axis_size("pz")
    ly, lz, nx = solution.shape
    ny, nz = npy * ly, npz * lz
    count, devices = ly * lz, npy * npz
    modes = nx // devices
    field = solution.reshape(count, nx)
    right = right_side.reshape(count, nx)
    block, zrim, yrim = (count, nx), (ly * REACH, nx), (up8(REACH * lz + 2 * REACH * REACH), nx)
    zrims = (2 * ly * REACH, nx)
    cell = count * nx * 4
    dma = pltpu.SemaphoreType.DMA

    coef, weighted, even, odd, yodd, yeven = call(
        lambda *refs: coefficient_kernel(ly, lz, *refs),
        [(block, F32)] * 2 + [(zrims, F32)] * 2 + [((REACH * lz, nx), F32)] * 2,
        [HBM] * 3, count * nx * 16, 4 * cell,
        [pltpu.SMEM(coef_table.shape, F32), pltpu.VMEM(block, jnp.int32), pltpu.VMEM(block, F32), dma((3,))],
    )(*in_hbm(coef_table, span_index.reshape(count, nx), field))

    points = point_columns(ly, lz)
    width = points.shape[1] // 2
    bands = [array.transpose(1, 0, 2) for array in (yaxis_bands, zaxis_bands, xaxis_bands)]
    stencil, taps = call(
        lambda *refs: stencil_kernel(ly, lz, ny, nz, *refs),
        [((4 * count, width), BF16), ((2 * (2 * REACH + 1), 8, nx), F32)],
        [HBM] * 4 + [ANY], count * width * 60, 8 * count * width,
        [pltpu.VMEM(points.shape, jnp.int32)] + [pltpu.VMEM(array.shape, F32) for array in bands] + [dma((4,))],
    )(*in_hbm(jnp.asarray(points), *bands), even)

    fast = (
        modes % 16 == 0 and npz % 2 == 0 and 2 * ly * REACH <= LANES // 2 and npy % 8 == 0 and lz % 16 == 0 and ly % 4 == 0
        and 2 * nz == LANES and 2 * ny == LANES and count == LANES and nx % LANES == 0
    )
    if fast:
        zmat, ymat, rmat = (npz * count // 2, ly * nz // 2), (ny, 4 * ny), (npz * LANES // 2, ly * nz)
        vectors, *tables = call(
            lambda *refs: tables_kernel(npy, npz, ly, lz, *refs),
            [((2 * nx, nx), BF16), (zmat, BF16), (zmat, BF16), (ymat, BF16), (ymat, BF16), ((ny, modes * nz), F32)]
            + [(rmat, BF16)] * 2,
            [HBM] * 6 + [ANY], npz * count * ly * nz * 8, npz * count * ly * nz * 4,
            [pltpu.VMEM(array.shape, F32) for array in (xaxis_vectors, yaxis_vectors, zaxis_vectors)]
            + [pltpu.SMEM((nx,), F32), pltpu.VMEM((1, ny), F32), pltpu.VMEM((1, nz), F32), dma((6,))],
        )(
            *in_hbm(
                xaxis_vectors, yaxis_vectors, zaxis_vectors, xaxis_values,
                yaxis_values.reshape(1, ny), zaxis_values.reshape(1, nz),
            ),
            taps,
        )

        def precondition(received, rims):
            size = modes * 3 // 2 if rims else modes
            return call(
                lambda *refs: modes_kernel(npy, npz, rims, *refs),
                [((devices * size, count), F32)], [VMEM] * (8 if rims else 6), 6 * 2 * count * nx * ly * nz, 2 * cell,
                [pltpu.VMEM((ly * nz // LANES * npy * (modes + 8), LANES), F32)],
            )(*(tables if rims else tables[:5]), received)[0]
    else:
        tables = [taps]
        vectors = call(
            xvectors_kernel, [((2 * nx, nx), BF16)], [HBM], nx * nx * 40, 8 * nx * nx,
            [pltpu.VMEM((nx, nx), F32), dma((1,))],
        )(*in_hbm(xaxis_vectors))[0]
        part = lax.axis_index(BOTH)
        xpart = lax.dynamic_slice_in_dim(xaxis_values, part * modes, modes)

        def precondition(received, rims):
            return plain_modes(
                received, npy, npz, ly, lz, xpart, yaxis_values, zaxis_values, yaxis_vectors, zaxis_vectors
            )

    even, odd = staggered(even, 1), staggered(odd, 0)
    zlow, zhigh, *corner = call(
        lambda *refs: y_rims_kernel(ly, *refs),
        [(zrims, F32)] * 2 + [((up8(2 * REACH * REACH), nx), F32)] * 2,
        [VMEM] * 2 + [ANY], nx, 4 * nx * 4 * zrims[0],
    )(odd, even, taps)
    yodd, yeven = [yodd, corner[0]], [yeven, corner[1]]
    for iteration in range(ITERS):
        last = iteration + 1 == ITERS
        yodd, yeven = [paired(value, "py") for value in yodd], [pairwise(value, "py", 0) for value in yeven]
        parts = len(yodd)
        spectral, *residual = call(
            lambda *refs: residual_kernel(lz, zrim[0], parts, *refs),
            [((nx, count), F32)] + [(block, F32)] * last,
            [VMEM] * (8 + 2 * parts) + [ANY], 6 * count * nx * (nx + 2 * width), 5 * cell + 4 * nx * nx,
            [pltpu.VMEM(block, F32)] * (not last),
        )(weighted, zlow, zhigh, *yodd, *yeven, stencil, taps, coef, right, vectors, tables[0])
        spectral = lax.all_to_all(spectral, BOTH, split_axis=0, concat_axis=0, tiled=True)
        spectral = precondition(spectral, not last)
        spectral = lax.all_to_all(spectral, BOTH, split_axis=0, concat_axis=0, tiled=True)
        cost = (6 * count * nx * nx, 4 * cell + 4 * nx * nx)
        if last:
            field, residual = call(
                last_update_kernel, [(block, F32), (block, F32)], [VMEM] * 4, *cost,
                [pltpu.VMEM(block, F32), dma((2,))], [HBM] * 2,
            )(spectral, vectors, field, *residual)
        elif fast:
            field, weighted, zlow, zhigh, *yrims = call(
                lambda *refs: rim_update_kernel(ly, lz, devices, *refs),
                [(block, F32)] * 2 + [(zrim, F32)] * 2 + [(yrim, F32)] * 2, [VMEM] * 6, *cost,
            )(spectral, vectors, field, coef, zlow, zhigh)
        else:
            field, weighted, zlow, zhigh = call(
                lambda *refs: update_kernel(ly, lz, *refs), [(block, F32)] * 2 + [(zrim, F32)] * 2, [VMEM] * 4, *cost,
            )(spectral, vectors, field, coef)
            zlow, zhigh = around(zhigh, "pz", 1), around(zlow, "pz", -1)
            yrims = call(
                lambda *refs: next_y_rims_kernel(ly, lz, *refs),
                [(yrim, F32)] * 2, [VMEM] * 3, nx, 4 * nx * 4 * yrim[0],
            )(weighted, zlow, zhigh)
        yodd, yeven = ([value] for value in yrims) if not last else (None, None)
    return (field.reshape(solution.shape), residual.reshape(solution.shape))


def solution(mesh):
    return jax.shard_map(
        shards,
        mesh=mesh,
        in_specs=(
            P("py", "pz", None),
            P("py", "pz", None),
            P("py", "pz", None),
            P(),
            P(),
            P(None, None, "py"),
            P(None, None, "pz"),
            P(),
            P(),
            P(),
            P(),
            P(),
            P(),
        ),
        out_specs=(P("py", "pz", None), P("py", "pz", None)),
        check_vma=False,
    )
```

```python
import jax
import jax.numpy as jnp
import numpy as np
from jax import lax
from jax.experimental import pallas as pl
from jax.experimental.pallas import tpu as pltpu
from jax.sharding import PartitionSpec as P

ITERS = 2
REACH = 3
LANES = 128
HIGH = lax.Precision.HIGHEST
BOTH = ("py", "pz")
F32 = jnp.float32
BF16 = jnp.bfloat16
VMEM = pl.BlockSpec(memory_space=pltpu.VMEM)
HBM = pl.BlockSpec(memory_space=pltpu.HBM)
ANY = pl.BlockSpec(memory_space=pl.ANY)


def up8(count):
    return -(-count // 8) * 8


def split(value):
    high = value.astype(BF16)
    return high, (value - high.astype(F32)).astype(BF16)


def exact(left, right, sides=(1, 0)):
    return lax.dot_general(
        left, right, (((sides[0],), (sides[1],)), ((), ())), precision=HIGH, preferred_element_type=F32
    )


def fetch(pairs, sem):
    copies = [pltpu.make_async_copy(source, target, sem.at[i]) for i, (source, target) in enumerate(pairs)]
    for copy in copies:
        copy.start()
    for copy in copies:
        copy.wait()


def in_hbm(*arrays):
    return [pltpu.with_memory_space_constraint(array, pltpu.HBM) for array in arrays]


def mul(left, right):
    return lax.dot_general(left, right, (((1,), (0,)), ((), ())), preferred_element_type=F32)


def mul_t(left, right):
    return lax.dot_general(left, right, (((1,), (1,)), ((), ())), preferred_element_type=F32)


def call(kernel, outs, specs, flops, cost_bytes, scratch=(), out_specs=None):
    return pl.pallas_call(
        kernel,
        out_shape=[jax.ShapeDtypeStruct(shape, dtype) for shape, dtype in outs],
        in_specs=specs,
        out_specs=out_specs or [VMEM] * len(outs),
        scratch_shapes=list(scratch),
        compiler_params=pltpu.CompilerParams(vmem_limit_bytes=32 * 1024 * 1024),
        cost_estimate=pl.CostEstimate(flops=flops, bytes_accessed=cost_bytes, transcendentals=0),
    )


def store_z_rims(ly, lz, weighted, low_ref, high_ref):
    for y in range(ly):
        low_ref[y * REACH : (y + 1) * REACH, :] = weighted[y * lz : y * lz + REACH, :]
        high_ref[y * REACH : (y + 1) * REACH, :] = weighted[(y + 1) * lz - REACH : (y + 1) * lz, :]


def coefficient_kernel(ly, lz, small, *refs):
    table_ref, span_ref, field_ref, *refs = refs
    sources, refs = refs[:small], refs[small:]
    coef_ref, weighted_ref, even_ref, odd_ref, yodd_ref, yeven_ref, *refs = refs
    targets, (table, span, field, sem) = refs[:small], refs[small:]
    fetch([(table_ref, table), (span_ref, span), (field_ref, field), *zip(sources, targets)], sem)
    first = lax.rem(lax.axis_index("py") + lax.axis_index("pz"), 2) == 1
    half = ly * REACH
    entries = [table[entry] for entry in range(table_ref.shape[0])]
    for start in range(0, span.shape[0], lz):
        rows = pl.ds(start, lz)
        index = span[rows, :]
        coef = jnp.full(index.shape, entries[0], F32)
        for entry in range(1, len(entries)):
            coef = jnp.where(index == entry, entries[entry], coef)
        coef_ref[rows, :] = coef
        weighted = coef * field[rows, :]
        weighted_ref[rows, :] = weighted
        for value, at in ((weighted, 0), (coef, half)):
            rim = pl.ds(at + start // lz * REACH, REACH)
            low, high = value[:REACH], value[lz - REACH :]
            even_ref[rim, :] = jnp.where(first, high, low)
            odd_ref[rim, :] = jnp.where(first, low, high)
    store_y_rims(own_rim(ly, lz, weighted_ref), yodd_ref, yeven_ref)
    ybands = targets[1]
    for ref in (yodd_ref, yeven_ref):
        for matrix in range(2):
            at = REACH * lz + 8 * matrix
            ref[at : at + ybands.shape[0], :ly] = ybands[:, matrix, :]


def store_y_rims(pieces, odd_ref, even_ref):
    first = lax.rem(lax.axis_index("py"), 2) == 0
    at = 0
    for value, count, rows in pieces:
        low, high = value[:count, :], value[rows - count : rows, :]
        even_ref[at : at + count, :] = jnp.where(first, high, low)
        odd_ref[at : at + count, :] = jnp.where(first, low, high)
        at += count
    if at < even_ref.shape[0]:
        for ref in (even_ref, odd_ref):
            ref[at:, :] = jnp.zeros((ref.shape[0] - at, ref.shape[1]), F32)


def own_rim(ly, lz, weighted):
    return [(weighted, REACH * lz, ly * lz)]


def corners(ly, zlow, zhigh):
    return [(value, REACH * REACH, ly * REACH) for value in (zlow, zhigh)]


def y_rims_kernel(ly, odd_ref, even_ref, _, zlow_ref, zhigh_ref, yodd_ref, yeven_ref):
    first = lax.rem(lax.axis_index("py") + lax.axis_index("pz"), 2) == 1
    zlow_ref[...] = jnp.where(first, odd_ref[...], even_ref[...])
    zhigh_ref[...] = jnp.where(first, even_ref[...], odd_ref[...])
    store_y_rims(corners(ly, zlow_ref, zhigh_ref), yodd_ref, yeven_ref)


def next_y_rims_kernel(ly, lz, weighted_ref, zlow_ref, zhigh_ref, yodd_ref, yeven_ref):
    store_y_rims(own_rim(ly, lz, weighted_ref) + corners(ly, zlow_ref, zhigh_ref), yodd_ref, yeven_ref)


def point_columns(ly, lz):
    below, above = range(-REACH, 0), range(REACH)
    halves = []
    for half in range(2):
        first = 0 if half == 0 else ly // 2 - REACH
        points = [(first + y, z) for y in range(ly // 2 + REACH) for z in range(lz)]
        points += [(y, z) for y in range(ly) for z in below]
        points += [(y, lz + z) for y in range(ly) for z in above]
        ys = below if half == 0 else [ly + y for y in above]
        points += [(y, z) for y in ys for z in range(lz)]
        points += [(y, z) for y in ys for z in below]
        points += [(y, lz + z) for y in ys for z in above]
        halves += points + [(1 << 20, 1 << 20)] * (-len(points) % LANES)
    return np.array(halves, np.int32).T.copy()


def stencil_kernel(ly, lz, ny, nz, later, points_ref, ybands_ref, zbands_ref, *refs):
    sources, (_, out_ref, *refs) = refs[:later], refs[later:]
    copies = [pltpu.make_async_copy(*pair, refs[-1].at[i]) for i, pair in enumerate(zip(sources, refs[:later]))]
    for copy in copies:
        copy.start()
    count = ly * lz // 2
    width = out_ref.shape[1]
    for half in range(2):
        rows = lax.broadcasted_iota(jnp.int32, (count, 1), 0) + half * count
        columns = pl.ds(half * width, width)
        factors = []
        for bands_ref, length, row, column, first, whole in (
            (ybands_ref, ly, lax.div(rows, lz), points_ref[0:1, columns], lax.axis_index("py") * ly, ny),
            (zbands_ref, lz, lax.rem(rows, lz), points_ref[1:2, columns], lax.axis_index("pz") * lz, nz),
        ):
            pick = (lax.broadcasted_iota(jnp.int32, (count, length), 1) == row).astype(F32)
            spot = column + first
            inside = (spot >= 0) & (spot < whole)
            distance = jnp.where(inside, column, 1 << 20) - row
            here = [distance == offset - REACH for offset in range(2 * REACH + 1)]
            for matrix in range(2):
                taps = exact(pick, bands_ref[:, matrix, :], (1, 1))
                dense = jnp.zeros(distance.shape, F32)
                for offset in range(2 * REACH + 1):
                    dense = jnp.where(here[offset], taps[:, offset : offset + 1], dense)
                factors.append(dense)
        ystiff, ymass, zstiff, zmass = factors
        for part, value in enumerate((ymass * zmass, ystiff * zmass + ymass * zstiff)):
            at = (4 * half + part) * count
            out_ref[at : at + count, :], out_ref[at + 2 * count : at + 3 * count, :] = split(value)
    for copy in copies:
        copy.wait()


def store_taps(xbands_ref, taps_ref):
    nx = xbands_ref.shape[2]
    lane = lax.broadcasted_iota(jnp.int32, (1, nx), 1)
    for offset in range(2 * REACH + 1):
        move = offset - REACH
        inside = (lane - move >= 0) & (lane - move < nx)
        for matrix in range(2):
            band = xbands_ref[offset, matrix : matrix + 1, :]
            band = pltpu.roll(band, move % nx, 1) if move else band
            taps_ref[2 * offset + matrix] = jnp.broadcast_to(jnp.where(inside, band, 0.0), (8, nx))


def doubled(size):
    row = lax.broadcasted_iota(jnp.int32, (size, 2 * size), 0)
    return (row == lax.rem(lax.broadcasted_iota(jnp.int32, (size, 2 * size), 1), size)).astype(F32)


def xvectors_kernel(source, xbands_ref, out_ref, taps_ref, held, sem):
    store_taps(xbands_ref, taps_ref)
    fetch(((source, held),), sem)
    high, low = split(held[...].T)
    out_ref[: high.shape[0], :] = high
    out_ref[high.shape[0] :, :] = low


def tables_kernel(
    npy, npz, ly, lz, xvec_ref, yvec_ref, zvec_ref, yval_ref, zval_ref, xbands_ref, xval_hbm, _,
    xout_ref, taps_ref, sums_ref, zhigh_ref, zlow_ref, ydown_ref, yup_ref, rimhigh_ref, rimlow_ref, xval_ref, sem,
):
    fetching = pltpu.make_async_copy(xval_hbm, xval_ref, sem.at[0])
    fetching.start()
    store_taps(xbands_ref, taps_ref)
    ny, nz = npy * ly, npz * lz
    nx = xvec_ref.shape[0]
    high, low = split(xvec_ref[...].T)
    xout_ref[:nx, :] = high
    xout_ref[nx:, :] = low
    pair = exact(zvec_ref[...], doubled(nz))
    half = lax.broadcasted_iota(jnp.int32, pair.shape, 1) >= nz
    zhigh_ref[...] = jnp.zeros(zhigh_ref.shape, BF16)
    zlow_ref[...] = jnp.zeros(zlow_ref.shape, BF16)
    for parity in range(2):
        high, low = split(jnp.where(half == (parity == 1), pair, 0.0))
        for yl in range(parity, ly // 2, 2):
            for block in range(npz):
                to = (pl.ds((block * ly // 2 + yl) * lz, lz), pl.ds(yl // 2 * 2 * nz, 2 * nz))
                zhigh_ref[to] = high[block * lz : (block + 1) * lz, :]
                zlow_ref[to] = low[block * lz : (block + 1) * lz, :]
    shape = (rimhigh_ref.shape[0], 1)
    row = lax.broadcasted_iota(jnp.int32, shape, 0)
    block, spot = lax.div(row, LANES // 2), lax.rem(row, LANES // 2)
    above = spot >= ly * REACH
    spot = jnp.where(above, spot - ly * REACH, spot)
    yrow = jnp.where(spot < ly * REACH, lax.div(spot, REACH), 2 * ly)
    z = block * lz + lax.rem(spot, REACH) + jnp.where(above, lz, -REACH)
    rim = exact((lax.broadcasted_iota(jnp.int32, (shape[0], nz), 1) == z).astype(F32), pair)
    late = (lax.broadcasted_iota(jnp.int32, rim.shape, 1) >= nz).astype(jnp.int32)
    for chunk in range(ly // 2):
        columns = pl.ds(chunk * 2 * nz, 2 * nz)
        rimhigh_ref[:, columns], rimlow_ref[:, columns] = split(jnp.where(yrow - 2 * chunk == late, rim, 0.0))

    def y_of(p):
        spot = lax.div(p, npy)
        return lax.rem(p, npy) * ly + 2 * lax.rem(spot, ly // 2) + lax.div(spot, ly // 2)

    def four(array):
        high, low = split(array)
        late = lax.broadcasted_iota(jnp.int32, array.shape, 1) >= 2 * ny
        return jnp.where(late, low.astype(F32), high.astype(F32)).astype(BF16)

    lane = lax.broadcasted_iota(jnp.int32, (ny, 4 * ny), 1)
    row = lax.broadcasted_iota(jnp.int32, (ny, 4 * ny), 0)
    moved = (row == y_of(lax.rem(lane, ny))).astype(F32)
    ydown_ref[...] = four(exact(yvec_ref[...].T, moved))
    order = (
        lax.broadcasted_iota(jnp.int32, (ny, ny), 1) == y_of(lax.broadcasted_iota(jnp.int32, (ny, ny), 0))
    ).astype(F32)
    copies = (row == lax.rem(lane, ny)).astype(F32)
    yup_ref[...] = four(exact(exact(order, yvec_ref[...]), copies))
    fetching.wait()
    square = (ny, ny)
    diagonal = lax.broadcasted_iota(jnp.int32, square, 0) == lax.broadcasted_iota(jnp.int32, square, 1)
    ycolumn = jnp.sum(jnp.where(diagonal, yval_ref[...], 0.0), axis=1, keepdims=True)
    yz = ycolumn + exact(jnp.broadcast_to(zval_ref[...], (8, nz)), doubled(nz))[0:1]
    late = lax.broadcasted_iota(jnp.int32, (1, 2 * nz), 1) >= nz
    modes = sums_ref.shape[1] // nz
    first = (lax.axis_index("py") * (nz // lz) + lax.axis_index("pz")) * modes
    for mode in range(0, modes, 2):
        x = jnp.where(late, xval_ref[first + mode + 1], xval_ref[first + mode])
        sums_ref[:, mode * nz : (mode + 2) * nz] = yz + x


def y_sides(odd, even):
    first = lax.rem(lax.axis_index("py"), 2) == 0
    return jnp.where(first, odd, even), jnp.where(first, even, odd)


def three_products(matrix, high, low):
    rows = matrix.shape[0] // 2
    both = mul(matrix, high)
    return both[:rows] + both[rows:] + mul(matrix[:rows], low)


def yz_fields(lz, zrim, weighted_ref, zlow_ref, zhigh_ref, sides, stencil_ref):
    count, nx = weighted_ref.shape
    part, need = count // 2, count // 2 + REACH * lz
    own = split(weighted_ref[...])
    zrims = split(jnp.concatenate([zlow_ref[:zrim, :], zhigh_ref[:zrim, :]], axis=0))
    left = stencil_ref.shape[1] - need - 2 * zrim
    fields = []
    for half in range(2):
        if sides is None:
            yrim = [jnp.zeros((left, nx), BF16)] * 2
        else:
            rim = sides[half]
            missing = left - rim.shape[0]
            yrim = split(jnp.concatenate([rim, jnp.zeros((missing, nx), F32)], axis=0) if missing else rim)
        first = half * (count - need)
        high, low = (
            jnp.concatenate([own[k][first : first + need], zrims[k], yrim[k]], axis=0) for k in range(2)
        )
        both = three_products(stencil_ref[4 * half * part : 4 * (half + 1) * part, :], high, low)
        fields.append((both[:part], both[part:]))
    return fields


def x_banded(taps_ref, mass, stiff):
    nx = mass.shape[1]
    applied = None
    for offset in range(2 * REACH + 1):
        move = offset - REACH
        term = taps_ref[2 * offset] * mass + taps_ref[2 * offset + 1] * stiff
        term = pltpu.roll(term, -move % nx, 1) if move else term
        applied = term if applied is None else applied + term
    return applied


def store_modes(points, vectors_ref, spectral_ref):
    count, nx = points.shape
    high, low = split(points)
    product = mul_t(jnp.concatenate([high, low], axis=0), vectors_ref[:nx, :])
    spectral_ref[...] = (product[:count] + product[count:] + mul_t(high, vectors_ref[nx:, :])).T


def residual_kernel(lz, zrim, parts, *refs):
    weighted_ref, zlow_ref, zhigh_ref, *refs = refs
    yodd_refs, yeven_refs, refs = refs[:parts], refs[parts : 2 * parts], refs[2 * parts :]
    stencil_ref, taps_ref, coef_ref, right_ref, vectors_ref, _, spectral_ref, residual_ref = refs
    if parts == 2:
        (yodd_ref, odd_corner_ref), (yeven_ref, even_corner_ref) = yodd_refs, yeven_refs
        own = REACH * lz
        yodd = jnp.concatenate([yodd_ref[:own, :], odd_corner_ref[...]], axis=0)
        yeven = jnp.concatenate([yeven_ref[:own, :], even_corner_ref[...]], axis=0)
    else:
        yodd, yeven = yodd_refs[0][...], yeven_refs[0][...]
    fields = yz_fields(lz, zrim, weighted_ref, zlow_ref, zhigh_ref, y_sides(yodd, yeven), stencil_ref)
    part = weighted_ref.shape[0] // 2
    for start in range(0, 2 * part, 8):
        mass, stiff = (field[start % part : start % part + 8] for field in fields[start // part])
        rows = pl.ds(start, 8)
        residual_ref[rows, :] = right_ref[rows, :] - coef_ref[rows, :] * x_banded(taps_ref, mass, stiff)
    store_modes(residual_ref[...], vectors_ref, spectral_ref)


def own_part_kernel(lz, zrim, weighted_ref, zlow_ref, zhigh_ref, stencil_ref, taps_ref, applied_ref):
    fields = yz_fields(lz, zrim, weighted_ref, zlow_ref, zhigh_ref, None, stencil_ref)
    part = weighted_ref.shape[0] // 2
    for start in range(0, 2 * part, 8):
        mass, stiff = (field[start % part : start % part + 8] for field in fields[start // part])
        applied_ref[pl.ds(start, 8), :] = x_banded(taps_ref, mass, stiff)


def joined_residual_kernel(applied_ref, yodd_ref, yeven_ref, coef_ref, right_ref, vectors_ref, spectral_ref, residual_ref):
    count, rim = applied_ref.shape[0], yodd_ref.shape[0]
    for at, side in zip((0, count - rim), y_sides(yodd_ref[...], yeven_ref[...])):
        rows = pl.ds(at, rim)
        residual_ref[rows, :] = right_ref[rows, :] - coef_ref[rows, :] * (applied_ref[rows, :] + side)
    rows = pl.ds(rim, count - 2 * rim)
    residual_ref[rows, :] = right_ref[rows, :] - coef_ref[rows, :] * applied_ref[rows, :]
    store_modes(residual_ref[...], vectors_ref, spectral_ref)


def outward_kernel(ly, lz, nz, zbands_ref, yodd_ref, yeven_ref, _, out_ref):
    rim, side = REACH * lz, REACH * REACH
    width = out_ref.shape[1]
    row = lax.broadcasted_iota(jnp.int32, (rim, 1), 0)
    column = lax.broadcasted_iota(jnp.int32, (1, width), 1)
    spot = jnp.where(column < rim + side, column - rim, column - rim - side)
    yin = jnp.where(column < rim, lax.div(column, lz), lax.div(spot, REACH))
    zin = jnp.where(
        column < rim, lax.rem(column, lz), lax.rem(spot, REACH) + jnp.where(column < rim + side, -REACH, lz)
    )
    place = zin + lax.axis_index("pz") * lz
    inside = (column < rim + 2 * side) & (place >= 0) & (place < nz)
    yout, zout = lax.div(row, lz), lax.rem(row, lz)

    def dense(taps, tap):
        value = jnp.zeros(tap.shape, F32)
        for k in range(2 * REACH + 1):
            value = jnp.where(tap == k, taps[:, k : k + 1], value)
        return value

    def picked(length, at, bands):
        return exact((lax.broadcasted_iota(jnp.int32, (rim, length), 1) == at).astype(F32), bands, (1, 1))

    ztap = jnp.where(inside, zin - zout + REACH, -1)
    zstiff, zmass = (dense(picked(lz, zout, zbands_ref[:, matrix, :]), ztap) for matrix in range(2))
    sides = y_sides(yodd_ref[rim : rim + 16, :ly], yeven_ref[rim : rim + 16, :ly])
    spot, count = lax.axis_index("py"), lax.axis_size("py")
    for k, (bands, at, shift, there) in enumerate(
        ((sides[0], yout + ly - REACH, 2 * REACH, spot > 0), (sides[1], yout, 0, spot < count - 1))
    ):
        ytap = jnp.where(there, yin - yout + shift, -1)
        ystiff, ymass = (dense(picked(ly, at, bands[8 * matrix : 8 * matrix + 8]), ytap) for matrix in range(2))
        for part, value in enumerate((ymass * zmass, ystiff * zmass + ymass * zstiff)):
            start = (4 * k + part) * rim
            out_ref[start : start + rim, :], out_ref[start + 2 * rim : start + 3 * rim, :] = split(value)


def modes_kernel(npy, npz, rims, *refs):
    sums_ref, zhigh_ref, zlow_ref, ydown_ref, yup_ref, *rim_refs, in_ref, out_ref, turn_ref = refs
    count = in_ref.shape[0] // (npy * npz)
    size = out_ref.shape[0] // (npy * npz)
    nz = sums_ref.shape[1] // count
    width = zhigh_ref.shape[1]
    chunks = 2 * width // LANES
    step = turn_ref.shape[0] // (npy * chunks)
    zhigh, zlow = zhigh_ref[...], zlow_ref[...]

    def three(value, product, whigh, wlow):
        rows = value.shape[0]
        high, low = split(value)
        both = product(jnp.concatenate([high, low], axis=0), whigh)
        return both[:rows] + both[rows:] + product(high, wlow)

    def early(first, second):
        late = lax.broadcasted_iota(jnp.int32, first.shape, 1) >= LANES // 2
        return jnp.where(late, pltpu.roll(second, LANES // 2, 1), first)

    def later(first, second):
        late = lax.broadcasted_iota(jnp.int32, first.shape, 1) >= LANES // 2
        return jnp.where(late, second, pltpu.roll(first, LANES // 2, 1))

    def by_mode(mode, chunk):
        return pl.ds(chunk * npy * step + mode, npy, stride=step)

    def by_device(device, chunk):
        return pl.ds((chunk * npy + device) * step, count)

    halves = [[], []]
    for p in range(npy):
        blocks = [in_ref[(p * npz + b) * count : (p * npz + b + 1) * count, :] for b in range(npz)]
        for half, joined in zip(halves, (early, later)):
            half.append(jnp.concatenate([joined(blocks[b], blocks[b + 1]) for b in range(0, npz, 2)], axis=1))
    part = three(jnp.concatenate(halves[0] + halves[1], axis=0), mul, zhigh, zlow)
    for chunk in range(chunks):
        half, lane = divmod(chunk * LANES, width)
        for p in range(npy):
            row = (half * npy + p) * count
            turn_ref[by_device(p, chunk), :] = part[row : row + count, lane : lane + LANES]
    pairs = []
    for mode in range(0, count, 2):
        tiles = [(turn_ref[by_mode(mode, c), :], turn_ref[by_mode(mode + 1, c), :]) for c in range(chunks)]
        pairs.append(jnp.concatenate([early(*tile) for tile in tiles] + [later(*tile) for tile in tiles], axis=0))
    stacked = jnp.concatenate(pairs, axis=1)

    def four(value):
        high, low = split(value)
        return jnp.concatenate([high, low, high, low], axis=0)

    modes = mul(ydown_ref[...], four(stacked)) / sums_ref[...]
    restored = mul(yup_ref[...], four(modes))
    for mode in range(0, count, 2):
        block = restored[:, mode * nz : (mode + 2) * nz]
        for c in range(chunks):
            even = block[c * npy : (c + 1) * npy]
            odd = block[(chunks + c) * npy : (chunks + c + 1) * npy]
            turn_ref[by_mode(mode, c), :] = early(even, odd)
            turn_ref[by_mode(mode + 1, c), :] = later(even, odd)
    rows = [
        jnp.concatenate(
            [turn_ref[by_device(p, half * chunks // 2 + c), :] for c in range(chunks // 2)], axis=1
        )
        for half in range(2)
        for p in range(npy)
    ]
    spectral = jnp.concatenate(rows, axis=0)
    back = three(spectral, mul_t, zhigh, zlow)
    total = npy * count
    if rims:
        side = [
            three(spectral[half * total : (half + 1) * total], mul_t, *(ref[:, pl.ds(half * width, width)] for ref in rim_refs))
            for half in range(2)
        ]
        side = side[0] + side[1]
    for p in range(npy):
        for b in range(0, npz, 2):
            first, second = (
                back[k * total + p * count : k * total + (p + 1) * count, b * LANES // 2 : b * LANES // 2 + LANES]
                for k in range(2)
            )
            at = (p * npz + b) * size
            out_ref[at : at + count, :] = early(first, second)
            out_ref[at + size : at + size + count, :] = later(first, second)
            if rims:
                row, middle = p * count, p * count + count // 2
                first = side[row:middle, b * LANES // 2 : b * LANES // 2 + LANES]
                second = side[middle : row + count, b * LANES // 2 : b * LANES // 2 + LANES]
                out_ref[at + count : at + size, :] = early(first, second)
                out_ref[at + size + count : at + 2 * size, :] = later(first, second)


def transformed(points, vectors_ref):
    rows, nx = points.shape
    high, low = split(points)
    both = mul(jnp.concatenate([high, low], axis=0), vectors_ref[:nx, :])
    return both[:rows] + both[rows:] + mul(high, vectors_ref[nx:, :])


def from_modes(spectral_ref, vectors_ref):
    return transformed(spectral_ref[...].T, vectors_ref)


def update_kernel(ly, lz, spectral_ref, vectors_ref, field_ref, coef_ref, updated_ref, weighted_ref, low_ref, high_ref):
    updated = field_ref[...] + from_modes(spectral_ref, vectors_ref)
    updated_ref[...] = updated
    weighted = coef_ref[...] * updated
    weighted_ref[...] = weighted
    store_z_rims(ly, lz, weighted, low_ref, high_ref)


def rim_update_kernel(
    ly, lz, devices, spectral_ref, vectors_ref, field_ref, coef_ref, before_low_ref, before_high_ref,
    outward_ref, taps_ref, updated_ref, weighted_ref, zlow_ref, zhigh_ref, yodd_ref, yeven_ref, below_ref, above_ref,
):
    nx = vectors_ref.shape[1]
    modes = nx // devices
    size = spectral_ref.shape[0] // devices
    own, rims = [], []
    for d in range(devices):
        own.append(spectral_ref[d * size : d * size + modes, :])
        rim = spectral_ref[d * size + modes : (d + 1) * size, :]
        rims += [rim, pltpu.roll(rim, LANES // 2, 1)]
    points = [jnp.concatenate(own, axis=0).T, jnp.concatenate(rims, axis=0).T[: LANES // 2]]
    update = transformed(jnp.concatenate(points, axis=0), vectors_ref)
    count, half = ly * lz, ly * REACH
    updated = field_ref[...] + update[:count]
    updated_ref[...] = updated
    weighted_ref[...] = coef_ref[...] * updated
    for side, (ref, before_ref) in enumerate(((zlow_ref, before_low_ref), (zhigh_ref, before_high_ref))):
        start = count + side * half
        ref[...] = before_ref[:half, :] + before_ref[half:, :] * update[start : start + half]
    at = 0
    for value, rows, whole in own_rim(ly, lz, weighted_ref) + corners(ly, zlow_ref, zhigh_ref):
        below_ref[at : at + rows, :] = value[:rows, :]
        above_ref[at : at + rows, :] = value[whole - rows : whole, :]
        at += rows
    rim, adds = yodd_ref.shape[0], []
    for k, ref in enumerate((below_ref, above_ref)):
        ref[at:, :] = jnp.zeros((ref.shape[0] - at, nx), F32)
        both = three_products(outward_ref[4 * k * rim : 4 * (k + 1) * rim, :], *split(ref[...]))
        adds.append((both[:rim], both[rim:]))
    first = lax.rem(lax.axis_index("py"), 2) == 0
    for start in range(0, rim, 8):
        below, above = (x_banded(taps_ref, *(field[start : start + 8] for field in fields)) for fields in adds)
        yodd_ref[start : start + 8, :] = jnp.where(first, below, above)
        yeven_ref[start : start + 8, :] = jnp.where(first, above, below)


def last_update_kernel(spectral_ref, vectors_ref, field_ref, residual_ref, updated_hbm, residual_hbm, held, sem):
    leaving = pltpu.make_async_copy(residual_ref, residual_hbm, sem.at[0])
    leaving.start()
    held[...] = field_ref[...] + from_modes(spectral_ref, vectors_ref)
    fetch(((held, updated_hbm),), sem.at[pl.ds(1, 1)])
    leaving.wait()


def pairwise(value, axis, odd):
    count = lax.axis_size(axis)
    other = [((i + odd) ^ 1) - odd for i in range(count)]
    return lax.ppermute(value, axis, [(i, j if 0 <= j < count else i) for i, j in enumerate(other)])


def paired(value, axis):
    count = lax.axis_size(axis)
    return lax.ppermute(value, axis, [(i, (i + 1 if i % 2 else i - 1) % count) for i in range(count)])


def odd_pairs(value, axis, other):
    count, across = lax.axis_size(axis), lax.axis_size(other)
    first = BOTH.index(axis) == 0

    def spot(i, k):
        return i * across + k if first else k * count + i

    pairs = []
    for i in range(count):
        for k in range(across):
            j = i + 1 if i % 2 else i - 1
            pairs.append((spot(i, k), spot(j, k) if 0 <= j < count else spot(i, k ^ 1)))
    return lax.ppermute(value, BOTH, pairs)


def staggered(value, parity):
    across, count = lax.axis_size("py"), lax.axis_size("pz")
    pairs = []
    for i in range(across):
        for k in range(count):
            j = k + 1 if (i + k) % 2 == parity else k - 1
            other = i ^ 2 if i ^ 2 < across else i
            pairs.append((i * count + k, i * count + j if 0 <= j < count else other * count + k))
    return lax.ppermute(value, BOTH, pairs)


def around(value, axis, step):
    count = lax.axis_size(axis)
    return lax.ppermute(value, axis, [(i, (i + step) % count) for i in range(count)])


def plain_modes(received, npy, npz, ly, lz, xvalues, yvalues, zvalues, yvectors, zvectors):
    count = received.shape[0] // (npy * npz)
    field = received.reshape(npy, npz, count, ly, lz).transpose(2, 0, 3, 1, 4).reshape(count, npy * ly, npz * lz)
    field = jnp.einsum("xyz,yj->xjz", field, yvectors, precision=HIGH)
    field = jnp.einsum("xyz,zk->xyk", field, zvectors, precision=HIGH)
    field = field / (yvalues[None, :, None] + zvalues[None, None, :] + xvalues[:, None, None])
    field = jnp.einsum("xjz,yj->xyz", field, yvectors, precision=HIGH)
    field = jnp.einsum("xyk,zk->xyz", field, zvectors, precision=HIGH)
    field = field.reshape(count, npy, ly, npz, lz).transpose(1, 3, 0, 2, 4)
    return field.reshape(npy * npz * count, ly * lz)


def shards(
    solution,
    right_side,
    span_index,
    coef_table,
    xaxis_bands,
    yaxis_bands,
    zaxis_bands,
    xaxis_vectors,
    yaxis_vectors,
    zaxis_vectors,
    xaxis_values,
    yaxis_values,
    zaxis_values,
):
    npy, npz = lax.axis_size("py"), lax.axis_size("pz")
    ly, lz, nx = solution.shape
    ny, nz = npy * ly, npz * lz
    count, devices = ly * lz, npy * npz
    modes = nx // devices
    field = solution.reshape(count, nx)
    right = right_side.reshape(count, nx)
    block, zrim, yrim = (count, nx), (ly * REACH, nx), (up8(REACH * lz + 2 * REACH * REACH), nx)
    zrims = (2 * ly * REACH, nx)
    cell = count * nx * 4
    dma = pltpu.SemaphoreType.DMA

    points = point_columns(ly, lz)
    width = points.shape[1] // 2
    small = [jnp.asarray(points), *(array.transpose(1, 0, 2) for array in (yaxis_bands, zaxis_bands, xaxis_bands))]
    fast = (
        modes % 16 == 0 and npz % 2 == 0 and 2 * ly * REACH <= LANES // 2 and npy % 8 == 0 and lz % 16 == 0 and ly % 4 == 0
        and 2 * nz == LANES and 2 * ny == LANES and count == LANES and nx % LANES == 0
    )
    later = [xaxis_vectors, yaxis_vectors, zaxis_vectors, yaxis_values.reshape(1, ny), zaxis_values.reshape(1, nz)] * fast

    coef, weighted, even, odd, yodd, yeven, *small = call(
        lambda *refs: coefficient_kernel(ly, lz, len(small), *refs),
        [(block, F32)] * 2 + [(zrims, F32)] * 2 + [((REACH * lz + 16, nx), F32)] * 2
        + [(array.shape, array.dtype) for array in small],
        [HBM] * (3 + len(small)), count * nx * 16, 4 * cell,
        [pltpu.SMEM(coef_table.shape, F32), pltpu.VMEM(block, jnp.int32), pltpu.VMEM(block, F32)]
        + [dma((3 + len(small),))],
    )(*in_hbm(coef_table, span_index.reshape(count, nx), field, *small))

    *bands, xbands = small
    stencil, *held = call(
        lambda *refs: stencil_kernel(ly, lz, ny, nz, len(later), *refs),
        [((4 * count, width), BF16)] + [(array.shape, F32) for array in later],
        [VMEM] * 3 + [HBM] * len(later) + [ANY], count * width * 60, 8 * count * width,
        [dma((len(later),))] * fast,
    )(*bands, *in_hbm(*later), even)

    even, odd = staggered(even, 1), staggered(odd, 0)
    zlow, zhigh, *corner = call(
        lambda *refs: y_rims_kernel(ly, *refs),
        [(zrims, F32)] * 2 + [((up8(2 * REACH * REACH), nx), F32)] * 2,
        [VMEM] * 2 + [ANY], nx, 4 * nx * 4 * zrims[0],
    )(odd, even, stencil)
    yodd, yeven = [yodd, corner[0]], [yeven, corner[1]]

    if fast:
        zmat, ymat, rmat = (npz * count // 2, ly * nz // 2), (ny, 4 * ny), (npz * LANES // 2, ly * nz)
        vectors, taps, *tables = call(
            lambda *refs: tables_kernel(npy, npz, ly, lz, *refs),
            [((2 * nx, nx), BF16), ((2 * (2 * REACH + 1), 8, nx), F32), ((ny, modes * nz), F32)]
            + [(zmat, BF16), (zmat, BF16), (ymat, BF16), (ymat, BF16), (rmat, BF16), (rmat, BF16)],
            [VMEM] * 6 + [HBM, ANY], npz * count * ly * nz * 8, npz * count * ly * nz * 4,
            [pltpu.SMEM((nx,), F32), dma((1,))],
        )(*held, xbands, *in_hbm(xaxis_values), corner[0])

        def precondition(received, rims):
            size = modes * 3 // 2 if rims else modes
            return call(
                lambda *refs: modes_kernel(npy, npz, rims, *refs),
                [((devices * size, count), F32)], [VMEM] * (8 if rims else 6), 6 * 2 * count * nx * ly * nz, 2 * cell,
                [pltpu.VMEM((ly * nz // LANES * npy * (modes + 8), LANES), F32)],
            )(*(tables if rims else tables[:5]), received)[0]
    else:
        vectors, taps = call(
            xvectors_kernel, [((2 * nx, nx), BF16), ((2 * (2 * REACH + 1), 8, nx), F32)], [HBM, VMEM],
            nx * nx * 40, 8 * nx * nx, [pltpu.VMEM((nx, nx), F32), dma((1,))],
        )(*in_hbm(xaxis_vectors), xbands)
        tables = [taps]
        part = lax.axis_index(BOTH)
        xpart = lax.dynamic_slice_in_dim(xaxis_values, part * modes, modes)

        def precondition(received, rims):
            return plain_modes(
                received, npy, npz, ly, lz, xpart, yaxis_values, zaxis_values, yaxis_vectors, zaxis_vectors
            )

    outward = None
    for iteration in range(ITERS):
        last = iteration + 1 == ITERS
        yodd, yeven = [paired(value, "py") for value in yodd], [pairwise(value, "py", 0) for value in yeven]
        parts = len(yodd)
        if fast and iteration == 0:
            outward = call(
                lambda *refs: outward_kernel(ly, lz, nz, *refs),
                [((8 * REACH * lz, LANES), BF16)], [VMEM] * 3 + [ANY], 1 << 20, 1 << 18,
            )(bands[2], yodd[0], yeven[0], tables[0])[0]
        outs = [((nx, count), F32)] + [(block, F32)] * last
        scratch = [pltpu.VMEM(block, F32)] * (not last)
        cost = (6 * count * nx * (nx + 2 * width), 5 * cell + 4 * nx * nx)
        if fast and iteration > 0:
            applied = call(
                lambda *refs: own_part_kernel(lz, zrim[0], *refs), [(block, F32)], [VMEM] * 5, *cost,
            )(weighted, zlow, zhigh, stencil, taps)[0]
            spectral, *residual = call(joined_residual_kernel, outs, [VMEM] * 6, *cost, scratch)(
                applied, *yodd, *yeven, coef, right, vectors
            )
        else:
            spectral, *residual = call(
                lambda *refs: residual_kernel(lz, zrim[0], parts, *refs),
                outs, [VMEM] * (8 + 2 * parts) + [ANY], *cost, scratch,
            )(weighted, zlow, zhigh, *yodd, *yeven, stencil, taps, coef, right, vectors, outward if fast else tables[0])
        spectral = lax.all_to_all(spectral, BOTH, split_axis=0, concat_axis=0, tiled=True)
        spectral = precondition(spectral, not last)
        spectral = lax.all_to_all(spectral, BOTH, split_axis=0, concat_axis=0, tiled=True)
        cost = (6 * count * nx * nx, 4 * cell + 4 * nx * nx)
        if last:
            field, residual = call(
                last_update_kernel, [(block, F32), (block, F32)], [VMEM] * 4, *cost,
                [pltpu.VMEM(block, F32), dma((2,))], [HBM] * 2,
            )(spectral, vectors, field, *residual)
        elif fast:
            field, weighted, zlow, zhigh, *yrims = call(
                lambda *refs: rim_update_kernel(ly, lz, devices, *refs),
                [(block, F32)] * 2 + [(zrim, F32)] * 2 + [((REACH * lz, nx), F32)] * 2, [VMEM] * 8, *cost,
                [pltpu.VMEM((LANES, nx), F32)] * 2,
            )(spectral, vectors, field, coef, zlow, zhigh, outward, taps)
        else:
            field, weighted, zlow, zhigh = call(
                lambda *refs: update_kernel(ly, lz, *refs), [(block, F32)] * 2 + [(zrim, F32)] * 2, [VMEM] * 4, *cost,
            )(spectral, vectors, field, coef)
            zlow, zhigh = around(zhigh, "pz", 1), around(zlow, "pz", -1)
            yrims = call(
                lambda *refs: next_y_rims_kernel(ly, lz, *refs),
                [(yrim, F32)] * 2, [VMEM] * 3, nx, 4 * nx * 4 * yrim[0],
            )(weighted, zlow, zhigh)
        yodd, yeven = ([value] for value in yrims) if not last else (None, None)
    return (field.reshape(solution.shape), residual.reshape(solution.shape))


def solution(mesh):
    return jax.shard_map(
        shards,
        mesh=mesh,
        in_specs=(
            P("py", "pz", None),
            P("py", "pz", None),
            P("py", "pz", None),
            P(),
            P(),
            P(None, None, "py"),
            P(None, None, "pz"),
            P(),
            P(),
            P(),
            P(),
            P(),
            P(),
        ),
        out_specs=(P("py", "pz", None), P("py", "pz", None)),
        check_vma=False,
    )
```

```python
import jax
import jax.numpy as jnp
import numpy as np
from jax import lax
from jax.experimental import pallas as pl
from jax.experimental.pallas import tpu as pltpu
from jax.sharding import PartitionSpec as P

ITERS = 2
REACH = 3
LANES = 128
HIGH = lax.Precision.HIGHEST
BOTH = ("py", "pz")
F32 = jnp.float32
BF16 = jnp.bfloat16
VMEM = pl.BlockSpec(memory_space=pltpu.VMEM)
HBM = pl.BlockSpec(memory_space=pltpu.HBM)
ANY = pl.BlockSpec(memory_space=pl.ANY)


def up8(count):
    return -(-count // 8) * 8


def split(value):
    high = value.astype(BF16)
    return high, (value - high.astype(F32)).astype(BF16)


def exact(left, right, sides=(1, 0)):
    return lax.dot_general(
        left, right, (((sides[0],), (sides[1],)), ((), ())), precision=HIGH, preferred_element_type=F32
    )


def fetch(pairs, sem):
    copies = [pltpu.make_async_copy(source, target, sem.at[i]) for i, (source, target) in enumerate(pairs)]
    for copy in copies:
        copy.start()
    for copy in copies:
        copy.wait()


def in_hbm(*arrays):
    return [pltpu.with_memory_space_constraint(array, pltpu.HBM) for array in arrays]


def mul(left, right):
    return lax.dot_general(left, right, (((1,), (0,)), ((), ())), preferred_element_type=F32)


def mul_t(left, right):
    return lax.dot_general(left, right, (((1,), (1,)), ((), ())), preferred_element_type=F32)


def call(kernel, outs, specs, flops, cost_bytes, scratch=(), out_specs=None):
    return pl.pallas_call(
        kernel,
        out_shape=[jax.ShapeDtypeStruct(shape, dtype) for shape, dtype in outs],
        in_specs=specs,
        out_specs=out_specs or [VMEM] * len(outs),
        scratch_shapes=list(scratch),
        compiler_params=pltpu.CompilerParams(vmem_limit_bytes=32 * 1024 * 1024),
        cost_estimate=pl.CostEstimate(flops=flops, bytes_accessed=cost_bytes, transcendentals=0),
    )


def store_z_rims(ly, lz, weighted, low_ref, high_ref):
    for y in range(ly):
        low_ref[y * REACH : (y + 1) * REACH, :] = weighted[y * lz : y * lz + REACH, :]
        high_ref[y * REACH : (y + 1) * REACH, :] = weighted[(y + 1) * lz - REACH : (y + 1) * lz, :]


def coefficient_kernel(ly, lz, small, *refs):
    table_ref, span_ref, field_ref, *refs = refs
    sources, refs = refs[:small], refs[small:]
    coef_ref, weighted_ref, even_ref, odd_ref, yodd_ref, yeven_ref, *refs = refs
    targets, (table, span, field, sem) = refs[:small], refs[small:]
    fetch([(table_ref, table), (span_ref, span), (field_ref, field), *zip(sources, targets)], sem)
    first = lax.rem(lax.axis_index("py") + lax.axis_index("pz"), 2) == 1
    half = ly * REACH
    entries = [table[entry] for entry in range(table_ref.shape[0])]
    for start in range(0, span.shape[0], lz):
        rows = pl.ds(start, lz)
        index = span[rows, :]
        coef = jnp.full(index.shape, entries[0], F32)
        for entry in range(1, len(entries)):
            coef = jnp.where(index == entry, entries[entry], coef)
        coef_ref[rows, :] = coef
        weighted = coef * field[rows, :]
        weighted_ref[rows, :] = weighted
        for value, at in ((weighted, 0), (coef, half)):
            rim = pl.ds(at + start // lz * REACH, REACH)
            low, high = value[:REACH], value[lz - REACH :]
            even_ref[rim, :] = jnp.where(first, high, low)
            odd_ref[rim, :] = jnp.where(first, low, high)
    store_y_rims(own_rim(ly, lz, weighted_ref), yodd_ref, yeven_ref)
    ybands = targets[1]
    for ref in (yodd_ref, yeven_ref):
        for matrix in range(2):
            at = REACH * lz + 8 * matrix
            ref[at : at + ybands.shape[0], :ly] = ybands[:, matrix, :]


def store_y_rims(pieces, odd_ref, even_ref):
    first = lax.rem(lax.axis_index("py"), 2) == 0
    at = 0
    for value, count, rows in pieces:
        low, high = value[:count, :], value[rows - count : rows, :]
        even_ref[at : at + count, :] = jnp.where(first, high, low)
        odd_ref[at : at + count, :] = jnp.where(first, low, high)
        at += count
    if at < even_ref.shape[0]:
        for ref in (even_ref, odd_ref):
            ref[at:, :] = jnp.zeros((ref.shape[0] - at, ref.shape[1]), F32)


def own_rim(ly, lz, weighted):
    return [(weighted, REACH * lz, ly * lz)]


def corners(ly, zlow, zhigh):
    return [(value, REACH * REACH, ly * REACH) for value in (zlow, zhigh)]


def y_rims_kernel(ly, odd_ref, even_ref, _, zlow_ref, zhigh_ref, yodd_ref, yeven_ref):
    first = lax.rem(lax.axis_index("py") + lax.axis_index("pz"), 2) == 1
    zlow_ref[...] = jnp.where(first, odd_ref[...], even_ref[...])
    zhigh_ref[...] = jnp.where(first, even_ref[...], odd_ref[...])
    store_y_rims(corners(ly, zlow_ref, zhigh_ref), yodd_ref, yeven_ref)


def next_y_rims_kernel(ly, lz, weighted_ref, zlow_ref, zhigh_ref, yodd_ref, yeven_ref):
    store_y_rims(own_rim(ly, lz, weighted_ref) + corners(ly, zlow_ref, zhigh_ref), yodd_ref, yeven_ref)


def point_columns(ly, lz):
    below, above = range(-REACH, 0), range(REACH)
    halves = []
    for half in range(2):
        first = 0 if half == 0 else ly // 2 - REACH
        points = [(first + y, z) for y in range(ly // 2 + REACH) for z in range(lz)]
        points += [(y, z) for y in range(ly) for z in below]
        points += [(y, lz + z) for y in range(ly) for z in above]
        ys = below if half == 0 else [ly + y for y in above]
        points += [(y, z) for y in ys for z in range(lz)]
        points += [(y, z) for y in ys for z in below]
        points += [(y, lz + z) for y in ys for z in above]
        halves += points + [(1 << 20, 1 << 20)] * (-len(points) % LANES)
    return np.array(halves, np.int32).T.copy()


def stencil_kernel(ly, lz, ny, nz, later, points_ref, ybands_ref, zbands_ref, *refs):
    sources, (_, out_ref, *refs) = refs[:later], refs[later:]
    copies = [pltpu.make_async_copy(*pair, refs[-1].at[i]) for i, pair in enumerate(zip(sources, refs[:later]))]
    for copy in copies:
        copy.start()
    count = ly * lz // 2
    width = out_ref.shape[1]
    for half in range(2):
        rows = lax.broadcasted_iota(jnp.int32, (count, 1), 0) + half * count
        columns = pl.ds(half * width, width)
        factors = []
        for bands_ref, length, row, column, first, whole in (
            (ybands_ref, ly, lax.div(rows, lz), points_ref[0:1, columns], lax.axis_index("py") * ly, ny),
            (zbands_ref, lz, lax.rem(rows, lz), points_ref[1:2, columns], lax.axis_index("pz") * lz, nz),
        ):
            pick = (lax.broadcasted_iota(jnp.int32, (count, length), 1) == row).astype(F32)
            spot = column + first
            inside = (spot >= 0) & (spot < whole)
            distance = jnp.where(inside, column, 1 << 20) - row
            here = [distance == offset - REACH for offset in range(2 * REACH + 1)]
            for matrix in range(2):
                taps = exact(pick, bands_ref[:, matrix, :], (1, 1))
                dense = jnp.zeros(distance.shape, F32)
                for offset in range(2 * REACH + 1):
                    dense = jnp.where(here[offset], taps[:, offset : offset + 1], dense)
                factors.append(dense)
        ystiff, ymass, zstiff, zmass = factors
        for part, value in enumerate((ymass * zmass, ystiff * zmass + ymass * zstiff)):
            at = (4 * half + part) * count
            out_ref[at : at + count, :], out_ref[at + 2 * count : at + 3 * count, :] = split(value)
    for copy in copies:
        copy.wait()


def store_taps(xbands_ref, taps_ref):
    nx = xbands_ref.shape[2]
    lane = lax.broadcasted_iota(jnp.int32, (1, nx), 1)
    for offset in range(2 * REACH + 1):
        move = offset - REACH
        inside = (lane - move >= 0) & (lane - move < nx)
        for matrix in range(2):
            band = xbands_ref[offset, matrix : matrix + 1, :]
            band = pltpu.roll(band, move % nx, 1) if move else band
            taps_ref[2 * offset + matrix] = jnp.broadcast_to(jnp.where(inside, band, 0.0), (8, nx))


def doubled(size):
    row = lax.broadcasted_iota(jnp.int32, (size, 2 * size), 0)
    return (row == lax.rem(lax.broadcasted_iota(jnp.int32, (size, 2 * size), 1), size)).astype(F32)


def xvectors_kernel(source, xbands_ref, out_ref, taps_ref, held, sem):
    store_taps(xbands_ref, taps_ref)
    fetch(((source, held),), sem)
    high, low = split(held[...].T)
    out_ref[: high.shape[0], :] = high
    out_ref[high.shape[0] :, :] = low


def tables_kernel(
    npy, npz, ly, lz, xvec_ref, yvec_ref, zvec_ref, yval_ref, zval_ref, xbands_ref, xval_hbm, _,
    xout_ref, taps_ref, sums_ref, zhigh_ref, zlow_ref, ydown_ref, yup_ref, rimhigh_ref, rimlow_ref, xval_ref, sem,
):
    fetching = pltpu.make_async_copy(xval_hbm, xval_ref, sem.at[0])
    fetching.start()
    store_taps(xbands_ref, taps_ref)
    ny, nz = npy * ly, npz * lz
    nx = xvec_ref.shape[0]
    high, low = split(xvec_ref[...].T)
    xout_ref[:nx, :] = high
    xout_ref[nx:, :] = low
    pair = exact(zvec_ref[...], doubled(nz))
    half = lax.broadcasted_iota(jnp.int32, pair.shape, 1) >= nz
    zhigh_ref[...] = jnp.zeros(zhigh_ref.shape, BF16)
    zlow_ref[...] = jnp.zeros(zlow_ref.shape, BF16)
    for parity in range(2):
        high, low = split(jnp.where(half == (parity == 1), pair, 0.0))
        for yl in range(parity, ly // 2, 2):
            for block in range(npz):
                to = (pl.ds((block * ly // 2 + yl) * lz, lz), pl.ds(yl // 2 * 2 * nz, 2 * nz))
                zhigh_ref[to] = high[block * lz : (block + 1) * lz, :]
                zlow_ref[to] = low[block * lz : (block + 1) * lz, :]
    shape = (rimhigh_ref.shape[0], 1)
    row = lax.broadcasted_iota(jnp.int32, shape, 0)
    block, spot = lax.div(row, LANES // 2), lax.rem(row, LANES // 2)
    above = spot >= ly * REACH
    spot = jnp.where(above, spot - ly * REACH, spot)
    yrow = jnp.where(spot < ly * REACH, lax.div(spot, REACH), 2 * ly)
    z = block * lz + lax.rem(spot, REACH) + jnp.where(above, lz, -REACH)
    rim = exact((lax.broadcasted_iota(jnp.int32, (shape[0], nz), 1) == z).astype(F32), pair)
    late = (lax.broadcasted_iota(jnp.int32, rim.shape, 1) >= nz).astype(jnp.int32)
    for chunk in range(ly // 2):
        columns = pl.ds(chunk * 2 * nz, 2 * nz)
        rimhigh_ref[:, columns], rimlow_ref[:, columns] = split(jnp.where(yrow - 2 * chunk == late, rim, 0.0))

    def y_of(p):
        spot = lax.div(p, npy)
        return lax.rem(p, npy) * ly + 2 * lax.rem(spot, ly // 2) + lax.div(spot, ly // 2)

    def parts(array):
        high, low = split(array)
        late = lax.broadcasted_iota(jnp.int32, array.shape, 1) >= 2 * ny
        return jnp.where(late, low.astype(F32), high.astype(F32)).astype(BF16)

    lane = lax.broadcasted_iota(jnp.int32, (ny, 3 * ny), 1)
    row = lax.broadcasted_iota(jnp.int32, (ny, 3 * ny), 0)
    moved = (row == y_of(lax.rem(lane, ny))).astype(F32)
    ydown_ref[...] = parts(exact(yvec_ref[...].T, moved))
    order = (
        lax.broadcasted_iota(jnp.int32, (ny, ny), 1) == y_of(lax.broadcasted_iota(jnp.int32, (ny, ny), 0))
    ).astype(F32)
    copies = (row == lax.rem(lane, ny)).astype(F32)
    yup_ref[...] = parts(exact(exact(order, yvec_ref[...]), copies))
    fetching.wait()
    square = (ny, ny)
    diagonal = lax.broadcasted_iota(jnp.int32, square, 0) == lax.broadcasted_iota(jnp.int32, square, 1)
    ycolumn = jnp.sum(jnp.where(diagonal, yval_ref[...], 0.0), axis=1, keepdims=True)
    yz = ycolumn + exact(jnp.broadcast_to(zval_ref[...], (8, nz)), doubled(nz))[0:1]
    late = lax.broadcasted_iota(jnp.int32, (1, 2 * nz), 1) >= nz
    modes = sums_ref.shape[1] // nz
    first = (lax.axis_index("py") * (nz // lz) + lax.axis_index("pz")) * modes
    for mode in range(0, modes, 2):
        x = jnp.where(late, xval_ref[first + mode + 1], xval_ref[first + mode])
        sums_ref[:, mode * nz : (mode + 2) * nz] = yz + x


def y_sides(odd, even):
    first = lax.rem(lax.axis_index("py"), 2) == 0
    return jnp.where(first, odd, even), jnp.where(first, even, odd)


def three_products(matrix, high, low):
    rows = matrix.shape[0] // 2
    both = mul(matrix, high)
    return both[:rows] + both[rows:] + mul(matrix[:rows], low)


def yz_fields(lz, zrim, weighted_ref, zlow_ref, zhigh_ref, sides, stencil_ref):
    count, nx = weighted_ref.shape
    part, need = count // 2, count // 2 + REACH * lz
    own = split(weighted_ref[...])
    zrims = split(jnp.concatenate([zlow_ref[:zrim, :], zhigh_ref[:zrim, :]], axis=0))
    left = stencil_ref.shape[1] - need - 2 * zrim
    fields = []
    for half in range(2):
        if sides is None:
            yrim = [jnp.zeros((left, nx), BF16)] * 2
        else:
            rim = sides[half]
            missing = left - rim.shape[0]
            yrim = split(jnp.concatenate([rim, jnp.zeros((missing, nx), F32)], axis=0) if missing else rim)
        first = half * (count - need)
        high, low = (
            jnp.concatenate([own[k][first : first + need], zrims[k], yrim[k]], axis=0) for k in range(2)
        )
        both = three_products(stencil_ref[4 * half * part : 4 * (half + 1) * part, :], high, low)
        fields.append((both[:part], both[part:]))
    return fields


def x_banded(taps_ref, mass, stiff):
    nx = mass.shape[1]
    applied = None
    for offset in range(2 * REACH + 1):
        move = offset - REACH
        term = taps_ref[2 * offset] * mass + taps_ref[2 * offset + 1] * stiff
        term = pltpu.roll(term, -move % nx, 1) if move else term
        applied = term if applied is None else applied + term
    return applied


def store_modes(points, vectors_ref, spectral_ref):
    count, nx = points.shape
    high, low = split(points)
    product = mul_t(jnp.concatenate([high, low], axis=0), vectors_ref[:nx, :])
    spectral_ref[...] = (product[:count] + product[count:] + mul_t(high, vectors_ref[nx:, :])).T


def residual_kernel(lz, zrim, parts, *refs):
    weighted_ref, zlow_ref, zhigh_ref, *refs = refs
    yodd_refs, yeven_refs, refs = refs[:parts], refs[parts : 2 * parts], refs[2 * parts :]
    stencil_ref, taps_ref, coef_ref, right_ref, vectors_ref, _, spectral_ref, residual_ref = refs
    if parts == 2:
        (yodd_ref, odd_corner_ref), (yeven_ref, even_corner_ref) = yodd_refs, yeven_refs
        own = REACH * lz
        yodd = jnp.concatenate([yodd_ref[:own, :], odd_corner_ref[...]], axis=0)
        yeven = jnp.concatenate([yeven_ref[:own, :], even_corner_ref[...]], axis=0)
    else:
        yodd, yeven = yodd_refs[0][...], yeven_refs[0][...]
    fields = yz_fields(lz, zrim, weighted_ref, zlow_ref, zhigh_ref, y_sides(yodd, yeven), stencil_ref)
    part = weighted_ref.shape[0] // 2
    for start in range(0, 2 * part, 8):
        mass, stiff = (field[start % part : start % part + 8] for field in fields[start // part])
        rows = pl.ds(start, 8)
        residual_ref[rows, :] = right_ref[rows, :] - coef_ref[rows, :] * x_banded(taps_ref, mass, stiff)
    store_modes(residual_ref[...], vectors_ref, spectral_ref)


def own_part_kernel(lz, zrim, weighted_ref, zlow_ref, zhigh_ref, stencil_ref, taps_ref, applied_ref):
    fields = yz_fields(lz, zrim, weighted_ref, zlow_ref, zhigh_ref, None, stencil_ref)
    part = weighted_ref.shape[0] // 2
    for start in range(0, 2 * part, 8):
        mass, stiff = (field[start % part : start % part + 8] for field in fields[start // part])
        applied_ref[pl.ds(start, 8), :] = x_banded(taps_ref, mass, stiff)


def joined_residual_kernel(applied_ref, yodd_ref, yeven_ref, coef_ref, right_ref, vectors_ref, spectral_ref, residual_ref):
    count, rim = applied_ref.shape[0], yodd_ref.shape[0]
    for at, side in zip((0, count - rim), y_sides(yodd_ref[...], yeven_ref[...])):
        rows = pl.ds(at, rim)
        residual_ref[rows, :] = right_ref[rows, :] - coef_ref[rows, :] * (applied_ref[rows, :] + side)
    rows = pl.ds(rim, count - 2 * rim)
    residual_ref[rows, :] = right_ref[rows, :] - coef_ref[rows, :] * applied_ref[rows, :]
    store_modes(residual_ref[...], vectors_ref, spectral_ref)


def outward_kernel(ly, lz, nz, zbands_ref, yodd_ref, yeven_ref, _, out_ref):
    rim, side = REACH * lz, REACH * REACH
    width = out_ref.shape[1]
    row = lax.broadcasted_iota(jnp.int32, (rim, 1), 0)
    column = lax.broadcasted_iota(jnp.int32, (1, width), 1)
    spot = jnp.where(column < rim + side, column - rim, column - rim - side)
    yin = jnp.where(column < rim, lax.div(column, lz), lax.div(spot, REACH))
    zin = jnp.where(
        column < rim, lax.rem(column, lz), lax.rem(spot, REACH) + jnp.where(column < rim + side, -REACH, lz)
    )
    place = zin + lax.axis_index("pz") * lz
    inside = (column < rim + 2 * side) & (place >= 0) & (place < nz)
    yout, zout = lax.div(row, lz), lax.rem(row, lz)

    def dense(taps, tap):
        value = jnp.zeros(tap.shape, F32)
        for k in range(2 * REACH + 1):
            value = jnp.where(tap == k, taps[:, k : k + 1], value)
        return value

    def picked(length, at, bands):
        return exact((lax.broadcasted_iota(jnp.int32, (rim, length), 1) == at).astype(F32), bands, (1, 1))

    ztap = jnp.where(inside, zin - zout + REACH, -1)
    zstiff, zmass = (dense(picked(lz, zout, zbands_ref[:, matrix, :]), ztap) for matrix in range(2))
    sides = y_sides(yodd_ref[rim : rim + 16, :ly], yeven_ref[rim : rim + 16, :ly])
    spot, count = lax.axis_index("py"), lax.axis_size("py")
    for k, (bands, at, shift, there) in enumerate(
        ((sides[0], yout + ly - REACH, 2 * REACH, spot > 0), (sides[1], yout, 0, spot < count - 1))
    ):
        ytap = jnp.where(there, yin - yout + shift, -1)
        ystiff, ymass = (dense(picked(ly, at, bands[8 * matrix : 8 * matrix + 8]), ytap) for matrix in range(2))
        for part, value in enumerate((ymass * zmass, ystiff * zmass + ymass * zstiff)):
            start = (4 * k + part) * rim
            out_ref[start : start + rim, :], out_ref[start + 2 * rim : start + 3 * rim, :] = split(value)


def modes_kernel(npy, npz, rims, *refs):
    sums_ref, zhigh_ref, zlow_ref, ydown_ref, yup_ref, *rim_refs, in_ref, out_ref, turn_ref = refs
    count = in_ref.shape[0] // (npy * npz)
    size = out_ref.shape[0] // (npy * npz)
    nz = sums_ref.shape[1] // count
    width = zhigh_ref.shape[1]
    chunks = 2 * width // LANES
    step = turn_ref.shape[0] // (npy * chunks)
    zhigh, zlow = zhigh_ref[...], zlow_ref[...]

    def three(value, product, whigh, wlow):
        rows = value.shape[0]
        high, low = split(value)
        both = product(jnp.concatenate([high, low], axis=0), whigh)
        return both[:rows] + both[rows:] + product(high, wlow)

    def early(first, second):
        late = lax.broadcasted_iota(jnp.int32, first.shape, 1) >= LANES // 2
        return jnp.where(late, pltpu.roll(second, LANES // 2, 1), first)

    def later(first, second):
        late = lax.broadcasted_iota(jnp.int32, first.shape, 1) >= LANES // 2
        return jnp.where(late, second, pltpu.roll(first, LANES // 2, 1))

    def by_mode(mode, chunk):
        return pl.ds(chunk * npy * step + mode, npy, stride=step)

    def by_device(device, chunk):
        return pl.ds((chunk * npy + device) * step, count)

    halves = [[], []]
    for p in range(npy):
        blocks = [in_ref[(p * npz + b) * count : (p * npz + b + 1) * count, :] for b in range(npz)]
        for half, joined in zip(halves, (early, later)):
            half.append(jnp.concatenate([joined(blocks[b], blocks[b + 1]) for b in range(0, npz, 2)], axis=1))
    part = three(jnp.concatenate(halves[0] + halves[1], axis=0), mul, zhigh, zlow)
    for chunk in range(chunks):
        half, lane = divmod(chunk * LANES, width)
        for p in range(npy):
            row = (half * npy + p) * count
            turn_ref[by_device(p, chunk), :] = part[row : row + count, lane : lane + LANES]
    pairs = []
    for mode in range(0, count, 2):
        tiles = [(turn_ref[by_mode(mode, c), :], turn_ref[by_mode(mode + 1, c), :]) for c in range(chunks)]
        pairs.append(jnp.concatenate([early(*tile) for tile in tiles] + [later(*tile) for tile in tiles], axis=0))
    stacked = jnp.concatenate(pairs, axis=1)

    def stack(value):
        high, low = split(value)
        return jnp.concatenate([high, low, high], axis=0)

    modes = mul(ydown_ref[...], stack(stacked)) / sums_ref[...]
    restored = mul(yup_ref[...], stack(modes))
    for mode in range(0, count, 2):
        block = restored[:, mode * nz : (mode + 2) * nz]
        for c in range(chunks):
            even = block[c * npy : (c + 1) * npy]
            odd = block[(chunks + c) * npy : (chunks + c + 1) * npy]
            turn_ref[by_mode(mode, c), :] = early(even, odd)
            turn_ref[by_mode(mode + 1, c), :] = later(even, odd)
    rows = [
        jnp.concatenate(
            [turn_ref[by_device(p, half * chunks // 2 + c), :] for c in range(chunks // 2)], axis=1
        )
        for half in range(2)
        for p in range(npy)
    ]
    spectral = jnp.concatenate(rows, axis=0)
    back = three(spectral, mul_t, zhigh, zlow)
    total = npy * count
    if rims:
        side = [
            three(
                spectral[half * total : (half + 1) * total], mul_t,
                *(ref[:, pl.ds(half * width, width)] for ref in rim_refs),
            )
            for half in range(2)
        ]
        side = side[0] + side[1]
    for p in range(npy):
        for b in range(0, npz, 2):
            first, second = (
                back[k * total + p * count : k * total + (p + 1) * count, b * LANES // 2 : b * LANES // 2 + LANES]
                for k in range(2)
            )
            at = (p * npz + b) * size
            out_ref[at : at + count, :] = early(first, second)
            out_ref[at + size : at + size + count, :] = later(first, second)
            if rims:
                row, middle = p * count, p * count + count // 2
                first = side[row:middle, b * LANES // 2 : b * LANES // 2 + LANES]
                second = side[middle : row + count, b * LANES // 2 : b * LANES // 2 + LANES]
                out_ref[at + count : at + size, :] = early(first, second)
                out_ref[at + size + count : at + 2 * size, :] = later(first, second)


def transformed(points, vectors_ref):
    rows, nx = points.shape
    high, low = split(points)
    both = mul(jnp.concatenate([high, low], axis=0), vectors_ref[:nx, :])
    return both[:rows] + both[rows:] + mul(high, vectors_ref[nx:, :])


def from_modes(spectral_ref, vectors_ref):
    return transformed(spectral_ref[...].T, vectors_ref)


def update_kernel(ly, lz, spectral_ref, vectors_ref, field_ref, coef_ref, updated_ref, weighted_ref, low_ref, high_ref):
    updated = field_ref[...] + from_modes(spectral_ref, vectors_ref)
    updated_ref[...] = updated
    weighted = coef_ref[...] * updated
    weighted_ref[...] = weighted
    store_z_rims(ly, lz, weighted, low_ref, high_ref)


def rim_update_kernel(
    ly, lz, devices, spectral_ref, vectors_ref, field_ref, coef_ref, before_low_ref, before_high_ref,
    outward_ref, taps_ref, updated_ref, weighted_ref, zlow_ref, zhigh_ref, yodd_ref, yeven_ref, below_ref, above_ref,
):
    nx = vectors_ref.shape[1]
    modes = nx // devices
    size = spectral_ref.shape[0] // devices
    own, rims = [], []
    for d in range(devices):
        own.append(spectral_ref[d * size : d * size + modes, :])
        rim = spectral_ref[d * size + modes : (d + 1) * size, :]
        rims += [rim, pltpu.roll(rim, LANES // 2, 1)]
    points = [jnp.concatenate(own, axis=0).T, jnp.concatenate(rims, axis=0).T[: LANES // 2]]
    update = transformed(jnp.concatenate(points, axis=0), vectors_ref)
    count, half = ly * lz, ly * REACH
    updated = field_ref[...] + update[:count]
    updated_ref[...] = updated
    weighted_ref[...] = coef_ref[...] * updated
    for side, (ref, before_ref) in enumerate(((zlow_ref, before_low_ref), (zhigh_ref, before_high_ref))):
        start = count + side * half
        ref[...] = before_ref[:half, :] + before_ref[half:, :] * update[start : start + half]
    at = 0
    for value, rows, whole in own_rim(ly, lz, weighted_ref) + corners(ly, zlow_ref, zhigh_ref):
        below_ref[at : at + rows, :] = value[:rows, :]
        above_ref[at : at + rows, :] = value[whole - rows : whole, :]
        at += rows
    rim, adds = yodd_ref.shape[0], []
    for k, ref in enumerate((below_ref, above_ref)):
        ref[at:, :] = jnp.zeros((ref.shape[0] - at, nx), F32)
        both = three_products(outward_ref[4 * k * rim : 4 * (k + 1) * rim, :], *split(ref[...]))
        adds.append((both[:rim], both[rim:]))
    first = lax.rem(lax.axis_index("py"), 2) == 0
    for start in range(0, rim, 8):
        below, above = (x_banded(taps_ref, *(field[start : start + 8] for field in fields)) for fields in adds)
        yodd_ref[start : start + 8, :] = jnp.where(first, below, above)
        yeven_ref[start : start + 8, :] = jnp.where(first, above, below)


def last_update_kernel(spectral_ref, vectors_ref, field_ref, residual_ref, updated_hbm, residual_hbm, held, sem):
    leaving = pltpu.make_async_copy(residual_ref, residual_hbm, sem.at[0])
    leaving.start()
    held[...] = field_ref[...] + from_modes(spectral_ref, vectors_ref)
    fetch(((held, updated_hbm),), sem.at[pl.ds(1, 1)])
    leaving.wait()


def pairwise(value, axis, odd):
    count = lax.axis_size(axis)
    other = [((i + odd) ^ 1) - odd for i in range(count)]
    return lax.ppermute(value, axis, [(i, j if 0 <= j < count else i) for i, j in enumerate(other)])


def paired(value, axis):
    count = lax.axis_size(axis)
    return lax.ppermute(value, axis, [(i, (i + 1 if i % 2 else i - 1) % count) for i in range(count)])


def staggered(value, parity):
    across, count = lax.axis_size("py"), lax.axis_size("pz")
    pairs = []
    for i in range(across):
        for k in range(count):
            j = k + 1 if (i + k) % 2 == parity else k - 1
            other = i ^ 2 if i ^ 2 < across else i
            pairs.append((i * count + k, i * count + j if 0 <= j < count else other * count + k))
    return lax.ppermute(value, BOTH, pairs)


def around(value, axis, step):
    count = lax.axis_size(axis)
    return lax.ppermute(value, axis, [(i, (i + step) % count) for i in range(count)])


def plain_modes(received, npy, npz, ly, lz, xvalues, yvalues, zvalues, yvectors, zvectors):
    count = received.shape[0] // (npy * npz)
    field = received.reshape(npy, npz, count, ly, lz).transpose(2, 0, 3, 1, 4).reshape(count, npy * ly, npz * lz)
    field = jnp.einsum("xyz,yj->xjz", field, yvectors, precision=HIGH)
    field = jnp.einsum("xyz,zk->xyk", field, zvectors, precision=HIGH)
    field = field / (yvalues[None, :, None] + zvalues[None, None, :] + xvalues[:, None, None])
    field = jnp.einsum("xjz,yj->xyz", field, yvectors, precision=HIGH)
    field = jnp.einsum("xyk,zk->xyz", field, zvectors, precision=HIGH)
    field = field.reshape(count, npy, ly, npz, lz).transpose(1, 3, 0, 2, 4)
    return field.reshape(npy * npz * count, ly * lz)


def shards(
    solution,
    right_side,
    span_index,
    coef_table,
    xaxis_bands,
    yaxis_bands,
    zaxis_bands,
    xaxis_vectors,
    yaxis_vectors,
    zaxis_vectors,
    xaxis_values,
    yaxis_values,
    zaxis_values,
):
    npy, npz = lax.axis_size("py"), lax.axis_size("pz")
    ly, lz, nx = solution.shape
    ny, nz = npy * ly, npz * lz
    count, devices = ly * lz, npy * npz
    modes = nx // devices
    field = solution.reshape(count, nx)
    right = right_side.reshape(count, nx)
    block, zrim, yrim = (count, nx), (ly * REACH, nx), (up8(REACH * lz + 2 * REACH * REACH), nx)
    zrims = (2 * ly * REACH, nx)
    cell = count * nx * 4
    dma = pltpu.SemaphoreType.DMA

    points = point_columns(ly, lz)
    width = points.shape[1] // 2
    small = [jnp.asarray(points), *(array.transpose(1, 0, 2) for array in (yaxis_bands, zaxis_bands, xaxis_bands))]
    fast = (
        modes % 16 == 0 and npz % 2 == 0 and 2 * ly * REACH <= LANES // 2 and npy % 8 == 0 and lz % 16 == 0 and ly % 4 == 0
        and 2 * nz == LANES and 2 * ny == LANES and count == LANES and nx % LANES == 0
    )
    later = [xaxis_vectors, yaxis_vectors, zaxis_vectors, yaxis_values.reshape(1, ny), zaxis_values.reshape(1, nz)] * fast

    coef, weighted, even, odd, yodd, yeven, *small = call(
        lambda *refs: coefficient_kernel(ly, lz, len(small), *refs),
        [(block, F32)] * 2 + [(zrims, F32)] * 2 + [((REACH * lz + 16, nx), F32)] * 2
        + [(array.shape, array.dtype) for array in small],
        [HBM] * (3 + len(small)), count * nx * 16, 4 * cell,
        [pltpu.SMEM(coef_table.shape, F32), pltpu.VMEM(block, jnp.int32), pltpu.VMEM(block, F32)]
        + [dma((3 + len(small),))],
    )(*in_hbm(coef_table, span_index.reshape(count, nx), field, *small))

    *bands, xbands = small
    stencil, *held = call(
        lambda *refs: stencil_kernel(ly, lz, ny, nz, len(later), *refs),
        [((4 * count, width), BF16)] + [(array.shape, F32) for array in later],
        [VMEM] * 3 + [HBM] * len(later) + [ANY], count * width * 60, 8 * count * width,
        [dma((len(later),))] * fast,
    )(*bands, *in_hbm(*later), even)

    even, odd = staggered(even, 1), staggered(odd, 0)
    zlow, zhigh, *corner = call(
        lambda *refs: y_rims_kernel(ly, *refs),
        [(zrims, F32)] * 2 + [((up8(2 * REACH * REACH), nx), F32)] * 2,
        [VMEM] * 2 + [ANY], nx, 4 * nx * 4 * zrims[0],
    )(odd, even, stencil)
    yodd, yeven = [yodd, corner[0]], [yeven, corner[1]]

    if fast:
        zmat, ymat, rmat = (npz * count // 2, ly * nz // 2), (ny, 3 * ny), (npz * LANES // 2, ly * nz)
        vectors, taps, *tables = call(
            lambda *refs: tables_kernel(npy, npz, ly, lz, *refs),
            [((2 * nx, nx), BF16), ((2 * (2 * REACH + 1), 8, nx), F32), ((ny, modes * nz), F32)]
            + [(zmat, BF16), (zmat, BF16), (ymat, BF16), (ymat, BF16), (rmat, BF16), (rmat, BF16)],
            [VMEM] * 6 + [HBM, ANY], npz * count * ly * nz * 8, npz * count * ly * nz * 4,
            [pltpu.SMEM((nx,), F32), dma((1,))],
        )(*held, xbands, *in_hbm(xaxis_values), corner[0])

        def precondition(received, rims):
            size = modes * 3 // 2 if rims else modes
            return call(
                lambda *refs: modes_kernel(npy, npz, rims, *refs),
                [((devices * size, count), F32)], [VMEM] * (8 if rims else 6), 6 * 2 * count * nx * ly * nz, 2 * cell,
                [pltpu.VMEM(((ly * nz // LANES * npy + 1) * (modes + 8), LANES), F32)],
            )(*(tables if rims else tables[:5]), received)[0]
    else:
        vectors, taps = call(
            xvectors_kernel, [((2 * nx, nx), BF16), ((2 * (2 * REACH + 1), 8, nx), F32)], [HBM, VMEM],
            nx * nx * 40, 8 * nx * nx, [pltpu.VMEM((nx, nx), F32), dma((1,))],
        )(*in_hbm(xaxis_vectors), xbands)
        tables = [taps]
        part = lax.axis_index(BOTH)
        xpart = lax.dynamic_slice_in_dim(xaxis_values, part * modes, modes)

        def precondition(received, rims):
            return plain_modes(
                received, npy, npz, ly, lz, xpart, yaxis_values, zaxis_values, yaxis_vectors, zaxis_vectors
            )

    for iteration in range(ITERS):
        last = iteration + 1 == ITERS
        yodd, yeven = [paired(value, "py") for value in yodd], [pairwise(value, "py", 0) for value in yeven]
        parts = len(yodd)
        if fast and iteration == 0:
            outward = call(
                lambda *refs: outward_kernel(ly, lz, nz, *refs),
                [((8 * REACH * lz, LANES), BF16)], [VMEM] * 3 + [ANY], 1 << 20, 1 << 18,
            )(bands[2], yodd[0], yeven[0], tables[0])[0]
        outs = [((nx, count), F32)] + [(block, F32)] * last
        scratch = [pltpu.VMEM(block, F32)] * (not last)
        cost = (6 * count * nx * (nx + 2 * width), 5 * cell + 4 * nx * nx)
        if fast and iteration > 0:
            applied = call(
                lambda *refs: own_part_kernel(lz, zrim[0], *refs), [(block, F32)], [VMEM] * 5, *cost,
            )(weighted, zlow, zhigh, stencil, taps)[0]
            spectral, *residual = call(joined_residual_kernel, outs, [VMEM] * 6, *cost, scratch)(
                applied, *yodd, *yeven, coef, right, vectors
            )
        else:
            spectral, *residual = call(
                lambda *refs: residual_kernel(lz, zrim[0], parts, *refs),
                outs, [VMEM] * (8 + 2 * parts) + [ANY], *cost, scratch,
            )(weighted, zlow, zhigh, *yodd, *yeven, stencil, taps, coef, right, vectors, outward if fast else tables[0])
        spectral = lax.all_to_all(spectral, BOTH, split_axis=0, concat_axis=0, tiled=True)
        spectral = precondition(spectral, not last)
        spectral = lax.all_to_all(spectral, BOTH, split_axis=0, concat_axis=0, tiled=True)
        cost = (6 * count * nx * nx, 4 * cell + 4 * nx * nx)
        if last:
            field, residual = call(
                last_update_kernel, [(block, F32), (block, F32)], [VMEM] * 4, *cost,
                [pltpu.VMEM(block, F32), dma((2,))], [HBM] * 2,
            )(spectral, vectors, field, *residual)
        elif fast:
            field, weighted, zlow, zhigh, *yrims = call(
                lambda *refs: rim_update_kernel(ly, lz, devices, *refs),
                [(block, F32)] * 2 + [(zrim, F32)] * 2 + [((REACH * lz, nx), F32)] * 2, [VMEM] * 8, *cost,
                [pltpu.VMEM((LANES, nx), F32)] * 2,
            )(spectral, vectors, field, coef, zlow, zhigh, outward, taps)
        else:
            field, weighted, zlow, zhigh = call(
                lambda *refs: update_kernel(ly, lz, *refs), [(block, F32)] * 2 + [(zrim, F32)] * 2, [VMEM] * 4, *cost,
            )(spectral, vectors, field, coef)
            zlow, zhigh = around(zhigh, "pz", 1), around(zlow, "pz", -1)
            yrims = call(
                lambda *refs: next_y_rims_kernel(ly, lz, *refs),
                [(yrim, F32)] * 2, [VMEM] * 3, nx, 4 * nx * 4 * yrim[0],
            )(weighted, zlow, zhigh)
        yodd, yeven = ([value] for value in yrims) if not last else (None, None)
    return (field.reshape(solution.shape), residual.reshape(solution.shape))


def solution(mesh):
    return jax.shard_map(
        shards,
        mesh=mesh,
        in_specs=(
            P("py", "pz", None),
            P("py", "pz", None),
            P("py", "pz", None),
            P(),
            P(),
            P(None, None, "py"),
            P(None, None, "pz"),
            P(),
            P(),
            P(),
            P(),
            P(),
            P(),
        ),
        out_specs=(P("py", "pz", None), P("py", "pz", None)),
        check_vma=False,
    )
```

```python
import jax
import jax.numpy as jnp
import numpy as np
from jax import lax
from jax.experimental import pallas as pl
from jax.experimental.pallas import tpu as pltpu
from jax.sharding import PartitionSpec as P

ITERS = 2
REACH = 3
LANES = 128
HIGH = lax.Precision.HIGHEST
BOTH = ("py", "pz")
F32 = jnp.float32
BF16 = jnp.bfloat16
VMEM = pl.BlockSpec(memory_space=pltpu.VMEM)
HBM = pl.BlockSpec(memory_space=pltpu.HBM)
ANY = pl.BlockSpec(memory_space=pl.ANY)


def up8(count):
    return -(-count // 8) * 8


def split(value):
    high = value.astype(BF16)
    return high, (value - high.astype(F32)).astype(BF16)


def exact(left, right, sides=(1, 0)):
    return lax.dot_general(
        left, right, (((sides[0],), (sides[1],)), ((), ())), precision=HIGH, preferred_element_type=F32
    )


def fetch(pairs, sem):
    copies = [pltpu.make_async_copy(source, target, sem.at[i]) for i, (source, target) in enumerate(pairs)]
    for copy in copies:
        copy.start()
    for copy in copies:
        copy.wait()


def in_hbm(*arrays):
    return [pltpu.with_memory_space_constraint(array, pltpu.HBM) for array in arrays]


def mul(left, right):
    return lax.dot_general(left, right, (((1,), (0,)), ((), ())), preferred_element_type=F32)


def mul_t(left, right):
    return lax.dot_general(left, right, (((1,), (1,)), ((), ())), preferred_element_type=F32)


def call(kernel, outs, specs, flops, cost_bytes, scratch=(), out_specs=None):
    return pl.pallas_call(
        kernel,
        out_shape=[jax.ShapeDtypeStruct(shape, dtype) for shape, dtype in outs],
        in_specs=specs,
        out_specs=out_specs or [VMEM] * len(outs),
        scratch_shapes=list(scratch),
        compiler_params=pltpu.CompilerParams(vmem_limit_bytes=32 * 1024 * 1024),
        cost_estimate=pl.CostEstimate(flops=flops, bytes_accessed=cost_bytes, transcendentals=0),
    )


def store_z_rims(ly, lz, weighted, low_ref, high_ref):
    for y in range(ly):
        low_ref[y * REACH : (y + 1) * REACH, :] = weighted[y * lz : y * lz + REACH, :]
        high_ref[y * REACH : (y + 1) * REACH, :] = weighted[(y + 1) * lz - REACH : (y + 1) * lz, :]


def coefficient_kernel(ly, lz, small, *refs):
    table_ref, span_ref, field_ref, *refs = refs
    sources, refs = refs[:small], refs[small:]
    coef_ref, weighted_ref, even_ref, odd_ref, yodd_ref, yeven_ref, *refs = refs
    targets, (table, span, field, sem) = refs[:small], refs[small:]
    fetch([(table_ref, table), (span_ref, span), (field_ref, field), *zip(sources, targets)], sem)
    first = lax.rem(lax.axis_index("pz"), 2) == 0
    half = ly * REACH
    entries = [table[entry] for entry in range(table_ref.shape[0])]
    for start in range(0, span.shape[0], lz):
        rows = pl.ds(start, lz)
        index = span[rows, :]
        coef = jnp.full(index.shape, entries[0], F32)
        for entry in range(1, len(entries)):
            coef = jnp.where(index == entry, entries[entry], coef)
        coef_ref[rows, :] = coef
        weighted = coef * field[rows, :]
        weighted_ref[rows, :] = weighted
        for value, at in ((weighted, 0), (coef, half)):
            rim = pl.ds(at + start // lz * REACH, REACH)
            low, high = value[:REACH], value[lz - REACH :]
            even_ref[rim, :] = jnp.where(first, high, low)
            odd_ref[rim, :] = jnp.where(first, low, high)
    store_y_rims(own_rim(ly, lz, weighted_ref), yodd_ref, yeven_ref)
    ybands = targets[1]
    for ref in (yodd_ref, yeven_ref):
        for matrix in range(2):
            at = REACH * lz + 8 * matrix
            ref[at : at + ybands.shape[0], :ly] = ybands[:, matrix, :]


def store_y_rims(pieces, odd_ref, even_ref):
    first = lax.rem(lax.axis_index("py"), 2) == 0
    at = 0
    for value, count, rows in pieces:
        low, high = value[:count, :], value[rows - count : rows, :]
        even_ref[at : at + count, :] = jnp.where(first, high, low)
        odd_ref[at : at + count, :] = jnp.where(first, low, high)
        at += count
    if at < even_ref.shape[0]:
        for ref in (even_ref, odd_ref):
            ref[at:, :] = jnp.zeros((ref.shape[0] - at, ref.shape[1]), F32)


def own_rim(ly, lz, weighted):
    return [(weighted, REACH * lz, ly * lz)]


def corners(ly, zlow, zhigh):
    return [(value, REACH * REACH, ly * REACH) for value in (zlow, zhigh)]


def y_rims_kernel(ly, odd_ref, even_ref, _, zlow_ref, zhigh_ref, yodd_ref, yeven_ref):
    first = lax.rem(lax.axis_index("pz"), 2) == 0
    zlow_ref[...] = jnp.where(first, odd_ref[...], even_ref[...])
    zhigh_ref[...] = jnp.where(first, even_ref[...], odd_ref[...])
    store_y_rims(corners(ly, zlow_ref, zhigh_ref), yodd_ref, yeven_ref)


def next_y_rims_kernel(ly, lz, weighted_ref, zlow_ref, zhigh_ref, yodd_ref, yeven_ref):
    store_y_rims(own_rim(ly, lz, weighted_ref) + corners(ly, zlow_ref, zhigh_ref), yodd_ref, yeven_ref)


def point_columns(ly, lz):
    below, above = range(-REACH, 0), range(REACH)
    halves = []
    for half in range(2):
        first = 0 if half == 0 else ly // 2 - REACH
        points = [(first + y, z) for y in range(ly // 2 + REACH) for z in range(lz)]
        points += [(y, z) for y in range(ly) for z in below]
        points += [(y, lz + z) for y in range(ly) for z in above]
        ys = below if half == 0 else [ly + y for y in above]
        points += [(y, z) for y in ys for z in range(lz)]
        points += [(y, z) for y in ys for z in below]
        points += [(y, lz + z) for y in ys for z in above]
        halves += points + [(1 << 20, 1 << 20)] * (-len(points) % LANES)
    return np.array(halves, np.int32).T.copy()


def stencil_kernel(ly, lz, ny, nz, later, points_ref, ybands_ref, zbands_ref, *refs):
    sources, (_, out_ref, *refs) = refs[:later], refs[later:]
    copies = [pltpu.make_async_copy(*pair, refs[-1].at[i]) for i, pair in enumerate(zip(sources, refs[:later]))]
    for copy in copies:
        copy.start()
    count = ly * lz // 2
    width = out_ref.shape[1]
    for half in range(2):
        rows = lax.broadcasted_iota(jnp.int32, (count, 1), 0) + half * count
        columns = pl.ds(half * width, width)
        factors = []
        for bands_ref, length, row, column, first, whole in (
            (ybands_ref, ly, lax.div(rows, lz), points_ref[0:1, columns], lax.axis_index("py") * ly, ny),
            (zbands_ref, lz, lax.rem(rows, lz), points_ref[1:2, columns], lax.axis_index("pz") * lz, nz),
        ):
            pick = (lax.broadcasted_iota(jnp.int32, (count, length), 1) == row).astype(F32)
            spot = column + first
            inside = (spot >= 0) & (spot < whole)
            distance = jnp.where(inside, column, 1 << 20) - row
            here = [distance == offset - REACH for offset in range(2 * REACH + 1)]
            for matrix in range(2):
                taps = exact(pick, bands_ref[:, matrix, :], (1, 1))
                dense = jnp.zeros(distance.shape, F32)
                for offset in range(2 * REACH + 1):
                    dense = jnp.where(here[offset], taps[:, offset : offset + 1], dense)
                factors.append(dense)
        ystiff, ymass, zstiff, zmass = factors
        for part, value in enumerate((ymass * zmass, ystiff * zmass + ymass * zstiff)):
            at = (4 * half + part) * count
            out_ref[at : at + count, :], out_ref[at + 2 * count : at + 3 * count, :] = split(value)
    for copy in copies:
        copy.wait()


def store_taps(xbands_ref, taps_ref):
    nx = xbands_ref.shape[2]
    lane = lax.broadcasted_iota(jnp.int32, (1, nx), 1)
    for offset in range(2 * REACH + 1):
        move = offset - REACH
        inside = (lane - move >= 0) & (lane - move < nx)
        for matrix in range(2):
            band = xbands_ref[offset, matrix : matrix + 1, :]
            band = pltpu.roll(band, move % nx, 1) if move else band
            taps_ref[2 * offset + matrix] = jnp.broadcast_to(jnp.where(inside, band, 0.0), (8, nx))


def doubled(size):
    row = lax.broadcasted_iota(jnp.int32, (size, 2 * size), 0)
    return (row == lax.rem(lax.broadcasted_iota(jnp.int32, (size, 2 * size), 1), size)).astype(F32)


def xvectors_kernel(source, xbands_ref, out_ref, taps_ref, held, sem):
    store_taps(xbands_ref, taps_ref)
    fetch(((source, held),), sem)
    high, low = split(held[...].T)
    out_ref[: high.shape[0], :] = high
    out_ref[high.shape[0] :, :] = low


def tables_kernel(
    npy, npz, ly, lz, xvec_ref, yvec_ref, zvec_ref, yval_ref, zval_ref, xbands_ref, xval_hbm, _,
    xout_ref, taps_ref, sums_ref, zhigh_ref, zlow_ref, ydown_ref, yup_ref, rimhigh_ref, rimlow_ref, xval_ref, sem,
):
    fetching = pltpu.make_async_copy(xval_hbm, xval_ref, sem.at[0])
    fetching.start()
    store_taps(xbands_ref, taps_ref)
    ny, nz = npy * ly, npz * lz
    nx = xvec_ref.shape[0]
    high, low = split(xvec_ref[...].T)
    xout_ref[:nx, :] = high
    xout_ref[nx:, :] = low
    pair = exact(zvec_ref[...], doubled(nz))
    half = lax.broadcasted_iota(jnp.int32, pair.shape, 1) >= nz
    zhigh_ref[...] = jnp.zeros(zhigh_ref.shape, BF16)
    zlow_ref[...] = jnp.zeros(zlow_ref.shape, BF16)
    for parity in range(2):
        high, low = split(jnp.where(half == (parity == 1), pair, 0.0))
        for yl in range(parity, ly // 2, 2):
            for block in range(npz):
                to = (pl.ds((block * ly // 2 + yl) * lz, lz), pl.ds(yl // 2 * 2 * nz, 2 * nz))
                zhigh_ref[to] = high[block * lz : (block + 1) * lz, :]
                zlow_ref[to] = low[block * lz : (block + 1) * lz, :]
    shape = (rimhigh_ref.shape[0], 1)
    row = lax.broadcasted_iota(jnp.int32, shape, 0)
    block, spot = lax.div(row, LANES // 2), lax.rem(row, LANES // 2)
    above = spot >= ly * REACH
    spot = jnp.where(above, spot - ly * REACH, spot)
    yrow = jnp.where(spot < ly * REACH, lax.div(spot, REACH), 2 * ly)
    z = block * lz + lax.rem(spot, REACH) + jnp.where(above, lz, -REACH)
    rim = exact((lax.broadcasted_iota(jnp.int32, (shape[0], nz), 1) == z).astype(F32), pair)
    late = (lax.broadcasted_iota(jnp.int32, rim.shape, 1) >= nz).astype(jnp.int32)
    for chunk in range(ly // 2):
        columns = pl.ds(chunk * 2 * nz, 2 * nz)
        rimhigh_ref[:, columns], rimlow_ref[:, columns] = split(jnp.where(yrow - 2 * chunk == late, rim, 0.0))

    def y_of(p):
        spot = lax.div(p, npy)
        return lax.rem(p, npy) * ly + 2 * lax.rem(spot, ly // 2) + lax.div(spot, ly // 2)

    def parts(array):
        high, low = split(array)
        late = lax.broadcasted_iota(jnp.int32, array.shape, 1) >= 2 * ny
        return jnp.where(late, low.astype(F32), high.astype(F32)).astype(BF16)

    lane = lax.broadcasted_iota(jnp.int32, (ny, 3 * ny), 1)
    row = lax.broadcasted_iota(jnp.int32, (ny, 3 * ny), 0)
    moved = (row == y_of(lax.rem(lane, ny))).astype(F32)
    ydown_ref[...] = parts(exact(yvec_ref[...].T, moved))
    order = (
        lax.broadcasted_iota(jnp.int32, (ny, ny), 1) == y_of(lax.broadcasted_iota(jnp.int32, (ny, ny), 0))
    ).astype(F32)
    copies = (row == lax.rem(lane, ny)).astype(F32)
    yup_ref[...] = parts(exact(exact(order, yvec_ref[...]), copies))
    fetching.wait()
    square = (ny, ny)
    diagonal = lax.broadcasted_iota(jnp.int32, square, 0) == lax.broadcasted_iota(jnp.int32, square, 1)
    ycolumn = jnp.sum(jnp.where(diagonal, yval_ref[...], 0.0), axis=1, keepdims=True)
    yz = ycolumn + exact(jnp.broadcast_to(zval_ref[...], (8, nz)), doubled(nz))[0:1]
    late = lax.broadcasted_iota(jnp.int32, (1, 2 * nz), 1) >= nz
    modes = sums_ref.shape[1] // nz
    first = (lax.axis_index("py") * (nz // lz) + lax.axis_index("pz")) * modes
    for mode in range(0, modes, 2):
        x = jnp.where(late, xval_ref[first + mode + 1], xval_ref[first + mode])
        sums_ref[:, mode * nz : (mode + 2) * nz] = yz + x


def y_sides(odd, even):
    first = lax.rem(lax.axis_index("py"), 2) == 0
    return jnp.where(first, odd, even), jnp.where(first, even, odd)


def three_products(matrix, high, low):
    rows = matrix.shape[0] // 2
    both = mul(matrix, high)
    return both[:rows] + both[rows:] + mul(matrix[:rows], low)


def yz_fields(lz, zrim, weighted_ref, zlow_ref, zhigh_ref, sides, stencil_ref):
    count, nx = weighted_ref.shape
    part, need = count // 2, count // 2 + REACH * lz
    own = split(weighted_ref[...])
    zrims = split(jnp.concatenate([zlow_ref[:zrim, :], zhigh_ref[:zrim, :]], axis=0))
    left = stencil_ref.shape[1] - need - 2 * zrim
    fields = []
    for half in range(2):
        if sides is None:
            yrim = [jnp.zeros((left, nx), BF16)] * 2
        else:
            rim = sides[half]
            missing = left - rim.shape[0]
            yrim = split(jnp.concatenate([rim, jnp.zeros((missing, nx), F32)], axis=0) if missing else rim)
        first = half * (count - need)
        high, low = (
            jnp.concatenate([own[k][first : first + need], zrims[k], yrim[k]], axis=0) for k in range(2)
        )
        both = three_products(stencil_ref[4 * half * part : 4 * (half + 1) * part, :], high, low)
        fields.append((both[:part], both[part:]))
    return fields


def x_banded(taps_ref, mass, stiff):
    nx = mass.shape[1]
    applied = None
    for offset in range(2 * REACH + 1):
        move = offset - REACH
        term = taps_ref[2 * offset] * mass + taps_ref[2 * offset + 1] * stiff
        term = pltpu.roll(term, -move % nx, 1) if move else term
        applied = term if applied is None else applied + term
    return applied


def store_modes(points, vectors_ref, spectral_ref):
    count, nx = points.shape
    high, low = split(points)
    product = mul_t(jnp.concatenate([high, low], axis=0), vectors_ref[:nx, :])
    spectral_ref[...] = (product[:count] + product[count:] + mul_t(high, vectors_ref[nx:, :])).T


def residual_kernel(lz, zrim, parts, *refs):
    weighted_ref, zlow_ref, zhigh_ref, *refs = refs
    yodd_refs, yeven_refs, refs = refs[:parts], refs[parts : 2 * parts], refs[2 * parts :]
    stencil_ref, taps_ref, coef_ref, right_ref, vectors_ref, _, spectral_ref, residual_ref = refs
    if parts == 2:
        (yodd_ref, odd_corner_ref), (yeven_ref, even_corner_ref) = yodd_refs, yeven_refs
        own = REACH * lz
        yodd = jnp.concatenate([yodd_ref[:own, :], odd_corner_ref[...]], axis=0)
        yeven = jnp.concatenate([yeven_ref[:own, :], even_corner_ref[...]], axis=0)
    else:
        yodd, yeven = yodd_refs[0][...], yeven_refs[0][...]
    fields = yz_fields(lz, zrim, weighted_ref, zlow_ref, zhigh_ref, y_sides(yodd, yeven), stencil_ref)
    part = weighted_ref.shape[0] // 2
    for start in range(0, 2 * part, 8):
        mass, stiff = (field[start % part : start % part + 8] for field in fields[start // part])
        rows = pl.ds(start, 8)
        residual_ref[rows, :] = right_ref[rows, :] - coef_ref[rows, :] * x_banded(taps_ref, mass, stiff)
    store_modes(residual_ref[...], vectors_ref, spectral_ref)


def own_part_kernel(lz, zrim, weighted_ref, zlow_ref, zhigh_ref, stencil_ref, taps_ref, applied_ref):
    fields = yz_fields(lz, zrim, weighted_ref, zlow_ref, zhigh_ref, None, stencil_ref)
    part = weighted_ref.shape[0] // 2
    for start in range(0, 2 * part, 8):
        mass, stiff = (field[start % part : start % part + 8] for field in fields[start // part])
        applied_ref[pl.ds(start, 8), :] = x_banded(taps_ref, mass, stiff)


def joined_residual_kernel(applied_ref, yodd_ref, yeven_ref, coef_ref, right_ref, vectors_ref, spectral_ref, residual_ref):
    count, rim = applied_ref.shape[0], yodd_ref.shape[0]
    for at, side in zip((0, count - rim), y_sides(yodd_ref[...], yeven_ref[...])):
        rows = pl.ds(at, rim)
        residual_ref[rows, :] = right_ref[rows, :] - coef_ref[rows, :] * (applied_ref[rows, :] + side)
    rows = pl.ds(rim, count - 2 * rim)
    residual_ref[rows, :] = right_ref[rows, :] - coef_ref[rows, :] * applied_ref[rows, :]
    store_modes(residual_ref[...], vectors_ref, spectral_ref)


def outward_kernel(ly, lz, nz, zbands_ref, yodd_ref, yeven_ref, _, out_ref):
    rim, side = REACH * lz, REACH * REACH
    width = out_ref.shape[1]
    row = lax.broadcasted_iota(jnp.int32, (rim, 1), 0)
    column = lax.broadcasted_iota(jnp.int32, (1, width), 1)
    spot = jnp.where(column < rim + side, column - rim, column - rim - side)
    yin = jnp.where(column < rim, lax.div(column, lz), lax.div(spot, REACH))
    zin = jnp.where(
        column < rim, lax.rem(column, lz), lax.rem(spot, REACH) + jnp.where(column < rim + side, -REACH, lz)
    )
    place = zin + lax.axis_index("pz") * lz
    inside = (column < rim + 2 * side) & (place >= 0) & (place < nz)
    yout, zout = lax.div(row, lz), lax.rem(row, lz)

    def dense(taps, tap):
        value = jnp.zeros(tap.shape, F32)
        for k in range(2 * REACH + 1):
            value = jnp.where(tap == k, taps[:, k : k + 1], value)
        return value

    def picked(length, at, bands):
        return exact((lax.broadcasted_iota(jnp.int32, (rim, length), 1) == at).astype(F32), bands, (1, 1))

    ztap = jnp.where(inside, zin - zout + REACH, -1)
    zstiff, zmass = (dense(picked(lz, zout, zbands_ref[:, matrix, :]), ztap) for matrix in range(2))
    sides = y_sides(yodd_ref[rim : rim + 16, :ly], yeven_ref[rim : rim + 16, :ly])
    spot, count = lax.axis_index("py"), lax.axis_size("py")
    for k, (bands, at, shift, there) in enumerate(
        ((sides[0], yout + ly - REACH, 2 * REACH, spot > 0), (sides[1], yout, 0, spot < count - 1))
    ):
        ytap = jnp.where(there, yin - yout + shift, -1)
        ystiff, ymass = (dense(picked(ly, at, bands[8 * matrix : 8 * matrix + 8]), ytap) for matrix in range(2))
        for part, value in enumerate((ymass * zmass, ystiff * zmass + ymass * zstiff)):
            start = (4 * k + part) * rim
            out_ref[start : start + rim, :], out_ref[start + 2 * rim : start + 3 * rim, :] = split(value)


def modes_kernel(npy, npz, rims, *refs):
    sums_ref, zhigh_ref, zlow_ref, ydown_ref, yup_ref, *rim_refs, in_ref, out_ref, turn_ref = refs
    count = in_ref.shape[0] // (npy * npz)
    size = out_ref.shape[0] // (npy * npz)
    nz = sums_ref.shape[1] // count
    width = zhigh_ref.shape[1]
    chunks = 2 * width // LANES
    step = turn_ref.shape[0] // (npy * chunks)
    zhigh, zlow = zhigh_ref[...], zlow_ref[...]

    def three(value, product, whigh, wlow):
        rows = value.shape[0]
        high, low = split(value)
        both = product(jnp.concatenate([high, low], axis=0), whigh)
        return both[:rows] + both[rows:] + product(high, wlow)

    def early(first, second):
        late = lax.broadcasted_iota(jnp.int32, first.shape, 1) >= LANES // 2
        return jnp.where(late, pltpu.roll(second, LANES // 2, 1), first)

    def later(first, second):
        late = lax.broadcasted_iota(jnp.int32, first.shape, 1) >= LANES // 2
        return jnp.where(late, second, pltpu.roll(first, LANES // 2, 1))

    def by_mode(mode, chunk):
        return pl.ds(chunk * npy * step + mode, npy, stride=step)

    def by_device(device, chunk):
        return pl.ds((chunk * npy + device) * step, count)

    halves = [[], []]
    for p in range(npy):
        blocks = [in_ref[(p * npz + b) * count : (p * npz + b + 1) * count, :] for b in range(npz)]
        for half, joined in zip(halves, (early, later)):
            half.append(jnp.concatenate([joined(blocks[b], blocks[b + 1]) for b in range(0, npz, 2)], axis=1))
    part = three(jnp.concatenate(halves[0] + halves[1], axis=0), mul, zhigh, zlow)
    for chunk in range(chunks):
        half, lane = divmod(chunk * LANES, width)
        for p in range(npy):
            row = (half * npy + p) * count
            turn_ref[by_device(p, chunk), :] = part[row : row + count, lane : lane + LANES]
    pairs = []
    for mode in range(0, count, 2):
        tiles = [(turn_ref[by_mode(mode, c), :], turn_ref[by_mode(mode + 1, c), :]) for c in range(chunks)]
        pairs.append(jnp.concatenate([early(*tile) for tile in tiles] + [later(*tile) for tile in tiles], axis=0))
    stacked = jnp.concatenate(pairs, axis=1)

    def stack(value):
        high, low = split(value)
        return jnp.concatenate([high, low, high], axis=0)

    modes = mul(ydown_ref[...], stack(stacked)) / sums_ref[...]
    restored = mul(yup_ref[...], stack(modes))
    for mode in range(0, count, 2):
        block = restored[:, mode * nz : (mode + 2) * nz]
        for c in range(chunks):
            even = block[c * npy : (c + 1) * npy]
            odd = block[(chunks + c) * npy : (chunks + c + 1) * npy]
            turn_ref[by_mode(mode, c), :] = early(even, odd)
            turn_ref[by_mode(mode + 1, c), :] = later(even, odd)
    rows = [
        jnp.concatenate(
            [turn_ref[by_device(p, half * chunks // 2 + c), :] for c in range(chunks // 2)], axis=1
        )
        for half in range(2)
        for p in range(npy)
    ]
    spectral = jnp.concatenate(rows, axis=0)
    back = three(spectral, mul_t, zhigh, zlow)
    total = npy * count
    if rims:
        side = [
            three(
                spectral[half * total : (half + 1) * total], mul_t,
                *(ref[:, pl.ds(half * width, width)] for ref in rim_refs),
            )
            for half in range(2)
        ]
        side = side[0] + side[1]
    for p in range(npy):
        for b in range(0, npz, 2):
            first, second = (
                back[k * total + p * count : k * total + (p + 1) * count, b * LANES // 2 : b * LANES // 2 + LANES]
                for k in range(2)
            )
            at = (p * npz + b) * size
            out_ref[at : at + count, :] = early(first, second)
            out_ref[at + size : at + size + count, :] = later(first, second)
            if rims:
                row, middle = p * count, p * count + count // 2
                first = side[row:middle, b * LANES // 2 : b * LANES // 2 + LANES]
                second = side[middle : row + count, b * LANES // 2 : b * LANES // 2 + LANES]
                out_ref[at + count : at + size, :] = early(first, second)
                out_ref[at + size + count : at + 2 * size, :] = later(first, second)


def transformed(points, vectors_ref):
    rows, nx = points.shape
    high, low = split(points)
    both = mul(jnp.concatenate([high, low], axis=0), vectors_ref[:nx, :])
    return both[:rows] + both[rows:] + mul(high, vectors_ref[nx:, :])


def from_modes(spectral_ref, vectors_ref):
    return transformed(spectral_ref[...].T, vectors_ref)


def update_kernel(ly, lz, spectral_ref, vectors_ref, field_ref, coef_ref, updated_ref, weighted_ref, low_ref, high_ref):
    updated = field_ref[...] + from_modes(spectral_ref, vectors_ref)
    updated_ref[...] = updated
    weighted = coef_ref[...] * updated
    weighted_ref[...] = weighted
    store_z_rims(ly, lz, weighted, low_ref, high_ref)


def rim_update_kernel(
    ly, lz, devices, spectral_ref, vectors_ref, field_ref, coef_ref, before_low_ref, before_high_ref,
    outward_ref, taps_ref, updated_ref, weighted_ref, zlow_ref, zhigh_ref, yodd_ref, yeven_ref, below_ref, above_ref,
):
    nx = vectors_ref.shape[1]
    modes = nx // devices
    size = spectral_ref.shape[0] // devices
    own, rims = [], []
    for d in range(devices):
        own.append(spectral_ref[d * size : d * size + modes, :])
        rim = spectral_ref[d * size + modes : (d + 1) * size, :]
        rims += [rim, pltpu.roll(rim, LANES // 2, 1)]
    points = [jnp.concatenate(own, axis=0).T, jnp.concatenate(rims, axis=0).T[: LANES // 2]]
    update = transformed(jnp.concatenate(points, axis=0), vectors_ref)
    count, half = ly * lz, ly * REACH
    updated = field_ref[...] + update[:count]
    updated_ref[...] = updated
    weighted_ref[...] = coef_ref[...] * updated
    for side, (ref, before_ref) in enumerate(((zlow_ref, before_low_ref), (zhigh_ref, before_high_ref))):
        start = count + side * half
        ref[...] = before_ref[:half, :] + before_ref[half:, :] * update[start : start + half]
    at = 0
    for value, rows, whole in own_rim(ly, lz, weighted_ref) + corners(ly, zlow_ref, zhigh_ref):
        below_ref[at : at + rows, :] = value[:rows, :]
        above_ref[at : at + rows, :] = value[whole - rows : whole, :]
        at += rows
    rim, adds = yodd_ref.shape[0], []
    for k, ref in enumerate((below_ref, above_ref)):
        ref[at:, :] = jnp.zeros((ref.shape[0] - at, nx), F32)
        both = three_products(outward_ref[4 * k * rim : 4 * (k + 1) * rim, :], *split(ref[...]))
        adds.append((both[:rim], both[rim:]))
    first = lax.rem(lax.axis_index("py"), 2) == 0
    for start in range(0, rim, 8):
        below, above = (x_banded(taps_ref, *(field[start : start + 8] for field in fields)) for fields in adds)
        yodd_ref[start : start + 8, :] = jnp.where(first, below, above)
        yeven_ref[start : start + 8, :] = jnp.where(first, above, below)


def last_update_kernel(spectral_ref, vectors_ref, field_ref, residual_ref, updated_hbm, residual_hbm, held, sem):
    leaving = pltpu.make_async_copy(residual_ref, residual_hbm, sem.at[0])
    leaving.start()
    held[...] = field_ref[...] + from_modes(spectral_ref, vectors_ref)
    fetch(((held, updated_hbm),), sem.at[pl.ds(1, 1)])
    leaving.wait()


def pairwise(value, axis, odd):
    count = lax.axis_size(axis)
    other = [((i + odd) ^ 1) - odd for i in range(count)]
    return lax.ppermute(value, axis, [(i, j if 0 <= j < count else i) for i, j in enumerate(other)])


def paired(value, axis):
    count = lax.axis_size(axis)
    return lax.ppermute(value, axis, [(i, (i + 1 if i % 2 else i - 1) % count) for i in range(count)])


def odd_pairs(value):
    across, count = lax.axis_size("py"), lax.axis_size("pz")
    pairs = []
    for i in range(across):
        for k in range(count):
            j = k + 1 if k % 2 else k - 1
            pairs.append((i * count + k, i * count + j if 0 <= j < count else (i ^ 1) * count + k))
    return lax.ppermute(value, BOTH, pairs)


def around(value, axis, step):
    count = lax.axis_size(axis)
    return lax.ppermute(value, axis, [(i, (i + step) % count) for i in range(count)])


def plain_modes(received, npy, npz, ly, lz, xvalues, yvalues, zvalues, yvectors, zvectors):
    count = received.shape[0] // (npy * npz)
    field = received.reshape(npy, npz, count, ly, lz).transpose(2, 0, 3, 1, 4).reshape(count, npy * ly, npz * lz)
    field = jnp.einsum("xyz,yj->xjz", field, yvectors, precision=HIGH)
    field = jnp.einsum("xyz,zk->xyk", field, zvectors, precision=HIGH)
    field = field / (yvalues[None, :, None] + zvalues[None, None, :] + xvalues[:, None, None])
    field = jnp.einsum("xjz,yj->xyz", field, yvectors, precision=HIGH)
    field = jnp.einsum("xyk,zk->xyz", field, zvectors, precision=HIGH)
    field = field.reshape(count, npy, ly, npz, lz).transpose(1, 3, 0, 2, 4)
    return field.reshape(npy * npz * count, ly * lz)


def shards(
    solution,
    right_side,
    span_index,
    coef_table,
    xaxis_bands,
    yaxis_bands,
    zaxis_bands,
    xaxis_vectors,
    yaxis_vectors,
    zaxis_vectors,
    xaxis_values,
    yaxis_values,
    zaxis_values,
):
    npy, npz = lax.axis_size("py"), lax.axis_size("pz")
    ly, lz, nx = solution.shape
    ny, nz = npy * ly, npz * lz
    count, devices = ly * lz, npy * npz
    modes = nx // devices
    field = solution.reshape(count, nx)
    right = right_side.reshape(count, nx)
    block, zrim, yrim = (count, nx), (ly * REACH, nx), (up8(REACH * lz + 2 * REACH * REACH), nx)
    zrims = (2 * ly * REACH, nx)
    cell = count * nx * 4
    dma = pltpu.SemaphoreType.DMA

    points = point_columns(ly, lz)
    width = points.shape[1] // 2
    small = [jnp.asarray(points), *(array.transpose(1, 0, 2) for array in (yaxis_bands, zaxis_bands, xaxis_bands))]
    fast = (
        modes % 16 == 0 and npz % 2 == 0 and 2 * ly * REACH <= LANES // 2 and npy % 8 == 0 and lz % 16 == 0 and ly % 4 == 0
        and 2 * nz == LANES and 2 * ny == LANES and count == LANES and nx % LANES == 0
    )
    later = [xaxis_vectors, yaxis_vectors, zaxis_vectors, yaxis_values.reshape(1, ny), zaxis_values.reshape(1, nz)] * fast

    coef, weighted, even, odd, yodd, yeven, *small = call(
        lambda *refs: coefficient_kernel(ly, lz, len(small), *refs),
        [(block, F32)] * 2 + [(zrims, F32)] * 2 + [((REACH * lz + 16, nx), F32)] * 2
        + [(array.shape, array.dtype) for array in small],
        [HBM] * (3 + len(small)), count * nx * 16, 4 * cell,
        [pltpu.SMEM(coef_table.shape, F32), pltpu.VMEM(block, jnp.int32), pltpu.VMEM(block, F32)]
        + [dma((3 + len(small),))],
    )(*in_hbm(coef_table, span_index.reshape(count, nx), field, *small))

    *bands, xbands = small
    stencil, *held = call(
        lambda *refs: stencil_kernel(ly, lz, ny, nz, len(later), *refs),
        [((4 * count, width), BF16)] + [(array.shape, F32) for array in later],
        [VMEM] * 3 + [HBM] * len(later) + [ANY], count * width * 60, 8 * count * width,
        [dma((len(later),))] * fast,
    )(*bands, *in_hbm(*later), even)

    even, odd = pairwise(even, "pz", 0), odd_pairs(odd)
    zlow, zhigh, *corner = call(
        lambda *refs: y_rims_kernel(ly, *refs),
        [(zrims, F32)] * 2 + [((up8(2 * REACH * REACH), nx), F32)] * 2,
        [VMEM] * 2 + [ANY], nx, 4 * nx * 4 * zrims[0],
    )(odd, even, stencil)
    yodd, yeven = [yodd, corner[0]], [yeven, corner[1]]

    if fast:
        zmat, ymat, rmat = (npz * count // 2, ly * nz // 2), (ny, 3 * ny), (npz * LANES // 2, ly * nz)
        vectors, taps, *tables = call(
            lambda *refs: tables_kernel(npy, npz, ly, lz, *refs),
            [((2 * nx, nx), BF16), ((2 * (2 * REACH + 1), 8, nx), F32), ((ny, modes * nz), F32)]
            + [(zmat, BF16), (zmat, BF16), (ymat, BF16), (ymat, BF16), (rmat, BF16), (rmat, BF16)],
            [VMEM] * 6 + [HBM, ANY], npz * count * ly * nz * 8, npz * count * ly * nz * 4,
            [pltpu.SMEM((nx,), F32), dma((1,))],
        )(*held, xbands, *in_hbm(xaxis_values), corner[0])

        def precondition(received, rims):
            size = modes * 3 // 2 if rims else modes
            return call(
                lambda *refs: modes_kernel(npy, npz, rims, *refs),
                [((devices * size, count), F32)], [VMEM] * (8 if rims else 6), 6 * 2 * count * nx * ly * nz, 2 * cell,
                [pltpu.VMEM(((ly * nz // LANES * npy + 1) * (modes + 8), LANES), F32)],
            )(*(tables if rims else tables[:5]), received)[0]
    else:
        vectors, taps = call(
            xvectors_kernel, [((2 * nx, nx), BF16), ((2 * (2 * REACH + 1), 8, nx), F32)], [HBM, VMEM],
            nx * nx * 40, 8 * nx * nx, [pltpu.VMEM((nx, nx), F32), dma((1,))],
        )(*in_hbm(xaxis_vectors), xbands)
        tables = [taps]
        part = lax.axis_index(BOTH)
        xpart = lax.dynamic_slice_in_dim(xaxis_values, part * modes, modes)

        def precondition(received, rims):
            return plain_modes(
                received, npy, npz, ly, lz, xpart, yaxis_values, zaxis_values, yaxis_vectors, zaxis_vectors
            )

    for iteration in range(ITERS):
        last = iteration + 1 == ITERS
        yodd, yeven = [paired(value, "py") for value in yodd], [pairwise(value, "py", 0) for value in yeven]
        parts = len(yodd)
        if fast and iteration == 0:
            outward = call(
                lambda *refs: outward_kernel(ly, lz, nz, *refs),
                [((8 * REACH * lz, LANES), BF16)], [VMEM] * 3 + [ANY], 1 << 20, 1 << 18,
            )(bands[2], yodd[0], yeven[0], tables[0])[0]
        outs = [((nx, count), F32)] + [(block, F32)] * last
        scratch = [pltpu.VMEM(block, F32)] * (not last)
        cost = (6 * count * nx * (nx + 2 * width), 5 * cell + 4 * nx * nx)
        if fast and iteration > 0:
            applied = call(
                lambda *refs: own_part_kernel(lz, zrim[0], *refs), [(block, F32)], [VMEM] * 5, *cost,
            )(weighted, zlow, zhigh, stencil, taps)[0]
            spectral, *residual = call(joined_residual_kernel, outs, [VMEM] * 6, *cost, scratch)(
                applied, *yodd, *yeven, coef, right, vectors
            )
        else:
            spectral, *residual = call(
                lambda *refs: residual_kernel(lz, zrim[0], parts, *refs),
                outs, [VMEM] * (8 + 2 * parts) + [ANY], *cost, scratch,
            )(weighted, zlow, zhigh, *yodd, *yeven, stencil, taps, coef, right, vectors, outward if fast else tables[0])
        spectral = lax.all_to_all(spectral, BOTH, split_axis=0, concat_axis=0, tiled=True)
        spectral = precondition(spectral, not last)
        spectral = lax.all_to_all(spectral, BOTH, split_axis=0, concat_axis=0, tiled=True)
        cost = (6 * count * nx * nx, 4 * cell + 4 * nx * nx)
        if last:
            field, residual = call(
                last_update_kernel, [(block, F32), (block, F32)], [VMEM] * 4, *cost,
                [pltpu.VMEM(block, F32), dma((2,))], [HBM] * 2,
            )(spectral, vectors, field, *residual)
        elif fast:
            field, weighted, zlow, zhigh, *yrims = call(
                lambda *refs: rim_update_kernel(ly, lz, devices, *refs),
                [(block, F32)] * 2 + [(zrim, F32)] * 2 + [((REACH * lz, nx), F32)] * 2, [VMEM] * 8, *cost,
                [pltpu.VMEM((LANES, nx), F32)] * 2,
            )(spectral, vectors, field, coef, zlow, zhigh, outward, taps)
        else:
            field, weighted, zlow, zhigh = call(
                lambda *refs: update_kernel(ly, lz, *refs), [(block, F32)] * 2 + [(zrim, F32)] * 2, [VMEM] * 4, *cost,
            )(spectral, vectors, field, coef)
            zlow, zhigh = around(zhigh, "pz", 1), around(zlow, "pz", -1)
            yrims = call(
                lambda *refs: next_y_rims_kernel(ly, lz, *refs),
                [(yrim, F32)] * 2, [VMEM] * 3, nx, 4 * nx * 4 * yrim[0],
            )(weighted, zlow, zhigh)
        yodd, yeven = ([value] for value in yrims) if not last else (None, None)
    return (field.reshape(solution.shape), residual.reshape(solution.shape))


def solution(mesh):
    return jax.shard_map(
        shards,
        mesh=mesh,
        in_specs=(
            P("py", "pz", None),
            P("py", "pz", None),
            P("py", "pz", None),
            P(),
            P(),
            P(None, None, "py"),
            P(None, None, "pz"),
            P(),
            P(),
            P(),
            P(),
            P(),
            P(),
        ),
        out_specs=(P("py", "pz", None), P("py", "pz", None)),
        check_vma=False,
    )
```

```python
import jax
import jax.numpy as jnp
import numpy as np
from jax import lax
from jax.experimental import pallas as pl
from jax.experimental.pallas import tpu as pltpu
from jax.sharding import PartitionSpec as P

ITERS = 2
REACH = 3
LANES = 128
HIGH = lax.Precision.HIGHEST
BOTH = ("py", "pz")
F32 = jnp.float32
BF16 = jnp.bfloat16
VMEM = pl.BlockSpec(memory_space=pltpu.VMEM)
HBM = pl.BlockSpec(memory_space=pltpu.HBM)
ANY = pl.BlockSpec(memory_space=pl.ANY)


def up8(count):
    return -(-count // 8) * 8


def split(value):
    high = value.astype(BF16)
    return high, (value - high.astype(F32)).astype(BF16)


def exact(left, right, sides=(1, 0)):
    return lax.dot_general(
        left, right, (((sides[0],), (sides[1],)), ((), ())), precision=HIGH, preferred_element_type=F32
    )


def fetch(pairs, sem):
    copies = [pltpu.make_async_copy(source, target, sem.at[i]) for i, (source, target) in enumerate(pairs)]
    for copy in copies:
        copy.start()
    for copy in copies:
        copy.wait()


def in_hbm(*arrays):
    return [pltpu.with_memory_space_constraint(array, pltpu.HBM) for array in arrays]


def mul(left, right):
    return lax.dot_general(left, right, (((1,), (0,)), ((), ())), preferred_element_type=F32)


def mul_t(left, right):
    return lax.dot_general(left, right, (((1,), (1,)), ((), ())), preferred_element_type=F32)


def call(kernel, outs, specs, flops, cost_bytes, scratch=(), out_specs=None):
    return pl.pallas_call(
        kernel,
        out_shape=[jax.ShapeDtypeStruct(shape, dtype) for shape, dtype in outs],
        in_specs=specs,
        out_specs=out_specs or [VMEM] * len(outs),
        scratch_shapes=list(scratch),
        compiler_params=pltpu.CompilerParams(vmem_limit_bytes=32 * 1024 * 1024),
        cost_estimate=pl.CostEstimate(flops=flops, bytes_accessed=cost_bytes, transcendentals=0),
    )


def store_z_rims(ly, lz, weighted, low_ref, high_ref):
    for y in range(ly):
        low_ref[y * REACH : (y + 1) * REACH, :] = weighted[y * lz : y * lz + REACH, :]
        high_ref[y * REACH : (y + 1) * REACH, :] = weighted[(y + 1) * lz - REACH : (y + 1) * lz, :]


def coefficient_kernel(ly, lz, small, *refs):
    table_ref, span_ref, field_ref, *refs = refs
    sources, refs = refs[:small], refs[small:]
    coef_ref, weighted_ref, even_ref, odd_ref, yodd_ref, yeven_ref, *refs = refs
    targets, (table, span, field, sem) = refs[:small], refs[small:]
    count = span.shape[0]
    pieces = [pl.ds(start, count // 4) for start in range(0, count, count // 4)]
    pairs = [(table_ref, table)]
    for piece in pieces:
        pairs += [(span_ref.at[piece, :], span.at[piece, :]), (field_ref.at[piece, :], field.at[piece, :])]
    pairs += list(zip(sources, targets))
    copies = [pltpu.make_async_copy(*pair, sem.at[i]) for i, pair in enumerate(pairs)]
    for copy in copies:
        copy.start()
    copies[0].wait()
    first = lax.rem(lax.axis_index("pz"), 2) == 0
    half = ly * REACH
    entries = [table[entry] for entry in range(table_ref.shape[0])]
    for start in range(0, span.shape[0], lz):
        if start % (count // 4) == 0:
            for copy in copies[1 + start * 8 // count : 3 + start * 8 // count]:
                copy.wait()
        rows = pl.ds(start, lz)
        index = span[rows, :]
        coef = jnp.full(index.shape, entries[0], F32)
        for entry in range(1, len(entries)):
            coef = jnp.where(index == entry, entries[entry], coef)
        coef_ref[rows, :] = coef
        weighted = coef * field[rows, :]
        weighted_ref[rows, :] = weighted
        for value, at in ((weighted, 0), (coef, half)):
            rim = pl.ds(at + start // lz * REACH, REACH)
            low, high = value[:REACH], value[lz - REACH :]
            even_ref[rim, :] = jnp.where(first, high, low)
            odd_ref[rim, :] = jnp.where(first, low, high)
    store_y_rims(own_rim(ly, lz, weighted_ref), yodd_ref, yeven_ref)
    for copy in copies[1 + 2 * len(pieces) :]:
        copy.wait()
    ybands = targets[1]
    for ref in (yodd_ref, yeven_ref):
        for matrix in range(2):
            at = REACH * lz + 8 * matrix
            ref[at : at + ybands.shape[0], :ly] = ybands[:, matrix, :]


def store_y_rims(pieces, odd_ref, even_ref):
    first = lax.rem(lax.axis_index("py"), 2) == 0
    at = 0
    for value, count, rows in pieces:
        low, high = value[:count, :], value[rows - count : rows, :]
        even_ref[at : at + count, :] = jnp.where(first, high, low)
        odd_ref[at : at + count, :] = jnp.where(first, low, high)
        at += count
    if at < even_ref.shape[0]:
        for ref in (even_ref, odd_ref):
            ref[at:, :] = jnp.zeros((ref.shape[0] - at, ref.shape[1]), F32)


def own_rim(ly, lz, weighted):
    return [(weighted, REACH * lz, ly * lz)]


def corners(ly, zlow, zhigh):
    return [(value, REACH * REACH, ly * REACH) for value in (zlow, zhigh)]


def y_rims_kernel(ly, odd_ref, even_ref, _, zlow_ref, zhigh_ref, yodd_ref, yeven_ref):
    first = lax.rem(lax.axis_index("pz"), 2) == 0
    zlow_ref[...] = jnp.where(first, odd_ref[...], even_ref[...])
    zhigh_ref[...] = jnp.where(first, even_ref[...], odd_ref[...])
    store_y_rims(corners(ly, zlow_ref, zhigh_ref), yodd_ref, yeven_ref)


def next_y_rims_kernel(ly, lz, weighted_ref, zlow_ref, zhigh_ref, yodd_ref, yeven_ref):
    store_y_rims(own_rim(ly, lz, weighted_ref) + corners(ly, zlow_ref, zhigh_ref), yodd_ref, yeven_ref)


def point_columns(ly, lz):
    below, above = range(-REACH, 0), range(REACH)
    halves = []
    for half in range(2):
        first = 0 if half == 0 else ly // 2 - REACH
        points = [(first + y, z) for y in range(ly // 2 + REACH) for z in range(lz)]
        points += [(y, z) for y in range(ly) for z in below]
        points += [(y, lz + z) for y in range(ly) for z in above]
        ys = below if half == 0 else [ly + y for y in above]
        points += [(y, z) for y in ys for z in range(lz)]
        points += [(y, z) for y in ys for z in below]
        points += [(y, lz + z) for y in ys for z in above]
        halves += points + [(1 << 20, 1 << 20)] * (-len(points) % LANES)
    return np.array(halves, np.int32).T.copy()


def stencil_kernel(ly, lz, ny, nz, later, points_ref, ybands_ref, zbands_ref, *refs):
    sources, (_, out_ref, *refs) = refs[:later], refs[later:]
    copies = [pltpu.make_async_copy(*pair, refs[-1].at[i]) for i, pair in enumerate(zip(sources, refs[:later]))]
    for copy in copies:
        copy.start()
    count = ly * lz // 2
    width = out_ref.shape[1]
    for half in range(2):
        rows = lax.broadcasted_iota(jnp.int32, (count, 1), 0) + half * count
        columns = pl.ds(half * width, width)
        factors = []
        for bands_ref, length, row, column, first, whole in (
            (ybands_ref, ly, lax.div(rows, lz), points_ref[0:1, columns], lax.axis_index("py") * ly, ny),
            (zbands_ref, lz, lax.rem(rows, lz), points_ref[1:2, columns], lax.axis_index("pz") * lz, nz),
        ):
            pick = (lax.broadcasted_iota(jnp.int32, (count, length), 1) == row).astype(F32)
            spot = column + first
            inside = (spot >= 0) & (spot < whole)
            distance = jnp.where(inside, column, 1 << 20) - row
            here = [distance == offset - REACH for offset in range(2 * REACH + 1)]
            for matrix in range(2):
                taps = exact(pick, bands_ref[:, matrix, :], (1, 1))
                dense = jnp.zeros(distance.shape, F32)
                for offset in range(2 * REACH + 1):
                    dense = jnp.where(here[offset], taps[:, offset : offset + 1], dense)
                factors.append(dense)
        ystiff, ymass, zstiff, zmass = factors
        for part, value in enumerate((ymass * zmass, ystiff * zmass + ymass * zstiff)):
            at = (4 * half + part) * count
            out_ref[at : at + count, :], out_ref[at + 2 * count : at + 3 * count, :] = split(value)
    for copy in copies:
        copy.wait()


def store_taps(xbands_ref, taps_ref):
    nx = xbands_ref.shape[2]
    lane = lax.broadcasted_iota(jnp.int32, (1, nx), 1)
    for offset in range(2 * REACH + 1):
        move = offset - REACH
        inside = (lane - move >= 0) & (lane - move < nx)
        for matrix in range(2):
            band = xbands_ref[offset, matrix : matrix + 1, :]
            band = pltpu.roll(band, move % nx, 1) if move else band
            taps_ref[2 * offset + matrix] = jnp.broadcast_to(jnp.where(inside, band, 0.0), (8, nx))


def doubled(size):
    row = lax.broadcasted_iota(jnp.int32, (size, 2 * size), 0)
    return (row == lax.rem(lax.broadcasted_iota(jnp.int32, (size, 2 * size), 1), size)).astype(F32)


def xvectors_kernel(source, xbands_ref, out_ref, taps_ref, held, sem):
    store_taps(xbands_ref, taps_ref)
    fetch(((source, held),), sem)
    high, low = split(held[...].T)
    out_ref[: high.shape[0], :] = high
    out_ref[high.shape[0] :, :] = low


def tables_kernel(
    npy, npz, ly, lz, xvec_ref, yvec_ref, zvec_ref, yval_ref, zval_ref, xbands_ref, xval_hbm, _,
    xout_ref, taps_ref, sums_ref, zhigh_ref, zlow_ref, ydown_ref, yup_ref, rimhigh_ref, rimlow_ref, xval_ref, sem,
):
    fetching = pltpu.make_async_copy(xval_hbm, xval_ref, sem.at[0])
    fetching.start()
    store_taps(xbands_ref, taps_ref)
    ny, nz = npy * ly, npz * lz
    nx = xvec_ref.shape[0]
    high, low = split(xvec_ref[...].T)
    xout_ref[:nx, :] = high
    xout_ref[nx:, :] = low
    pair = exact(zvec_ref[...], doubled(nz))
    half = lax.broadcasted_iota(jnp.int32, pair.shape, 1) >= nz
    zhigh_ref[...] = jnp.zeros(zhigh_ref.shape, BF16)
    zlow_ref[...] = jnp.zeros(zlow_ref.shape, BF16)
    for parity in range(2):
        high, low = split(jnp.where(half == (parity == 1), pair, 0.0))
        for yl in range(parity, ly // 2, 2):
            for block in range(npz):
                to = (pl.ds((block * ly // 2 + yl) * lz, lz), pl.ds(yl // 2 * 2 * nz, 2 * nz))
                zhigh_ref[to] = high[block * lz : (block + 1) * lz, :]
                zlow_ref[to] = low[block * lz : (block + 1) * lz, :]
    shape = (rimhigh_ref.shape[0], 1)
    row = lax.broadcasted_iota(jnp.int32, shape, 0)
    block, spot = lax.div(row, LANES // 2), lax.rem(row, LANES // 2)
    above = spot >= ly * REACH
    spot = jnp.where(above, spot - ly * REACH, spot)
    yrow = jnp.where(spot < ly * REACH, lax.div(spot, REACH), 2 * ly)
    z = block * lz + lax.rem(spot, REACH) + jnp.where(above, lz, -REACH)
    rim = exact((lax.broadcasted_iota(jnp.int32, (shape[0], nz), 1) == z).astype(F32), pair)
    late = (lax.broadcasted_iota(jnp.int32, rim.shape, 1) >= nz).astype(jnp.int32)
    for chunk in range(ly // 2):
        columns = pl.ds(chunk * 2 * nz, 2 * nz)
        rimhigh_ref[:, columns], rimlow_ref[:, columns] = split(jnp.where(yrow - 2 * chunk == late, rim, 0.0))

    def y_of(p):
        spot = lax.div(p, npy)
        return lax.rem(p, npy) * ly + 2 * lax.rem(spot, ly // 2) + lax.div(spot, ly // 2)

    def parts(array):
        high, low = split(array)
        late = lax.broadcasted_iota(jnp.int32, array.shape, 1) >= 2 * ny
        return jnp.where(late, low.astype(F32), high.astype(F32)).astype(BF16)

    lane = lax.broadcasted_iota(jnp.int32, (ny, 3 * ny), 1)
    row = lax.broadcasted_iota(jnp.int32, (ny, 3 * ny), 0)
    moved = (row == y_of(lax.rem(lane, ny))).astype(F32)
    ydown_ref[...] = parts(exact(yvec_ref[...].T, moved))
    order = (
        lax.broadcasted_iota(jnp.int32, (ny, ny), 1) == y_of(lax.broadcasted_iota(jnp.int32, (ny, ny), 0))
    ).astype(F32)
    copies = (row == lax.rem(lane, ny)).astype(F32)
    yup_ref[...] = parts(exact(exact(order, yvec_ref[...]), copies))
    fetching.wait()
    square = (ny, ny)
    diagonal = lax.broadcasted_iota(jnp.int32, square, 0) == lax.broadcasted_iota(jnp.int32, square, 1)
    ycolumn = jnp.sum(jnp.where(diagonal, yval_ref[...], 0.0), axis=1, keepdims=True)
    yz = ycolumn + exact(jnp.broadcast_to(zval_ref[...], (8, nz)), doubled(nz))[0:1]
    late = lax.broadcasted_iota(jnp.int32, (1, 2 * nz), 1) >= nz
    modes = sums_ref.shape[1] // nz
    first = (lax.axis_index("py") * (nz // lz) + lax.axis_index("pz")) * modes
    for mode in range(0, modes, 2):
        x = jnp.where(late, xval_ref[first + mode + 1], xval_ref[first + mode])
        sums_ref[:, mode * nz : (mode + 2) * nz] = yz + x


def y_sides(odd, even):
    first = lax.rem(lax.axis_index("py"), 2) == 0
    return jnp.where(first, odd, even), jnp.where(first, even, odd)


def three_products(matrix, high, low):
    rows = matrix.shape[0] // 2
    both = mul(matrix, high)
    return both[:rows] + both[rows:] + mul(matrix[:rows], low)


def yz_fields(lz, zrim, weighted_ref, zlow_ref, zhigh_ref, sides, stencil_ref):
    count, nx = weighted_ref.shape
    part, need = count // 2, count // 2 + REACH * lz
    own = split(weighted_ref[...])
    zrims = split(jnp.concatenate([zlow_ref[:zrim, :], zhigh_ref[:zrim, :]], axis=0))
    left = stencil_ref.shape[1] - need - 2 * zrim
    fields = []
    for half in range(2):
        if sides is None:
            yrim = [jnp.zeros((left, nx), BF16)] * 2
        else:
            rim = sides[half]
            missing = left - rim.shape[0]
            yrim = split(jnp.concatenate([rim, jnp.zeros((missing, nx), F32)], axis=0) if missing else rim)
        first = half * (count - need)
        high, low = (
            jnp.concatenate([own[k][first : first + need], zrims[k], yrim[k]], axis=0) for k in range(2)
        )
        both = three_products(stencil_ref[4 * half * part : 4 * (half + 1) * part, :], high, low)
        fields.append((both[:part], both[part:]))
    return fields


def x_banded(taps_ref, mass, stiff):
    nx = mass.shape[1]
    applied = None
    for offset in range(2 * REACH + 1):
        move = offset - REACH
        term = taps_ref[2 * offset] * mass + taps_ref[2 * offset + 1] * stiff
        term = pltpu.roll(term, -move % nx, 1) if move else term
        applied = term if applied is None else applied + term
    return applied


def store_modes(points, vectors_ref, spectral_ref):
    count, nx = points.shape
    high, low = split(points)
    product = mul_t(jnp.concatenate([high, low], axis=0), vectors_ref[:nx, :])
    spectral_ref[...] = (product[:count] + product[count:] + mul_t(high, vectors_ref[nx:, :])).T


def residual_kernel(lz, zrim, parts, *refs):
    weighted_ref, zlow_ref, zhigh_ref, *refs = refs
    yodd_refs, yeven_refs, refs = refs[:parts], refs[parts : 2 * parts], refs[2 * parts :]
    stencil_ref, taps_ref, coef_ref, right_ref, vectors_ref, _, spectral_ref, residual_ref = refs
    if parts == 2:
        (yodd_ref, odd_corner_ref), (yeven_ref, even_corner_ref) = yodd_refs, yeven_refs
        own = REACH * lz
        yodd = jnp.concatenate([yodd_ref[:own, :], odd_corner_ref[...]], axis=0)
        yeven = jnp.concatenate([yeven_ref[:own, :], even_corner_ref[...]], axis=0)
    else:
        yodd, yeven = yodd_refs[0][...], yeven_refs[0][...]
    fields = yz_fields(lz, zrim, weighted_ref, zlow_ref, zhigh_ref, y_sides(yodd, yeven), stencil_ref)
    part = weighted_ref.shape[0] // 2
    for start in range(0, 2 * part, 8):
        mass, stiff = (field[start % part : start % part + 8] for field in fields[start // part])
        rows = pl.ds(start, 8)
        residual_ref[rows, :] = right_ref[rows, :] - coef_ref[rows, :] * x_banded(taps_ref, mass, stiff)
    store_modes(residual_ref[...], vectors_ref, spectral_ref)


def own_part_kernel(lz, zrim, weighted_ref, zlow_ref, zhigh_ref, stencil_ref, taps_ref, applied_ref):
    fields = yz_fields(lz, zrim, weighted_ref, zlow_ref, zhigh_ref, None, stencil_ref)
    part = weighted_ref.shape[0] // 2
    for start in range(0, 2 * part, 8):
        mass, stiff = (field[start % part : start % part + 8] for field in fields[start // part])
        applied_ref[pl.ds(start, 8), :] = x_banded(taps_ref, mass, stiff)


def joined_residual_kernel(applied_ref, yodd_ref, yeven_ref, coef_ref, right_ref, vectors_ref, spectral_ref, residual_ref):
    count, rim = applied_ref.shape[0], yodd_ref.shape[0]
    for at, side in zip((0, count - rim), y_sides(yodd_ref[...], yeven_ref[...])):
        rows = pl.ds(at, rim)
        residual_ref[rows, :] = right_ref[rows, :] - coef_ref[rows, :] * (applied_ref[rows, :] + side)
    rows = pl.ds(rim, count - 2 * rim)
    residual_ref[rows, :] = right_ref[rows, :] - coef_ref[rows, :] * applied_ref[rows, :]
    store_modes(residual_ref[...], vectors_ref, spectral_ref)


def outward_kernel(ly, lz, nz, zbands_ref, yodd_ref, yeven_ref, _, out_ref):
    rim, side = REACH * lz, REACH * REACH
    width = out_ref.shape[1]
    row = lax.broadcasted_iota(jnp.int32, (rim, 1), 0)
    column = lax.broadcasted_iota(jnp.int32, (1, width), 1)
    spot = jnp.where(column < rim + side, column - rim, column - rim - side)
    yin = jnp.where(column < rim, lax.div(column, lz), lax.div(spot, REACH))
    zin = jnp.where(
        column < rim, lax.rem(column, lz), lax.rem(spot, REACH) + jnp.where(column < rim + side, -REACH, lz)
    )
    place = zin + lax.axis_index("pz") * lz
    inside = (column < rim + 2 * side) & (place >= 0) & (place < nz)
    yout, zout = lax.div(row, lz), lax.rem(row, lz)

    def dense(taps, tap):
        value = jnp.zeros(tap.shape, F32)
        for k in range(2 * REACH + 1):
            value = jnp.where(tap == k, taps[:, k : k + 1], value)
        return value

    def picked(length, at, bands):
        return exact((lax.broadcasted_iota(jnp.int32, (rim, length), 1) == at).astype(F32), bands, (1, 1))

    ztap = jnp.where(inside, zin - zout + REACH, -1)
    zstiff, zmass = (dense(picked(lz, zout, zbands_ref[:, matrix, :]), ztap) for matrix in range(2))
    sides = y_sides(yodd_ref[rim : rim + 16, :ly], yeven_ref[rim : rim + 16, :ly])
    spot, count = lax.axis_index("py"), lax.axis_size("py")
    for k, (bands, at, shift, there) in enumerate(
        ((sides[0], yout + ly - REACH, 2 * REACH, spot > 0), (sides[1], yout, 0, spot < count - 1))
    ):
        ytap = jnp.where(there, yin - yout + shift, -1)
        ystiff, ymass = (dense(picked(ly, at, bands[8 * matrix : 8 * matrix + 8]), ytap) for matrix in range(2))
        for part, value in enumerate((ymass * zmass, ystiff * zmass + ymass * zstiff)):
            start = (4 * k + part) * rim
            out_ref[start : start + rim, :], out_ref[start + 2 * rim : start + 3 * rim, :] = split(value)


def modes_kernel(npy, npz, rims, *refs):
    sums_ref, zhigh_ref, zlow_ref, ydown_ref, yup_ref, *rim_refs, in_ref, out_ref, turn_ref = refs
    count = in_ref.shape[0] // (npy * npz)
    size = out_ref.shape[0] // (npy * npz)
    nz = sums_ref.shape[1] // count
    width = zhigh_ref.shape[1]
    chunks = 2 * width // LANES
    step = turn_ref.shape[0] // (npy * chunks)
    zhigh, zlow = zhigh_ref[...], zlow_ref[...]

    def three(value, product, whigh, wlow):
        rows = value.shape[0]
        high, low = split(value)
        both = product(jnp.concatenate([high, low], axis=0), whigh)
        return both[:rows] + both[rows:] + product(high, wlow)

    def early(first, second):
        late = lax.broadcasted_iota(jnp.int32, first.shape, 1) >= LANES // 2
        return jnp.where(late, pltpu.roll(second, LANES // 2, 1), first)

    def later(first, second):
        late = lax.broadcasted_iota(jnp.int32, first.shape, 1) >= LANES // 2
        return jnp.where(late, second, pltpu.roll(first, LANES // 2, 1))

    def by_mode(mode, chunk):
        return pl.ds(chunk * npy * step + mode, npy, stride=step)

    def by_device(device, chunk):
        return pl.ds((chunk * npy + device) * step, count)

    halves = [[], []]
    for p in range(npy):
        blocks = [in_ref[(p * npz + b) * count : (p * npz + b + 1) * count, :] for b in range(npz)]
        for half, joined in zip(halves, (early, later)):
            half.append(jnp.concatenate([joined(blocks[b], blocks[b + 1]) for b in range(0, npz, 2)], axis=1))
    part = three(jnp.concatenate(halves[0] + halves[1], axis=0), mul, zhigh, zlow)
    for chunk in range(chunks):
        half, lane = divmod(chunk * LANES, width)
        for p in range(npy):
            row = (half * npy + p) * count
            turn_ref[by_device(p, chunk), :] = part[row : row + count, lane : lane + LANES]
    pairs = []
    for mode in range(0, count, 2):
        tiles = [(turn_ref[by_mode(mode, c), :], turn_ref[by_mode(mode + 1, c), :]) for c in range(chunks)]
        pairs.append(jnp.concatenate([early(*tile) for tile in tiles] + [later(*tile) for tile in tiles], axis=0))
    stacked = jnp.concatenate(pairs, axis=1)

    def stack(value):
        high, low = split(value)
        return jnp.concatenate([high, low, high], axis=0)

    modes = mul(ydown_ref[...], stack(stacked)) / sums_ref[...]
    restored = mul(yup_ref[...], stack(modes))
    for mode in range(0, count, 2):
        block = restored[:, mode * nz : (mode + 2) * nz]
        for c in range(chunks):
            even = block[c * npy : (c + 1) * npy]
            odd = block[(chunks + c) * npy : (chunks + c + 1) * npy]
            turn_ref[by_mode(mode, c), :] = early(even, odd)
            turn_ref[by_mode(mode + 1, c), :] = later(even, odd)
    rows = [
        jnp.concatenate(
            [turn_ref[by_device(p, half * chunks // 2 + c), :] for c in range(chunks // 2)], axis=1
        )
        for half in range(2)
        for p in range(npy)
    ]
    spectral = jnp.concatenate(rows, axis=0)
    back = three(spectral, mul_t, zhigh, zlow)
    total = npy * count
    if rims:
        side = [
            three(
                spectral[half * total : (half + 1) * total], mul_t,
                *(ref[:, pl.ds(half * width, width)] for ref in rim_refs),
            )
            for half in range(2)
        ]
        side = side[0] + side[1]
    for p in range(npy):
        for b in range(0, npz, 2):
            first, second = (
                back[k * total + p * count : k * total + (p + 1) * count, b * LANES // 2 : b * LANES // 2 + LANES]
                for k in range(2)
            )
            at = (p * npz + b) * size
            out_ref[at : at + count, :] = early(first, second)
            out_ref[at + size : at + size + count, :] = later(first, second)
            if rims:
                row, middle = p * count, p * count + count // 2
                first = side[row:middle, b * LANES // 2 : b * LANES // 2 + LANES]
                second = side[middle : row + count, b * LANES // 2 : b * LANES // 2 + LANES]
                out_ref[at + count : at + size, :] = early(first, second)
                out_ref[at + size + count : at + 2 * size, :] = later(first, second)


def transformed(points, vectors_ref):
    rows, nx = points.shape
    high, low = split(points)
    both = mul(jnp.concatenate([high, low], axis=0), vectors_ref[:nx, :])
    return both[:rows] + both[rows:] + mul(high, vectors_ref[nx:, :])


def from_modes(spectral_ref, vectors_ref):
    return transformed(spectral_ref[...].T, vectors_ref)


def update_kernel(ly, lz, spectral_ref, vectors_ref, field_ref, coef_ref, updated_ref, weighted_ref, low_ref, high_ref):
    updated = field_ref[...] + from_modes(spectral_ref, vectors_ref)
    updated_ref[...] = updated
    weighted = coef_ref[...] * updated
    weighted_ref[...] = weighted
    store_z_rims(ly, lz, weighted, low_ref, high_ref)


def rim_update_kernel(
    ly, lz, devices, spectral_ref, vectors_ref, field_ref, coef_ref, before_low_ref, before_high_ref,
    outward_ref, taps_ref, updated_ref, weighted_ref, zlow_ref, zhigh_ref, yodd_ref, yeven_ref, below_ref, above_ref,
):
    nx = vectors_ref.shape[1]
    modes = nx // devices
    size = spectral_ref.shape[0] // devices
    own, rims = [], []
    for d in range(devices):
        own.append(spectral_ref[d * size : d * size + modes, :])
        rim = spectral_ref[d * size + modes : (d + 1) * size, :]
        rims += [rim, pltpu.roll(rim, LANES // 2, 1)]
    points = [jnp.concatenate(own, axis=0).T, jnp.concatenate(rims, axis=0).T[: LANES // 2]]
    update = transformed(jnp.concatenate(points, axis=0), vectors_ref)
    count, half = ly * lz, ly * REACH
    updated = field_ref[...] + update[:count]
    updated_ref[...] = updated
    weighted_ref[...] = coef_ref[...] * updated
    for side, (ref, before_ref) in enumerate(((zlow_ref, before_low_ref), (zhigh_ref, before_high_ref))):
        start = count + side * half
        ref[...] = before_ref[:half, :] + before_ref[half:, :] * update[start : start + half]
    at = 0
    for value, rows, whole in own_rim(ly, lz, weighted_ref) + corners(ly, zlow_ref, zhigh_ref):
        below_ref[at : at + rows, :] = value[:rows, :]
        above_ref[at : at + rows, :] = value[whole - rows : whole, :]
        at += rows
    rim, adds = yodd_ref.shape[0], []
    for k, ref in enumerate((below_ref, above_ref)):
        ref[at:, :] = jnp.zeros((ref.shape[0] - at, nx), F32)
        both = three_products(outward_ref[4 * k * rim : 4 * (k + 1) * rim, :], *split(ref[...]))
        adds.append((both[:rim], both[rim:]))
    first = lax.rem(lax.axis_index("py"), 2) == 0
    for start in range(0, rim, 8):
        below, above = (x_banded(taps_ref, *(field[start : start + 8] for field in fields)) for fields in adds)
        yodd_ref[start : start + 8, :] = jnp.where(first, below, above)
        yeven_ref[start : start + 8, :] = jnp.where(first, above, below)


def last_update_kernel(spectral_ref, vectors_ref, field_ref, residual_ref, updated_hbm, residual_hbm, held, sem):
    leaving = pltpu.make_async_copy(residual_ref, residual_hbm, sem.at[0])
    leaving.start()
    held[...] = field_ref[...] + from_modes(spectral_ref, vectors_ref)
    fetch(((held, updated_hbm),), sem.at[pl.ds(1, 1)])
    leaving.wait()


def pairwise(value, axis, odd):
    count = lax.axis_size(axis)
    other = [((i + odd) ^ 1) - odd for i in range(count)]
    return lax.ppermute(value, axis, [(i, j if 0 <= j < count else i) for i, j in enumerate(other)])


def paired(value, near):
    across, count = lax.axis_size("py"), lax.axis_size("pz")
    pairs = []
    for i in range(across):
        for k in range(count):
            j = i + 1 if i % 2 else i - 1
            end = i * count + (k ^ 1) if near and k ^ 1 < count else j % across * count + k
            pairs.append((i * count + k, j * count + k if 0 <= j < across else end))
    return lax.ppermute(value, BOTH, pairs)


def odd_pairs(value):
    across, count = lax.axis_size("py"), lax.axis_size("pz")
    pairs = []
    for i in range(across):
        for k in range(count):
            j = k + 1 if k % 2 else k - 1
            pairs.append((i * count + k, i * count + j if 0 <= j < count else (i ^ 1) * count + k))
    return lax.ppermute(value, BOTH, pairs)


def around(value, axis, step):
    count = lax.axis_size(axis)
    return lax.ppermute(value, axis, [(i, (i + step) % count) for i in range(count)])


def plain_modes(received, npy, npz, ly, lz, xvalues, yvalues, zvalues, yvectors, zvectors):
    count = received.shape[0] // (npy * npz)
    field = received.reshape(npy, npz, count, ly, lz).transpose(2, 0, 3, 1, 4).reshape(count, npy * ly, npz * lz)
    field = jnp.einsum("xyz,yj->xjz", field, yvectors, precision=HIGH)
    field = jnp.einsum("xyz,zk->xyk", field, zvectors, precision=HIGH)
    field = field / (yvalues[None, :, None] + zvalues[None, None, :] + xvalues[:, None, None])
    field = jnp.einsum("xjz,yj->xyz", field, yvectors, precision=HIGH)
    field = jnp.einsum("xyk,zk->xyz", field, zvectors, precision=HIGH)
    field = field.reshape(count, npy, ly, npz, lz).transpose(1, 3, 0, 2, 4)
    return field.reshape(npy * npz * count, ly * lz)


def shards(
    solution,
    right_side,
    span_index,
    coef_table,
    xaxis_bands,
    yaxis_bands,
    zaxis_bands,
    xaxis_vectors,
    yaxis_vectors,
    zaxis_vectors,
    xaxis_values,
    yaxis_values,
    zaxis_values,
):
    npy, npz = lax.axis_size("py"), lax.axis_size("pz")
    ly, lz, nx = solution.shape
    ny, nz = npy * ly, npz * lz
    count, devices = ly * lz, npy * npz
    modes = nx // devices
    field = solution.reshape(count, nx)
    right = right_side.reshape(count, nx)
    block, zrim, yrim = (count, nx), (ly * REACH, nx), (up8(REACH * lz + 2 * REACH * REACH), nx)
    zrims = (2 * ly * REACH, nx)
    cell = count * nx * 4
    dma = pltpu.SemaphoreType.DMA

    points = point_columns(ly, lz)
    width = points.shape[1] // 2
    small = [jnp.asarray(points), *(array.transpose(1, 0, 2) for array in (yaxis_bands, zaxis_bands, xaxis_bands))]
    fast = (
        modes % 16 == 0 and npz % 2 == 0 and 2 * ly * REACH <= LANES // 2 and npy % 8 == 0 and lz % 16 == 0 and ly % 4 == 0
        and 2 * nz == LANES and 2 * ny == LANES and count == LANES and nx % LANES == 0
    )
    later = [xaxis_vectors, yaxis_vectors, zaxis_vectors, yaxis_values.reshape(1, ny), zaxis_values.reshape(1, nz)] * fast

    coef, weighted, even, odd, yodd, yeven, *small = call(
        lambda *refs: coefficient_kernel(ly, lz, len(small), *refs),
        [(block, F32)] * 2 + [(zrims, F32)] * 2 + [((REACH * lz + 16, nx), F32)] * 2
        + [(array.shape, array.dtype) for array in small],
        [HBM] * (3 + len(small)), count * nx * 16, 4 * cell,
        [pltpu.SMEM(coef_table.shape, F32), pltpu.VMEM(block, jnp.int32), pltpu.VMEM(block, F32)]
        + [dma((9 + len(small),))],
    )(*in_hbm(coef_table, span_index.reshape(count, nx), field, *small))

    *bands, xbands = small
    stencil, *held = call(
        lambda *refs: stencil_kernel(ly, lz, ny, nz, len(later), *refs),
        [((4 * count, width), BF16)] + [(array.shape, F32) for array in later],
        [VMEM] * 3 + [HBM] * len(later) + [ANY], count * width * 60, 8 * count * width,
        [dma((len(later),))] * fast,
    )(*bands, *in_hbm(*later), even)

    even, odd = pairwise(even, "pz", 0), odd_pairs(odd)
    zlow, zhigh, *corner = call(
        lambda *refs: y_rims_kernel(ly, *refs),
        [(zrims, F32)] * 2 + [((up8(2 * REACH * REACH), nx), F32)] * 2,
        [VMEM] * 2 + [ANY], nx, 4 * nx * 4 * zrims[0],
    )(odd, even, stencil)
    yodd, yeven = [yodd, corner[0]], [yeven, corner[1]]

    if fast:
        zmat, ymat, rmat = (npz * count // 2, ly * nz // 2), (ny, 3 * ny), (npz * LANES // 2, ly * nz)
        vectors, taps, *tables = call(
            lambda *refs: tables_kernel(npy, npz, ly, lz, *refs),
            [((2 * nx, nx), BF16), ((2 * (2 * REACH + 1), 8, nx), F32), ((ny, modes * nz), F32)]
            + [(zmat, BF16), (zmat, BF16), (ymat, BF16), (ymat, BF16), (rmat, BF16), (rmat, BF16)],
            [VMEM] * 6 + [HBM, ANY], npz * count * ly * nz * 8, npz * count * ly * nz * 4,
            [pltpu.SMEM((nx,), F32), dma((1,))],
        )(*held, xbands, *in_hbm(xaxis_values), corner[0])

        def precondition(received, rims):
            size = modes * 3 // 2 if rims else modes
            return call(
                lambda *refs: modes_kernel(npy, npz, rims, *refs),
                [((devices * size, count), F32)], [VMEM] * (8 if rims else 6), 6 * 2 * count * nx * ly * nz, 2 * cell,
                [pltpu.VMEM(((ly * nz // LANES * npy + 1) * (modes + 8), LANES), F32)],
            )(*(tables if rims else tables[:5]), received)[0]
    else:
        vectors, taps = call(
            xvectors_kernel, [((2 * nx, nx), BF16), ((2 * (2 * REACH + 1), 8, nx), F32)], [HBM, VMEM],
            nx * nx * 40, 8 * nx * nx, [pltpu.VMEM((nx, nx), F32), dma((1,))],
        )(*in_hbm(xaxis_vectors), xbands)
        tables = [taps]
        part = lax.axis_index(BOTH)
        xpart = lax.dynamic_slice_in_dim(xaxis_values, part * modes, modes)

        def precondition(received, rims):
            return plain_modes(
                received, npy, npz, ly, lz, xpart, yaxis_values, zaxis_values, yaxis_vectors, zaxis_vectors
            )

    for iteration in range(ITERS):
        last = iteration + 1 == ITERS
        yodd, yeven = [paired(value, iteration > 0) for value in yodd], [pairwise(value, "py", 0) for value in yeven]
        parts = len(yodd)
        if fast and iteration == 0:
            outward = call(
                lambda *refs: outward_kernel(ly, lz, nz, *refs),
                [((8 * REACH * lz, LANES), BF16)], [VMEM] * 3 + [ANY], 1 << 20, 1 << 18,
            )(bands[2], yodd[0], yeven[0], tables[0])[0]
        outs = [((nx, count), F32)] + [(block, F32)] * last
        scratch = [pltpu.VMEM(block, F32)] * (not last)
        cost = (6 * count * nx * (nx + 2 * width), 5 * cell + 4 * nx * nx)
        if fast and iteration > 0:
            applied = call(
                lambda *refs: own_part_kernel(lz, zrim[0], *refs), [(block, F32)], [VMEM] * 5, *cost,
            )(weighted, zlow, zhigh, stencil, taps)[0]
            spectral, *residual = call(joined_residual_kernel, outs, [VMEM] * 6, *cost, scratch)(
                applied, *yodd, *yeven, coef, right, vectors
            )
        else:
            spectral, *residual = call(
                lambda *refs: residual_kernel(lz, zrim[0], parts, *refs),
                outs, [VMEM] * (8 + 2 * parts) + [ANY], *cost, scratch,
            )(weighted, zlow, zhigh, *yodd, *yeven, stencil, taps, coef, right, vectors, outward if fast else tables[0])
        spectral = lax.all_to_all(spectral, BOTH, split_axis=0, concat_axis=0, tiled=True)
        spectral = precondition(spectral, not last)
        spectral = lax.all_to_all(spectral, BOTH, split_axis=0, concat_axis=0, tiled=True)
        cost = (6 * count * nx * nx, 4 * cell + 4 * nx * nx)
        if last:
            field, residual = call(
                last_update_kernel, [(block, F32), (block, F32)], [VMEM] * 4, *cost,
                [pltpu.VMEM(block, F32), dma((2,))], [HBM] * 2,
            )(spectral, vectors, field, *residual)
        elif fast:
            field, weighted, zlow, zhigh, *yrims = call(
                lambda *refs: rim_update_kernel(ly, lz, devices, *refs),
                [(block, F32)] * 2 + [(zrim, F32)] * 2 + [((REACH * lz, nx), F32)] * 2, [VMEM] * 8, *cost,
                [pltpu.VMEM((LANES, nx), F32)] * 2,
            )(spectral, vectors, field, coef, zlow, zhigh, outward, taps)
        else:
            field, weighted, zlow, zhigh = call(
                lambda *refs: update_kernel(ly, lz, *refs), [(block, F32)] * 2 + [(zrim, F32)] * 2, [VMEM] * 4, *cost,
            )(spectral, vectors, field, coef)
            zlow, zhigh = around(zhigh, "pz", 1), around(zlow, "pz", -1)
            yrims = call(
                lambda *refs: next_y_rims_kernel(ly, lz, *refs),
                [(yrim, F32)] * 2, [VMEM] * 3, nx, 4 * nx * 4 * yrim[0],
            )(weighted, zlow, zhigh)
        yodd, yeven = ([value] for value in yrims) if not last else (None, None)
    return (field.reshape(solution.shape), residual.reshape(solution.shape))


def solution(mesh):
    return jax.shard_map(
        shards,
        mesh=mesh,
        in_specs=(
            P("py", "pz", None),
            P("py", "pz", None),
            P("py", "pz", None),
            P(),
            P(),
            P(None, None, "py"),
            P(None, None, "pz"),
            P(),
            P(),
            P(),
            P(),
            P(),
            P(),
        ),
        out_specs=(P("py", "pz", None), P("py", "pz", None)),
        check_vma=False,
    )
```

```python
import jax
import jax.numpy as jnp
import numpy as np
from jax import lax
from jax.experimental import pallas as pl
from jax.experimental.pallas import tpu as pltpu
from jax.sharding import PartitionSpec as P

ITERS = 2
REACH = 3
LANES = 128
HIGH = lax.Precision.HIGHEST
BOTH = ("py", "pz")
F32 = jnp.float32
BF16 = jnp.bfloat16
VMEM = pl.BlockSpec(memory_space=pltpu.VMEM)
HBM = pl.BlockSpec(memory_space=pltpu.HBM)
ANY = pl.BlockSpec(memory_space=pl.ANY)


def up8(count):
    return -(-count // 8) * 8


def split(value):
    high = value.astype(BF16)
    return high, (value - high.astype(F32)).astype(BF16)


def exact(left, right, sides=(1, 0)):
    return lax.dot_general(
        left, right, (((sides[0],), (sides[1],)), ((), ())), precision=HIGH, preferred_element_type=F32
    )


def fetch(pairs, sem):
    copies = [pltpu.make_async_copy(source, target, sem.at[i]) for i, (source, target) in enumerate(pairs)]
    for copy in copies:
        copy.start()
    for copy in copies:
        copy.wait()


def in_hbm(*arrays):
    return [pltpu.with_memory_space_constraint(array, pltpu.HBM) for array in arrays]


def mul(left, right):
    return lax.dot_general(left, right, (((1,), (0,)), ((), ())), preferred_element_type=F32)


def mul_t(left, right):
    return lax.dot_general(left, right, (((1,), (1,)), ((), ())), preferred_element_type=F32)


def call(kernel, outs, specs, flops, cost_bytes, scratch=(), out_specs=None):
    return pl.pallas_call(
        kernel,
        out_shape=[jax.ShapeDtypeStruct(shape, dtype) for shape, dtype in outs],
        in_specs=specs,
        out_specs=out_specs or [VMEM] * len(outs),
        scratch_shapes=list(scratch),
        compiler_params=pltpu.CompilerParams(vmem_limit_bytes=32 * 1024 * 1024),
        cost_estimate=pl.CostEstimate(flops=flops, bytes_accessed=cost_bytes, transcendentals=0),
    )


def store_z_rims(ly, lz, weighted, low_ref, high_ref):
    for y in range(ly):
        low_ref[y * REACH : (y + 1) * REACH, :] = weighted[y * lz : y * lz + REACH, :]
        high_ref[y * REACH : (y + 1) * REACH, :] = weighted[(y + 1) * lz - REACH : (y + 1) * lz, :]


def coefficient_kernel(ly, lz, small, *refs):
    table_ref, span_ref, field_ref, *refs = refs
    sources, refs = refs[:small], refs[small:]
    coef_ref, weighted_ref, even_ref, odd_ref, yodd_ref, yeven_ref, *refs = refs
    targets, (table, span, field, sem) = refs[:small], refs[small:]
    fetch([(table_ref, table), (span_ref, span), (field_ref, field), *zip(sources, targets)], sem)
    first = lax.rem(lax.axis_index("pz"), 2) == 0
    half = ly * REACH
    entries = [table[entry] for entry in range(table_ref.shape[0])]
    for start in range(0, span.shape[0], lz):
        rows = pl.ds(start, lz)
        index = span[rows, :]
        coef = jnp.full(index.shape, entries[0], F32)
        for entry in range(1, len(entries)):
            coef = jnp.where(index == entry, entries[entry], coef)
        coef_ref[rows, :] = coef
        weighted = coef * field[rows, :]
        weighted_ref[rows, :] = weighted
        for value, at in ((weighted, 0), (coef, half)):
            rim = pl.ds(at + start // lz * REACH, REACH)
            low, high = value[:REACH], value[lz - REACH :]
            even_ref[rim, :] = jnp.where(first, high, low)
            odd_ref[rim, :] = jnp.where(first, low, high)
    store_y_rims(own_rim(ly, lz, weighted_ref), yodd_ref, yeven_ref)
    ybands = targets[1]
    for ref in (yodd_ref, yeven_ref):
        for matrix in range(2):
            at = REACH * lz + 8 * matrix
            ref[at : at + ybands.shape[0], :ly] = ybands[:, matrix, :]


def store_y_rims(pieces, odd_ref, even_ref):
    first = lax.rem(lax.axis_index("py"), 2) == 0
    at = 0
    for value, count, rows in pieces:
        low, high = value[:count, :], value[rows - count : rows, :]
        even_ref[at : at + count, :] = jnp.where(first, high, low)
        odd_ref[at : at + count, :] = jnp.where(first, low, high)
        at += count
    if at < even_ref.shape[0]:
        for ref in (even_ref, odd_ref):
            ref[at:, :] = jnp.zeros((ref.shape[0] - at, ref.shape[1]), F32)


def own_rim(ly, lz, weighted):
    return [(weighted, REACH * lz, ly * lz)]


def corners(ly, zlow, zhigh):
    return [(value, REACH * REACH, ly * REACH) for value in (zlow, zhigh)]


def y_rims_kernel(ly, odd_ref, even_ref, _, zlow_ref, zhigh_ref, yodd_ref, yeven_ref):
    first = lax.rem(lax.axis_index("pz"), 2) == 0
    zlow_ref[...] = jnp.where(first, odd_ref[...], even_ref[...])
    zhigh_ref[...] = jnp.where(first, even_ref[...], odd_ref[...])
    store_y_rims(corners(ly, zlow_ref, zhigh_ref), yodd_ref, yeven_ref)


def next_y_rims_kernel(ly, lz, weighted_ref, zlow_ref, zhigh_ref, yodd_ref, yeven_ref):
    store_y_rims(own_rim(ly, lz, weighted_ref) + corners(ly, zlow_ref, zhigh_ref), yodd_ref, yeven_ref)


def point_columns(ly, lz):
    below, above = range(-REACH, 0), range(REACH)
    halves = []
    for half in range(2):
        first = 0 if half == 0 else ly // 2 - REACH
        points = [(first + y, z) for y in range(ly // 2 + REACH) for z in range(lz)]
        points += [(y, z) for y in range(ly) for z in below]
        points += [(y, lz + z) for y in range(ly) for z in above]
        ys = below if half == 0 else [ly + y for y in above]
        points += [(y, z) for y in ys for z in range(lz)]
        points += [(y, z) for y in ys for z in below]
        points += [(y, lz + z) for y in ys for z in above]
        halves += points + [(1 << 20, 1 << 20)] * (-len(points) % LANES)
    return np.array(halves, np.int32).T.copy()


def stencil_kernel(ly, lz, ny, nz, later, points_ref, ybands_ref, zbands_ref, *refs):
    sources, (_, out_ref, *refs) = refs[:later], refs[later:]
    copies = [pltpu.make_async_copy(*pair, refs[-1].at[i]) for i, pair in enumerate(zip(sources, refs[:later]))]
    for copy in copies:
        copy.start()
    count = ly * lz // 2
    width = out_ref.shape[1]
    for half in range(2):
        rows = lax.broadcasted_iota(jnp.int32, (count, 1), 0) + half * count
        columns = pl.ds(half * width, width)
        factors = []
        for bands_ref, length, row, column, first, whole in (
            (ybands_ref, ly, lax.div(rows, lz), points_ref[0:1, columns], lax.axis_index("py") * ly, ny),
            (zbands_ref, lz, lax.rem(rows, lz), points_ref[1:2, columns], lax.axis_index("pz") * lz, nz),
        ):
            pick = (lax.broadcasted_iota(jnp.int32, (count, length), 1) == row).astype(F32)
            spot = column + first
            inside = (spot >= 0) & (spot < whole)
            distance = jnp.where(inside, column, 1 << 20) - row
            here = [distance == offset - REACH for offset in range(2 * REACH + 1)]
            for matrix in range(2):
                taps = exact(pick, bands_ref[:, matrix, :], (1, 1))
                dense = jnp.zeros(distance.shape, F32)
                for offset in range(2 * REACH + 1):
                    dense = jnp.where(here[offset], taps[:, offset : offset + 1], dense)
                factors.append(dense)
        ystiff, ymass, zstiff, zmass = factors
        for part, value in enumerate((ymass * zmass, ystiff * zmass + ymass * zstiff)):
            at = (4 * half + part) * count
            out_ref[at : at + count, :], out_ref[at + 2 * count : at + 3 * count, :] = split(value)
    for copy in copies:
        copy.wait()


def store_taps(xbands_ref, taps_ref):
    nx = xbands_ref.shape[2]
    lane = lax.broadcasted_iota(jnp.int32, (1, nx), 1)
    for offset in range(2 * REACH + 1):
        move = offset - REACH
        inside = (lane - move >= 0) & (lane - move < nx)
        for matrix in range(2):
            band = xbands_ref[offset, matrix : matrix + 1, :]
            band = pltpu.roll(band, move % nx, 1) if move else band
            taps_ref[2 * offset + matrix] = jnp.broadcast_to(jnp.where(inside, band, 0.0), (8, nx))


def doubled(size):
    row = lax.broadcasted_iota(jnp.int32, (size, 2 * size), 0)
    return (row == lax.rem(lax.broadcasted_iota(jnp.int32, (size, 2 * size), 1), size)).astype(F32)


def xvectors_kernel(source, xbands_ref, out_ref, taps_ref, held, sem):
    store_taps(xbands_ref, taps_ref)
    fetch(((source, held),), sem)
    high, low = split(held[...].T)
    out_ref[: high.shape[0], :] = high
    out_ref[high.shape[0] :, :] = low


def tables_kernel(
    npy, npz, ly, lz, xvec_ref, yvec_ref, zvec_ref, yval_ref, zval_ref, xbands_ref, xval_hbm, _,
    xout_ref, taps_ref, sums_ref, zhigh_ref, zlow_ref, ydown_ref, yup_ref, rimhigh_ref, rimlow_ref, xval_ref, sem,
):
    fetching = pltpu.make_async_copy(xval_hbm, xval_ref, sem.at[0])
    fetching.start()
    store_taps(xbands_ref, taps_ref)
    ny, nz = npy * ly, npz * lz
    nx = xvec_ref.shape[0]
    high, low = split(xvec_ref[...].T)
    xout_ref[:nx, :] = high
    xout_ref[nx:, :] = low
    pair = exact(zvec_ref[...], doubled(nz))
    half = lax.broadcasted_iota(jnp.int32, pair.shape, 1) >= nz
    zhigh_ref[...] = jnp.zeros(zhigh_ref.shape, BF16)
    zlow_ref[...] = jnp.zeros(zlow_ref.shape, BF16)
    for parity in range(2):
        high, low = split(jnp.where(half == (parity == 1), pair, 0.0))
        for yl in range(parity, ly // 2, 2):
            for block in range(npz):
                to = (pl.ds((block * ly // 2 + yl) * lz, lz), pl.ds(yl // 2 * 2 * nz, 2 * nz))
                zhigh_ref[to] = high[block * lz : (block + 1) * lz, :]
                zlow_ref[to] = low[block * lz : (block + 1) * lz, :]
    shape = (rimhigh_ref.shape[0], 1)
    row = lax.broadcasted_iota(jnp.int32, shape, 0)
    block, spot = lax.div(row, LANES // 2), lax.rem(row, LANES // 2)
    above = spot >= ly * REACH
    spot = jnp.where(above, spot - ly * REACH, spot)
    yrow = jnp.where(spot < ly * REACH, lax.div(spot, REACH), 2 * ly)
    z = block * lz + lax.rem(spot, REACH) + jnp.where(above, lz, -REACH)
    rim = exact((lax.broadcasted_iota(jnp.int32, (shape[0], nz), 1) == z).astype(F32), pair)
    late = (lax.broadcasted_iota(jnp.int32, rim.shape, 1) >= nz).astype(jnp.int32)
    for chunk in range(ly // 2):
        columns = pl.ds(chunk * 2 * nz, 2 * nz)
        rimhigh_ref[:, columns], rimlow_ref[:, columns] = split(jnp.where(yrow - 2 * chunk == late, rim, 0.0))

    def y_of(p):
        spot = lax.div(p, npy)
        return lax.rem(p, npy) * ly + 2 * lax.rem(spot, ly // 2) + lax.div(spot, ly // 2)

    def parts(array):
        high, low = split(array)
        late = lax.broadcasted_iota(jnp.int32, array.shape, 1) >= 2 * ny
        return jnp.where(late, low.astype(F32), high.astype(F32)).astype(BF16)

    lane = lax.broadcasted_iota(jnp.int32, (ny, 3 * ny), 1)
    row = lax.broadcasted_iota(jnp.int32, (ny, 3 * ny), 0)
    moved = (row == y_of(lax.rem(lane, ny))).astype(F32)
    ydown_ref[...] = parts(exact(yvec_ref[...].T, moved))
    order = (
        lax.broadcasted_iota(jnp.int32, (ny, ny), 1) == y_of(lax.broadcasted_iota(jnp.int32, (ny, ny), 0))
    ).astype(F32)
    copies = (row == lax.rem(lane, ny)).astype(F32)
    yup_ref[...] = parts(exact(exact(order, yvec_ref[...]), copies))
    fetching.wait()
    square = (ny, ny)
    diagonal = lax.broadcasted_iota(jnp.int32, square, 0) == lax.broadcasted_iota(jnp.int32, square, 1)
    ycolumn = jnp.sum(jnp.where(diagonal, yval_ref[...], 0.0), axis=1, keepdims=True)
    yz = ycolumn + exact(jnp.broadcast_to(zval_ref[...], (8, nz)), doubled(nz))[0:1]
    late = lax.broadcasted_iota(jnp.int32, (1, 2 * nz), 1) >= nz
    modes = sums_ref.shape[1] // nz
    first = (lax.axis_index("py") * (nz // lz) + lax.axis_index("pz")) * modes
    for mode in range(0, modes, 2):
        x = jnp.where(late, xval_ref[first + mode + 1], xval_ref[first + mode])
        sums_ref[:, mode * nz : (mode + 2) * nz] = yz + x


def y_sides(odd, even):
    first = lax.rem(lax.axis_index("py"), 2) == 0
    return jnp.where(first, odd, even), jnp.where(first, even, odd)


def three_products(matrix, high, low):
    rows = matrix.shape[0] // 2
    both = mul(matrix, high)
    return both[:rows] + both[rows:] + mul(matrix[:rows], low)


def yz_fields(lz, zrim, weighted_ref, zlow_ref, zhigh_ref, sides, stencil_ref):
    count, nx = weighted_ref.shape
    part, need = count // 2, count // 2 + REACH * lz
    own = split(weighted_ref[...])
    zrims = split(jnp.concatenate([zlow_ref[:zrim, :], zhigh_ref[:zrim, :]], axis=0))
    left = stencil_ref.shape[1] - need - 2 * zrim
    fields = []
    for half in range(2):
        if sides is None:
            yrim = [jnp.zeros((left, nx), BF16)] * 2
        else:
            rim = sides[half]
            missing = left - rim.shape[0]
            yrim = split(jnp.concatenate([rim, jnp.zeros((missing, nx), F32)], axis=0) if missing else rim)
        first = half * (count - need)
        high, low = (
            jnp.concatenate([own[k][first : first + need], zrims[k], yrim[k]], axis=0) for k in range(2)
        )
        both = three_products(stencil_ref[4 * half * part : 4 * (half + 1) * part, :], high, low)
        fields.append((both[:part], both[part:]))
    return fields


def x_banded(taps_ref, mass, stiff):
    nx = mass.shape[1]
    applied = None
    for offset in range(2 * REACH + 1):
        move = offset - REACH
        term = taps_ref[2 * offset] * mass + taps_ref[2 * offset + 1] * stiff
        term = pltpu.roll(term, -move % nx, 1) if move else term
        applied = term if applied is None else applied + term
    return applied


def store_modes(points, vectors_ref, spectral_ref):
    count, nx = points.shape
    high, low = split(points)
    product = mul_t(jnp.concatenate([high, low], axis=0), vectors_ref[:nx, :])
    spectral_ref[...] = (product[:count] + product[count:] + mul_t(high, vectors_ref[nx:, :])).T


def residual_kernel(lz, zrim, parts, *refs):
    weighted_ref, zlow_ref, zhigh_ref, *refs = refs
    yodd_refs, yeven_refs, refs = refs[:parts], refs[parts : 2 * parts], refs[2 * parts :]
    stencil_ref, taps_ref, coef_ref, right_ref, vectors_ref, _, spectral_ref, residual_ref = refs
    if parts == 2:
        (yodd_ref, odd_corner_ref), (yeven_ref, even_corner_ref) = yodd_refs, yeven_refs
        own = REACH * lz
        yodd = jnp.concatenate([yodd_ref[:own, :], odd_corner_ref[...]], axis=0)
        yeven = jnp.concatenate([yeven_ref[:own, :], even_corner_ref[...]], axis=0)
    else:
        yodd, yeven = yodd_refs[0][...], yeven_refs[0][...]
    fields = yz_fields(lz, zrim, weighted_ref, zlow_ref, zhigh_ref, y_sides(yodd, yeven), stencil_ref)
    part = weighted_ref.shape[0] // 2
    for start in range(0, 2 * part, 8):
        mass, stiff = (field[start % part : start % part + 8] for field in fields[start // part])
        rows = pl.ds(start, 8)
        residual_ref[rows, :] = right_ref[rows, :] - coef_ref[rows, :] * x_banded(taps_ref, mass, stiff)
    store_modes(residual_ref[...], vectors_ref, spectral_ref)


def own_part_kernel(lz, zrim, weighted_ref, zlow_ref, zhigh_ref, stencil_ref, taps_ref, applied_ref):
    fields = yz_fields(lz, zrim, weighted_ref, zlow_ref, zhigh_ref, None, stencil_ref)
    part = weighted_ref.shape[0] // 2
    for start in range(0, 2 * part, 8):
        mass, stiff = (field[start % part : start % part + 8] for field in fields[start // part])
        applied_ref[pl.ds(start, 8), :] = x_banded(taps_ref, mass, stiff)


def joined_residual_kernel(applied_ref, yodd_ref, yeven_ref, coef_ref, right_ref, vectors_ref, spectral_ref, residual_ref):
    count, rim = applied_ref.shape[0], yodd_ref.shape[0]
    for at, side in zip((0, count - rim), y_sides(yodd_ref[...], yeven_ref[...])):
        rows = pl.ds(at, rim)
        residual_ref[rows, :] = right_ref[rows, :] - coef_ref[rows, :] * (applied_ref[rows, :] + side)
    rows = pl.ds(rim, count - 2 * rim)
    residual_ref[rows, :] = right_ref[rows, :] - coef_ref[rows, :] * applied_ref[rows, :]
    store_modes(residual_ref[...], vectors_ref, spectral_ref)


def outward_kernel(ly, lz, nz, zbands_ref, yodd_ref, yeven_ref, _, out_ref):
    rim, side = REACH * lz, REACH * REACH
    width = out_ref.shape[1]
    row = lax.broadcasted_iota(jnp.int32, (rim, 1), 0)
    column = lax.broadcasted_iota(jnp.int32, (1, width), 1)
    spot = jnp.where(column < rim + side, column - rim, column - rim - side)
    yin = jnp.where(column < rim, lax.div(column, lz), lax.div(spot, REACH))
    zin = jnp.where(
        column < rim, lax.rem(column, lz), lax.rem(spot, REACH) + jnp.where(column < rim + side, -REACH, lz)
    )
    place = zin + lax.axis_index("pz") * lz
    inside = (column < rim + 2 * side) & (place >= 0) & (place < nz)
    yout, zout = lax.div(row, lz), lax.rem(row, lz)

    def dense(taps, tap):
        value = jnp.zeros(tap.shape, F32)
        for k in range(2 * REACH + 1):
            value = jnp.where(tap == k, taps[:, k : k + 1], value)
        return value

    def picked(length, at, bands):
        return exact((lax.broadcasted_iota(jnp.int32, (rim, length), 1) == at).astype(F32), bands, (1, 1))

    ztap = jnp.where(inside, zin - zout + REACH, -1)
    zstiff, zmass = (dense(picked(lz, zout, zbands_ref[:, matrix, :]), ztap) for matrix in range(2))
    sides = y_sides(yodd_ref[rim : rim + 16, :ly], yeven_ref[rim : rim + 16, :ly])
    spot, count = lax.axis_index("py"), lax.axis_size("py")
    for k, (bands, at, shift, there) in enumerate(
        ((sides[0], yout + ly - REACH, 2 * REACH, spot > 0), (sides[1], yout, 0, spot < count - 1))
    ):
        ytap = jnp.where(there, yin - yout + shift, -1)
        ystiff, ymass = (dense(picked(ly, at, bands[8 * matrix : 8 * matrix + 8]), ytap) for matrix in range(2))
        for part, value in enumerate((ymass * zmass, ystiff * zmass + ymass * zstiff)):
            start = (4 * k + part) * rim
            out_ref[start : start + rim, :], out_ref[start + 2 * rim : start + 3 * rim, :] = split(value)


def modes_kernel(npy, npz, rims, *refs):
    sums_ref, zhigh_ref, zlow_ref, ydown_ref, yup_ref, *rim_refs, in_ref, out_ref, turn_ref = refs
    count = in_ref.shape[0] // (npy * npz)
    size = out_ref.shape[0] // (npy * npz)
    nz = sums_ref.shape[1] // count
    width = zhigh_ref.shape[1]
    chunks = 2 * width // LANES
    step = turn_ref.shape[0] // (npy * chunks)
    zhigh, zlow = zhigh_ref[...], zlow_ref[...]

    def three(value, product, whigh, wlow):
        rows = value.shape[0]
        high, low = split(value)
        both = product(jnp.concatenate([high, low], axis=0), whigh)
        return both[:rows] + both[rows:] + product(high, wlow)

    def early(first, second):
        late = lax.broadcasted_iota(jnp.int32, first.shape, 1) >= LANES // 2
        return jnp.where(late, pltpu.roll(second, LANES // 2, 1), first)

    def later(first, second):
        late = lax.broadcasted_iota(jnp.int32, first.shape, 1) >= LANES // 2
        return jnp.where(late, second, pltpu.roll(first, LANES // 2, 1))

    def by_mode(mode, chunk):
        return pl.ds(chunk * npy * step + mode, npy, stride=step)

    def by_device(device, chunk):
        return pl.ds((chunk * npy + device) * step, count)

    halves = [[], []]
    for p in range(npy):
        blocks = [in_ref[(p * npz + b) * count : (p * npz + b + 1) * count, :] for b in range(npz)]
        for half, joined in zip(halves, (early, later)):
            half.append(jnp.concatenate([joined(blocks[b], blocks[b + 1]) for b in range(0, npz, 2)], axis=1))
    part = three(jnp.concatenate(halves[0] + halves[1], axis=0), mul, zhigh, zlow)
    for chunk in range(chunks):
        half, lane = divmod(chunk * LANES, width)
        for p in range(npy):
            row = (half * npy + p) * count
            turn_ref[by_device(p, chunk), :] = part[row : row + count, lane : lane + LANES]
    pairs = []
    for mode in range(0, count, 2):
        tiles = [(turn_ref[by_mode(mode, c), :], turn_ref[by_mode(mode + 1, c), :]) for c in range(chunks)]
        pairs.append(jnp.concatenate([early(*tile) for tile in tiles] + [later(*tile) for tile in tiles], axis=0))
    stacked = jnp.concatenate(pairs, axis=1)

    def stack(value):
        high, low = split(value)
        return jnp.concatenate([high, low, high], axis=0)

    modes = mul(ydown_ref[...], stack(stacked)) / sums_ref[...]
    restored = mul(yup_ref[...], stack(modes))
    for mode in range(0, count, 2):
        block = restored[:, mode * nz : (mode + 2) * nz]
        for c in range(chunks):
            even = block[c * npy : (c + 1) * npy]
            odd = block[(chunks + c) * npy : (chunks + c + 1) * npy]
            turn_ref[by_mode(mode, c), :] = early(even, odd)
            turn_ref[by_mode(mode + 1, c), :] = later(even, odd)
    rows = [
        jnp.concatenate(
            [turn_ref[by_device(p, half * chunks // 2 + c), :] for c in range(chunks // 2)], axis=1
        )
        for half in range(2)
        for p in range(npy)
    ]
    spectral = jnp.concatenate(rows, axis=0)
    back = three(spectral, mul_t, zhigh, zlow)
    total = npy * count
    if rims:
        side = [
            three(
                spectral[half * total : (half + 1) * total], mul_t,
                *(ref[:, pl.ds(half * width, width)] for ref in rim_refs),
            )
            for half in range(2)
        ]
        side = side[0] + side[1]
    for p in range(npy):
        for b in range(0, npz, 2):
            first, second = (
                back[k * total + p * count : k * total + (p + 1) * count, b * LANES // 2 : b * LANES // 2 + LANES]
                for k in range(2)
            )
            at = (p * npz + b) * size
            out_ref[at : at + count, :] = early(first, second)
            out_ref[at + size : at + size + count, :] = later(first, second)
            if rims:
                row, middle = p * count, p * count + count // 2
                first = side[row:middle, b * LANES // 2 : b * LANES // 2 + LANES]
                second = side[middle : row + count, b * LANES // 2 : b * LANES // 2 + LANES]
                out_ref[at + count : at + size, :] = early(first, second)
                out_ref[at + size + count : at + 2 * size, :] = later(first, second)


def transformed(points, vectors_ref):
    rows, nx = points.shape
    high, low = split(points)
    both = mul(jnp.concatenate([high, low], axis=0), vectors_ref[:nx, :])
    return both[:rows] + both[rows:] + mul(high, vectors_ref[nx:, :])


def from_modes(spectral_ref, vectors_ref):
    return transformed(spectral_ref[...].T, vectors_ref)


def update_kernel(ly, lz, spectral_ref, vectors_ref, field_ref, coef_ref, updated_ref, weighted_ref, low_ref, high_ref):
    updated = field_ref[...] + from_modes(spectral_ref, vectors_ref)
    updated_ref[...] = updated
    weighted = coef_ref[...] * updated
    weighted_ref[...] = weighted
    store_z_rims(ly, lz, weighted, low_ref, high_ref)


def rim_update_kernel(
    ly, lz, devices, spectral_ref, vectors_ref, field_ref, coef_ref, before_low_ref, before_high_ref,
    outward_ref, taps_ref, updated_ref, weighted_ref, zlow_ref, zhigh_ref, yodd_ref, yeven_ref, below_ref, above_ref,
):
    nx = vectors_ref.shape[1]
    modes = nx // devices
    size = spectral_ref.shape[0] // devices
    own, rims = [], []
    for d in range(devices):
        own.append(spectral_ref[d * size : d * size + modes, :])
        rim = spectral_ref[d * size + modes : (d + 1) * size, :]
        rims += [rim, pltpu.roll(rim, LANES // 2, 1)]
    points = [jnp.concatenate(own, axis=0).T, jnp.concatenate(rims, axis=0).T[: LANES // 2]]
    update = transformed(jnp.concatenate(points, axis=0), vectors_ref)
    count, half = ly * lz, ly * REACH
    updated = field_ref[...] + update[:count]
    updated_ref[...] = updated
    weighted_ref[...] = coef_ref[...] * updated
    for side, (ref, before_ref) in enumerate(((zlow_ref, before_low_ref), (zhigh_ref, before_high_ref))):
        start = count + side * half
        ref[...] = before_ref[:half, :] + before_ref[half:, :] * update[start : start + half]
    at = 0
    for value, rows, whole in own_rim(ly, lz, weighted_ref) + corners(ly, zlow_ref, zhigh_ref):
        below_ref[at : at + rows, :] = value[:rows, :]
        above_ref[at : at + rows, :] = value[whole - rows : whole, :]
        at += rows
    rim, adds = yodd_ref.shape[0], []
    for k, ref in enumerate((below_ref, above_ref)):
        ref[at:, :] = jnp.zeros((ref.shape[0] - at, nx), F32)
        both = three_products(outward_ref[4 * k * rim : 4 * (k + 1) * rim, :], *split(ref[...]))
        adds.append((both[:rim], both[rim:]))
    first = lax.rem(lax.axis_index("py"), 2) == 0
    for start in range(0, rim, 8):
        below, above = (x_banded(taps_ref, *(field[start : start + 8] for field in fields)) for fields in adds)
        yodd_ref[start : start + 8, :] = jnp.where(first, below, above)
        yeven_ref[start : start + 8, :] = jnp.where(first, above, below)


def last_modes_kernel(npy, npz, *refs):
    *tables, residual_ref, in_ref, out_ref, residual_hbm, turn_ref, sem = refs
    leaving = pltpu.make_async_copy(residual_ref, residual_hbm, sem.at[0])
    leaving.start()
    modes_kernel(npy, npz, False, *tables, in_ref, out_ref, turn_ref)
    leaving.wait()


def last_update_kernel(spectral_ref, vectors_ref, field_ref, updated_hbm, held, sem):
    held[...] = field_ref[...] + from_modes(spectral_ref, vectors_ref)
    fetch(((held, updated_hbm),), sem)


def pairwise(value, axis, odd):
    count = lax.axis_size(axis)
    other = [((i + odd) ^ 1) - odd for i in range(count)]
    return lax.ppermute(value, axis, [(i, j if 0 <= j < count else i) for i, j in enumerate(other)])


def paired(value, axis):
    count = lax.axis_size(axis)
    return lax.ppermute(value, axis, [(i, (i + 1 if i % 2 else i - 1) % count) for i in range(count)])


def odd_pairs(value):
    across, count = lax.axis_size("py"), lax.axis_size("pz")
    pairs = []
    for i in range(across):
        for k in range(count):
            j = k + 1 if k % 2 else k - 1
            pairs.append((i * count + k, i * count + j if 0 <= j < count else (i ^ 1) * count + k))
    return lax.ppermute(value, BOTH, pairs)


def around(value, axis, step):
    count = lax.axis_size(axis)
    return lax.ppermute(value, axis, [(i, (i + step) % count) for i in range(count)])


def plain_modes(received, npy, npz, ly, lz, xvalues, yvalues, zvalues, yvectors, zvectors):
    count = received.shape[0] // (npy * npz)
    field = received.reshape(npy, npz, count, ly, lz).transpose(2, 0, 3, 1, 4).reshape(count, npy * ly, npz * lz)
    field = jnp.einsum("xyz,yj->xjz", field, yvectors, precision=HIGH)
    field = jnp.einsum("xyz,zk->xyk", field, zvectors, precision=HIGH)
    field = field / (yvalues[None, :, None] + zvalues[None, None, :] + xvalues[:, None, None])
    field = jnp.einsum("xjz,yj->xyz", field, yvectors, precision=HIGH)
    field = jnp.einsum("xyk,zk->xyz", field, zvectors, precision=HIGH)
    field = field.reshape(count, npy, ly, npz, lz).transpose(1, 3, 0, 2, 4)
    return field.reshape(npy * npz * count, ly * lz)


def shards(
    solution,
    right_side,
    span_index,
    coef_table,
    xaxis_bands,
    yaxis_bands,
    zaxis_bands,
    xaxis_vectors,
    yaxis_vectors,
    zaxis_vectors,
    xaxis_values,
    yaxis_values,
    zaxis_values,
):
    npy, npz = lax.axis_size("py"), lax.axis_size("pz")
    ly, lz, nx = solution.shape
    ny, nz = npy * ly, npz * lz
    count, devices = ly * lz, npy * npz
    modes = nx // devices
    field = solution.reshape(count, nx)
    right = right_side.reshape(count, nx)
    block, zrim, yrim = (count, nx), (ly * REACH, nx), (up8(REACH * lz + 2 * REACH * REACH), nx)
    zrims = (2 * ly * REACH, nx)
    cell = count * nx * 4
    dma = pltpu.SemaphoreType.DMA

    points = point_columns(ly, lz)
    width = points.shape[1] // 2
    small = [jnp.asarray(points), *(array.transpose(1, 0, 2) for array in (yaxis_bands, zaxis_bands, xaxis_bands))]
    fast = (
        modes % 16 == 0 and npz % 2 == 0 and 2 * ly * REACH <= LANES // 2 and npy % 8 == 0 and lz % 16 == 0 and ly % 4 == 0
        and 2 * nz == LANES and 2 * ny == LANES and count == LANES and nx % LANES == 0
    )
    later = [xaxis_vectors, yaxis_vectors, zaxis_vectors, yaxis_values.reshape(1, ny), zaxis_values.reshape(1, nz)] * fast

    coef, weighted, even, odd, yodd, yeven, *small = call(
        lambda *refs: coefficient_kernel(ly, lz, len(small), *refs),
        [(block, F32)] * 2 + [(zrims, F32)] * 2 + [((REACH * lz + 16, nx), F32)] * 2
        + [(array.shape, array.dtype) for array in small],
        [HBM] * (3 + len(small)), count * nx * 16, 4 * cell,
        [pltpu.SMEM(coef_table.shape, F32), pltpu.VMEM(block, jnp.int32), pltpu.VMEM(block, F32)]
        + [dma((3 + len(small),))],
    )(*in_hbm(coef_table, span_index.reshape(count, nx), field, *small))

    *bands, xbands = small
    stencil, *held = call(
        lambda *refs: stencil_kernel(ly, lz, ny, nz, len(later), *refs),
        [((4 * count, width), BF16)] + [(array.shape, F32) for array in later],
        [VMEM] * 3 + [HBM] * len(later) + [ANY], count * width * 60, 8 * count * width,
        [dma((len(later),))] * fast,
    )(*bands, *in_hbm(*later), even)

    even, odd = pairwise(even, "pz", 0), odd_pairs(odd)
    zlow, zhigh, *corner = call(
        lambda *refs: y_rims_kernel(ly, *refs),
        [(zrims, F32)] * 2 + [((up8(2 * REACH * REACH), nx), F32)] * 2,
        [VMEM] * 2 + [ANY], nx, 4 * nx * 4 * zrims[0],
    )(odd, even, stencil)
    yodd, yeven = [yodd, corner[0]], [yeven, corner[1]]

    if fast:
        zmat, ymat, rmat = (npz * count // 2, ly * nz // 2), (ny, 3 * ny), (npz * LANES // 2, ly * nz)
        vectors, taps, *tables = call(
            lambda *refs: tables_kernel(npy, npz, ly, lz, *refs),
            [((2 * nx, nx), BF16), ((2 * (2 * REACH + 1), 8, nx), F32), ((ny, modes * nz), F32)]
            + [(zmat, BF16), (zmat, BF16), (ymat, BF16), (ymat, BF16), (rmat, BF16), (rmat, BF16)],
            [VMEM] * 6 + [HBM, ANY], npz * count * ly * nz * 8, npz * count * ly * nz * 4,
            [pltpu.SMEM((nx,), F32), dma((1,))],
        )(*held, xbands, *in_hbm(xaxis_values), corner[0])

        def precondition(received, rims, residual):
            turn = pltpu.VMEM(((ly * nz // LANES * npy + 1) * (modes + 8), LANES), F32)
            if not rims:
                return call(
                    lambda *refs: last_modes_kernel(npy, npz, *refs),
                    [((nx, count), F32), (block, F32)], [VMEM] * 7, 6 * 2 * count * nx * ly * nz, 4 * cell,
                    [turn, dma((1,))], [VMEM, HBM],
                )(*tables[:5], *residual, received)
            size = modes * 3 // 2 if rims else modes
            return call(
                lambda *refs: modes_kernel(npy, npz, rims, *refs),
                [((devices * size, count), F32)], [VMEM] * (8 if rims else 6), 6 * 2 * count * nx * ly * nz, 2 * cell,
                [turn],
            )(*(tables if rims else tables[:5]), received)[0], None
    else:
        vectors, taps = call(
            xvectors_kernel, [((2 * nx, nx), BF16), ((2 * (2 * REACH + 1), 8, nx), F32)], [HBM, VMEM],
            nx * nx * 40, 8 * nx * nx, [pltpu.VMEM((nx, nx), F32), dma((1,))],
        )(*in_hbm(xaxis_vectors), xbands)
        tables = [taps]
        part = lax.axis_index(BOTH)
        xpart = lax.dynamic_slice_in_dim(xaxis_values, part * modes, modes)

        def precondition(received, rims, residual):
            return plain_modes(
                received, npy, npz, ly, lz, xpart, yaxis_values, zaxis_values, yaxis_vectors, zaxis_vectors
            ), *(residual or [None])

    for iteration in range(ITERS):
        last = iteration + 1 == ITERS
        yodd, yeven = [paired(value, "py") for value in yodd], [pairwise(value, "py", 0) for value in yeven]
        parts = len(yodd)
        if fast and iteration == 0:
            outward = call(
                lambda *refs: outward_kernel(ly, lz, nz, *refs),
                [((8 * REACH * lz, LANES), BF16)], [VMEM] * 3 + [ANY], 1 << 20, 1 << 18,
            )(bands[2], yodd[0], yeven[0], tables[0])[0]
        outs = [((nx, count), F32)] + [(block, F32)] * last
        scratch = [pltpu.VMEM(block, F32)] * (not last)
        cost = (6 * count * nx * (nx + 2 * width), 5 * cell + 4 * nx * nx)
        if fast and iteration > 0:
            applied = call(
                lambda *refs: own_part_kernel(lz, zrim[0], *refs), [(block, F32)], [VMEM] * 5, *cost,
            )(weighted, zlow, zhigh, stencil, taps)[0]
            spectral, *residual = call(joined_residual_kernel, outs, [VMEM] * 6, *cost, scratch)(
                applied, *yodd, *yeven, coef, right, vectors
            )
        else:
            spectral, *residual = call(
                lambda *refs: residual_kernel(lz, zrim[0], parts, *refs),
                outs, [VMEM] * (8 + 2 * parts) + [ANY], *cost, scratch,
            )(weighted, zlow, zhigh, *yodd, *yeven, stencil, taps, coef, right, vectors, outward if fast else tables[0])
        spectral = lax.all_to_all(spectral, BOTH, split_axis=0, concat_axis=0, tiled=True)
        spectral, residual = precondition(spectral, not last, residual)
        spectral = lax.all_to_all(spectral, BOTH, split_axis=0, concat_axis=0, tiled=True)
        cost = (6 * count * nx * nx, 4 * cell + 4 * nx * nx)
        if last:
            field = call(
                last_update_kernel, [(block, F32)], [VMEM] * 3, *cost, [pltpu.VMEM(block, F32), dma((1,))], [HBM],
            )(spectral, vectors, field)[0]
        elif fast:
            field, weighted, zlow, zhigh, *yrims = call(
                lambda *refs: rim_update_kernel(ly, lz, devices, *refs),
                [(block, F32)] * 2 + [(zrim, F32)] * 2 + [((REACH * lz, nx), F32)] * 2, [VMEM] * 8, *cost,
                [pltpu.VMEM((LANES, nx), F32)] * 2,
            )(spectral, vectors, field, coef, zlow, zhigh, outward, taps)
        else:
            field, weighted, zlow, zhigh = call(
                lambda *refs: update_kernel(ly, lz, *refs), [(block, F32)] * 2 + [(zrim, F32)] * 2, [VMEM] * 4, *cost,
            )(spectral, vectors, field, coef)
            zlow, zhigh = around(zhigh, "pz", 1), around(zlow, "pz", -1)
            yrims = call(
                lambda *refs: next_y_rims_kernel(ly, lz, *refs),
                [(yrim, F32)] * 2, [VMEM] * 3, nx, 4 * nx * 4 * yrim[0],
            )(weighted, zlow, zhigh)
        yodd, yeven = ([value] for value in yrims) if not last else (None, None)
    return (field.reshape(solution.shape), residual.reshape(solution.shape))


def solution(mesh):
    return jax.shard_map(
        shards,
        mesh=mesh,
        in_specs=(
            P("py", "pz", None),
            P("py", "pz", None),
            P("py", "pz", None),
            P(),
            P(),
            P(None, None, "py"),
            P(None, None, "pz"),
            P(),
            P(),
            P(),
            P(),
            P(),
            P(),
        ),
        out_specs=(P("py", "pz", None), P("py", "pz", None)),
        check_vma=False,
    )
```

```python
import jax
import jax.numpy as jnp
import numpy as np
from jax import lax
from jax.experimental import pallas as pl
from jax.experimental.pallas import tpu as pltpu
from jax.sharding import PartitionSpec as P

ITERS = 2
REACH = 3
LANES = 128
HIGH = lax.Precision.HIGHEST
BOTH = ("py", "pz")
F32 = jnp.float32
BF16 = jnp.bfloat16
VMEM = pl.BlockSpec(memory_space=pltpu.VMEM)
HBM = pl.BlockSpec(memory_space=pltpu.HBM)
ANY = pl.BlockSpec(memory_space=pl.ANY)


def up8(count):
    return -(-count // 8) * 8


def split(value):
    high = value.astype(BF16)
    return high, (value - high.astype(F32)).astype(BF16)


def exact(left, right, sides=(1, 0)):
    return lax.dot_general(
        left, right, (((sides[0],), (sides[1],)), ((), ())), precision=HIGH, preferred_element_type=F32
    )


def fetch(pairs, sem):
    copies = [pltpu.make_async_copy(source, target, sem.at[i]) for i, (source, target) in enumerate(pairs)]
    for copy in copies:
        copy.start()
    for copy in copies:
        copy.wait()


def in_hbm(*arrays):
    return [pltpu.with_memory_space_constraint(array, pltpu.HBM) for array in arrays]


def mul(left, right):
    return lax.dot_general(left, right, (((1,), (0,)), ((), ())), preferred_element_type=F32)


def mul_t(left, right):
    return lax.dot_general(left, right, (((1,), (1,)), ((), ())), preferred_element_type=F32)


def call(kernel, outs, specs, flops, cost_bytes, scratch=(), out_specs=None):
    return pl.pallas_call(
        kernel,
        out_shape=[jax.ShapeDtypeStruct(shape, dtype) for shape, dtype in outs],
        in_specs=specs,
        out_specs=out_specs or [VMEM] * len(outs),
        scratch_shapes=list(scratch),
        compiler_params=pltpu.CompilerParams(vmem_limit_bytes=32 * 1024 * 1024),
        cost_estimate=pl.CostEstimate(flops=flops, bytes_accessed=cost_bytes, transcendentals=0),
    )


def store_z_rims(ly, lz, weighted, low_ref, high_ref):
    for y in range(ly):
        low_ref[y * REACH : (y + 1) * REACH, :] = weighted[y * lz : y * lz + REACH, :]
        high_ref[y * REACH : (y + 1) * REACH, :] = weighted[(y + 1) * lz - REACH : (y + 1) * lz, :]


def coefficient_kernel(ly, lz, small, *refs):
    table_ref, span_ref, field_ref, *refs = refs
    sources, refs = refs[:small], refs[small:]
    coef_ref, weighted_ref, even_ref, odd_ref, yodd_ref, yeven_ref, *refs = refs
    targets, (table, span, field, sem) = refs[:small], refs[small:]
    fetch([(table_ref, table), (span_ref, span), (field_ref, field), *zip(sources, targets)], sem)
    first = lax.rem(lax.axis_index("pz"), 2) == 0
    half = ly * REACH
    entries = [table[entry] for entry in range(table_ref.shape[0])]
    for start in range(0, span.shape[0], lz):
        rows = pl.ds(start, lz)
        index = span[rows, :]
        coef = jnp.full(index.shape, entries[0], F32)
        for entry in range(1, len(entries)):
            coef = jnp.where(index == entry, entries[entry], coef)
        coef_ref[rows, :] = coef
        weighted = coef * field[rows, :]
        weighted_ref[rows, :] = weighted
        for value, at in ((weighted, 0), (coef, half)):
            rim = pl.ds(at + start // lz * REACH, REACH)
            low, high = value[:REACH], value[lz - REACH :]
            even_ref[rim, :] = jnp.where(first, high, low)
            odd_ref[rim, :] = jnp.where(first, low, high)
    store_y_rims(own_rim(ly, lz, weighted_ref), yodd_ref, yeven_ref)
    ybands = targets[1]
    for ref in (yodd_ref, yeven_ref):
        for matrix in range(2):
            at = REACH * lz + 8 * matrix
            ref[at : at + ybands.shape[0], :ly] = ybands[:, matrix, :]


def store_y_rims(pieces, odd_ref, even_ref):
    first = lax.rem(lax.axis_index("py"), 2) == 0
    at = 0
    for value, count, rows in pieces:
        low, high = value[:count, :], value[rows - count : rows, :]
        even_ref[at : at + count, :] = jnp.where(first, high, low)
        odd_ref[at : at + count, :] = jnp.where(first, low, high)
        at += count
    if at < even_ref.shape[0]:
        for ref in (even_ref, odd_ref):
            ref[at:, :] = jnp.zeros((ref.shape[0] - at, ref.shape[1]), F32)


def own_rim(ly, lz, weighted):
    return [(weighted, REACH * lz, ly * lz)]


def corners(ly, zlow, zhigh):
    return [(value, REACH * REACH, ly * REACH) for value in (zlow, zhigh)]


def y_rims_kernel(ly, odd_ref, even_ref, _, zlow_ref, zhigh_ref, yodd_ref, yeven_ref):
    first = lax.rem(lax.axis_index("pz"), 2) == 0
    zlow_ref[...] = jnp.where(first, odd_ref[...], even_ref[...])
    zhigh_ref[...] = jnp.where(first, even_ref[...], odd_ref[...])
    store_y_rims(corners(ly, zlow_ref, zhigh_ref), yodd_ref, yeven_ref)


def next_y_rims_kernel(ly, lz, weighted_ref, zlow_ref, zhigh_ref, yodd_ref, yeven_ref):
    store_y_rims(own_rim(ly, lz, weighted_ref) + corners(ly, zlow_ref, zhigh_ref), yodd_ref, yeven_ref)


def point_columns(ly, lz):
    below, above = range(-REACH, 0), range(REACH)
    halves = []
    for half in range(2):
        first = 0 if half == 0 else ly // 2 - REACH
        points = [(first + y, z) for y in range(ly // 2 + REACH) for z in range(lz)]
        points += [(y, z) for y in range(ly) for z in below]
        points += [(y, lz + z) for y in range(ly) for z in above]
        ys = below if half == 0 else [ly + y for y in above]
        points += [(y, z) for y in ys for z in range(lz)]
        points += [(y, z) for y in ys for z in below]
        points += [(y, lz + z) for y in ys for z in above]
        halves += points + [(1 << 20, 1 << 20)] * (-len(points) % LANES)
    return np.array(halves, np.int32).T.copy()


def stencil_kernel(ly, lz, ny, nz, later, points_ref, ybands_ref, zbands_ref, *refs):
    sources, (_, out_ref, *refs) = refs[:later], refs[later:]
    copies = [pltpu.make_async_copy(*pair, refs[-1].at[i]) for i, pair in enumerate(zip(sources, refs[:later]))]
    for copy in copies:
        copy.start()
    count = ly * lz // 2
    width = out_ref.shape[1]
    for half in range(2):
        rows = lax.broadcasted_iota(jnp.int32, (count, 1), 0) + half * count
        columns = pl.ds(half * width, width)
        factors = []
        for bands_ref, length, row, column, first, whole in (
            (ybands_ref, ly, lax.div(rows, lz), points_ref[0:1, columns], lax.axis_index("py") * ly, ny),
            (zbands_ref, lz, lax.rem(rows, lz), points_ref[1:2, columns], lax.axis_index("pz") * lz, nz),
        ):
            pick = (lax.broadcasted_iota(jnp.int32, (count, length), 1) == row).astype(F32)
            spot = column + first
            inside = (spot >= 0) & (spot < whole)
            distance = jnp.where(inside, column, 1 << 20) - row
            here = [distance == offset - REACH for offset in range(2 * REACH + 1)]
            for matrix in range(2):
                taps = exact(pick, bands_ref[:, matrix, :], (1, 1))
                dense = jnp.zeros(distance.shape, F32)
                for offset in range(2 * REACH + 1):
                    dense = jnp.where(here[offset], taps[:, offset : offset + 1], dense)
                factors.append(dense)
        ystiff, ymass, zstiff, zmass = factors
        for part, value in enumerate((ymass * zmass, ystiff * zmass + ymass * zstiff)):
            at = (4 * half + part) * count
            out_ref[at : at + count, :], out_ref[at + 2 * count : at + 3 * count, :] = split(value)
    for copy in copies:
        copy.wait()


def store_taps(xbands_ref, taps_ref):
    nx = xbands_ref.shape[2]
    lane = lax.broadcasted_iota(jnp.int32, (1, nx), 1)
    for offset in range(2 * REACH + 1):
        move = offset - REACH
        inside = (lane - move >= 0) & (lane - move < nx)
        for matrix in range(2):
            band = xbands_ref[offset, matrix : matrix + 1, :]
            band = pltpu.roll(band, move % nx, 1) if move else band
            taps_ref[2 * offset + matrix] = jnp.broadcast_to(jnp.where(inside, band, 0.0), (8, nx))


def doubled(size):
    row = lax.broadcasted_iota(jnp.int32, (size, 2 * size), 0)
    return (row == lax.rem(lax.broadcasted_iota(jnp.int32, (size, 2 * size), 1), size)).astype(F32)


def xvectors_kernel(source, xbands_ref, out_ref, taps_ref, held, sem):
    store_taps(xbands_ref, taps_ref)
    fetch(((source, held),), sem)
    high, low = split(held[...].T)
    out_ref[: high.shape[0], :] = high
    out_ref[high.shape[0] :, :] = low


def tables_kernel(
    npy, npz, ly, lz, xvec_ref, yvec_ref, zvec_ref, yval_ref, zval_ref, xbands_ref, xval_hbm, _,
    xout_ref, taps_ref, sums_ref, zhigh_ref, zlow_ref, ydown_ref, yup_ref, rimhigh_ref, rimlow_ref, xval_ref, sem,
):
    fetching = pltpu.make_async_copy(xval_hbm, xval_ref, sem.at[0])
    fetching.start()
    store_taps(xbands_ref, taps_ref)
    ny, nz = npy * ly, npz * lz
    nx = xvec_ref.shape[0]
    high, low = split(xvec_ref[...].T)
    xout_ref[:nx, :] = high
    xout_ref[nx:, :] = low
    pair = exact(zvec_ref[...], doubled(nz))
    half = lax.broadcasted_iota(jnp.int32, pair.shape, 1) >= nz
    zhigh_ref[...] = jnp.zeros(zhigh_ref.shape, BF16)
    zlow_ref[...] = jnp.zeros(zlow_ref.shape, BF16)
    for parity in range(2):
        high, low = split(jnp.where(half == (parity == 1), pair, 0.0))
        for yl in range(parity, ly // 2, 2):
            for block in range(npz):
                to = (pl.ds((block * ly // 2 + yl) * lz, lz), pl.ds(yl // 2 * 2 * nz, 2 * nz))
                zhigh_ref[to] = high[block * lz : (block + 1) * lz, :]
                zlow_ref[to] = low[block * lz : (block + 1) * lz, :]
    shape = (rimhigh_ref.shape[0], 1)
    row = lax.broadcasted_iota(jnp.int32, shape, 0)
    block, spot = lax.div(row, LANES // 2), lax.rem(row, LANES // 2)
    above = spot >= ly * REACH
    spot = jnp.where(above, spot - ly * REACH, spot)
    yrow = jnp.where(spot < ly * REACH, lax.div(spot, REACH), 2 * ly)
    z = block * lz + lax.rem(spot, REACH) + jnp.where(above, lz, -REACH)
    rim = exact((lax.broadcasted_iota(jnp.int32, (shape[0], nz), 1) == z).astype(F32), pair)
    late = (lax.broadcasted_iota(jnp.int32, rim.shape, 1) >= nz).astype(jnp.int32)
    for chunk in range(ly // 2):
        columns = pl.ds(chunk * 2 * nz, 2 * nz)
        rimhigh_ref[:, columns], rimlow_ref[:, columns] = split(jnp.where(yrow - 2 * chunk == late, rim, 0.0))

    def y_of(p):
        spot = lax.div(p, npy)
        return lax.rem(p, npy) * ly + 2 * lax.rem(spot, ly // 2) + lax.div(spot, ly // 2)

    def parts(array):
        high, low = split(array)
        late = lax.broadcasted_iota(jnp.int32, array.shape, 1) >= 2 * ny
        return jnp.where(late, low.astype(F32), high.astype(F32)).astype(BF16)

    lane = lax.broadcasted_iota(jnp.int32, (ny, 3 * ny), 1)
    row = lax.broadcasted_iota(jnp.int32, (ny, 3 * ny), 0)
    moved = (row == y_of(lax.rem(lane, ny))).astype(F32)
    ydown_ref[...] = parts(exact(yvec_ref[...].T, moved))
    order = (
        lax.broadcasted_iota(jnp.int32, (ny, ny), 1) == y_of(lax.broadcasted_iota(jnp.int32, (ny, ny), 0))
    ).astype(F32)
    copies = (row == lax.rem(lane, ny)).astype(F32)
    yup_ref[...] = parts(exact(exact(order, yvec_ref[...]), copies))
    fetching.wait()
    square = (ny, ny)
    diagonal = lax.broadcasted_iota(jnp.int32, square, 0) == lax.broadcasted_iota(jnp.int32, square, 1)
    ycolumn = jnp.sum(jnp.where(diagonal, yval_ref[...], 0.0), axis=1, keepdims=True)
    yz = ycolumn + exact(jnp.broadcast_to(zval_ref[...], (8, nz)), doubled(nz))[0:1]
    late = lax.broadcasted_iota(jnp.int32, (1, 2 * nz), 1) >= nz
    modes = sums_ref.shape[1] // nz
    first = (lax.axis_index("py") * (nz // lz) + lax.axis_index("pz")) * modes
    for mode in range(0, modes, 2):
        x = jnp.where(late, xval_ref[first + mode + 1], xval_ref[first + mode])
        sums_ref[:, mode * nz : (mode + 2) * nz] = yz + x


def y_sides(odd, even):
    first = lax.rem(lax.axis_index("py"), 2) == 0
    return jnp.where(first, odd, even), jnp.where(first, even, odd)


def three_products(matrix, high, low):
    rows = matrix.shape[0] // 2
    both = mul(matrix, high)
    return both[:rows] + both[rows:] + mul(matrix[:rows], low)


def yz_fields(lz, zrim, weighted_ref, zlow_ref, zhigh_ref, sides, stencil_ref):
    count, nx = weighted_ref.shape
    part, need = count // 2, count // 2 + REACH * lz
    own = split(weighted_ref[...])
    zrims = split(jnp.concatenate([zlow_ref[:zrim, :], zhigh_ref[:zrim, :]], axis=0))
    left = stencil_ref.shape[1] - need - 2 * zrim
    fields = []
    for half in range(2):
        if sides is None:
            yrim = [jnp.zeros((left, nx), BF16)] * 2
        else:
            rim = sides[half]
            missing = left - rim.shape[0]
            yrim = split(jnp.concatenate([rim, jnp.zeros((missing, nx), F32)], axis=0) if missing else rim)
        first = half * (count - need)
        high, low = (
            jnp.concatenate([own[k][first : first + need], zrims[k], yrim[k]], axis=0) for k in range(2)
        )
        both = three_products(stencil_ref[4 * half * part : 4 * (half + 1) * part, :], high, low)
        fields.append((both[:part], both[part:]))
    return fields


def x_banded(taps_ref, mass, stiff):
    nx = mass.shape[1]
    applied = None
    for offset in range(2 * REACH + 1):
        move = offset - REACH
        term = taps_ref[2 * offset] * mass + taps_ref[2 * offset + 1] * stiff
        term = pltpu.roll(term, -move % nx, 1) if move else term
        applied = term if applied is None else applied + term
    return applied


def store_modes(points, vectors_ref, spectral_ref):
    count, nx = points.shape
    high, low = split(points)
    product = mul_t(jnp.concatenate([high, low], axis=0), vectors_ref[:nx, :])
    spectral_ref[...] = (product[:count] + product[count:] + mul_t(high, vectors_ref[nx:, :])).T


def residual_kernel(lz, zrim, parts, *refs):
    weighted_ref, zlow_ref, zhigh_ref, *refs = refs
    yodd_refs, yeven_refs, refs = refs[:parts], refs[parts : 2 * parts], refs[2 * parts :]
    stencil_ref, taps_ref, coef_ref, right_ref, vectors_ref, _, spectral_ref, residual_ref = refs
    if parts == 2:
        (yodd_ref, odd_corner_ref), (yeven_ref, even_corner_ref) = yodd_refs, yeven_refs
        own = REACH * lz
        yodd = jnp.concatenate([yodd_ref[:own, :], odd_corner_ref[...]], axis=0)
        yeven = jnp.concatenate([yeven_ref[:own, :], even_corner_ref[...]], axis=0)
    else:
        yodd, yeven = yodd_refs[0][...], yeven_refs[0][...]
    fields = yz_fields(lz, zrim, weighted_ref, zlow_ref, zhigh_ref, y_sides(yodd, yeven), stencil_ref)
    part = weighted_ref.shape[0] // 2
    for start in range(0, 2 * part, 8):
        mass, stiff = (field[start % part : start % part + 8] for field in fields[start // part])
        rows = pl.ds(start, 8)
        residual_ref[rows, :] = right_ref[rows, :] - coef_ref[rows, :] * x_banded(taps_ref, mass, stiff)
    store_modes(residual_ref[...], vectors_ref, spectral_ref)


def own_part_kernel(lz, zrim, weighted_ref, zlow_ref, zhigh_ref, stencil_ref, taps_ref, applied_ref):
    fields = yz_fields(lz, zrim, weighted_ref, zlow_ref, zhigh_ref, None, stencil_ref)
    part = weighted_ref.shape[0] // 2
    for start in range(0, 2 * part, 8):
        mass, stiff = (field[start % part : start % part + 8] for field in fields[start // part])
        applied_ref[pl.ds(start, 8), :] = x_banded(taps_ref, mass, stiff)


def joined_residual_kernel(applied_ref, yodd_ref, yeven_ref, coef_ref, right_ref, vectors_ref, spectral_ref, residual_ref):
    count, rim = applied_ref.shape[0], yodd_ref.shape[0]
    for at, side in zip((0, count - rim), y_sides(yodd_ref[...], yeven_ref[...])):
        rows = pl.ds(at, rim)
        residual_ref[rows, :] = right_ref[rows, :] - coef_ref[rows, :] * (applied_ref[rows, :] + side)
    rows = pl.ds(rim, count - 2 * rim)
    residual_ref[rows, :] = right_ref[rows, :] - coef_ref[rows, :] * applied_ref[rows, :]
    store_modes(residual_ref[...], vectors_ref, spectral_ref)


def outward_kernel(ly, lz, nz, zbands_ref, yodd_ref, yeven_ref, _, out_ref):
    rim, side = REACH * lz, REACH * REACH
    width = out_ref.shape[1]
    row = lax.broadcasted_iota(jnp.int32, (rim, 1), 0)
    column = lax.broadcasted_iota(jnp.int32, (1, width), 1)
    spot = jnp.where(column < rim + side, column - rim, column - rim - side)
    yin = jnp.where(column < rim, lax.div(column, lz), lax.div(spot, REACH))
    zin = jnp.where(
        column < rim, lax.rem(column, lz), lax.rem(spot, REACH) + jnp.where(column < rim + side, -REACH, lz)
    )
    place = zin + lax.axis_index("pz") * lz
    inside = (column < rim + 2 * side) & (place >= 0) & (place < nz)
    yout, zout = lax.div(row, lz), lax.rem(row, lz)

    def dense(taps, tap):
        value = jnp.zeros(tap.shape, F32)
        for k in range(2 * REACH + 1):
            value = jnp.where(tap == k, taps[:, k : k + 1], value)
        return value

    def picked(length, at, bands):
        return exact((lax.broadcasted_iota(jnp.int32, (rim, length), 1) == at).astype(F32), bands, (1, 1))

    ztap = jnp.where(inside, zin - zout + REACH, -1)
    zstiff, zmass = (dense(picked(lz, zout, zbands_ref[:, matrix, :]), ztap) for matrix in range(2))
    sides = y_sides(yodd_ref[rim : rim + 16, :ly], yeven_ref[rim : rim + 16, :ly])
    spot, count = lax.axis_index("py"), lax.axis_size("py")
    for k, (bands, at, shift, there) in enumerate(
        ((sides[0], yout + ly - REACH, 2 * REACH, spot > 0), (sides[1], yout, 0, spot < count - 1))
    ):
        ytap = jnp.where(there, yin - yout + shift, -1)
        ystiff, ymass = (dense(picked(ly, at, bands[8 * matrix : 8 * matrix + 8]), ytap) for matrix in range(2))
        for part, value in enumerate((ymass * zmass, ystiff * zmass + ymass * zstiff)):
            start = (4 * k + part) * rim
            out_ref[start : start + rim, :], out_ref[start + 2 * rim : start + 3 * rim, :] = split(value)


def modes_kernel(npy, npz, rims, *refs):
    sums_ref, zhigh_ref, zlow_ref, ydown_ref, yup_ref, *rim_refs, in_ref, out_ref, turn_ref = refs
    count = in_ref.shape[0] // (npy * npz)
    size = out_ref.shape[0] // (npy * npz)
    nz = sums_ref.shape[1] // count
    width = zhigh_ref.shape[1]
    chunks = 2 * width // LANES
    step = turn_ref.shape[0] // (npy * chunks)
    zhigh, zlow = zhigh_ref[...], zlow_ref[...]

    def three(high, low, product, whigh, wlow):
        rows = high.shape[0]
        both = product(jnp.concatenate([high, low], axis=0), whigh)
        return both[:rows] + both[rows:] + product(high, wlow)

    def early(first, second):
        late = lax.broadcasted_iota(jnp.int32, first.shape, 1) >= LANES // 2
        return jnp.where(late, pltpu.roll(second, LANES // 2, 1), first)

    def later(first, second):
        late = lax.broadcasted_iota(jnp.int32, first.shape, 1) >= LANES // 2
        return jnp.where(late, second, pltpu.roll(first, LANES // 2, 1))

    def by_mode(mode, chunk):
        return pl.ds(chunk * npy * step + mode, npy, stride=step)

    def by_device(device, chunk):
        return pl.ds((chunk * npy + device) * step, count)

    halves = [[], []]
    for p in range(npy):
        blocks = [in_ref[(p * npz + b) * count : (p * npz + b + 1) * count, :] for b in range(npz)]
        for half, joined in zip(halves, (early, later)):
            half.append(jnp.concatenate([joined(blocks[b], blocks[b + 1]) for b in range(0, npz, 2)], axis=1))
    part = three(*split(jnp.concatenate(halves[0] + halves[1], axis=0)), mul, zhigh, zlow)
    for chunk in range(chunks):
        half, lane = divmod(chunk * LANES, width)
        for p in range(npy):
            row = (half * npy + p) * count
            turn_ref[by_device(p, chunk), :] = part[row : row + count, lane : lane + LANES]
    pairs = []
    for mode in range(0, count, 2):
        tiles = [(turn_ref[by_mode(mode, c), :], turn_ref[by_mode(mode + 1, c), :]) for c in range(chunks)]
        pairs.append(jnp.concatenate([early(*tile) for tile in tiles] + [later(*tile) for tile in tiles], axis=0))
    stacked = jnp.concatenate(pairs, axis=1)

    def stack(value):
        high, low = split(value)
        return jnp.concatenate([high, low, high], axis=0)

    modes = mul(ydown_ref[...], stack(stacked)) / sums_ref[...]
    restored = mul(yup_ref[...], stack(modes))
    for mode in range(0, count, 2):
        block = restored[:, mode * nz : (mode + 2) * nz]
        for c in range(chunks):
            even = block[c * npy : (c + 1) * npy]
            odd = block[(chunks + c) * npy : (chunks + c + 1) * npy]
            turn_ref[by_mode(mode, c), :] = early(even, odd)
            turn_ref[by_mode(mode + 1, c), :] = later(even, odd)
    rows = [
        jnp.concatenate(
            [turn_ref[by_device(p, half * chunks // 2 + c), :] for c in range(chunks // 2)], axis=1
        )
        for half in range(2)
        for p in range(npy)
    ]
    spectral = split(jnp.concatenate(rows, axis=0))
    back = three(*spectral, mul_t, zhigh, zlow)
    total = npy * count
    if rims:
        side = [
            three(
                *(piece[half * total : (half + 1) * total] for piece in spectral), mul_t,
                *(ref[:, pl.ds(half * width, width)] for ref in rim_refs),
            )
            for half in range(2)
        ]
        side = side[0] + side[1]
    for p in range(npy):
        for b in range(0, npz, 2):
            first, second = (
                back[k * total + p * count : k * total + (p + 1) * count, b * LANES // 2 : b * LANES // 2 + LANES]
                for k in range(2)
            )
            at = (p * npz + b) * size
            out_ref[at : at + count, :] = early(first, second)
            out_ref[at + size : at + size + count, :] = later(first, second)
            if rims:
                row, middle = p * count, p * count + count // 2
                first = side[row:middle, b * LANES // 2 : b * LANES // 2 + LANES]
                second = side[middle : row + count, b * LANES // 2 : b * LANES // 2 + LANES]
                out_ref[at + count : at + size, :] = early(first, second)
                out_ref[at + size + count : at + 2 * size, :] = later(first, second)


def transformed(points, vectors_ref):
    rows, nx = points.shape
    high, low = split(points)
    both = mul(jnp.concatenate([high, low], axis=0), vectors_ref[:nx, :])
    return both[:rows] + both[rows:] + mul(high, vectors_ref[nx:, :])


def from_modes(spectral_ref, vectors_ref):
    return transformed(spectral_ref[...].T, vectors_ref)


def update_kernel(ly, lz, spectral_ref, vectors_ref, field_ref, coef_ref, updated_ref, weighted_ref, low_ref, high_ref):
    updated = field_ref[...] + from_modes(spectral_ref, vectors_ref)
    updated_ref[...] = updated
    weighted = coef_ref[...] * updated
    weighted_ref[...] = weighted
    store_z_rims(ly, lz, weighted, low_ref, high_ref)


def rim_update_kernel(
    ly, lz, devices, spectral_ref, vectors_ref, field_ref, coef_ref, before_low_ref, before_high_ref,
    outward_ref, taps_ref, updated_ref, weighted_ref, zlow_ref, zhigh_ref, yodd_ref, yeven_ref, below_ref, above_ref,
):
    nx = vectors_ref.shape[1]
    modes = nx // devices
    size = spectral_ref.shape[0] // devices
    own, rims = [], []
    for d in range(devices):
        own.append(spectral_ref[d * size : d * size + modes, :])
        rim = spectral_ref[d * size + modes : (d + 1) * size, :]
        rims += [rim, pltpu.roll(rim, LANES // 2, 1)]
    points = [jnp.concatenate(own, axis=0).T, jnp.concatenate(rims, axis=0).T[: LANES // 2]]
    update = transformed(jnp.concatenate(points, axis=0), vectors_ref)
    count, half = ly * lz, ly * REACH
    updated = field_ref[...] + update[:count]
    updated_ref[...] = updated
    weighted_ref[...] = coef_ref[...] * updated
    for side, (ref, before_ref) in enumerate(((zlow_ref, before_low_ref), (zhigh_ref, before_high_ref))):
        start = count + side * half
        ref[...] = before_ref[:half, :] + before_ref[half:, :] * update[start : start + half]
    at = 0
    for value, rows, whole in own_rim(ly, lz, weighted_ref) + corners(ly, zlow_ref, zhigh_ref):
        below_ref[at : at + rows, :] = value[:rows, :]
        above_ref[at : at + rows, :] = value[whole - rows : whole, :]
        at += rows
    rim, adds = yodd_ref.shape[0], []
    for k, ref in enumerate((below_ref, above_ref)):
        ref[at:, :] = jnp.zeros((ref.shape[0] - at, nx), F32)
        both = three_products(outward_ref[4 * k * rim : 4 * (k + 1) * rim, :], *split(ref[...]))
        adds.append((both[:rim], both[rim:]))
    first = lax.rem(lax.axis_index("py"), 2) == 0
    for start in range(0, rim, 8):
        below, above = (x_banded(taps_ref, *(field[start : start + 8] for field in fields)) for fields in adds)
        yodd_ref[start : start + 8, :] = jnp.where(first, below, above)
        yeven_ref[start : start + 8, :] = jnp.where(first, above, below)


def last_update_kernel(spectral_ref, vectors_ref, field_ref, residual_ref, updated_hbm, residual_hbm, held, sem):
    leaving = pltpu.make_async_copy(residual_ref, residual_hbm, sem.at[0])
    leaving.start()
    held[...] = field_ref[...] + from_modes(spectral_ref, vectors_ref)
    fetch(((held, updated_hbm),), sem.at[pl.ds(1, 1)])
    leaving.wait()


def pairwise(value, axis, odd):
    count = lax.axis_size(axis)
    other = [((i + odd) ^ 1) - odd for i in range(count)]
    return lax.ppermute(value, axis, [(i, j if 0 <= j < count else i) for i, j in enumerate(other)])


def paired(value, axis):
    count = lax.axis_size(axis)
    return lax.ppermute(value, axis, [(i, (i + 1 if i % 2 else i - 1) % count) for i in range(count)])


def odd_pairs(value):
    across, count = lax.axis_size("py"), lax.axis_size("pz")
    pairs = []
    for i in range(across):
        for k in range(count):
            j = k + 1 if k % 2 else k - 1
            pairs.append((i * count + k, i * count + j if 0 <= j < count else (i ^ 1) * count + k))
    return lax.ppermute(value, BOTH, pairs)


def around(value, axis, step):
    count = lax.axis_size(axis)
    return lax.ppermute(value, axis, [(i, (i + step) % count) for i in range(count)])


def plain_modes(received, npy, npz, ly, lz, xvalues, yvalues, zvalues, yvectors, zvectors):
    count = received.shape[0] // (npy * npz)
    field = received.reshape(npy, npz, count, ly, lz).transpose(2, 0, 3, 1, 4).reshape(count, npy * ly, npz * lz)
    field = jnp.einsum("xyz,yj->xjz", field, yvectors, precision=HIGH)
    field = jnp.einsum("xyz,zk->xyk", field, zvectors, precision=HIGH)
    field = field / (yvalues[None, :, None] + zvalues[None, None, :] + xvalues[:, None, None])
    field = jnp.einsum("xjz,yj->xyz", field, yvectors, precision=HIGH)
    field = jnp.einsum("xyk,zk->xyz", field, zvectors, precision=HIGH)
    field = field.reshape(count, npy, ly, npz, lz).transpose(1, 3, 0, 2, 4)
    return field.reshape(npy * npz * count, ly * lz)


def shards(
    solution,
    right_side,
    span_index,
    coef_table,
    xaxis_bands,
    yaxis_bands,
    zaxis_bands,
    xaxis_vectors,
    yaxis_vectors,
    zaxis_vectors,
    xaxis_values,
    yaxis_values,
    zaxis_values,
):
    npy, npz = lax.axis_size("py"), lax.axis_size("pz")
    ly, lz, nx = solution.shape
    ny, nz = npy * ly, npz * lz
    count, devices = ly * lz, npy * npz
    modes = nx // devices
    field = solution.reshape(count, nx)
    right = right_side.reshape(count, nx)
    block, zrim, yrim = (count, nx), (ly * REACH, nx), (up8(REACH * lz + 2 * REACH * REACH), nx)
    zrims = (2 * ly * REACH, nx)
    cell = count * nx * 4
    dma = pltpu.SemaphoreType.DMA

    points = point_columns(ly, lz)
    width = points.shape[1] // 2
    small = [jnp.asarray(points), *(array.transpose(1, 0, 2) for array in (yaxis_bands, zaxis_bands, xaxis_bands))]
    fast = (
        modes % 16 == 0 and npz % 2 == 0 and 2 * ly * REACH <= LANES // 2 and npy % 8 == 0 and lz % 16 == 0 and ly % 4 == 0
        and 2 * nz == LANES and 2 * ny == LANES and count == LANES and nx % LANES == 0
    )
    later = [xaxis_vectors, yaxis_vectors, zaxis_vectors, yaxis_values.reshape(1, ny), zaxis_values.reshape(1, nz)] * fast

    coef, weighted, even, odd, yodd, yeven, *small = call(
        lambda *refs: coefficient_kernel(ly, lz, len(small), *refs),
        [(block, F32)] * 2 + [(zrims, F32)] * 2 + [((REACH * lz + 16, nx), F32)] * 2
        + [(array.shape, array.dtype) for array in small],
        [HBM] * (3 + len(small)), count * nx * 16, 4 * cell,
        [pltpu.SMEM(coef_table.shape, F32), pltpu.VMEM(block, jnp.int32), pltpu.VMEM(block, F32)]
        + [dma((3 + len(small),))],
    )(*in_hbm(coef_table, span_index.reshape(count, nx), field, *small))

    *bands, xbands = small
    stencil, *held = call(
        lambda *refs: stencil_kernel(ly, lz, ny, nz, len(later), *refs),
        [((4 * count, width), BF16)] + [(array.shape, F32) for array in later],
        [VMEM] * 3 + [HBM] * len(later) + [ANY], count * width * 60, 8 * count * width,
        [dma((len(later),))] * fast,
    )(*bands, *in_hbm(*later), even)

    even, odd = pairwise(even, "pz", 0), odd_pairs(odd)
    zlow, zhigh, *corner = call(
        lambda *refs: y_rims_kernel(ly, *refs),
        [(zrims, F32)] * 2 + [((up8(2 * REACH * REACH), nx), F32)] * 2,
        [VMEM] * 2 + [ANY], nx, 4 * nx * 4 * zrims[0],
    )(odd, even, stencil)
    yodd, yeven = [yodd, corner[0]], [yeven, corner[1]]

    if fast:
        zmat, ymat, rmat = (npz * count // 2, ly * nz // 2), (ny, 3 * ny), (npz * LANES // 2, ly * nz)
        vectors, taps, *tables = call(
            lambda *refs: tables_kernel(npy, npz, ly, lz, *refs),
            [((2 * nx, nx), BF16), ((2 * (2 * REACH + 1), 8, nx), F32), ((ny, modes * nz), F32)]
            + [(zmat, BF16), (zmat, BF16), (ymat, BF16), (ymat, BF16), (rmat, BF16), (rmat, BF16)],
            [VMEM] * 6 + [HBM, ANY], npz * count * ly * nz * 8, npz * count * ly * nz * 4,
            [pltpu.SMEM((nx,), F32), dma((1,))],
        )(*held, xbands, *in_hbm(xaxis_values), corner[0])

        def precondition(received, rims):
            size = modes * 3 // 2 if rims else modes
            return call(
                lambda *refs: modes_kernel(npy, npz, rims, *refs),
                [((devices * size, count), F32)], [VMEM] * (8 if rims else 6), 6 * 2 * count * nx * ly * nz, 2 * cell,
                [pltpu.VMEM(((ly * nz // LANES * npy + 1) * (modes + 8), LANES), F32)],
            )(*(tables if rims else tables[:5]), received)[0]
    else:
        vectors, taps = call(
            xvectors_kernel, [((2 * nx, nx), BF16), ((2 * (2 * REACH + 1), 8, nx), F32)], [HBM, VMEM],
            nx * nx * 40, 8 * nx * nx, [pltpu.VMEM((nx, nx), F32), dma((1,))],
        )(*in_hbm(xaxis_vectors), xbands)
        tables = [taps]
        part = lax.axis_index(BOTH)
        xpart = lax.dynamic_slice_in_dim(xaxis_values, part * modes, modes)

        def precondition(received, rims):
            return plain_modes(
                received, npy, npz, ly, lz, xpart, yaxis_values, zaxis_values, yaxis_vectors, zaxis_vectors
            )

    for iteration in range(ITERS):
        last = iteration + 1 == ITERS
        yodd, yeven = [paired(value, "py") for value in yodd], [pairwise(value, "py", 0) for value in yeven]
        parts = len(yodd)
        if fast and iteration == 0:
            outward = call(
                lambda *refs: outward_kernel(ly, lz, nz, *refs),
                [((8 * REACH * lz, LANES), BF16)], [VMEM] * 3 + [ANY], 1 << 20, 1 << 18,
            )(bands[2], yodd[0], yeven[0], tables[0])[0]
        outs = [((nx, count), F32)] + [(block, F32)] * last
        scratch = [pltpu.VMEM(block, F32)] * (not last)
        cost = (6 * count * nx * (nx + 2 * width), 5 * cell + 4 * nx * nx)
        if fast and iteration > 0:
            applied = call(
                lambda *refs: own_part_kernel(lz, zrim[0], *refs), [(block, F32)], [VMEM] * 5, *cost,
            )(weighted, zlow, zhigh, stencil, taps)[0]
            spectral, *residual = call(joined_residual_kernel, outs, [VMEM] * 6, *cost, scratch)(
                applied, *yodd, *yeven, coef, right, vectors
            )
        else:
            spectral, *residual = call(
                lambda *refs: residual_kernel(lz, zrim[0], parts, *refs),
                outs, [VMEM] * (8 + 2 * parts) + [ANY], *cost, scratch,
            )(weighted, zlow, zhigh, *yodd, *yeven, stencil, taps, coef, right, vectors, outward if fast else tables[0])
        spectral = lax.all_to_all(spectral, BOTH, split_axis=0, concat_axis=0, tiled=True)
        spectral = precondition(spectral, not last)
        spectral = lax.all_to_all(spectral, BOTH, split_axis=0, concat_axis=0, tiled=True)
        cost = (6 * count * nx * nx, 4 * cell + 4 * nx * nx)
        if last:
            field, residual = call(
                last_update_kernel, [(block, F32), (block, F32)], [VMEM] * 4, *cost,
                [pltpu.VMEM(block, F32), dma((2,))], [HBM] * 2,
            )(spectral, vectors, field, *residual)
        elif fast:
            field, weighted, zlow, zhigh, *yrims = call(
                lambda *refs: rim_update_kernel(ly, lz, devices, *refs),
                [(block, F32)] * 2 + [(zrim, F32)] * 2 + [((REACH * lz, nx), F32)] * 2, [VMEM] * 8, *cost,
                [pltpu.VMEM((LANES, nx), F32)] * 2,
            )(spectral, vectors, field, coef, zlow, zhigh, outward, taps)
        else:
            field, weighted, zlow, zhigh = call(
                lambda *refs: update_kernel(ly, lz, *refs), [(block, F32)] * 2 + [(zrim, F32)] * 2, [VMEM] * 4, *cost,
            )(spectral, vectors, field, coef)
            zlow, zhigh = around(zhigh, "pz", 1), around(zlow, "pz", -1)
            yrims = call(
                lambda *refs: next_y_rims_kernel(ly, lz, *refs),
                [(yrim, F32)] * 2, [VMEM] * 3, nx, 4 * nx * 4 * yrim[0],
            )(weighted, zlow, zhigh)
        yodd, yeven = ([value] for value in yrims) if not last else (None, None)
    return (field.reshape(solution.shape), residual.reshape(solution.shape))


def solution(mesh):
    return jax.shard_map(
        shards,
        mesh=mesh,
        in_specs=(
            P("py", "pz", None),
            P("py", "pz", None),
            P("py", "pz", None),
            P(),
            P(),
            P(None, None, "py"),
            P(None, None, "pz"),
            P(),
            P(),
            P(),
            P(),
            P(),
            P(),
        ),
        out_specs=(P("py", "pz", None), P("py", "pz", None)),
        check_vma=False,
    )
```

```python
import jax
import jax.numpy as jnp
import numpy as np
from jax import lax
from jax.experimental import pallas as pl
from jax.experimental.pallas import tpu as pltpu
from jax.sharding import PartitionSpec as P

ITERS = 2
REACH = 3
LANES = 128
HIGH = lax.Precision.HIGHEST
BOTH = ("py", "pz")
F32 = jnp.float32
BF16 = jnp.bfloat16
VMEM = pl.BlockSpec(memory_space=pltpu.VMEM)
HBM = pl.BlockSpec(memory_space=pltpu.HBM)
ANY = pl.BlockSpec(memory_space=pl.ANY)


def up8(count):
    return -(-count // 8) * 8


def split(value):
    high = value.astype(BF16)
    return high, (value - high.astype(F32)).astype(BF16)


def exact(left, right, sides=(1, 0)):
    return lax.dot_general(
        left, right, (((sides[0],), (sides[1],)), ((), ())), precision=HIGH, preferred_element_type=F32
    )


def fetch(pairs, sem):
    copies = [pltpu.make_async_copy(source, target, sem.at[i]) for i, (source, target) in enumerate(pairs)]
    for copy in copies:
        copy.start()
    for copy in copies:
        copy.wait()


def in_hbm(*arrays):
    return [pltpu.with_memory_space_constraint(array, pltpu.HBM) for array in arrays]


def mul(left, right):
    return lax.dot_general(left, right, (((1,), (0,)), ((), ())), preferred_element_type=F32)


def mul_t(left, right):
    return lax.dot_general(left, right, (((1,), (1,)), ((), ())), preferred_element_type=F32)


def call(kernel, outs, specs, flops, cost_bytes, scratch=(), out_specs=None):
    return pl.pallas_call(
        kernel,
        out_shape=[jax.ShapeDtypeStruct(shape, dtype) for shape, dtype in outs],
        in_specs=specs,
        out_specs=out_specs or [VMEM] * len(outs),
        scratch_shapes=list(scratch),
        compiler_params=pltpu.CompilerParams(vmem_limit_bytes=32 * 1024 * 1024),
        cost_estimate=pl.CostEstimate(flops=flops, bytes_accessed=cost_bytes, transcendentals=0),
    )


def store_z_rims(ly, lz, weighted, low_ref, high_ref):
    for y in range(ly):
        low_ref[y * REACH : (y + 1) * REACH, :] = weighted[y * lz : y * lz + REACH, :]
        high_ref[y * REACH : (y + 1) * REACH, :] = weighted[(y + 1) * lz - REACH : (y + 1) * lz, :]


def coefficient_kernel(ly, lz, small, *refs):
    table_ref, span_ref, field_ref, *refs = refs
    sources, refs = refs[:small], refs[small:]
    coef_ref, weighted_ref, even_ref, odd_ref, yodd_ref, yeven_ref, *refs = refs
    targets, (table, span, field, sem) = refs[:small], refs[small:]
    fetch([(table_ref, table), (span_ref, span), (field_ref, field), *zip(sources, targets)], sem)
    first = lax.rem(lax.axis_index("pz"), 2) == 0
    half = ly * REACH
    entries = [table[entry] for entry in range(table_ref.shape[0])]
    for start in range(0, span.shape[0], lz):
        rows = pl.ds(start, lz)
        index = span[rows, :]
        coef = jnp.full(index.shape, entries[0], F32)
        for entry in range(1, len(entries)):
            coef = jnp.where(index == entry, entries[entry], coef)
        coef_ref[rows, :] = coef
        weighted = coef * field[rows, :]
        weighted_ref[rows, :] = weighted
        for value, at in ((weighted, 0), (coef, half)):
            rim = pl.ds(at + start // lz * REACH, REACH)
            low, high = value[:REACH], value[lz - REACH :]
            even_ref[rim, :] = jnp.where(first, high, low)
            odd_ref[rim, :] = jnp.where(first, low, high)
    store_y_rims(own_rim(ly, lz, weighted_ref), yodd_ref, yeven_ref)
    ybands = targets[1]
    for ref in (yodd_ref, yeven_ref):
        for matrix in range(2):
            at = REACH * lz + 8 * matrix
            ref[at : at + ybands.shape[0], :ly] = ybands[:, matrix, :]


def store_y_rims(pieces, odd_ref, even_ref):
    first = lax.rem(lax.axis_index("py"), 2) == 0
    at = 0
    for value, count, rows in pieces:
        low, high = value[:count, :], value[rows - count : rows, :]
        even_ref[at : at + count, :] = jnp.where(first, high, low)
        odd_ref[at : at + count, :] = jnp.where(first, low, high)
        at += count
    if at < even_ref.shape[0]:
        for ref in (even_ref, odd_ref):
            ref[at:, :] = jnp.zeros((ref.shape[0] - at, ref.shape[1]), F32)


def own_rim(ly, lz, weighted):
    return [(weighted, REACH * lz, ly * lz)]


def corners(ly, zlow, zhigh):
    return [(value, REACH * REACH, ly * REACH) for value in (zlow, zhigh)]


def y_rims_kernel(ly, odd_ref, even_ref, _, zlow_ref, zhigh_ref, yodd_ref, yeven_ref):
    first = lax.rem(lax.axis_index("pz"), 2) == 0
    zlow_ref[...] = jnp.where(first, odd_ref[...], even_ref[...])
    zhigh_ref[...] = jnp.where(first, even_ref[...], odd_ref[...])
    store_y_rims(corners(ly, zlow_ref, zhigh_ref), yodd_ref, yeven_ref)


def next_y_rims_kernel(ly, lz, weighted_ref, zlow_ref, zhigh_ref, yodd_ref, yeven_ref):
    store_y_rims(own_rim(ly, lz, weighted_ref) + corners(ly, zlow_ref, zhigh_ref), yodd_ref, yeven_ref)


def point_columns(ly, lz):
    below, above = range(-REACH, 0), range(REACH)
    halves = []
    for half in range(2):
        first = 0 if half == 0 else ly // 2 - REACH
        points = [(first + y, z) for y in range(ly // 2 + REACH) for z in range(lz)]
        points += [(y, z) for y in range(ly) for z in below]
        points += [(y, lz + z) for y in range(ly) for z in above]
        ys = below if half == 0 else [ly + y for y in above]
        points += [(y, z) for y in ys for z in range(lz)]
        points += [(y, z) for y in ys for z in below]
        points += [(y, lz + z) for y in ys for z in above]
        halves += points + [(1 << 20, 1 << 20)] * (-len(points) % LANES)
    return np.array(halves, np.int32).T.copy()


def stencil_kernel(ly, lz, ny, nz, later, points_ref, ybands_ref, zbands_ref, *refs):
    sources, (_, out_ref, *refs) = refs[:later], refs[later:]
    copies = [pltpu.make_async_copy(*pair, refs[-1].at[i]) for i, pair in enumerate(zip(sources, refs[:later]))]
    for copy in copies:
        copy.start()
    count = ly * lz // 2
    width = out_ref.shape[1]
    for half in range(2):
        rows = lax.broadcasted_iota(jnp.int32, (count, 1), 0) + half * count
        columns = pl.ds(half * width, width)
        factors = []
        for bands_ref, length, row, column, first, whole in (
            (ybands_ref, ly, lax.div(rows, lz), points_ref[0:1, columns], lax.axis_index("py") * ly, ny),
            (zbands_ref, lz, lax.rem(rows, lz), points_ref[1:2, columns], lax.axis_index("pz") * lz, nz),
        ):
            pick = (lax.broadcasted_iota(jnp.int32, (count, length), 1) == row).astype(F32)
            spot = column + first
            inside = (spot >= 0) & (spot < whole)
            distance = jnp.where(inside, column, 1 << 20) - row
            here = [distance == offset - REACH for offset in range(2 * REACH + 1)]
            for matrix in range(2):
                taps = exact(pick, bands_ref[:, matrix, :], (1, 1))
                dense = jnp.zeros(distance.shape, F32)
                for offset in range(2 * REACH + 1):
                    dense = jnp.where(here[offset], taps[:, offset : offset + 1], dense)
                factors.append(dense)
        ystiff, ymass, zstiff, zmass = factors
        for part, value in enumerate((ymass * zmass, ystiff * zmass + ymass * zstiff)):
            at = (4 * half + part) * count
            out_ref[at : at + count, :], out_ref[at + 2 * count : at + 3 * count, :] = split(value)
    for copy in copies:
        copy.wait()


def store_taps(xbands_ref, taps_ref):
    nx = xbands_ref.shape[2]
    lane = lax.broadcasted_iota(jnp.int32, (1, nx), 1)
    for offset in range(2 * REACH + 1):
        move = offset - REACH
        inside = (lane - move >= 0) & (lane - move < nx)
        for matrix in range(2):
            band = xbands_ref[offset, matrix : matrix + 1, :]
            band = pltpu.roll(band, move % nx, 1) if move else band
            taps_ref[2 * offset + matrix] = jnp.broadcast_to(jnp.where(inside, band, 0.0), (8, nx))


def doubled(size):
    row = lax.broadcasted_iota(jnp.int32, (size, 2 * size), 0)
    return (row == lax.rem(lax.broadcasted_iota(jnp.int32, (size, 2 * size), 1), size)).astype(F32)


def xvectors_kernel(source, xbands_ref, out_ref, taps_ref, held, sem):
    store_taps(xbands_ref, taps_ref)
    fetch(((source, held),), sem)
    high, low = split(held[...].T)
    out_ref[: high.shape[0], :] = high
    out_ref[high.shape[0] :, :] = low


def tables_kernel(
    npy, npz, ly, lz, xvec_ref, yvec_ref, zvec_ref, yval_ref, zval_ref, xbands_ref, xval_hbm, _,
    xout_ref, taps_ref, sums_ref, zhigh_ref, zlow_ref, ydown_ref, yup_ref, rimhigh_ref, rimlow_ref, xval_ref, sem,
):
    fetching = pltpu.make_async_copy(xval_hbm, xval_ref, sem.at[0])
    fetching.start()
    store_taps(xbands_ref, taps_ref)
    ny, nz = npy * ly, npz * lz
    nx = xvec_ref.shape[0]
    high, low = split(xvec_ref[...].T)
    xout_ref[:nx, :] = high
    xout_ref[nx:, :] = low
    pair = exact(zvec_ref[...], doubled(nz))
    half = lax.broadcasted_iota(jnp.int32, pair.shape, 1) >= nz
    zhigh_ref[...] = jnp.zeros(zhigh_ref.shape, BF16)
    zlow_ref[...] = jnp.zeros(zlow_ref.shape, BF16)
    for parity in range(2):
        high, low = split(jnp.where(half == (parity == 1), pair, 0.0))
        for yl in range(parity, ly // 2, 2):
            for block in range(npz):
                to = (pl.ds((block * ly // 2 + yl) * lz, lz), pl.ds(yl // 2 * 2 * nz, 2 * nz))
                zhigh_ref[to] = high[block * lz : (block + 1) * lz, :]
                zlow_ref[to] = low[block * lz : (block + 1) * lz, :]
    shape = (rimhigh_ref.shape[0], 1)
    row = lax.broadcasted_iota(jnp.int32, shape, 0)
    block, spot = lax.div(row, LANES // 2), lax.rem(row, LANES // 2)
    above = spot >= ly * REACH
    spot = jnp.where(above, spot - ly * REACH, spot)
    yrow = jnp.where(spot < ly * REACH, lax.div(spot, REACH), 2 * ly)
    z = block * lz + lax.rem(spot, REACH) + jnp.where(above, lz, -REACH)
    rim = exact((lax.broadcasted_iota(jnp.int32, (shape[0], nz), 1) == z).astype(F32), pair)
    late = (lax.broadcasted_iota(jnp.int32, rim.shape, 1) >= nz).astype(jnp.int32)
    for chunk in range(ly // 2):
        columns = pl.ds(chunk * 2 * nz, 2 * nz)
        rimhigh_ref[:, columns], rimlow_ref[:, columns] = split(jnp.where(yrow - 2 * chunk == late, rim, 0.0))

    def y_of(p):
        spot = lax.div(p, npy)
        return lax.rem(p, npy) * ly + 2 * lax.rem(spot, ly // 2) + lax.div(spot, ly // 2)

    def parts(array):
        high, low = split(array)
        late = lax.broadcasted_iota(jnp.int32, array.shape, 1) >= 2 * ny
        return jnp.where(late, low.astype(F32), high.astype(F32)).astype(BF16)

    lane = lax.broadcasted_iota(jnp.int32, (ny, 3 * ny), 1)
    row = lax.broadcasted_iota(jnp.int32, (ny, 3 * ny), 0)
    moved = (row == y_of(lax.rem(lane, ny))).astype(F32)
    ydown_ref[...] = parts(exact(yvec_ref[...].T, moved))
    order = (
        lax.broadcasted_iota(jnp.int32, (ny, ny), 1) == y_of(lax.broadcasted_iota(jnp.int32, (ny, ny), 0))
    ).astype(F32)
    copies = (row == lax.rem(lane, ny)).astype(F32)
    yup_ref[...] = parts(exact(exact(order, yvec_ref[...]), copies))
    fetching.wait()
    square = (ny, ny)
    diagonal = lax.broadcasted_iota(jnp.int32, square, 0) == lax.broadcasted_iota(jnp.int32, square, 1)
    ycolumn = jnp.sum(jnp.where(diagonal, yval_ref[...], 0.0), axis=1, keepdims=True)
    yz = ycolumn + exact(jnp.broadcast_to(zval_ref[...], (8, nz)), doubled(nz))[0:1]
    late = lax.broadcasted_iota(jnp.int32, (1, 2 * nz), 1) >= nz
    modes = sums_ref.shape[1] // nz
    first = (lax.axis_index("py") * (nz // lz) + lax.axis_index("pz")) * modes
    for mode in range(0, modes, 2):
        x = jnp.where(late, xval_ref[first + mode + 1], xval_ref[first + mode])
        sums_ref[:, mode * nz : (mode + 2) * nz] = yz + x


def y_sides(odd, even):
    first = lax.rem(lax.axis_index("py"), 2) == 0
    return jnp.where(first, odd, even), jnp.where(first, even, odd)


def three_products(matrix, high, low):
    rows = matrix.shape[0] // 2
    both = mul(matrix, high)
    return both[:rows] + both[rows:] + mul(matrix[:rows], low)


def yz_fields(lz, zrim, weighted_ref, zlow_ref, zhigh_ref, sides, stencil_ref):
    count, nx = weighted_ref.shape
    part, need = count // 2, count // 2 + REACH * lz
    own = split(weighted_ref[...])
    zrims = split(jnp.concatenate([zlow_ref[:zrim, :], zhigh_ref[:zrim, :]], axis=0))
    left = stencil_ref.shape[1] - need - 2 * zrim
    fields = []
    for half in range(2):
        if sides is None:
            yrim = [jnp.zeros((left, nx), BF16)] * 2
        else:
            rim = sides[half]
            missing = left - rim.shape[0]
            yrim = split(jnp.concatenate([rim, jnp.zeros((missing, nx), F32)], axis=0) if missing else rim)
        first = half * (count - need)
        high, low = (
            jnp.concatenate([own[k][first : first + need], zrims[k], yrim[k]], axis=0) for k in range(2)
        )
        both = three_products(stencil_ref[4 * half * part : 4 * (half + 1) * part, :], high, low)
        fields.append((both[:part], both[part:]))
    return fields


def x_banded(taps_ref, mass, stiff):
    nx = mass.shape[1]
    applied = None
    for offset in range(2 * REACH + 1):
        move = offset - REACH
        term = taps_ref[2 * offset] * mass + taps_ref[2 * offset + 1] * stiff
        term = pltpu.roll(term, -move % nx, 1) if move else term
        applied = term if applied is None else applied + term
    return applied


def store_modes(points, vectors_ref, spectral_ref):
    count, nx = points.shape
    high, low = split(points)
    product = mul_t(jnp.concatenate([high, low], axis=0), vectors_ref[:nx, :])
    spectral_ref[...] = (product[:count] + product[count:] + mul_t(high, vectors_ref[nx:, :])).T


def residual_kernel(lz, zrim, parts, *refs):
    weighted_ref, zlow_ref, zhigh_ref, *refs = refs
    yodd_refs, yeven_refs, refs = refs[:parts], refs[parts : 2 * parts], refs[2 * parts :]
    stencil_ref, taps_ref, coef_ref, right_ref, vectors_ref, _, spectral_ref, residual_ref = refs
    if parts == 2:
        (yodd_ref, odd_corner_ref), (yeven_ref, even_corner_ref) = yodd_refs, yeven_refs
        own = REACH * lz
        yodd = jnp.concatenate([yodd_ref[:own, :], odd_corner_ref[...]], axis=0)
        yeven = jnp.concatenate([yeven_ref[:own, :], even_corner_ref[...]], axis=0)
    else:
        yodd, yeven = yodd_refs[0][...], yeven_refs[0][...]
    fields = yz_fields(lz, zrim, weighted_ref, zlow_ref, zhigh_ref, y_sides(yodd, yeven), stencil_ref)
    part = weighted_ref.shape[0] // 2
    for start in range(0, 2 * part, 8):
        mass, stiff = (field[start % part : start % part + 8] for field in fields[start // part])
        rows = pl.ds(start, 8)
        residual_ref[rows, :] = right_ref[rows, :] - coef_ref[rows, :] * x_banded(taps_ref, mass, stiff)
    store_modes(residual_ref[...], vectors_ref, spectral_ref)


def own_part_kernel(lz, zrim, weighted_ref, zlow_ref, zhigh_ref, stencil_ref, taps_ref, applied_ref):
    fields = yz_fields(lz, zrim, weighted_ref, zlow_ref, zhigh_ref, None, stencil_ref)
    part = weighted_ref.shape[0] // 2
    for start in range(0, 2 * part, 8):
        mass, stiff = (field[start % part : start % part + 8] for field in fields[start // part])
        applied_ref[pl.ds(start, 8), :] = x_banded(taps_ref, mass, stiff)


def joined_residual_kernel(applied_ref, yodd_ref, yeven_ref, coef_ref, right_ref, vectors_ref, spectral_ref, residual_ref):
    count, rim = applied_ref.shape[0], yodd_ref.shape[0]
    for at, side in zip((0, count - rim), y_sides(yodd_ref[...], yeven_ref[...])):
        rows = pl.ds(at, rim)
        residual_ref[rows, :] = right_ref[rows, :] - coef_ref[rows, :] * (applied_ref[rows, :] + side)
    rows = pl.ds(rim, count - 2 * rim)
    residual_ref[rows, :] = right_ref[rows, :] - coef_ref[rows, :] * applied_ref[rows, :]
    store_modes(residual_ref[...], vectors_ref, spectral_ref)


def outward_kernel(ly, lz, nz, zbands_ref, yodd_ref, yeven_ref, _, out_ref):
    rim, side = REACH * lz, REACH * REACH
    width = out_ref.shape[1]
    row = lax.broadcasted_iota(jnp.int32, (rim, 1), 0)
    column = lax.broadcasted_iota(jnp.int32, (1, width), 1)
    spot = jnp.where(column < rim + side, column - rim, column - rim - side)
    yin = jnp.where(column < rim, lax.div(column, lz), lax.div(spot, REACH))
    zin = jnp.where(
        column < rim, lax.rem(column, lz), lax.rem(spot, REACH) + jnp.where(column < rim + side, -REACH, lz)
    )
    place = zin + lax.axis_index("pz") * lz
    inside = (column < rim + 2 * side) & (place >= 0) & (place < nz)
    yout, zout = lax.div(row, lz), lax.rem(row, lz)

    def dense(taps, tap):
        value = jnp.zeros(tap.shape, F32)
        for k in range(2 * REACH + 1):
            value = jnp.where(tap == k, taps[:, k : k + 1], value)
        return value

    def picked(length, at, bands):
        return exact((lax.broadcasted_iota(jnp.int32, (rim, length), 1) == at).astype(F32), bands, (1, 1))

    ztap = jnp.where(inside, zin - zout + REACH, -1)
    zstiff, zmass = (dense(picked(lz, zout, zbands_ref[:, matrix, :]), ztap) for matrix in range(2))
    sides = y_sides(yodd_ref[rim : rim + 16, :ly], yeven_ref[rim : rim + 16, :ly])
    spot, count = lax.axis_index("py"), lax.axis_size("py")
    for k, (bands, at, shift, there) in enumerate(
        ((sides[0], yout + ly - REACH, 2 * REACH, spot > 0), (sides[1], yout, 0, spot < count - 1))
    ):
        ytap = jnp.where(there, yin - yout + shift, -1)
        ystiff, ymass = (dense(picked(ly, at, bands[8 * matrix : 8 * matrix + 8]), ytap) for matrix in range(2))
        for part, value in enumerate((ymass * zmass, ystiff * zmass + ymass * zstiff)):
            start = (4 * k + part) * rim
            out_ref[start : start + rim, :], out_ref[start + 2 * rim : start + 3 * rim, :] = split(value)


def modes_kernel(npy, npz, rims, *refs):
    sums_ref, zhigh_ref, zlow_ref, ydown_ref, yup_ref, *rim_refs, in_ref, out_ref, turn_ref = refs
    count = in_ref.shape[0] // (npy * npz)
    size = out_ref.shape[0] // (npy * npz)
    nz = sums_ref.shape[1] // count
    width = zhigh_ref.shape[1]
    chunks = 2 * width // LANES
    step = turn_ref.shape[0] // (npy * chunks)
    zhigh, zlow = zhigh_ref[...], zlow_ref[...]

    def three(value, product, whigh, wlow):
        rows = value.shape[0]
        high, low = split(value)
        both = product(jnp.concatenate([high, low], axis=0), whigh)
        return both[:rows] + both[rows:] + product(high, wlow)

    def early(first, second):
        late = lax.broadcasted_iota(jnp.int32, first.shape, 1) >= LANES // 2
        return jnp.where(late, pltpu.roll(second, LANES // 2, 1), first)

    def later(first, second):
        late = lax.broadcasted_iota(jnp.int32, first.shape, 1) >= LANES // 2
        return jnp.where(late, second, pltpu.roll(first, LANES // 2, 1))

    def by_mode(mode, chunk):
        return pl.ds(chunk * npy * step + mode, npy, stride=step)

    def by_device(device, chunk):
        return pl.ds((chunk * npy + device) * step, count)

    halves = [[], []]
    for p in range(npy):
        blocks = [in_ref[(p * npz + b) * count : (p * npz + b + 1) * count, :] for b in range(npz)]
        for half, joined in zip(halves, (early, later)):
            half.append(jnp.concatenate([joined(blocks[b], blocks[b + 1]) for b in range(0, npz, 2)], axis=1))
    part = three(jnp.concatenate(halves[0] + halves[1], axis=0), mul, zhigh, zlow)
    for chunk in range(chunks):
        half, lane = divmod(chunk * LANES, width)
        for p in range(npy):
            row = (half * npy + p) * count
            turn_ref[by_device(p, chunk), :] = part[row : row + count, lane : lane + LANES]
    pairs = []
    for mode in range(0, count, 2):
        tiles = [(turn_ref[by_mode(mode, c), :], turn_ref[by_mode(mode + 1, c), :]) for c in range(chunks)]
        pairs.append(jnp.concatenate([early(*tile) for tile in tiles] + [later(*tile) for tile in tiles], axis=0))
    stacked = jnp.concatenate(pairs, axis=1)

    def stack(value):
        high, low = split(value)
        return jnp.concatenate([high, low, high], axis=0)

    modes = mul(ydown_ref[...], stack(stacked)) / sums_ref[...]
    restored = mul(yup_ref[...], stack(modes))
    for mode in range(0, count, 2):
        block = restored[:, mode * nz : (mode + 2) * nz]
        for c in range(chunks):
            even = block[c * npy : (c + 1) * npy]
            odd = block[(chunks + c) * npy : (chunks + c + 1) * npy]
            turn_ref[by_mode(mode, c), :] = early(even, odd)
            turn_ref[by_mode(mode + 1, c), :] = later(even, odd)
    rows = [
        jnp.concatenate(
            [turn_ref[by_device(p, half * chunks // 2 + c), :] for c in range(chunks // 2)], axis=1
        )
        for half in range(2)
        for p in range(npy)
    ]
    spectral = jnp.concatenate(rows, axis=0)
    back = three(spectral, mul_t, zhigh, zlow)
    total = npy * count
    if rims:
        side = [
            three(
                spectral[half * total : (half + 1) * total], mul_t,
                *(ref[:, pl.ds(half * width, width)] for ref in rim_refs),
            )
            for half in range(2)
        ]
        side = side[0] + side[1]
    for p in range(npy):
        for b in range(0, npz, 2):
            first, second = (
                back[k * total + p * count : k * total + (p + 1) * count, b * LANES // 2 : b * LANES // 2 + LANES]
                for k in range(2)
            )
            at = (p * npz + b) * size
            out_ref[at : at + count, :] = early(first, second)
            out_ref[at + size : at + size + count, :] = later(first, second)
            if rims:
                row, middle = p * count, p * count + count // 2
                first = side[row:middle, b * LANES // 2 : b * LANES // 2 + LANES]
                second = side[middle : row + count, b * LANES // 2 : b * LANES // 2 + LANES]
                out_ref[at + count : at + size, :] = early(first, second)
                out_ref[at + size + count : at + 2 * size, :] = later(first, second)


def transformed(points, vectors_ref):
    rows, nx = points.shape
    high, low = split(points)
    both = mul(jnp.concatenate([high, low], axis=0), vectors_ref[:nx, :])
    return both[:rows] + both[rows:] + mul(high, vectors_ref[nx:, :])


def from_modes(spectral_ref, vectors_ref):
    return transformed(spectral_ref[...].T, vectors_ref)


def update_kernel(ly, lz, spectral_ref, vectors_ref, field_ref, coef_ref, updated_ref, weighted_ref, low_ref, high_ref):
    updated = field_ref[...] + from_modes(spectral_ref, vectors_ref)
    updated_ref[...] = updated
    weighted = coef_ref[...] * updated
    weighted_ref[...] = weighted
    store_z_rims(ly, lz, weighted, low_ref, high_ref)


def rim_update_kernel(
    ly, lz, devices, spectral_ref, vectors_ref, field_ref, coef_ref, before_low_ref, before_high_ref,
    outward_ref, taps_ref, updated_ref, weighted_ref, zlow_ref, zhigh_ref, yodd_ref, yeven_ref, below_ref, above_ref,
):
    nx = vectors_ref.shape[1]
    modes = nx // devices
    size = spectral_ref.shape[0] // devices
    own, rims = [], []
    for d in range(devices):
        own.append(spectral_ref[d * size : d * size + modes, :])
        rim = spectral_ref[d * size + modes : (d + 1) * size, :]
        rims += [rim, pltpu.roll(rim, LANES // 2, 1)]
    points = [jnp.concatenate(own, axis=0).T, jnp.concatenate(rims, axis=0).T[: LANES // 2]]
    update = transformed(jnp.concatenate(points, axis=0), vectors_ref)
    count, half = ly * lz, ly * REACH
    updated = field_ref[...] + update[:count]
    updated_ref[...] = updated
    weighted_ref[...] = coef_ref[...] * updated
    for side, (ref, before_ref) in enumerate(((zlow_ref, before_low_ref), (zhigh_ref, before_high_ref))):
        start = count + side * half
        ref[...] = before_ref[:half, :] + before_ref[half:, :] * update[start : start + half]
    at = 0
    for value, rows, whole in own_rim(ly, lz, weighted_ref) + corners(ly, zlow_ref, zhigh_ref):
        below_ref[at : at + rows, :] = value[:rows, :]
        above_ref[at : at + rows, :] = value[whole - rows : whole, :]
        at += rows
    rim, adds = yodd_ref.shape[0], []
    for k, ref in enumerate((below_ref, above_ref)):
        ref[at:, :] = jnp.zeros((ref.shape[0] - at, nx), F32)
        both = three_products(outward_ref[4 * k * rim : 4 * (k + 1) * rim, :], *split(ref[...]))
        adds.append((both[:rim], both[rim:]))
    first = lax.rem(lax.axis_index("py"), 2) == 0
    for start in range(0, rim, 8):
        below, above = (x_banded(taps_ref, *(field[start : start + 8] for field in fields)) for fields in adds)
        yodd_ref[start : start + 8, :] = jnp.where(first, below, above)
        yeven_ref[start : start + 8, :] = jnp.where(first, above, below)


def last_update_kernel(spectral_ref, vectors_ref, field_ref, residual_ref, updated_hbm, residual_hbm, held, sem):
    leaving = pltpu.make_async_copy(residual_ref, residual_hbm, sem.at[0])
    leaving.start()
    held[...] = field_ref[...] + from_modes(spectral_ref, vectors_ref)
    fetch(((held, updated_hbm),), sem.at[pl.ds(1, 1)])
    leaving.wait()


def pairwise(value, axis, odd):
    count = lax.axis_size(axis)
    other = [((i + odd) ^ 1) - odd for i in range(count)]
    return lax.ppermute(value, axis, [(i, j if 0 <= j < count else i) for i, j in enumerate(other)])


def paired(value, near):
    across, count = lax.axis_size("py"), lax.axis_size("pz")
    pairs = []
    for i in range(across):
        for k in range(count):
            j = i + 1 if i % 2 else i - 1
            end = i * count + (k ^ 1) if near and k ^ 1 < count else j % across * count + k
            pairs.append((i * count + k, j * count + k if 0 <= j < across else end))
    return lax.ppermute(value, BOTH, pairs)


def odd_pairs(value):
    across, count = lax.axis_size("py"), lax.axis_size("pz")
    pairs = []
    for i in range(across):
        for k in range(count):
            j = k + 1 if k % 2 else k - 1
            pairs.append((i * count + k, i * count + j if 0 <= j < count else (i ^ 1) * count + k))
    return lax.ppermute(value, BOTH, pairs)


def around(value, axis, step):
    count = lax.axis_size(axis)
    return lax.ppermute(value, axis, [(i, (i + step) % count) for i in range(count)])


def plain_modes(received, npy, npz, ly, lz, xvalues, yvalues, zvalues, yvectors, zvectors):
    count = received.shape[0] // (npy * npz)
    field = received.reshape(npy, npz, count, ly, lz).transpose(2, 0, 3, 1, 4).reshape(count, npy * ly, npz * lz)
    field = jnp.einsum("xyz,yj->xjz", field, yvectors, precision=HIGH)
    field = jnp.einsum("xyz,zk->xyk", field, zvectors, precision=HIGH)
    field = field / (yvalues[None, :, None] + zvalues[None, None, :] + xvalues[:, None, None])
    field = jnp.einsum("xjz,yj->xyz", field, yvectors, precision=HIGH)
    field = jnp.einsum("xyk,zk->xyz", field, zvectors, precision=HIGH)
    field = field.reshape(count, npy, ly, npz, lz).transpose(1, 3, 0, 2, 4)
    return field.reshape(npy * npz * count, ly * lz)


def shards(
    solution,
    right_side,
    span_index,
    coef_table,
    xaxis_bands,
    yaxis_bands,
    zaxis_bands,
    xaxis_vectors,
    yaxis_vectors,
    zaxis_vectors,
    xaxis_values,
    yaxis_values,
    zaxis_values,
):
    npy, npz = lax.axis_size("py"), lax.axis_size("pz")
    ly, lz, nx = solution.shape
    ny, nz = npy * ly, npz * lz
    count, devices = ly * lz, npy * npz
    modes = nx // devices
    field = solution.reshape(count, nx)
    right = right_side.reshape(count, nx)
    block, zrim, yrim = (count, nx), (ly * REACH, nx), (up8(REACH * lz + 2 * REACH * REACH), nx)
    zrims = (2 * ly * REACH, nx)
    cell = count * nx * 4
    dma = pltpu.SemaphoreType.DMA

    points = point_columns(ly, lz)
    width = points.shape[1] // 2
    small = [jnp.asarray(points), *(array.transpose(1, 0, 2) for array in (yaxis_bands, zaxis_bands, xaxis_bands))]
    fast = (
        modes % 16 == 0 and npz % 2 == 0 and 2 * ly * REACH <= LANES // 2 and npy % 8 == 0 and lz % 16 == 0 and ly % 4 == 0
        and 2 * nz == LANES and 2 * ny == LANES and count == LANES and nx % LANES == 0
    )
    later = [xaxis_vectors, yaxis_vectors, zaxis_vectors, yaxis_values.reshape(1, ny), zaxis_values.reshape(1, nz)] * fast

    coef, weighted, even, odd, yodd, yeven, *small = call(
        lambda *refs: coefficient_kernel(ly, lz, len(small), *refs),
        [(block, F32)] * 2 + [(zrims, F32)] * 2 + [((REACH * lz + 16, nx), F32)] * 2
        + [(array.shape, array.dtype) for array in small],
        [HBM] * (3 + len(small)), count * nx * 16, 4 * cell,
        [pltpu.SMEM(coef_table.shape, F32), pltpu.VMEM(block, jnp.int32), pltpu.VMEM(block, F32)]
        + [dma((3 + len(small),))],
    )(*in_hbm(coef_table, span_index.reshape(count, nx), field, *small))

    *bands, xbands = small
    stencil, *held = call(
        lambda *refs: stencil_kernel(ly, lz, ny, nz, len(later), *refs),
        [((4 * count, width), BF16)] + [(array.shape, F32) for array in later],
        [VMEM] * 3 + [HBM] * len(later) + [ANY], count * width * 60, 8 * count * width,
        [dma((len(later),))] * fast,
    )(*bands, *in_hbm(*later), even)

    even, odd = pairwise(even, "pz", 0), odd_pairs(odd)
    zlow, zhigh, *corner = call(
        lambda *refs: y_rims_kernel(ly, *refs),
        [(zrims, F32)] * 2 + [((up8(2 * REACH * REACH), nx), F32)] * 2,
        [VMEM] * 2 + [ANY], nx, 4 * nx * 4 * zrims[0],
    )(odd, even, stencil)
    yodd, yeven = [yodd, corner[0]], [yeven, corner[1]]

    if fast:
        zmat, ymat, rmat = (npz * count // 2, ly * nz // 2), (ny, 3 * ny), (npz * LANES // 2, ly * nz)
        vectors, taps, *tables = call(
            lambda *refs: tables_kernel(npy, npz, ly, lz, *refs),
            [((2 * nx, nx), BF16), ((2 * (2 * REACH + 1), 8, nx), F32), ((ny, modes * nz), F32)]
            + [(zmat, BF16), (zmat, BF16), (ymat, BF16), (ymat, BF16), (rmat, BF16), (rmat, BF16)],
            [VMEM] * 6 + [HBM, ANY], npz * count * ly * nz * 8, npz * count * ly * nz * 4,
            [pltpu.SMEM((nx,), F32), dma((1,))],
        )(*held, xbands, *in_hbm(xaxis_values), corner[0])

        def precondition(received, rims):
            size = modes * 3 // 2 if rims else modes
            return call(
                lambda *refs: modes_kernel(npy, npz, rims, *refs),
                [((devices * size, count), F32)], [VMEM] * (8 if rims else 6), 6 * 2 * count * nx * ly * nz, 2 * cell,
                [pltpu.VMEM(((ly * nz // LANES * npy + 1) * (modes + 8), LANES), F32)],
            )(*(tables if rims else tables[:5]), received)[0]
    else:
        vectors, taps = call(
            xvectors_kernel, [((2 * nx, nx), BF16), ((2 * (2 * REACH + 1), 8, nx), F32)], [HBM, VMEM],
            nx * nx * 40, 8 * nx * nx, [pltpu.VMEM((nx, nx), F32), dma((1,))],
        )(*in_hbm(xaxis_vectors), xbands)
        tables = [taps]
        part = lax.axis_index(BOTH)
        xpart = lax.dynamic_slice_in_dim(xaxis_values, part * modes, modes)

        def precondition(received, rims):
            return plain_modes(
                received, npy, npz, ly, lz, xpart, yaxis_values, zaxis_values, yaxis_vectors, zaxis_vectors
            )

    for iteration in range(ITERS):
        last = iteration + 1 == ITERS
        yodd, yeven = [paired(value, k > 0) for k, value in enumerate(yodd)], [pairwise(value, "py", 0) for value in yeven]
        parts = len(yodd)
        if fast and iteration == 0:
            outward = call(
                lambda *refs: outward_kernel(ly, lz, nz, *refs),
                [((8 * REACH * lz, LANES), BF16)], [VMEM] * 3 + [ANY], 1 << 20, 1 << 18,
            )(bands[2], yodd[0], yeven[0], tables[0])[0]
        outs = [((nx, count), F32)] + [(block, F32)] * last
        scratch = [pltpu.VMEM(block, F32)] * (not last)
        cost = (6 * count * nx * (nx + 2 * width), 5 * cell + 4 * nx * nx)
        if fast and iteration > 0:
            applied = call(
                lambda *refs: own_part_kernel(lz, zrim[0], *refs), [(block, F32)], [VMEM] * 5, *cost,
            )(weighted, zlow, zhigh, stencil, taps)[0]
            spectral, *residual = call(joined_residual_kernel, outs, [VMEM] * 6, *cost, scratch)(
                applied, *yodd, *yeven, coef, right, vectors
            )
        else:
            spectral, *residual = call(
                lambda *refs: residual_kernel(lz, zrim[0], parts, *refs),
                outs, [VMEM] * (8 + 2 * parts) + [ANY], *cost, scratch,
            )(weighted, zlow, zhigh, *yodd, *yeven, stencil, taps, coef, right, vectors, outward if fast else tables[0])
        spectral = lax.all_to_all(spectral, BOTH, split_axis=0, concat_axis=0, tiled=True)
        spectral = precondition(spectral, not last)
        spectral = lax.all_to_all(spectral, BOTH, split_axis=0, concat_axis=0, tiled=True)
        cost = (6 * count * nx * nx, 4 * cell + 4 * nx * nx)
        if last:
            field, residual = call(
                last_update_kernel, [(block, F32), (block, F32)], [VMEM] * 4, *cost,
                [pltpu.VMEM(block, F32), dma((2,))], [HBM] * 2,
            )(spectral, vectors, field, *residual)
        elif fast:
            field, weighted, zlow, zhigh, *yrims = call(
                lambda *refs: rim_update_kernel(ly, lz, devices, *refs),
                [(block, F32)] * 2 + [(zrim, F32)] * 2 + [((REACH * lz, nx), F32)] * 2, [VMEM] * 8, *cost,
                [pltpu.VMEM((LANES, nx), F32)] * 2,
            )(spectral, vectors, field, coef, zlow, zhigh, outward, taps)
        else:
            field, weighted, zlow, zhigh = call(
                lambda *refs: update_kernel(ly, lz, *refs), [(block, F32)] * 2 + [(zrim, F32)] * 2, [VMEM] * 4, *cost,
            )(spectral, vectors, field, coef)
            zlow, zhigh = around(zhigh, "pz", 1), around(zlow, "pz", -1)
            yrims = call(
                lambda *refs: next_y_rims_kernel(ly, lz, *refs),
                [(yrim, F32)] * 2, [VMEM] * 3, nx, 4 * nx * 4 * yrim[0],
            )(weighted, zlow, zhigh)
        yodd, yeven = ([value] for value in yrims) if not last else (None, None)
    return (field.reshape(solution.shape), residual.reshape(solution.shape))


def solution(mesh):
    return jax.shard_map(
        shards,
        mesh=mesh,
        in_specs=(
            P("py", "pz", None),
            P("py", "pz", None),
            P("py", "pz", None),
            P(),
            P(),
            P(None, None, "py"),
            P(None, None, "pz"),
            P(),
            P(),
            P(),
            P(),
            P(),
            P(),
        ),
        out_specs=(P("py", "pz", None), P("py", "pz", None)),
        check_vma=False,
    )
```
